32 devices in a mesh: row: 4 (over z), col: 8 (over y, x, core).
Axes of the slice: x: 2, y: 2, z: 4, core: 2. Of those that a mesh axis runs over, the one named last changes fastest.
Arguments:
- token_ids: int32 [32, 1024], P(('row', 'col')), may hold values from 0 to 32783
- segment_ids: int32 [32, 1024], P(('row', 'col')), may hold values from 0 to 7, never falling along the last dimension, each value on 1 to 512 neighbouring positions
- loss_positions: int32 [32, 64], P(('row', 'col')), may hold values from 0 to 1023
- loss_targets: int32 [32, 64], P(('row', 'col')), may hold values from 0 to 32783
- loss_valid: int32 [32, 64], P(('row', 'col')), may hold values 0 or 1
- block_owner: int32 [48], replicated, may hold values from 0 to 47, each once
- step_count: int32 [1], replicated, may hold values from 1 to 20
- block_weights: float32 [48, 1024, 256], P('col', 'row'), may hold values from -0.1875 to 0.1875
- block_first: float32 [48, 1024, 256], P('col', 'row'), may hold values from -0.00015258789 to 0.00015258789
- block_second: float32 [48, 1024, 256], P('col', 'row'), may hold values from 1e-11 to 1e-09
- left_basis: float32 [48, 1024, 1024], P('col', 'row'), may hold values from -0.1875 to 0.1875
- right_basis: float32 [48, 256, 256], P('col'), may hold values from -0.375 to 0.375
- table: float32 [32784, 1024], P('col', 'row'), may hold values from -0.6875 to 0.6875
- table_first: float32 [32784, 1024], P('col', 'row'), may hold values from -0.00015258789 to 0.00015258789
- table_second: float32 [32784, 1024], P('col', 'row'), may hold values from 1e-11 to 1e-09
- vector_params: float32 [38216], replicated, may hold values from -7 to 3, as said below
- vector_first: float32 [38216], replicated, may hold values from -0.0014648438 to 0.0014648438
- vector_second: float32 [38216], replicated, may hold values from 1e-09 to 1e-07
Outputs:
- mean_loss: float32 [], replicated
- grad_norm: float32 [], replicated
- new_blocks: float32 [48, 1024, 256], P('col', 'row')
- new_block_first: float32 [48, 1024, 256], P('col', 'row')
- new_block_second: float32 [48, 1024, 256], P('col', 'row')
- new_table: float32 [32784, 1024], P('col', 'row')
- new_table_first: float32 [32784, 1024], P('col', 'row')
- new_table_second: float32 [32784, 1024], P('col', 'row')
- new_vectors: float32 [38216], replicated
- new_vector_first: float32 [38216], replicated
- new_vector_second: float32 [38216], replicated
The draws below stay inside these ranges and needn't reach their ends.
Inputs may be any that keep to these rules, and one draw needn't show every extreme that they name: `segment_ids`: in each sequence the document number starts at 0, never falls and steps by one; each of the 8 documents holds 1 to 512 positions, one exactly 512. `block_owner`: A permutation of the slots. `vector_params`: Time-step biases are softplus inverses of values in 0.001 to 0.1; decay logarithms lie in 0 to log 16; gains lie in 0.5 to 1.5.
All inputs are finite; a program needn't handle non-finite values. No bound on the sum of `loss_valid` on one device may be relied on, other than what follows from the above.
Results may differ from the reference program's by a relative error of at most 0.013.
The reference program's roundings to bfloat16 on the way count: a program that leaves them out, or rounds other values in their place, can miss the bound.
Values may be sent and summed in bfloat16 or wider, within the bound.
A program may use at most 384 MiB of HBM per device.

```python
import math
import jax
import jax.numpy as jnp
import numpy as np
from jax import lax

D = 1024
HEADS = 8
KV_HEADS = 2
HEAD_DIM = 64
SSM_HEADS = 24
SSM_HEAD_DIM = 64
STATE = 128
CONV = 4
FF = 2048
VOCAB = 32784
BLOCK_COLS = 256
SEQ = 1024
COUNT = 64
DOCS = 8
SSM_INNER = 1536
XBC_WIDTH = 1792
NBLK = 48
NVEC = 38216
SPAN = 256
QBLOCK = 512
SEQS = 32


def draw_vector_params(key, part):
    subkeys = jax.random.split(key, 8)
    conv_weight = jnp.clip(jax.random.normal(subkeys[0], (CONV * XBC_WIDTH,), jnp.float32), -3.0, 3.0) * 0.5
    time_proj = jnp.clip(jax.random.normal(subkeys[7], (D * SSM_HEADS,), jnp.float32), -4.0, 4.0) / math.sqrt(D)
    conv_bias = jnp.clip(jax.random.normal(subkeys[1], (XBC_WIDTH,), jnp.float32), -3.0, 3.0) * 0.2
    step_init = jnp.exp(jax.random.uniform(subkeys[2], (SSM_HEADS,), jnp.float32, math.log(0.001), math.log(0.1)))
    time_bias = step_init + jnp.log(-jnp.expm1(-step_init))
    decay_log = jax.random.uniform(subkeys[3], (SSM_HEADS,), jnp.float32, 0.0, math.log(16.0))
    skip_gain = jax.random.uniform(subkeys[4], (SSM_HEADS,), jnp.float32, 0.5, 1.5)
    mixer_gain = jax.random.uniform(subkeys[5], (SSM_INNER,), jnp.float32, 0.6, 1.4)
    norm_gains = jax.random.uniform(subkeys[6], (3 * D,), jnp.float32, 0.6, 1.4)
    return jnp.concatenate([conv_weight, conv_bias, time_bias, decay_log, skip_gain, mixer_gain, norm_gains, time_proj]).astype(jnp.float32)


def draw_table(key, part):
    subkeys = jax.random.split(jax.random.fold_in(key, 7), 3)
    group_rows = VOCAB // 16
    group_scale = jnp.exp(jax.random.uniform(subkeys[0], (16,), jnp.float32, 0.0, math.log(3.0)))
    group_index = jnp.minimum(jnp.arange(VOCAB, dtype=jnp.int32) // group_rows, 15)
    row_factor = jax.random.uniform(subkeys[1], (VOCAB,), jnp.float32, 0.8, 1.2)
    row_scale = jnp.take(group_scale, group_index) * row_factor / math.sqrt(D)
    noise = jnp.clip(jax.random.normal(subkeys[2], (VOCAB, D), jnp.float32), -6.0, 6.0)
    return (noise * row_scale[:, None]).astype(jnp.float32)


def with_ends(values, key, low, largest):
    index_at = [jax.random.randint(jax.random.fold_in(key, axis), (), 0, length) for axis, length in enumerate(values.shape)]
    longest = values.shape.index(max(values.shape))
    next_to = index_at[:longest] + [(index_at[longest] + 1) % values.shape[longest]] + index_at[longest + 1:]
    return values.at[tuple(index_at)].set(low).at[tuple(next_to)].set(largest)


def block_scale(rng, extent, cuts, least, high):
    loudness = 1.0
    for dim, parts in cuts:
        draws = jax.random.uniform(jax.random.fold_in(jax.random.fold_in(rng, 6), dim), (parts,), jnp.float32, least / len(cuts), high / len(cuts))
        loudness = loudness * jnp.repeat(jnp.exp(draws), extent[dim] // parts).reshape((-1,) + (1,) * (len(extent) - 1 - dim))
    return loudness


def rank_bounds(count, slope):
    weights = [(1 << 20) // math.isqrt(grade ** slope) + 1 for grade in range(1, count + 1)]
    width = 1 + sum(weights) // (1 << 30)
    return np.cumsum(np.array([max(1, weight // width) for weight in weights]))


def skewed_ids(rng, shape, number_of, slope):
    listing = rank_bounds(number_of, slope)
    pick = jax.random.randint(jax.random.fold_in(rng, 1), shape, 0, int(listing[number_of - 1]))
    standing = jnp.searchsorted(jnp.asarray(listing, jnp.int32), pick, side="right")
    return jax.random.permutation(jax.random.fold_in(rng, 2), number_of)[standing].astype(jnp.int32)


def split_up(amount, total, reach, slope):
    portions = [(1 << 20) // math.isqrt(grade ** slope) + 1 for grade in range(2, amount + 1)]
    rest, counts = total - reach - (amount - 1), [1] * (amount - 1)
    while rest > 0:
        candidates = [i for i in range(amount - 1) if counts[i] < reach]
        mass, budget = sum([portions[i] for i in candidates]), rest
        for i in candidates:
            addition = min(reach - counts[i], max(1, budget * portions[i] // mass), rest)
            counts[i] = counts[i] + addition
            rest = rest - addition
    return np.array([reach] + counts)


def uneven(own_key, amount, total, most, lean):
    if amount == 2:
        one = jax.random.randint(own_key, (), max(1, total - most), min(most, total - 1) + 1)
        return jnp.stack([one, total - one])
    sizes = jnp.asarray(split_up(amount, total, most, lean), jnp.int32)
    couples = (amount - 1) // 2
    donor, taker = sizes[1:1 + 2 * couples:2], sizes[2:2 + 2 * couples:2]
    room = jnp.minimum(donor - 1, most - taker)
    moved = jax.random.randint(jax.random.fold_in(own_key, 1), (couples,), 0, 1 << 20) % (room + 1)
    sizes = sizes.at[1:1 + 2 * couples:2].set(donor - moved).at[2:2 + 2 * couples:2].set(taker + moved)
    return sizes[jax.random.permutation(jax.random.fold_in(own_key, 2), amount)]


def bell_draw(key, dims, deviation, reach, cuts=(), held_as=jnp.bfloat16):
    values = jax.random.normal(key, dims, jnp.float32) * deviation
    if len(cuts) > 0:
        values = block_scale(key, dims, cuts, -0.22, 0.18) * values
    return jnp.clip(values, min=-reach, max=reach).astype(held_as)


def setup_inputs(seed: int = 0) -> dict:
    splits = jax.random.split(jax.random.key(seed), 19)
    return {
        "token_ids": with_ends(skewed_ids(splits[0], (SEQS, SEQ), VOCAB, 2), jax.random.fold_in(splits[0], 3), 0, VOCAB - 1).astype(jnp.int32),
        "segment_ids": jax.vmap(lambda own: jnp.searchsorted(jnp.cumsum(uneven(own, DOCS, SEQ, SEQ // 2, 2)), jnp.arange(SEQ), side="right"))(jax.random.split(splits[1], SEQS)).reshape((SEQS, SEQ)).astype(jnp.int32),
        "loss_positions": with_ends(jax.random.randint(splits[2], (SEQS, COUNT), 0, SEQ), jax.random.fold_in(splits[2], 1), 0, SEQ - 1).astype(jnp.int32),
        "loss_targets": with_ends(skewed_ids(splits[3], (SEQS, COUNT), VOCAB, 2), jax.random.fold_in(splits[3], 3), 0, VOCAB - 1).astype(jnp.int32),
        "loss_valid": with_ends((jax.random.randint(splits[4], (SEQS, COUNT), 0, 4) < 3).astype(jnp.int32), jax.random.fold_in(splits[4], 1), 0, 1),
        "block_owner": jax.random.permutation(splits[5], NBLK).astype(jnp.int32),
        "step_count": jax.random.randint(splits[6], (1,), 1, 21).astype(jnp.int32),
        "block_weights": bell_draw(splits[7], (NBLK, D, BLOCK_COLS), D ** -0.5, 0.1875, ((0, 8), (1, 4)), jnp.float32),
        "block_first": bell_draw(splits[8], (NBLK, D, BLOCK_COLS), 0.00001, 0.00015258789, ((0, 8), (1, 4)), jnp.float32),
        "block_second": jnp.clip(jnp.exp(math.log(9.999999717180685e-10) - 4.6051702 * jax.random.uniform(splits[9], (NBLK, D, BLOCK_COLS), jnp.float32) ** block_scale(splits[9], (NBLK, D, BLOCK_COLS), ((0, 8), (1, 4)), -0.2, 0.2)), 9.999999960041972e-12, 9.999999717180685e-10),
        "left_basis": bell_draw(splits[10], (NBLK, D, D), D ** -0.5, 0.1875, ((0, 8), (1, 4)), jnp.float32),
        "right_basis": bell_draw(splits[11], (NBLK, BLOCK_COLS, BLOCK_COLS), BLOCK_COLS ** -0.5, 0.375, ((0, 8),), jnp.float32),
        "table": draw_table(jax.random.fold_in(splits[18], 71), 0),
        "table_first": bell_draw(splits[13], (VOCAB, D), 0.00001, 0.00015258789, ((0, 8), (1, 4)), jnp.float32),
        "table_second": jnp.clip(jnp.exp(math.log(9.999999717180685e-10) - 4.6051702 * jax.random.uniform(splits[14], (VOCAB, D), jnp.float32) ** block_scale(splits[14], (VOCAB, D), ((0, 8), (1, 4)), -0.2, 0.2)), 9.999999960041972e-12, 9.999999717180685e-10),
        "vector_params": draw_vector_params(jax.random.fold_in(splits[18], 71), 0),
        "vector_first": bell_draw(splits[16], (NVEC,), 0.0001, 0.0014648438, (), jnp.float32),
        "vector_second": jnp.clip(jnp.exp(jax.random.uniform(splits[17], (NVEC,), jnp.float32, math.log(9.999999717180685e-10), math.log(1.0000000116860974e-07))), 9.999999717180685e-10, 1.0000000116860974e-07),
    }


@jax.custom_vjp
def low(v):
    return lax.optimization_barrier(v.astype(jnp.bfloat16)).astype(jnp.float32)

@jax.custom_vjp
def low_back(v):
    return v

def low_keep(v):
    return (low(v), None)

def low_pass(kept, grad):
    return (grad,)

def back_keep(v):
    return (v, None)

def back_low(kept, grad):
    return (low(grad),)
low.defvjp(low_keep, low_pass)
low_back.defvjp(back_keep, back_low)
highest = lax.Precision.HIGHEST
rope_base = 100000000000.0
clip_limit = 1.0
learn_rate = 0.01
vector_rate = 0.08
weight_decay = 0.1
soap_first = 0.95
soap_second = 0.95
adam_first = 0.9
adam_second = 0.95
adam_eps = 1e-08

def wide_dot(left_rows, right_cols):
    return jnp.dot(left_rows, right_cols, precision=highest, preferred_element_type=jnp.float32)

def rms_gain(values, gain_vec):
    inv_scale = lax.rsqrt(lax.optimization_barrier(jnp.mean(values * values, axis=-1, keepdims=True)) + 1e-05)
    return values * inv_scale * gain_vec

def swiglu(gate_val, up_val):
    return jax.nn.silu(gate_val) * up_val

def unpack(flattened):
    piece_sizes = [CONV * XBC_WIDTH, XBC_WIDTH, SSM_HEADS, SSM_HEADS, SSM_HEADS, SSM_INNER, 3 * D, D * SSM_HEADS]
    pieces = []
    offset = 0
    for length in piece_sizes:
        pieces.append(flattened[offset:offset + length])
        offset = offset + length
    return pieces

def rope_table(length):
    half_dim = HEAD_DIM // 2
    frequency = rope_base ** (-jnp.arange(half_dim, dtype=jnp.float32) * 2.0 / HEAD_DIM)
    angles = jnp.arange(length, dtype=jnp.float32)[:, None] * frequency[None, :]
    return (jnp.cos(angles), jnp.sin(angles))

def rotate(values, cosine, sine_table):
    half_dim = values.shape[-1] // 2
    first_half = values[..., :half_dim]
    second_half = values[..., half_dim:]
    cos_wide = cosine[:, None, :]
    sin_wide = sine_table[:, None, :]
    return jnp.concatenate([first_half * cos_wide - second_half * sin_wide, second_half * cos_wide + first_half * sin_wide], axis=-1)

def attention_core(packed, segment):
    length = packed.shape[0]
    groups = HEADS // KV_HEADS
    queries = packed[:, :HEADS * HEAD_DIM].reshape(length, HEADS, HEAD_DIM)
    keys_all = packed[:, HEADS * HEAD_DIM:(HEADS + KV_HEADS) * HEAD_DIM].reshape(length, KV_HEADS, HEAD_DIM)
    values_all = packed[:, (HEADS + KV_HEADS) * HEAD_DIM:].reshape(length, KV_HEADS, HEAD_DIM)
    cosine, sine_table = rope_table(length)
    queries = rotate(queries, cosine, sine_table) * HEAD_DIM ** (-0.5)
    keys_all = rotate(keys_all, cosine, sine_table)
    nblocks = length // QBLOCK
    queries = queries.reshape(nblocks, QBLOCK, KV_HEADS, groups, HEAD_DIM)
    doc_blocks = segment.reshape(nblocks, QBLOCK)
    starts = jnp.arange(nblocks, dtype=jnp.int32) * QBLOCK
    positions = jnp.arange(length, dtype=jnp.int32)

    def one_block(inputs):
        query_block, doc_block, start_row = inputs
        scores = jnp.einsum('qkgd,skd->kgqs', query_block, keys_all, precision=highest)
        row_pos = start_row + jnp.arange(QBLOCK, dtype=jnp.int32)
        allowed = (doc_block[:, None] == segment[None, :]) & (row_pos[:, None] >= positions[None, :])
        scores = jnp.where(allowed, scores, -1e+30)
        row_top = lax.optimization_barrier(jnp.max(scores, axis=-1, keepdims=True))
        weights = jnp.where(allowed, jnp.exp(scores - row_top), 0.0)
        row_total = lax.optimization_barrier(jnp.sum(weights, axis=-1, keepdims=True))
        return jnp.einsum('kgqs,skd->qkgd', weights / row_total, values_all, precision=highest)
    blocks = lax.map(jax.checkpoint(one_block), (queries, doc_blocks, starts))
    return blocks.reshape(length, HEADS * HEAD_DIM)

def ssd_scan(heads_in, step_size, decay_rate, input_map, output_map, segment):
    length = heads_in.shape[0]
    nspans = length // SPAN

    def span_step(carry_in, inputs):
        carry_state, carry_doc = carry_in
        heads_block, step_block, input_block, output_block, doc_block = inputs
        cum_decay = jnp.cumsum(step_block * decay_rate[None, :], axis=0)
        causal = jnp.arange(SPAN)[:, None] >= jnp.arange(SPAN)[None, :]
        same_doc = ((doc_block[:, None] == doc_block[None, :]) & causal)[:, :, None]
        cum_gaps = cum_decay[:, None, :] - cum_decay[None, :, :]
        decay_mat = jnp.where(same_doc, jnp.exp(jnp.where(same_doc, cum_gaps, 0.0)), 0.0)
        inner_bc = jnp.einsum('tn,sn->ts', output_block, input_block, precision=highest)
        mixing = decay_mat * (inner_bc[:, :, None] * step_block[None, :, :])
        result = jnp.einsum('tsh,shp->thp', mixing, heads_block, precision=highest)
        carried = (doc_block == carry_doc).astype(jnp.float32)[:, None] * jnp.exp(cum_decay)
        result = result + carried[:, :, None] * jnp.einsum('tn,hpn->thp', output_block, carry_state, precision=highest)
        last_doc = doc_block[SPAN - 1]
        tail_weight = jnp.where((doc_block == last_doc)[:, None], jnp.exp(cum_decay[SPAN - 1][None, :] - cum_decay), 0.0) * step_block
        keep_old = (carry_doc == last_doc).astype(jnp.float32) * jnp.exp(cum_decay[SPAN - 1])
        fresh_state = jnp.einsum('sh,shp,sn->hpn', tail_weight, heads_block, input_block, precision=highest)
        return ((keep_old[:, None, None] * carry_state + fresh_state, last_doc), result)
    initial = (jnp.zeros((SSM_HEADS, SSM_HEAD_DIM, STATE), jnp.float32), jnp.array(-1, jnp.int32))
    spanned = (heads_in.reshape(nspans, SPAN, SSM_HEADS, SSM_HEAD_DIM), step_size.reshape(nspans, SPAN, SSM_HEADS), input_map.reshape(nspans, SPAN, STATE), output_map.reshape(nspans, SPAN, STATE), segment.reshape(nspans, SPAN))
    _, outputs = lax.scan(jax.checkpoint(span_step), initial, spanned)
    return outputs.reshape(length, SSM_HEADS, SSM_HEAD_DIM)

def mixer_core(projected, time_raw, conv_weight, conv_bias, time_bias, decay_log, skip_gain, mixer_gain, segment):
    length = projected.shape[0]
    gate_part = projected[:, :SSM_INNER]
    conv_in = projected[:, SSM_INNER:]
    kernel = conv_weight.reshape(CONV, XBC_WIDTH)
    conv_sum = jnp.zeros_like(conv_in) + conv_bias[None, :]
    for offset in range(CONV):
        shift_by = CONV - 1 - offset
        shifted = jnp.pad(conv_in, ((shift_by, 0), (0, 0)))[:length]
        doc_shift = jnp.pad(segment, (shift_by, 0), constant_values=-1)[:length]
        same_doc = (doc_shift == segment).astype(jnp.float32)[:, None]
        conv_sum = conv_sum + kernel[offset][None, :] * shifted * same_doc
    activated = jax.nn.silu(conv_sum)
    heads_in = activated[:, :SSM_INNER].reshape(length, SSM_HEADS, SSM_HEAD_DIM)
    input_map = activated[:, SSM_INNER:SSM_INNER + STATE]
    output_map = activated[:, SSM_INNER + STATE:]
    step_size = jax.nn.softplus(time_raw + time_bias[None, :])
    decay_rate = -jnp.exp(decay_log)
    output = ssd_scan(heads_in, step_size, decay_rate, input_map, output_map, segment)
    output = output + skip_gain[None, :, None] * heads_in
    gated = output.reshape(length, SSM_INNER) * jax.nn.silu(gate_part)
    return rms_gain(gated, mixer_gain)

def sequence_loss(params, tokens, segment, positions, targets, valid):
    matrix, table_low, time_low, conv_weight, conv_bias, time_bias, decay_log, skip_gain, mixer_gain, gain_rows = params
    in_cols = 2 * SSM_INNER + 2 * STATE
    qkv_end = in_cols + (HEADS + 2 * KV_HEADS) * HEAD_DIM
    out_end = qkv_end + SSM_INNER
    attn_end = out_end + HEADS * HEAD_DIM
    gate_end = attn_end + FF
    up_end = gate_end + FF
    embedded = low_back(jnp.take(table_low, tokens, axis=0))
    normed = low(rms_gain(embedded, gain_rows[0]))
    projected = low_back(wide_dot(normed, matrix[:, :in_cols]))
    packed = low_back(wide_dot(normed, matrix[:, in_cols:qkv_end]))
    time_raw = low_back(wide_dot(normed, time_low))
    mixer_out = low(mixer_core(projected, time_raw, conv_weight, conv_bias, time_bias, decay_log, skip_gain, mixer_gain, segment))
    context = low(attention_core(packed, segment))
    hidden_one = embedded + low_back(wide_dot(mixer_out, matrix[:, qkv_end:out_end].T)) + low_back(wide_dot(context, matrix[:, out_end:attn_end].T))
    normed_two = low(rms_gain(hidden_one, gain_rows[1]))
    gate_val = low_back(wide_dot(normed_two, matrix[:, attn_end:gate_end]))
    up_val = low_back(wide_dot(normed_two, matrix[:, gate_end:up_end]))
    activated = low(swiglu(gate_val, up_val))
    hidden_two = hidden_one + low_back(wide_dot(activated, matrix[:, up_end:].T))
    final_out = low(rms_gain(hidden_two, gain_rows[2]))
    picked = jnp.take(final_out, positions, axis=0)
    logits = low_back(wide_dot(picked, table_low.T))
    log_total = jax.nn.logsumexp(logits, axis=1)
    target_logit = jnp.take_along_axis(logits, targets[:, None], axis=1)[:, 0]
    return jnp.sum(valid * (log_total - target_logit))

def adam_step(weights, grads, first, second, steps_done, decay, rate):
    first_new = adam_first * first + (1.0 - adam_first) * grads
    second_new = adam_second * second + (1.0 - adam_second) * grads * grads
    direction = first_new / (1.0 - adam_first ** steps_done) / (jnp.sqrt(second_new / (1.0 - adam_second ** steps_done)) + adam_eps)
    return (weights - rate * (direction + decay * weights), first_new, second_new)

def reference(token_ids, segment_ids, loss_positions, loss_targets, loss_valid, block_owner, step_count, block_weights, block_first, block_second, left_basis, right_basis, table, table_first, table_second, vector_params, vector_first, vector_second):
    total_cols = NBLK * BLOCK_COLS
    logical = jnp.take(low(block_weights), block_owner, axis=0)
    matrix = logical.transpose(1, 0, 2).reshape(D, total_cols)
    table_low = low(table)
    conv_weight, conv_bias, time_bias, decay_log, skip_gain, mixer_gain, norm_gains, time_proj = unpack(vector_params)
    params = (matrix, table_low, low(time_proj.reshape(D, SSM_HEADS)), conv_weight, conv_bias, time_bias, decay_log, skip_gain, mixer_gain, norm_gains.reshape(3, D))
    valid_wide = loss_valid.astype(jnp.float32)
    valid_count = jnp.sum(valid_wide)
    cotangent = 1.0 / valid_count

    def per_sequence(carry_in, inputs):
        loss_acc, grad_acc = carry_in
        tokens, segment, positions, targets, valid = inputs

        def local_loss(packed_params):
            return sequence_loss(packed_params, tokens, segment, positions, targets, valid)
        value, backward = jax.vjp(local_loss, params)
        grads, = backward(cotangent)
        return ((loss_acc + value, jax.tree.map(jnp.add, grad_acc, grads)), None)
    zero_grads = jax.tree.map(jnp.zeros_like, params)
    (loss_sum, grads), _ = lax.scan(per_sequence, (jnp.zeros((), jnp.float32), zero_grads), (token_ids, segment_ids, loss_positions, loss_targets, valid_wide))
    mean_loss = loss_sum / valid_count
    grad_matrix, grad_table, grad_time, grad_conv_w, grad_conv_b, grad_bias, grad_decay, grad_skip, grad_mixer, grad_gains = grads
    grad_logical = grad_matrix.reshape(D, NBLK, BLOCK_COLS).transpose(1, 0, 2)
    inverse = jnp.zeros((NBLK,), jnp.int32).at[block_owner].set(jnp.arange(NBLK, dtype=jnp.int32))
    grad_slots = jnp.take(grad_logical, inverse, axis=0)
    grad_vector = jnp.concatenate([grad_conv_w, grad_conv_b, grad_bias, grad_decay, grad_skip, grad_mixer, grad_gains.reshape(-1), grad_time.reshape(-1)])
    grad_norm = jnp.sqrt(jnp.sum(grad_slots * grad_slots) + jnp.sum(grad_table * grad_table) + jnp.sum(grad_vector * grad_vector))
    clip_scale = jnp.minimum(1.0, clip_limit / (grad_norm + 1e-06))
    steps_done = step_count[0].astype(jnp.float32)
    clipped = grad_slots * clip_scale
    rotated = jnp.einsum('sid,sdb->sib', left_basis, clipped, precision=highest)
    rotated = jnp.einsum('sib,sbc->sic', rotated, right_basis, precision=highest)
    first_new = soap_first * block_first + (1.0 - soap_first) * rotated
    second_new = soap_second * block_second + (1.0 - soap_second) * rotated * rotated
    direction = first_new / (1.0 - soap_first ** steps_done) / (jnp.sqrt(second_new / (1.0 - soap_second ** steps_done)) + adam_eps)
    turned = jnp.einsum('sic,sbc->sib', direction, right_basis, precision=highest)
    update = jnp.einsum('sid,sib->sdb', left_basis, turned, precision=highest)
    new_blocks = block_weights - learn_rate * (update + weight_decay * block_weights)
    new_table, table_first_new, table_second_new = adam_step(table, grad_table * clip_scale, table_first, table_second, steps_done, weight_decay, learn_rate)
    new_vectors, vector_first_new, vector_second_new = adam_step(vector_params, grad_vector * clip_scale, vector_first, vector_second, steps_done, 0.0, vector_rate)
    return (mean_loss, grad_norm, new_blocks, first_new, second_new, new_table, table_first_new, table_second_new, new_vectors, vector_first_new, vector_second_new)
```

```python
import functools

import jax
import jax.numpy as jnp
from jax import lax
from jax.experimental import pallas as pl
from jax.experimental.pallas import tpu as pltpu
from jax.sharding import PartitionSpec as P

D = 1024
HEADS = 8
KV_HEADS = 2
HEAD_DIM = 64
SSM_HEADS = 24
SSM_HEAD_DIM = 64
STATE = 128
CONV = 4
FF = 2048
BLOCK_COLS = 256
SSM_INNER = 1536
XBC_WIDTH = 1792
CHUNK = 128
QROWS = 256
LANES = 128
PAD_ROWS = 16

BF16 = jnp.bfloat16
F32 = jnp.float32
MESH = pl.DeviceIdType.MESH
highest = lax.Precision.HIGHEST
rope_base = 100000000000.0
clip_limit = 1.0
learn_rate = 0.01
vector_rate = 0.08
weight_decay = 0.1
soap_first = 0.95
soap_second = 0.95
adam_first = 0.9
adam_second = 0.95
adam_eps = 1e-08
vmem_bytes = 56 * 1024 * 1024


def params(**more):
    return pltpu.CompilerParams(vmem_limit_bytes=vmem_bytes, **more)


def cost(flops, nbytes, exps=0):
    return pl.CostEstimate(flops=int(flops), bytes_accessed=int(nbytes), transcendentals=int(exps))


def rms_gain(values, gain_vec):
    inv_scale = lax.rsqrt(jnp.mean(values * values, axis=-1, keepdims=True) + 1e-05)
    return values * inv_scale * gain_vec


def swiglu(gate_val, up_val):
    return jax.nn.silu(gate_val) * up_val


def unpack(flattened):
    piece_sizes = [
        CONV * XBC_WIDTH,
        XBC_WIDTH,
        SSM_HEADS,
        SSM_HEADS,
        SSM_HEADS,
        SSM_INNER,
        3 * D,
        D * SSM_HEADS,
    ]
    pieces = []
    offset = 0
    for length in piece_sizes:
        pieces.append(flattened[offset : offset + length])
        offset = offset + length
    return pieces


def dot_nt(left, right):
    return lax.dot_general(left, right, (((1,), (1,)), ((), ())), preferred_element_type=F32)


def dot_tn(left, right):
    return lax.dot_general(left, right, (((0,), (0,)), ((), ())), preferred_element_type=F32)


def dot_nn(left, right):
    return jnp.dot(left, right, preferred_element_type=F32)


def project_kernel(own_ref, x_ref, w_ref, o_ref):
    o_ref[...] = dot_nn(x_ref[...], w_ref[...].reshape(D, BLOCK_COLS))


def project(rows_in, gathered, owner, first, count):
    rows, _, depth, _ = gathered.shape
    length = rows_in.shape[0]
    return pl.pallas_call(
        project_kernel,
        grid_spec=pltpu.PrefetchScalarGridSpec(
            num_scalar_prefetch=1,
            grid=(count,),
            in_specs=[
                pl.BlockSpec((length, D), lambda k, own: (0, 0)),
                pl.BlockSpec(
                    (rows, 1, depth, BLOCK_COLS), lambda k, own: (0, own[first + k], 0, 0)
                ),
            ],
            out_specs=pl.BlockSpec((length, BLOCK_COLS), lambda k, own: (0, k)),
        ),
        out_shape=jax.ShapeDtypeStruct((length, count * BLOCK_COLS), F32),
        compiler_params=params(),
        cost_estimate=cost(
            2 * length * D * BLOCK_COLS * count, count * BLOCK_COLS * (2 * D + 4 * length)
        ),
    )(owner, rows_in, gathered)


def back_kernel(own_ref, c_ref, w_ref, base_ref, o_ref):
    @pl.when(pl.program_id(0) == 0)
    def _():
        o_ref[...] = base_ref[...]

    o_ref[...] += dot_nt(c_ref[...], w_ref[...].reshape(D, BLOCK_COLS))


def project_back(cols_in, gathered, owner, first, count, base):
    rows, _, depth, _ = gathered.shape
    length = cols_in.shape[0]
    return pl.pallas_call(
        back_kernel,
        grid_spec=pltpu.PrefetchScalarGridSpec(
            num_scalar_prefetch=1,
            grid=(count,),
            in_specs=[
                pl.BlockSpec((length, BLOCK_COLS), lambda k, own: (0, k)),
                pl.BlockSpec(
                    (rows, 1, depth, BLOCK_COLS), lambda k, own: (0, own[first + k], 0, 0)
                ),
                pl.BlockSpec((length, D), lambda k, own: (0, 0)),
            ],
            out_specs=pl.BlockSpec((length, D), lambda k, own: (0, 0)),
        ),
        out_shape=jax.ShapeDtypeStruct((length, D), F32),
        compiler_params=params(),
        cost_estimate=cost(
            2 * length * D * BLOCK_COLS * count, count * BLOCK_COLS * (2 * D + 2 * length)
        ),
    )(owner, cols_in, gathered, base)


def wgrad_kernel(own_ref, l_ref, r_ref, *rest):
    o_ref, turned = rest[-2], rest[-1]

    @pl.when(pl.program_id(0) == 0)
    def _():
        turned[...] = l_ref[...].T

    grad = dot_nn(turned[...], r_ref[...])
    o_ref[...] = grad.astype(BF16).reshape(o_ref.shape)


def weight_grad(left_rows, right_cols, owner, first, like, into):
    rows, nslots, depth, _ = like
    length = left_rows.shape[0]
    count = right_cols.shape[1] // BLOCK_COLS
    in_specs = [
        pl.BlockSpec((length, D), lambda k, own: (0, 0)),
        pl.BlockSpec((length, BLOCK_COLS), lambda k, own: (0, k)),
    ]
    operands = [owner, left_rows, right_cols]
    aliases = {}
    if into is not None:
        in_specs.append(pl.BlockSpec(memory_space=pl.ANY))
        operands.append(into)
        aliases = {3: 0}
    return pl.pallas_call(
        wgrad_kernel,
        grid_spec=pltpu.PrefetchScalarGridSpec(
            num_scalar_prefetch=1,
            grid=(count,),
            in_specs=in_specs,
            out_specs=pl.BlockSpec(
                (rows, 1, depth, BLOCK_COLS), lambda k, own: (0, own[first + k], 0, 0)
            ),
            scratch_shapes=[pltpu.VMEM((D, length), BF16)],
        ),
        out_shape=jax.ShapeDtypeStruct(like, BF16),
        input_output_aliases=aliases,
        compiler_params=params(),
        cost_estimate=cost(
            2 * length * D * BLOCK_COLS * count, count * BLOCK_COLS * (2 * D + 2 * length)
        ),
    )(*operands)


def rope_tables(length):
    half_dim = HEAD_DIM // 2
    frequency = rope_base ** (-jnp.arange(half_dim, dtype=F32) * 2.0 / HEAD_DIM)
    angles = jnp.arange(length, dtype=F32)[:, None] * frequency[None, :]
    cosine, sine = jnp.cos(angles), jnp.sin(angles)
    wide_cos = jnp.concatenate([cosine] * 4, axis=1)
    wide_sin = jnp.concatenate([-sine, sine, -sine, sine], axis=1)
    return wide_cos, wide_sin


def lane_iota():
    return lax.broadcasted_iota(jnp.int32, (1, LANES), 1)


def swap_halves(values):
    low_half = (lane_iota() % HEAD_DIM) < HEAD_DIM // 2
    return jnp.where(
        low_half,
        pltpu.roll(values, LANES - HEAD_DIM // 2, 1),
        pltpu.roll(values, HEAD_DIM // 2, 1),
    )


def turn(values, cosine, sine):
    return values * cosine + swap_halves(values) * sine


def turn_back(values, cosine, sine):
    return values * cosine - swap_halves(values) * sine


def doubled(values, group):
    moved = pltpu.roll(values, HEAD_DIM, 1)
    keep = (lane_iota() < HEAD_DIM) == (group == 0)
    return jnp.where(keep, values, moved)


def attention_mask(segc_ref, segr_ref, low_row, low_col, wide):
    doc_rows = segc_ref[low_row : low_row + QROWS, :]
    doc_cols = segr_ref[:, low_col : low_col + wide]
    row_pos = low_row + lax.broadcasted_iota(jnp.int32, (QROWS, wide), 0)
    col_pos = low_col + lax.broadcasted_iota(jnp.int32, (QROWS, wide), 1)
    return (doc_rows == doc_cols) & (row_pos >= col_pos)


def attention_probs(query, key, allowed):
    scores = jnp.where(allowed, dot_nt(query, key), -1e30)
    row_top = jnp.max(scores, axis=-1, keepdims=True)
    weights = jnp.exp(scores - row_top)
    return weights, jnp.sum(weights, axis=-1, keepdims=True)


def halves(values):
    high = values.astype(BF16).astype(F32)
    return high, values - high


def fold(values):
    return values + pltpu.roll(values, HEAD_DIM, 1)


def head_operands(values):
    low = lane_iota() < HEAD_DIM
    high, rest = halves(values)
    high_moved, rest_moved = pltpu.roll(high, HEAD_DIM, 1), pltpu.roll(rest, HEAD_DIM, 1)
    head_a = [jnp.where(low, high, rest_moved), jnp.where(low, high, 0.0)]
    head_b = [jnp.where(low, high_moved, rest), jnp.where(low, high_moved, 0.0)]
    return [jnp.concatenate(h, axis=1).astype(BF16) for h in (head_a, head_b)]


def group_operands(values):
    low = lane_iota() < HEAD_DIM
    high, rest = halves(values)
    inner = jnp.concatenate([high, rest], axis=1).astype(BF16)
    return inner, jnp.where(low, high, rest).astype(BF16)


def attn_fwd_kernel(q_ref, k_ref, v_ref, segc_ref, segr_ref, cos_ref, sin_ref, o_ref):
    group = pl.program_id(0) // 2
    low = lane_iota() < HEAD_DIM
    cosine, sine = cos_ref[...], sin_ref[...]
    length = cosine.shape[0]
    query_h = head_operands(turn(q_ref[...], cosine, sine) * HEAD_DIM ** (-0.5))
    key, _ = group_operands(doubled(turn(k_ref[...], cosine, sine), group))
    _, value = group_operands(doubled(v_ref[...], group))
    for block in range(length // QROWS):
        low_row = block * QROWS
        low_col = max(0, low_row - 2 * QROWS)
        wide = low_row + QROWS - low_col
        rows, cols = slice(low_row, low_row + QROWS), slice(low_col, low_col + wide)
        allowed = attention_mask(segc_ref, segr_ref, low_row, low_col, wide)
        outs = []
        for h in range(2):
            weights, total = attention_probs(query_h[h][rows], key[cols], allowed)
            weights_high, weights_rest = split(weights)
            mixed = dot_nn(weights_high, value[cols]) + dot_nn(weights_rest, value[cols])
            outs.append(fold(mixed) / total)
        o_ref[rows, :] = jnp.where(low, outs[0], outs[1]).astype(BF16)


def attn_bwd_kernel(
    q_ref, k_ref, v_ref, segc_ref, segr_ref, cos_ref, sin_ref, g_ref, dq_ref, dkv_ref, dk_s, dv_s
):
    step = pl.program_id(0)
    group = step // 2
    low = lane_iota() < HEAD_DIM
    cosine, sine = cos_ref[...], sin_ref[...]
    length = cosine.shape[0]

    @pl.when(step == 0)
    def _():
        dk_s[...] = jnp.zeros_like(dk_s)
        dv_s[...] = jnp.zeros_like(dv_s)

    scale = HEAD_DIM ** (-0.5)
    query_h = head_operands(turn(q_ref[...], cosine, sine) * scale)
    grad_h = head_operands(g_ref[...])
    key, key_out = group_operands(doubled(turn(k_ref[...], cosine, sine), group))
    value, _ = group_operands(doubled(v_ref[...], group))
    for block in range(length // QROWS):
        low_row = block * QROWS
        low_col = max(0, low_row - 2 * QROWS)
        wide = low_row + QROWS - low_col
        rows, cols = slice(low_row, low_row + QROWS), slice(low_col, low_col + wide)
        allowed = attention_mask(segc_ref, segr_ref, low_row, low_col, wide)
        dqs, ps, dss = [], [], []
        for h in range(2):
            weights, total = attention_probs(query_h[h][rows], key[cols], allowed)
            probs = weights * (1.0 / total)
            dprobs = dot_nt(grad_h[h][rows], value[cols])
            delta = jnp.sum(probs * dprobs, axis=-1, keepdims=True)
            dscores = split(probs * (dprobs - delta))
            dqs.append(fold(dot_nn(dscores[0], key_out[cols]) + dot_nn(dscores[1], key_out[cols])))
            ps.append(probs.astype(BF16))
            dss.append(dscores[0])
        both_p = jnp.concatenate(ps, axis=0)
        both_d = jnp.concatenate(dss, axis=0)
        both_g = jnp.concatenate([grad_h[h][rows, :LANES] for h in range(2)], axis=0)
        both_q = jnp.concatenate([query_h[h][rows, :LANES] for h in range(2)], axis=0)
        dv_s[group, cols, :] += dot_tn(both_p, both_g)
        dk_s[group, cols, :] += dot_tn(both_d, both_q)
        dq = jnp.where(low, dqs[0], dqs[1]) * scale
        dq_ref[rows, :] = turn_back(dq, cosine[rows], sine[rows]).astype(BF16)

    @pl.when(step == pl.num_programs(0) - 1)
    def _():
        dk = jnp.where(low, fold(dk_s[0]), fold(dk_s[1]))
        dv = jnp.where(low, fold(dv_s[0]), fold(dv_s[1]))
        dkv_ref[:, :LANES] = turn_back(dk, cosine, sine).astype(BF16)
        dkv_ref[:, LANES:] = dv.astype(BF16)


def attention_specs(length, base):
    return [
        pl.BlockSpec((length, LANES), lambda p: (0, base + p)),
        pl.BlockSpec((length, LANES), lambda p: (0, base + 4)),
        pl.BlockSpec((length, LANES), lambda p: (0, base + 5)),
        pl.BlockSpec((length, 1), lambda p: (0, 0)),
        pl.BlockSpec((1, length), lambda p: (0, 0)),
        pl.BlockSpec((length, LANES), lambda p: (0, 0)),
        pl.BlockSpec((length, LANES), lambda p: (0, 0)),
    ]


def attention_forward(both_proj, segc, segr, cosine, sine):
    length = both_proj.shape[0]
    base = (SSM_INNER + XBC_WIDTH) // LANES
    pairs = HEADS // 2
    return pl.pallas_call(
        attn_fwd_kernel,
        grid=(pairs,),
        in_specs=attention_specs(length, base),
        out_specs=pl.BlockSpec((length, LANES), lambda p: (0, p)),
        out_shape=jax.ShapeDtypeStruct((length, HEADS * HEAD_DIM), BF16),
        compiler_params=params(),
        cost_estimate=cost(4 * HEADS * length * length * HEAD_DIM, 6 * length * D, HEADS * length * length // 2),
    )(both_proj, both_proj, both_proj, segc, segr, cosine, sine)


def attention_backward(both_proj, segc, segr, cosine, sine, grads, grad_base):
    length = both_proj.shape[0]
    base = (SSM_INNER + XBC_WIDTH) // LANES
    pairs = HEADS // 2
    return pl.pallas_call(
        attn_bwd_kernel,
        grid=(pairs,),
        in_specs=attention_specs(length, base)
        + [pl.BlockSpec((length, LANES), lambda p: (0, grad_base + p))],
        out_specs=[
            pl.BlockSpec((length, LANES), lambda p: (0, p)),
            pl.BlockSpec((length, 2 * LANES), lambda p: (0, 0)),
        ],
        out_shape=[
            jax.ShapeDtypeStruct((length, HEADS * HEAD_DIM), BF16),
            jax.ShapeDtypeStruct((length, 2 * LANES), BF16),
        ],
        scratch_shapes=[pltpu.VMEM((2, length, LANES), F32)] * 2,
        compiler_params=params(),
        cost_estimate=cost(10 * HEADS * length * length * HEAD_DIM, 10 * length * D, HEADS * length * length // 2),
    )(both_proj, both_proj, both_proj, segc, segr, cosine, sine, grads)


def chunk_masks(segc_ref, segr_ref, last_ref, chunk):
    doc_rows, doc_cols = segc_ref[...], segr_ref[...]
    row_pos = lax.broadcasted_iota(jnp.int32, (CHUNK, CHUNK), 0)
    col_pos = lax.broadcasted_iota(jnp.int32, (CHUNK, CHUNK), 1)
    same = (doc_rows == doc_cols) & (row_pos >= col_pos)
    madd = jnp.where(same, 0.0, -1e30)
    last = last_ref[chunk]
    previous = jnp.where(chunk > 0, last_ref[jnp.maximum(chunk - 1, 0)], -1)
    carried = jnp.where(doc_rows == previous, 1.0, 0.0)
    tail = jnp.where(doc_rows == last, 1.0, 0.0)
    keep = jnp.where(last == previous, 1.0, 0.0)
    return madd, carried, tail, keep


def spread(low, columns, a):
    return jnp.where(low, columns[:, a : a + 1], columns[:, a + 1 : a + 2])


def split(values):
    high = values.astype(BF16)
    return high, (values - high.astype(F32)).astype(BF16)


def wide_split(values):
    return jnp.concatenate(split(values), axis=1)


def both_sides(values):
    return values[:, :LANES] + values[:, LANES:]


def ssm_fwd_kernel(
    last_ref, xbc_ref, dt_ref, cum_ref, cumt_ref, skip_ref, segc_ref, segr_ref,
    y_ref, s_ref, state,
):
    chunk = pl.program_id(0)

    @pl.when(chunk == 0)
    def _():
        state[...] = jnp.zeros_like(state)

    s_ref[...] = state[...].reshape(s_ref.shape)
    low = lane_iota() < SSM_HEAD_DIM
    madd, carried, tail, keep = chunk_masks(segc_ref, segr_ref, last_ref, chunk)
    dt, cum, cumt = dt_ref[...], cum_ref[...], cumt_ref[...]
    last_cum = cum[CHUNK - 1 : CHUNK, :]
    ecum = jnp.exp(cum) * carried
    tails = jnp.exp(last_cum - cum) * tail
    keeps = jnp.exp(last_cum) * keep
    into = xbc_ref[:, SSM_INNER : SSM_INNER + STATE]
    into_t = into.T
    into_high, into_rest = split(into_t)
    out_high, out_rest = split(xbc_ref[:, SSM_INNER + STATE :])
    out_both = jnp.concatenate([out_high, out_rest], axis=1)
    into_both = jnp.concatenate([into_high, into_rest], axis=1)
    gram = dot_nn(out_both, jnp.concatenate([into_high, into_high], axis=0)) + dot_nn(
        out_high, into_rest
    )
    for p in range(SSM_HEADS // 2):
        a, cols = 2 * p, slice(p * LANES, (p + 1) * LANES)
        heads = xbc_ref[:, cols]
        scaled = heads * spread(low, dt, a)
        decay_a = jnp.exp(cum[:, a : a + 1] - cumt[a : a + 1, :] + madd)
        decay_b = jnp.exp(cum[:, a + 1 : a + 2] - cumt[a + 1 : a + 2, :] + madd)
        mixing = wide_split(jnp.concatenate([decay_a * gram, decay_b * gram], axis=1))
        stacked_wide = wide_split(
            jnp.concatenate([jnp.where(low, scaled, 0.0), jnp.where(low, 0.0, scaled)], axis=0)
        )
        old = state[:, cols]
        old_wide = wide_split(old)
        carry_in = both_sides(dot_nn(out_both, jnp.concatenate([old_wide, old_wide], axis=0)))
        y_ref[:, cols] = (
            both_sides(dot_nn(mixing, jnp.concatenate([stacked_wide, stacked_wide], axis=0)))
            + spread(low, ecum, a) * carry_in
            + spread(low, skip_ref[...], a) * heads
        )
        tail_in = wide_split(scaled * spread(low, tails, a))
        fresh = both_sides(dot_nn(into_both, jnp.concatenate([tail_in, tail_in], axis=0)))
        state[:, cols] = spread(low, keeps, a) * old + fresh


def ssm_bwd_kernel(
    last_ref, xbc_ref, dt_ref, cum_ref, cumt_ref, skip_ref, segc_ref, segr_ref, s_ref, n_ref,
    y_ref, g_ref, dxbc_ref, sums_ref, ends_ref, dstate,
):
    chunk = pl.num_programs(0) - 1 - pl.program_id(0)

    @pl.when(pl.program_id(0) == 0)
    def _():
        dstate[...] = jnp.zeros_like(dstate)

    low = lane_iota() < SSM_HEAD_DIM
    madd, carried, tail, keep = chunk_masks(segc_ref, segr_ref, last_ref, chunk)
    dt, cum, cumt = dt_ref[...], cum_ref[...], cumt_ref[...]
    last_cum = cum[CHUNK - 1 : CHUNK, :]
    ecum = jnp.exp(cum) * carried
    tails = jnp.exp(last_cum - cum) * tail
    keeps = jnp.exp(last_cum) * keep
    into, into_rest = split(xbc_ref[:, SSM_INNER : SSM_INNER + STATE])
    outof, outof_rest = split(xbc_ref[:, SSM_INNER + STATE :])
    outof_t = outof.T
    into_both = jnp.concatenate([into, into_rest], axis=1)
    gram = dot_nt(
        jnp.concatenate([outof, outof_rest], axis=1), jnp.concatenate([into, into], axis=1)
    ) + dot_nt(outof, into_rest)
    dgram = jnp.zeros((CHUNK, CHUNK), F32)
    d_into = jnp.zeros((CHUNK, STATE), F32)
    d_outof = jnp.zeros((CHUNK, STATE), F32)
    sum_y = jnp.zeros((CHUNK, LANES), F32)
    sum_x = jnp.zeros((CHUNK, LANES), F32)
    sum_k = jnp.zeros((CHUNK, LANES), F32)
    ends = jnp.zeros((8, LANES), F32)
    lane_pos = lax.broadcasted_iota(jnp.int32, (LANES, LANES), 0) // SSM_HEAD_DIM
    head_pos = lax.broadcasted_iota(jnp.int32, (LANES, LANES), 1)

    def by_head(values, pick):
        high = values.astype(BF16)
        rest = (values - high.astype(F32)).astype(BF16)
        return dot_nn(jnp.concatenate([high, rest], axis=1), pick)

    for p in range(SSM_HEADS // 2):
        a, cols = 2 * p, slice(p * LANES, (p + 1) * LANES)
        pick = jnp.where(lane_pos + a == head_pos, 1.0, 0.0).astype(BF16)
        pick = jnp.concatenate([pick, pick], axis=0)
        heads, grad = xbc_ref[:, cols], g_ref[:, cols]
        dt_wide = spread(low, dt, a)
        skip_wide = spread(low, skip_ref[...], a)
        tail_wide = spread(low, tails, a)
        keep_wide = spread(low, keeps, a)
        scaled = heads * dt_wide
        scaled_low = scaled.astype(BF16)
        decay_a = jnp.exp(cum[:, a : a + 1] - cumt[a : a + 1, :] + madd)
        decay_b = jnp.exp(cum[:, a + 1 : a + 2] - cumt[a + 1 : a + 2, :] + madd)
        grads = wide_split(
            jnp.concatenate([jnp.where(low, grad, 0.0), jnp.where(low, 0.0, grad)], axis=0)
        )
        dmix = dot_nt(grads, jnp.concatenate([scaled_low, scaled_low], axis=1))
        dgram += decay_a * dmix[:CHUNK] + decay_b * dmix[CHUNK:]
        mixing = split(jnp.concatenate([decay_a * gram, decay_b * gram], axis=0))
        d_new = dstate[:, cols]
        d_new_wide = wide_split(d_new)
        d_new_low = d_new_wide[:, :LANES]
        d_inner = dot_tn(jnp.concatenate(mixing, axis=0), jnp.concatenate([grads, grads], axis=0))
        d_scaled = both_sides(d_inner) + tail_wide * both_sides(
            dot_nn(into_both, jnp.concatenate([d_new_wide, d_new_wide], axis=0))
        )
        old = s_ref[0, :, cols]
        d_carry = (spread(low, ecum, a) * grad).astype(BF16)
        d_outof += dot_nt(d_carry, old.astype(BF16))
        d_into += dot_nt((scaled * tail_wide).astype(BF16), d_new_low)
        ends += jnp.sum((d_new * n_ref[0, :, cols]).reshape(STATE // 8, 8, LANES), axis=0) @ pick[
            :LANES
        ].astype(F32)
        dstate[:, cols] = keep_wide * d_new + dot_nn(outof_t, d_carry)
        dxbc_ref[:, cols] = d_scaled * dt_wide + skip_wide * grad
        both = grad * heads
        sum_y += by_head(grad * y_ref[:, cols] - skip_wide * both - scaled * d_scaled, pick)
        sum_x += by_head(heads * d_scaled, pick)
        sum_k += by_head(both, pick)
    dgram_low = dgram.astype(BF16)
    dxbc_ref[:, SSM_INNER : SSM_INNER + STATE] = d_into + dot_tn(dgram_low, outof)
    dxbc_ref[:, SSM_INNER + STATE :] = d_outof + dot_nn(dgram_low, into)
    sums_ref[:, :LANES] = sum_y
    sums_ref[:, LANES : 2 * LANES] = sum_x
    sums_ref[:, 2 * LANES :] = sum_k
    ends_ref[...] = ends.reshape(ends_ref.shape)


def ssm_forward(last, xbc, dt, cum, cumt, skip, segc, segr):
    length = xbc.shape[0]
    chunks = length // CHUNK
    here = lambda c, last: (c, 0)
    across = lambda c, last: (0, c)
    return pl.pallas_call(
        ssm_fwd_kernel,
        grid_spec=pltpu.PrefetchScalarGridSpec(
            num_scalar_prefetch=1,
            grid=(chunks,),
            in_specs=[
                pl.BlockSpec((CHUNK, XBC_WIDTH), here),
                pl.BlockSpec((CHUNK, SSM_HEADS), here),
                pl.BlockSpec((CHUNK, SSM_HEADS), here),
                pl.BlockSpec((SSM_HEADS, CHUNK), across),
                pl.BlockSpec((1, SSM_HEADS), lambda c, last: (0, 0)),
                pl.BlockSpec((CHUNK, 1), here),
                pl.BlockSpec((1, CHUNK), across),
            ],
            out_specs=[
                pl.BlockSpec((CHUNK, SSM_INNER), here),
                pl.BlockSpec((1, STATE, SSM_INNER), lambda c, last: (c, 0, 0)),
            ],
            scratch_shapes=[pltpu.VMEM((STATE, SSM_INNER), F32)],
        ),
        out_shape=[
            jax.ShapeDtypeStruct((length, SSM_INNER), F32),
            jax.ShapeDtypeStruct((chunks, STATE, SSM_INNER), F32),
        ],
        compiler_params=params(),
        cost_estimate=cost(
            8 * length * SSM_INNER * STATE, 24 * length * SSM_INNER, length * CHUNK * SSM_HEADS
        ),
    )(last, xbc, dt, cum, cumt, skip, segc, segr)


def ssm_backward(last, xbc, dt, cum, cumt, skip, segc, segr, states, outputs, grads):
    length = xbc.shape[0]
    chunks = length // CHUNK
    end = chunks - 1
    here = lambda i, last: (end - i, 0)
    across = lambda i, last: (0, end - i)
    return pl.pallas_call(
        ssm_bwd_kernel,
        grid_spec=pltpu.PrefetchScalarGridSpec(
            num_scalar_prefetch=1,
            grid=(chunks,),
            in_specs=[
                pl.BlockSpec((CHUNK, XBC_WIDTH), here),
                pl.BlockSpec((CHUNK, SSM_HEADS), here),
                pl.BlockSpec((CHUNK, SSM_HEADS), here),
                pl.BlockSpec((SSM_HEADS, CHUNK), across),
                pl.BlockSpec((1, SSM_HEADS), lambda i, last: (0, 0)),
                pl.BlockSpec((CHUNK, 1), here),
                pl.BlockSpec((1, CHUNK), across),
                pl.BlockSpec((1, STATE, SSM_INNER), lambda i, last: (end - i, 0, 0)),
                pl.BlockSpec(
                    (1, STATE, SSM_INNER), lambda i, last: (jnp.minimum(end - i + 1, end), 0, 0)
                ),
                pl.BlockSpec((CHUNK, SSM_INNER), here),
                pl.BlockSpec((CHUNK, SSM_INNER), here),
            ],
            out_specs=[
                pl.BlockSpec((CHUNK, XBC_WIDTH), here),
                pl.BlockSpec((CHUNK, 3 * LANES), here),
                pl.BlockSpec((1, 8, LANES), lambda i, last: (end - i, 0, 0)),
            ],
            scratch_shapes=[pltpu.VMEM((STATE, SSM_INNER), F32)],
        ),
        out_shape=[
            jax.ShapeDtypeStruct((length, XBC_WIDTH), F32),
            jax.ShapeDtypeStruct((length, 3 * LANES), F32),
            jax.ShapeDtypeStruct((chunks, 8, LANES), F32),
        ],
        compiler_params=params(),
        cost_estimate=cost(
            24 * length * SSM_INNER * STATE, 40 * length * SSM_INNER, length * CHUNK * SSM_HEADS
        ),
    )(last, xbc, dt, cum, cumt, skip, segc, segr, states, states, outputs, grads)


def conv_act(conv_in, conv_weight, conv_bias, segment):
    length = conv_in.shape[0]
    kernel = conv_weight.reshape(CONV, XBC_WIDTH)
    conv_sum = jnp.zeros_like(conv_in) + conv_bias[None, :]
    for offset in range(CONV):
        shift_by = CONV - 1 - offset
        shifted = jnp.pad(conv_in, ((shift_by, 0), (0, 0)))[:length]
        doc_shift = jnp.pad(segment, (shift_by, 0), constant_values=-1)[:length]
        same_doc = (doc_shift == segment).astype(F32)[:, None]
        conv_sum = conv_sum + kernel[offset][None, :] * shifted * same_doc
    return jax.nn.silu(conv_sum)


def gated_norm(output, gate_part, mixer_gain):
    return rms_gain(output * jax.nn.silu(gate_part), mixer_gain)


def rows_kernel(lo_ref, hi_ref, ids_ref, g_ref, o_ref, wide):
    step = pl.program_id(0)

    @pl.when(step == 0)
    def _():
        o_ref[...] = jnp.zeros_like(o_ref)

    group = g_ref.shape[0]
    wide[...] = g_ref[...].astype(F32)
    low, high = lo_ref[step], hi_ref[step]

    def one(j):
        o_ref[pl.ds(ids_ref[step * group + j], 1), :] += wide[pl.ds(j, 1), :]

    def eight(k, carry):
        for u in range(8):
            one(low + 8 * k + u)
        return carry

    def rest(j, carry):
        one(j)
        return carry

    eights = (high - low) // 8
    lax.fori_loop(0, eights, eight, 0)
    lax.fori_loop(low + 8 * eights, high, rest, 0)


def rows_by_token(local_ids, grads, shard_rows, group):
    count, width = grads.shape
    lists = local_ids.reshape(-1, group)
    low = jnp.sum((lists < 0).astype(jnp.int32), axis=1)
    high = jnp.sum((lists < shard_rows).astype(jnp.int32), axis=1)
    return pl.pallas_call(
        rows_kernel,
        grid_spec=pltpu.PrefetchScalarGridSpec(
            num_scalar_prefetch=3,
            grid=(count // group,),
            in_specs=[pl.BlockSpec((group, width), lambda i, lo, hi, ids: (i, 0))],
            out_specs=pl.BlockSpec((shard_rows, width), lambda i, lo, hi, ids: (0, 0)),
            scratch_shapes=[pltpu.VMEM((group, width), F32)],
        ),
        out_shape=jax.ShapeDtypeStruct((shard_rows, width), F32),
        compiler_params=params(),
        cost_estimate=cost(count * width * LANES, count * width * 2),
    )(low, high, local_ids, grads)


def split_nn(left, right):
    left_high, left_rest = split(left)
    right_high, right_rest = split(right)
    return dot_nn(left_high, right_high) + dot_nn(left_rest, right_high) + dot_nn(left_high, right_rest)


def rotate_kernel(l_ref, g_ref, r_ref, o_ref):
    grad = g_ref[...].reshape(D, BLOCK_COLS)
    left_high, left_rest = split(l_ref[0])
    part = dot_nn(left_high, grad) + dot_nn(left_rest, grad)
    o_ref[0] = split_nn(part, r_ref[0])


def rotate_blocks(left_basis, grad_whole, right_basis):
    slots, depth, _ = left_basis.shape
    rows = grad_whole.shape[0]
    return pl.pallas_call(
        rotate_kernel,
        grid=(slots,),
        in_specs=[
            pl.BlockSpec((1, depth, D), lambda k: (k, 0, 0)),
            pl.BlockSpec((rows, 1, depth, BLOCK_COLS), lambda k: (0, k, 0, 0)),
            pl.BlockSpec((1, BLOCK_COLS, BLOCK_COLS), lambda k: (k, 0, 0)),
        ],
        out_specs=pl.BlockSpec((1, depth, BLOCK_COLS), lambda k: (k, 0, 0)),
        out_shape=jax.ShapeDtypeStruct((slots, depth, BLOCK_COLS), F32),
        compiler_params=params(),
        cost_estimate=cost(6 * slots * depth * D * BLOCK_COLS, slots * depth * D * 5),
    )(left_basis, grad_whole, right_basis)


def step_kernel(scale_ref, rot_ref, m_ref, v_ref, l_ref, r_ref, mo_ref, vo_ref, u_ref):
    rotated = rot_ref[0] * scale_ref[0]
    first_new = soap_first * m_ref[0] + (1.0 - soap_first) * rotated
    second_new = soap_second * v_ref[0] + (1.0 - soap_second) * rotated * rotated
    mo_ref[0], vo_ref[0] = first_new, second_new
    direction = (first_new / scale_ref[1]) / (jnp.sqrt(second_new / scale_ref[2]) + adam_eps)
    turned = split_nn(direction, r_ref[0].T).astype(BF16)
    left_high, left_rest = split(l_ref[0])
    update = dot_nn(left_high.T, turned) + dot_nn(left_rest.T, turned)
    u_ref[0] = update.astype(BF16)


def step_blocks(scales, rotated, block_first, block_second, left_basis, right_basis):
    slots, depth, _ = left_basis.shape
    own = pl.BlockSpec((1, depth, BLOCK_COLS), lambda k: (k, 0, 0))
    small = jax.ShapeDtypeStruct((slots, depth, BLOCK_COLS), F32)
    return pl.pallas_call(
        step_kernel,
        grid=(slots,),
        in_specs=[
            pl.BlockSpec(memory_space=pltpu.SMEM),
            own,
            own,
            own,
            pl.BlockSpec((1, depth, D), lambda k: (k, 0, 0)),
            pl.BlockSpec((1, BLOCK_COLS, BLOCK_COLS), lambda k: (k, 0, 0)),
        ],
        out_specs=[own, own, pl.BlockSpec((1, D, BLOCK_COLS), lambda k: (k, 0, 0))],
        out_shape=[small, small, jax.ShapeDtypeStruct((slots, D, BLOCK_COLS), BF16)],
        compiler_params=params(),
        cost_estimate=cost(6 * slots * depth * D * BLOCK_COLS, slots * depth * D * 7),
    )(scales, rotated, block_first, block_second, left_basis, right_basis)


def total_kernel(rows, cols, x_ref, o_ref, inbox, send_sem, recv_sem):
    row, col = lax.axis_index("row"), lax.axis_index("col")
    partners = []
    bit = 1
    while bit < cols:
        partners.append((row, col + bit - 2 * bit * (col // bit % 2)))
        bit = bit * 2
    bit = 1
    while bit < rows:
        partners.append((row + bit - 2 * bit * (row // bit % 2), col))
        bit = bit * 2
    barrier = pltpu.get_barrier_semaphore()
    for partner in partners:
        pl.semaphore_signal(barrier, inc=1, device_id=partner, device_id_type=MESH)
    pl.semaphore_wait(barrier, len(partners))
    o_ref[...] = x_ref[...]
    for step, partner in enumerate(partners):
        copy = pltpu.make_async_remote_copy(
            src_ref=o_ref,
            dst_ref=inbox.at[step],
            send_sem=send_sem.at[step],
            recv_sem=recv_sem.at[step],
            device_id=partner,
            device_id_type=MESH,
        )
        copy.start()
        copy.wait()
        o_ref[...] += inbox[step]


def total_over_all(values, rows, cols, collective_id):
    steps = (rows - 1).bit_length() + (cols - 1).bit_length()
    return pl.pallas_call(
        functools.partial(total_kernel, rows, cols),
        in_specs=[pl.BlockSpec(memory_space=pltpu.VMEM)],
        out_specs=pl.BlockSpec(memory_space=pltpu.VMEM),
        out_shape=jax.ShapeDtypeStruct(values.shape, F32),
        scratch_shapes=[
            pltpu.VMEM((steps,) + values.shape, F32),
            pltpu.SemaphoreType.DMA((steps,)),
            pltpu.SemaphoreType.DMA((steps,)),
        ],
        compiler_params=params(collective_id=collective_id, has_side_effects=True),
        cost_estimate=cost(steps * values.size, steps * values.size * 4),
    )(values)


def ring_bits(rows, cols):
    bits = []
    for axis, extent in ((0, rows), (1, cols)):
        bit = extent // 2
        while bit >= 1:
            bits.append((axis, bit))
            bit = bit // 2
    return bits


def scatter_orders(rows, cols):
    bits = ring_bits(rows, cols)
    row_bits = [b for b in reversed(bits) if b[0] == 0]
    col_bits = [b for b in reversed(bits) if b[0] == 1]
    return col_bits + row_bits, col_bits[:1] + col_bits[1:][::-1] + row_bits


def tail_kernel(rows, cols, slots, g_ref, p_ref, v_ref, whole_ref, tok_ref, vec_ref, own, *rest):
    bits = ring_bits(rows, cols)
    stages = len(bits)
    row_bits = [b for b in bits if b[0] == 0]
    col_bits = [b for b in bits if b[0] == 1]
    boxes, rest = rest[:stages], rest[stages:]
    vec_box, vec_sum, send_sem, recv_sem, own_sem = rest[:5]
    join_send, join_recv, tok_send, tok_recv, tok_own, vec_send, vec_recv = rest[5:]
    place = (lax.axis_index("row"), lax.axis_index("col"))
    half = whole_ref.shape[-2] // 2
    orders = scatter_orders(rows, cols)

    def side(which):
        axis, bit = which
        return place[axis] // bit % 2

    def partner(which):
        axis, bit = which
        moved = place[axis] + bit - 2 * bit * side(which)
        return (moved, place[1]) if axis == 0 else (place[0], moved)

    def remote(src, dst, send, recv, which):
        return pltpu.make_async_remote_copy(
            src_ref=src,
            dst_ref=dst,
            send_sem=send,
            recv_sem=recv,
            device_id=partner(which),
            device_id_type=MESH,
        )

    barrier = pltpu.get_barrier_semaphore()
    for which in bits:
        pl.semaphore_signal(barrier, inc=1, device_id=partner(which), device_id_type=MESH)
    pl.semaphore_wait(barrier, stages)
    units = [(slot, h) for slot in range(slots) for h in range(2)]

    def pick(ref, before, which, side_of, after):
        at = before.index(which)
        return ref.at[(slice(None),) * at + (side_of,) + (slice(None),) * (len(before) - at - 1) + after]

    def part(slot, h, side_of):
        return pick(g_ref, bits, orders[h][0], side_of, (slot, slice(h * half, (h + 1) * half)))

    def cut(stage, u, side_of):
        order = orders[units[u][1]]
        left = [b for b in bits if b not in order[: stage + 1]]
        return pick(boxes[stage].at[u], left, order[stage + 1], side_of, ())

    def send(stage, u):
        slot, h = units[u]
        which = orders[h][stage]
        other = 1 - side(which)
        return remote(
            part(slot, h, other) if stage == 0 else cut(stage - 1, u, other),
            boxes[stage].at[u],
            send_sem.at[stage, u],
            recv_sem.at[stage, u],
            which,
        )

    def keep(u):
        slot, h = units[u]
        return pltpu.make_async_copy(part(slot, h, side(orders[h][0])), own.at[u], own_sem.at[u])

    def joined(ref, order, of_bits, stage, after):
        at = tuple(slice(None) if b in order[:stage] else side(b) for b in of_bits)
        return ref.at[at + after]

    def join(stage, u):
        slot, h = units[u]
        region = joined(whole_ref, row_bits, row_bits, stage, (slot, slice(h * half, (h + 1) * half)))
        return remote(region, region, join_send.at[stage, u], join_recv.at[stage, u], row_bits[stage])

    def tok(stage, h):
        order = (orders[h][1 : len(col_bits)] + orders[h][:1])
        region = joined(tok_ref, order, col_bits, stage, (h,))
        return remote(
            p_ref.at[h] if stage == 0 else region, region, tok_send.at[stage, h],
            tok_recv.at[stage, h], order[stage],
        )

    def tok_keep():
        region = joined(tok_ref, [], col_bits, 0, ())
        return pltpu.make_async_copy(p_ref, region, tok_own)

    def vec(stage):
        return remote(
            vec_sum.at[stage], vec_box.at[stage], vec_send.at[stage], vec_recv.at[stage], bits[stage]
        )

    sent = []

    def start(copy):
        copy.start()
        sent.append(copy)
        return copy

    flying = {}
    vec_sum[0] = v_ref[...]
    flying["vec", 0] = start(vec(0))
    for u in range(len(units)):
        flying[0, u] = start(send(0, u))
        keep(u).start()
        if u == 1:
            tok_keep().start()
            for h in range(2):
                flying["tok", 0, h] = start(tok(0, h))
    steps = slots + stages + len(row_bits) - 1
    tok_at = [(k + 1) * steps // (len(col_bits) + 1) for k in range(len(col_bits))]
    for t in range(steps):
        if t < stages:
            flying["vec", t].wait_recv()
            if t + 1 < stages:
                vec_sum[t + 1] = vec_sum[t] + vec_box[t]
                flying["vec", t + 1] = start(vec(t + 1))
            else:
                vec_ref[...] = vec_sum[t] + vec_box[t]
        for k, at in enumerate(tok_at):
            if at == t:
                if k == 0:
                    tok_keep().wait()
                for h in range(2):
                    flying["tok", k, h].wait_recv()
                    if k + 1 < len(col_bits):
                        flying["tok", k + 1, h] = start(tok(k + 1, h))
        for stage in reversed(range(stages + len(row_bits))):
            slot = t - stage
            if not 0 <= slot < slots:
                continue
            for h in range(2):
                u = 2 * slot + h
                if stage >= stages:
                    flying["join", stage - stages, u].wait_recv()
                    if stage - stages + 1 < len(row_bits):
                        flying["join", stage - stages + 1, u] = start(join(stage - stages + 1, u))
                    continue
                flying[stage, u].wait_recv()
                box = boxes[stage].at[u]
                if stage == 0:
                    keep(u).wait()
                    held = own.at[u]
                else:
                    held = cut(stage - 1, u, side(orders[h][stage]))
                if stage == stages - 1:
                    total = held[...].astype(F32) + box[...].astype(F32)
                    mine = joined(
                        whole_ref, [], row_bits, 0, (slot, slice(h * half, (h + 1) * half))
                    )
                    mine[...] = total.astype(BF16)
                    flying["join", 0, u] = start(join(0, u))
                    continue
                extents = box.shape[:-2]

                def add(k, carry, box=box, held=held, extents=extents):
                    at = []
                    for extent in reversed(extents):
                        at.append(k % extent)
                        k = k // extent
                    at = tuple(reversed(at))
                    box[at] = (held[at].astype(F32) + box[at].astype(F32)).astype(BF16)
                    return carry

                lax.fori_loop(0, 2 ** len(extents), add, 0)
                flying[stage + 1, u] = start(send(stage + 1, u))
    for copy in sent:
        copy.wait_send()


def tail_exchange(grads, pieces, vectors, rows, cols, collective_id):
    _, nslots, depth, _ = grads.shape
    slots = nslots // cols
    bits = ring_bits(rows, cols)
    stages = len(bits)
    row_stages, col_stages = (rows - 1).bit_length(), (cols - 1).bit_length()
    units, half = 2 * slots, depth // 2
    count, width = pieces.shape
    boxes = [
        pltpu.VMEM((units,) + (2,) * (stages - s - 1) + (half, BLOCK_COLS), BF16)
        for s in range(stages)
    ]
    vec_shape = (stages,) + vectors.shape
    whole, tokens, total = pl.pallas_call(
        functools.partial(tail_kernel, rows, cols, slots),
        in_specs=[
            pl.BlockSpec(memory_space=pl.ANY),
            pl.BlockSpec(memory_space=pl.ANY),
            pl.BlockSpec(memory_space=pltpu.VMEM),
        ],
        out_specs=[
            pl.BlockSpec(memory_space=pltpu.VMEM),
            pl.BlockSpec(memory_space=pl.ANY),
            pl.BlockSpec(memory_space=pltpu.VMEM),
        ],
        out_shape=[
            jax.ShapeDtypeStruct((2,) * row_stages + (slots, depth, BLOCK_COLS), BF16),
            jax.ShapeDtypeStruct((2,) * col_stages + (2, count // 2, width), BF16),
            jax.ShapeDtypeStruct(vectors.shape, F32),
        ],
        scratch_shapes=[pltpu.VMEM(boxes[0].shape, BF16)]
        + boxes
        + [
            pltpu.VMEM(vec_shape, F32),
            pltpu.VMEM(vec_shape, F32),
            pltpu.SemaphoreType.DMA((stages, units)),
            pltpu.SemaphoreType.DMA((stages, units)),
            pltpu.SemaphoreType.DMA((units,)),
            pltpu.SemaphoreType.DMA((row_stages, units)),
            pltpu.SemaphoreType.DMA((row_stages, units)),
            pltpu.SemaphoreType.DMA((col_stages, 2)),
            pltpu.SemaphoreType.DMA((col_stages, 2)),
            pltpu.SemaphoreType.DMA,
            pltpu.SemaphoreType.DMA((stages,)),
            pltpu.SemaphoreType.DMA((stages,)),
        ],
        compiler_params=params(collective_id=collective_id, has_side_effects=True),
        cost_estimate=cost(rows * nslots * depth * BLOCK_COLS, rows * nslots * depth * BLOCK_COLS * 6),
    )(
        grads.reshape((2,) * stages + (slots, depth, BLOCK_COLS)),
        pieces.reshape(2, count // 2, width),
        vectors,
    )
    return whole.reshape(rows, slots, depth, BLOCK_COLS), tokens.reshape(cols * count, width), total


def exchange_rows(values, rows):
    row = lax.axis_index("row")
    width = values.shape[1] // rows
    arrived = []
    for k in range(rows):
        part = lax.dynamic_slice_in_dim(values, (row + k) % rows * width, width, 1)
        if k > 0:
            part = lax.ppermute(part, "row", [(r, (r + k) % rows) for r in range(rows)])
        arrived.append(part)
    return jnp.concatenate(arrived, axis=0)


def adam_step(weights, grads, first, second, steps_done, decay, rate):
    first_new = adam_first * first + (1.0 - adam_first) * grads
    second_new = adam_second * second + (1.0 - adam_second) * grads * grads
    direction = (
        first_new
        / (1.0 - adam_first**steps_done)
        / (jnp.sqrt(second_new / (1.0 - adam_second**steps_done)) + adam_eps)
    )
    return (weights - rate * (direction + decay * weights), first_new, second_new)


def body(
    rows,
    cols,
    token_ids,
    segment_ids,
    loss_positions,
    loss_targets,
    loss_valid,
    block_owner,
    step_count,
    block_weights,
    block_first,
    block_second,
    left_basis,
    right_basis,
    table,
    table_first,
    table_second,
    vector_params,
    vector_first,
    vector_second,
):
    col_index = lax.axis_index("col")
    tokens = token_ids[0]
    segment = segment_ids[0]
    length = tokens.shape[0]
    in_cols = 2 * SSM_INNER + 2 * STATE
    in_blocks = (in_cols + (HEADS + 2 * KV_HEADS) * HEAD_DIM) // BLOCK_COLS
    branch_blocks = (SSM_INNER + HEADS * HEAD_DIM) // BLOCK_COLS
    gate_blocks = 2 * FF // BLOCK_COLS
    down_blocks = FF // BLOCK_COLS
    branch_at = in_blocks
    gate_at = branch_at + branch_blocks
    down_at = gate_at + gate_blocks
    nblocks = block_owner.shape[0]
    depth = block_weights.shape[1]
    shard_rows = table.shape[0]

    row_index = lax.axis_index("row")
    devices = rows * cols
    count_rows = loss_positions.shape[1]
    table_low = table.astype(BF16)
    shard_padded = -(-shard_rows // PAD_ROWS) * PAD_ROWS
    padded = jnp.pad(table_low, ((0, shard_padded - shard_rows), (0, 0)))
    table_cols = lax.all_gather(padded, "col", axis=0, tiled=True)
    order = jnp.argsort(tokens)
    sent = jnp.concatenate(
        [tokens, jnp.sort(tokens), loss_targets[0], loss_valid[0]]
    ).reshape(1, -1)
    ints = lax.all_gather(sent, ("row", "col"), axis=0, tiled=True).reshape(rows, cols, -1)
    gathered = lax.all_gather(
        block_weights.astype(BF16), ("row", "col"), axis=0, tiled=True
    ).reshape(rows, nblocks, depth, BLOCK_COLS)
    table_rows = lax.all_gather(padded, "row", axis=1, tiled=True)
    token_list = lax.dynamic_index_in_dim(ints, col_index, 1, False)[:, :length].reshape(-1)
    owners = token_list // shard_rows
    looked_up = jnp.take(
        table_cols, token_list + owners * (shard_padded - shard_rows), axis=0, mode="clip"
    )
    embedded = lax.all_to_all(looked_up, "row", split_axis=0, concat_axis=1, tiled=True)
    sorted_ints = ints[:, :, length : 2 * length]
    sorted_all = jnp.stack(
        [
            lax.dynamic_index_in_dim(sorted_ints, (row_index - k) % rows, 0, False)
            for k in range(rows)
        ],
        axis=1,
    ).reshape(-1)
    labels_all = lax.dynamic_index_in_dim(ints, row_index, 0, False)[:, 2 * length :]
    targets_all = labels_all[:, :count_rows].reshape(-1)
    valid_all = labels_all[:, count_rows:].reshape(-1)
    valid_count = jnp.sum(ints[:, :, 2 * length + count_rows :]).astype(F32)

    conv_weight, conv_bias, time_bias, decay_log, skip_gain, mixer_gain, norm_gains, time_proj = (
        unpack(vector_params)
    )
    gain_rows = norm_gains.reshape(3, D)
    time_low = time_proj.reshape(D, SSM_HEADS).astype(BF16)
    segc, segr = segment[:, None], segment[None, :]
    chunks = length // CHUNK
    last_docs = segment.reshape(chunks, CHUNK)[:, CHUNK - 1]
    cosine, sine = rope_tables(length)

    embed_wide = embedded.astype(F32)
    normed_wide, first_norm_back = jax.vjp(rms_gain, embed_wide, gain_rows[0])
    normed = normed_wide.astype(BF16)
    both_proj = project(normed, gathered, block_owner, 0, in_blocks)
    time_raw = jnp.dot(normed, time_low, preferred_element_type=F32)

    def steps_of(time_in, bias_in, decay_in):
        step_size = jax.nn.softplus(time_in + bias_in[None, :])
        return step_size, step_size * -jnp.exp(decay_in)[None, :]

    (step_size, decays), steps_back = jax.vjp(steps_of, time_raw, time_bias, decay_log)
    earlier = jnp.tril(jnp.ones((CHUNK, CHUNK), F32))
    decays_cut = decays.reshape(chunks, CHUNK, SSM_HEADS)
    cum = jnp.einsum("ts,csh->cth", earlier, decays_cut, precision=highest).reshape(
        length, SSM_HEADS
    )
    cumt = cum.T
    act_xbc, conv_back = jax.vjp(
        lambda u, w, b: conv_act(u, w, b, segment),
        both_proj[:, SSM_INNER:in_cols],
        conv_weight,
        conv_bias,
    )
    skip_row = skip_gain[None, :]
    scan_in = (last_docs, act_xbc, step_size, cum, cumt, skip_row, segc, segr)
    scan_out, states = ssm_forward(*scan_in)
    mixer_wide, gated_back = jax.vjp(gated_norm, scan_out, both_proj[:, :SSM_INNER], mixer_gain)
    context = attention_forward(both_proj, segc, segr, cosine, sine)
    branch_in = jnp.concatenate([mixer_wide.astype(BF16), context], axis=1)
    hidden_one = project_back(branch_in, gathered, block_owner, branch_at, branch_blocks, embed_wide)
    second_wide, second_norm_back = jax.vjp(rms_gain, hidden_one, gain_rows[1])
    normed_two = second_wide.astype(BF16)
    gate_up = project(normed_two, gathered, block_owner, gate_at, gate_blocks)
    activated, swiglu_back = jax.vjp(swiglu, gate_up[:, :FF], gate_up[:, FF:])
    act_low = activated.astype(BF16)
    hidden_two = project_back(act_low, gathered, block_owner, down_at, down_blocks, hidden_one)
    final_wide, final_norm_back = jax.vjp(rms_gain, hidden_two, gain_rows[2])
    final_out = final_wide.astype(BF16)
    positions = loss_positions[0]
    chosen = (positions[:, None] == jnp.arange(length, dtype=jnp.int32)[None, :]).astype(BF16)
    picked_rows = jnp.dot(chosen, final_out, preferred_element_type=F32).astype(BF16)
    rows_all = lax.all_gather(picked_rows, "col", axis=0, tiled=True)

    logits = jnp.einsum("rd,vd->rv", rows_all, table_rows, preferred_element_type=F32)
    local_target = targets_all - col_index * shard_rows
    places = jnp.arange(shard_padded, dtype=jnp.int32)[None, :]
    onehot = (places == local_target[:, None]) & (places < shard_rows)
    logits = jnp.where(places < shard_rows, logits, -1e30)
    row_top = jnp.max(logits, axis=1)
    row_total = jnp.sum(jnp.exp(logits - row_top[:, None]), axis=1)
    target_logit = jnp.sum(jnp.where(onehot, logits, 0.0), axis=1)
    parts = lax.all_gather(jnp.stack([row_top, row_total, target_logit]), "col", axis=0)
    top_all = jnp.max(parts[:, 0], axis=0)
    total_all = jnp.sum(parts[:, 1] * jnp.exp(parts[:, 0] - top_all[None, :]), axis=0)
    target_all = jnp.sum(parts[:, 2], axis=0)
    log_total = top_all + jnp.log(total_all)
    valid_wide = valid_all.astype(F32)
    own_loss = lax.dynamic_slice_in_dim(
        (log_total - target_all) * valid_wide, col_index * count_rows, count_rows
    )
    logit_grad = (
        (jnp.exp(logits - log_total[:, None]) - onehot.astype(F32))
        * (valid_wide / valid_count)[:, None]
    ).astype(BF16)
    rows_grad = lax.psum_scatter(
        jnp.einsum("rv,vd->rd", logit_grad, table_rows, preferred_element_type=F32),
        "col",
        scatter_dimension=0,
        tiled=True,
    )
    table_loss_grad = jnp.einsum("rv,rd->vd", logit_grad, rows_all, preferred_element_type=F32)
    table_loss_low, rows_grad = lax.optimization_barrier((table_loss_grad.astype(BF16), rows_grad))
    table_loss_mine = lax.psum_scatter(table_loss_low, "row", scatter_dimension=1, tiled=True)
    final_grad = jnp.zeros((length, D), F32).at[positions].add(rows_grad)
    hidden_two_grad, gain_final_grad = final_norm_back(final_grad)
    down_in = hidden_two_grad.astype(BF16)
    act_grad = project(down_in, gathered, block_owner, down_at, down_blocks)
    like = (rows, nblocks, depth, BLOCK_COLS)
    gate_grad, up_grad = swiglu_back(act_grad)
    gate_up_grad = jnp.concatenate([gate_grad, up_grad], axis=1).astype(BF16)
    no_base = jnp.zeros((length, D), F32)
    normed_two_grad = project_back(
        gate_up_grad, gathered, block_owner, gate_at, gate_blocks, no_base
    )
    hidden_one_part, gain_ff_grad = second_norm_back(normed_two_grad)
    hidden_one_grad = hidden_two_grad + hidden_one_part
    branch_grad_low = hidden_one_grad.astype(BF16)
    branch_out_grad = project(branch_grad_low, gathered, block_owner, branch_at, branch_blocks)

    dq, dkv = attention_backward(
        both_proj, segc, segr, cosine, sine, branch_out_grad, SSM_INNER // LANES
    )
    scan_grad, gate_part_grad, mixer_gain_grad = gated_back(branch_out_grad[:, :SSM_INNER])
    xbc_grad, sums, ends = ssm_backward(*scan_in, states, scan_out, scan_grad)
    sum_y, sum_x, sum_k = (
        sums[:, i * LANES : i * LANES + SSM_HEADS] for i in range(3)
    )
    skip_grad = jnp.sum(sum_k, axis=0)
    cum_grad = sum_y.reshape(chunks, CHUNK, SSM_HEADS)
    decays_grad = jnp.einsum("ts,cth->csh", earlier, cum_grad, precision=highest)
    decays_grad = decays_grad + jnp.sum(ends, axis=1)[:, None, :SSM_HEADS]
    time_grad, time_bias_grad, decay_log_grad = steps_back(
        (sum_x, decays_grad.reshape(length, SSM_HEADS))
    )
    conv_in_grad, conv_weight_grad, conv_bias_grad = conv_back(xbc_grad)
    in_grad_low = jnp.concatenate(
        [gate_part_grad.astype(BF16), conv_in_grad.astype(BF16), dq, dkv], axis=1
    )
    in_grad_low, table_loss_mine = lax.optimization_barrier((in_grad_low, table_loss_mine))
    time_grad_low = time_grad.astype(BF16)
    grad_time = jnp.einsum("td,th->dh", normed, time_grad_low, preferred_element_type=F32)
    time_part = jnp.einsum("th,dh->td", time_grad_low, time_low, preferred_element_type=F32)
    normed_grad = project_back(in_grad_low, gathered, block_owner, 0, in_blocks, time_part)
    embed_part, gain_in_grad = first_norm_back(normed_grad)
    embed_grad = (hidden_one_grad + embed_part).astype(BF16)
    placed = (order[:, None] == jnp.arange(length, dtype=jnp.int32)[None, :]).astype(BF16)
    embed_sorted = jnp.dot(placed, embed_grad, preferred_element_type=F32).astype(BF16)
    embed_sorted, down_in, normed_two, branch_grad_low, normed = lax.optimization_barrier(
        (embed_sorted, down_in, normed_two, branch_grad_low, normed)
    )
    pieces = exchange_rows(embed_sorted, rows)
    grad_slots = weight_grad(down_in, act_low, block_owner, down_at, like, None)
    grad_slots = weight_grad(normed_two, gate_up_grad, block_owner, gate_at, like, grad_slots)
    grad_slots = weight_grad(branch_grad_low, branch_in, block_owner, branch_at, like, grad_slots)
    grad_slots = weight_grad(normed, in_grad_low, block_owner, 0, like, grad_slots)
    grad_slots, pieces = lax.optimization_barrier((grad_slots, pieces))
    vector_grad = jnp.concatenate(
        [
            conv_weight_grad,
            conv_bias_grad,
            time_bias_grad,
            decay_log_grad,
            skip_grad,
            mixer_gain_grad,
            gain_in_grad,
            gain_ff_grad,
            gain_final_grad,
            grad_time.reshape(-1),
            jnp.sum(own_loss)[None],
        ]
    )
    nvec = vector_params.shape[0]
    packed_len = -(-(nvec + 1) // (8 * LANES)) * 8 * LANES
    to_sum = jnp.pad(vector_grad, (0, packed_len - nvec - 1)).reshape(-1, LANES)
    grad_whole, grads_tokens, summed = tail_exchange(grad_slots, pieces, to_sum, rows, cols, 1)
    summed = summed.reshape(-1)
    vector_total, loss_sum = summed[:nvec], summed[nvec]
    local_tokens = sorted_all - col_index * shard_rows
    table_input_grad = rows_by_token(local_tokens, grads_tokens, shard_rows, length)
    table_grad = table_loss_mine[:shard_rows].astype(F32) + table_input_grad
    grad_mine_wide = lax.dynamic_index_in_dim(grad_whole, row_index, 0, False).astype(F32)
    square_part = jnp.sum(grad_mine_wide * grad_mine_wide) + jnp.sum(table_grad * table_grad)
    square_total = total_over_all(jnp.full((8, LANES), square_part), rows, cols, 0)[0, 0]
    rotated = rotate_blocks(left_basis, grad_whole, right_basis)
    mean_loss = loss_sum / valid_count
    grad_norm = jnp.sqrt(square_total + jnp.sum(vector_total * vector_total))
    clip_scale = jnp.minimum(1.0, clip_limit / (grad_norm + 1e-06))
    steps_done = step_count[0].astype(F32)
    scales = jnp.stack(
        [clip_scale, 1.0 - soap_first**steps_done, 1.0 - soap_second**steps_done]
    )
    first_new, second_new, partial_update = step_blocks(
        scales, rotated, block_first, block_second, left_basis, right_basis
    )
    update = lax.psum_scatter(
        partial_update, "row", scatter_dimension=1, tiled=True
    ).astype(F32)
    new_blocks = block_weights - learn_rate * (update + weight_decay * block_weights)
    new_table, table_first_new, table_second_new = adam_step(
        table,
        table_grad * clip_scale,
        table_first,
        table_second,
        steps_done,
        weight_decay,
        learn_rate,
    )
    new_vectors, vector_first_new, vector_second_new = adam_step(
        vector_params,
        vector_total * clip_scale,
        vector_first,
        vector_second,
        steps_done,
        0.0,
        vector_rate,
    )
    return (
        mean_loss,
        grad_norm,
        new_blocks,
        first_new,
        second_new,
        new_table,
        table_first_new,
        table_second_new,
        new_vectors,
        vector_first_new,
        vector_second_new,
    )


def solution(mesh):
    rows, cols = mesh.shape["row"], mesh.shape["col"]
    placed = (
        P(("row", "col"), None),
        P(("row", "col"), None),
        P(("row", "col"), None),
        P(("row", "col"), None),
        P(("row", "col"), None),
        P(),
        P(),
        P("col", "row", None),
        P("col", "row", None),
        P("col", "row", None),
        P("col", "row", None),
        P("col", None, None),
        P("col", "row"),
        P("col", "row"),
        P("col", "row"),
        P(),
        P(),
        P(),
    )
    return jax.shard_map(
        functools.partial(body, rows, cols),
        mesh=mesh,
        in_specs=placed,
        out_specs=(
            P(),
            P(),
            P("col", "row", None),
            P("col", "row", None),
            P("col", "row", None),
            P("col", "row"),
            P("col", "row"),
            P("col", "row"),
            P(),
            P(),
            P(),
        ),
        check_vma=False,
    )
```

```python
import functools

import jax
import jax.numpy as jnp
from jax import lax
from jax.experimental import pallas as pl
from jax.experimental.pallas import tpu as pltpu
from jax.sharding import PartitionSpec as P

D = 1024
HEADS = 8
KV_HEADS = 2
HEAD_DIM = 64
SSM_HEADS = 24
SSM_HEAD_DIM = 64
STATE = 128
CONV = 4
FF = 2048
BLOCK_COLS = 256
SSM_INNER = 1536
XBC_WIDTH = 1792
CHUNK = 128
QROWS = 256
LANES = 128
TABLE_PARTS = 4
PAD_ROWS = 16 * TABLE_PARTS
GROUP = 4
ROW_PART = 128

BF16 = jnp.bfloat16
F32 = jnp.float32
MESH = pl.DeviceIdType.MESH
highest = lax.Precision.HIGHEST
rope_base = 100000000000.0
clip_limit = 1.0
learn_rate = 0.01
vector_rate = 0.08
weight_decay = 0.1
soap_first = 0.95
soap_second = 0.95
adam_first = 0.9
adam_second = 0.95
adam_eps = 1e-08
vmem_bytes = 56 * 1024 * 1024


def params(**more):
    return pltpu.CompilerParams(vmem_limit_bytes=vmem_bytes, **more)


def cost(flops, nbytes, exps=0):
    return pl.CostEstimate(flops=int(flops), bytes_accessed=int(nbytes), transcendentals=int(exps))


def rms_gain(values, gain_vec):
    inv_scale = lax.rsqrt(jnp.mean(values * values, axis=-1, keepdims=True) + 1e-05)
    return values * inv_scale * gain_vec


def unpack(flattened):
    piece_sizes = [
        CONV * XBC_WIDTH,
        XBC_WIDTH,
        SSM_HEADS,
        SSM_HEADS,
        SSM_HEADS,
        SSM_INNER,
        3 * D,
        D * SSM_HEADS,
    ]
    pieces = []
    offset = 0
    for length in piece_sizes:
        pieces.append(flattened[offset : offset + length])
        offset = offset + length
    return pieces


def dot_nt(left, right):
    return lax.dot_general(left, right, (((1,), (1,)), ((), ())), preferred_element_type=F32)


def dot_tn(left, right):
    return lax.dot_general(left, right, (((0,), (0,)), ((), ())), preferred_element_type=F32)


def dot_nn(left, right):
    return jnp.dot(left, right, preferred_element_type=F32)


def slot_spec(gathered, at, every):
    rows, _, depth, _ = gathered.shape
    return pl.BlockSpec(
        (rows, 1, depth, BLOCK_COLS), lambda k, own: (0, own[at + every * k], 0, 0)
    )


def whole(shape):
    return pl.BlockSpec(shape, lambda k, own: (0,) * len(shape))


def block_of(w_ref):
    return w_ref[...].reshape(D, BLOCK_COLS)


def slot_call(kernel, owner, steps, in_specs, out_specs, out_shape, flops, operands):
    nbytes = sum(o.size * o.dtype.itemsize for o in operands[:1])
    return pl.pallas_call(
        kernel,
        grid_spec=pltpu.PrefetchScalarGridSpec(
            num_scalar_prefetch=1, grid=(steps,), in_specs=in_specs, out_specs=out_specs
        ),
        out_shape=out_shape,
        compiler_params=params(),
        cost_estimate=cost(flops, flops // 512 + nbytes),
    )(owner, *operands)


def cols_of(k):
    return slice(k * BLOCK_COLS, (k + 1) * BLOCK_COLS)


def project_kernel(own_ref, x_ref, *rest):
    o_ref = rest[-1]
    for g, w_ref in enumerate(rest[:-1]):
        o_ref[:, cols_of(g)] = dot_nn(x_ref[...], block_of(w_ref))


def project(rows_in, gathered, owner, first, count):
    length = rows_in.shape[0]
    return slot_call(
        project_kernel,
        owner,
        count // GROUP,
        [whole((length, D))] + [slot_spec(gathered, first + g, GROUP) for g in range(GROUP)],
        pl.BlockSpec((length, GROUP * BLOCK_COLS), lambda k, own: (0, k)),
        jax.ShapeDtypeStruct((length, count * BLOCK_COLS), F32),
        2 * length * D * BLOCK_COLS * count,
        [rows_in] + [gathered] * GROUP,
    )


def sigmoid(values):
    return 1.0 / (1.0 + jnp.exp(-values))


def gate_up_kernel(own_ref, x_ref, *rest):
    w_refs, (gate_ref, up_ref, act_ref) = rest[:-3], rest[-3:]
    half = len(w_refs) // 2
    for g in range(half):
        gate = dot_nn(x_ref[...], block_of(w_refs[g]))
        up = dot_nn(x_ref[...], block_of(w_refs[half + g]))
        gate_ref[:, cols_of(g)] = gate
        up_ref[:, cols_of(g)] = up
        act_ref[:, cols_of(g)] = (gate * sigmoid(gate) * up).astype(BF16)


def project_gate_up(rows_in, gathered, owner, first, count):
    length = rows_in.shape[0]
    pairs = GROUP // 2
    wide = pl.BlockSpec((length, pairs * BLOCK_COLS), lambda k, own: (0, k))
    shapes = [jax.ShapeDtypeStruct((length, count * BLOCK_COLS), t) for t in (F32, F32, BF16)]
    return slot_call(
        gate_up_kernel,
        owner,
        count // pairs,
        [whole((length, D))]
        + [slot_spec(gathered, first + g, pairs) for g in range(pairs)]
        + [slot_spec(gathered, first + count + g, pairs) for g in range(pairs)],
        [wide] * 3,
        shapes,
        4 * length * D * BLOCK_COLS * count,
        [rows_in] + [gathered] * (2 * pairs),
    )


def act_back_kernel(own_ref, x_ref, gate_ref, up_ref, *rest):
    o_ref = rest[-1]
    for g, w_ref in enumerate(rest[:-1]):
        act_grad = dot_nn(x_ref[...], block_of(w_ref))
        gate, up = gate_ref[:, cols_of(g)], up_ref[:, cols_of(g)]
        sig = sigmoid(gate)
        silu = gate * sig
        o_ref[0, :, cols_of(g)] = (act_grad * up * (sig + silu * (1.0 - sig))).astype(BF16)
        o_ref[1, :, cols_of(g)] = (act_grad * silu).astype(BF16)


def project_act_back(rows_in, gate, up, gathered, owner, first, count):
    length = rows_in.shape[0]
    pairs = GROUP // 2
    wide = pl.BlockSpec((length, pairs * BLOCK_COLS), lambda k, own: (0, k))
    return slot_call(
        act_back_kernel,
        owner,
        count // pairs,
        [whole((length, D)), wide, wide]
        + [slot_spec(gathered, first + g, pairs) for g in range(pairs)],
        pl.BlockSpec((2, length, pairs * BLOCK_COLS), lambda k, own: (0, 0, k)),
        jax.ShapeDtypeStruct((2, length, count * BLOCK_COLS), BF16),
        2 * length * D * BLOCK_COLS * count,
        [rows_in, gate, up] + [gathered] * pairs,
    )


def add_products(c_refs, w_refs, o_ref):
    cols = [c_ref[...].reshape(-1, c_ref.shape[-1]) for c_ref in c_refs]
    cols = cols[0] if len(cols) == 1 else jnp.concatenate(cols, axis=1)
    o_ref[...] += dot_nt(cols, jnp.concatenate([block_of(w) for w in w_refs], axis=1))


def row_parts(length):
    return [slice(i, i + ROW_PART) for i in range(0, length, ROW_PART)]


def back_norm_kernel(own_ref, c_ref, *rest):
    w_refs, (base_ref, gain_ref, o_ref, n_ref) = rest[:-4], rest[-4:]

    @pl.when(pl.program_id(0) == 0)
    def _():
        o_ref[...] = base_ref[...].astype(F32)

    add_products([c_ref], w_refs, o_ref)

    @pl.when(pl.program_id(0) == pl.num_programs(0) - 1)
    def _():
        for part in row_parts(o_ref.shape[0]):
            n_ref[part, :] = rms_gain(o_ref[part, :], gain_ref[...]).astype(BF16)


def back_then_norm(cols_in, gathered, owner, first, count, base, gain):
    length = cols_in.shape[0]
    return slot_call(
        back_norm_kernel,
        owner,
        count // GROUP,
        [pl.BlockSpec((length, GROUP * BLOCK_COLS), lambda k, own: (0, k))]
        + [slot_spec(gathered, first + g, GROUP) for g in range(GROUP)]
        + [whole((length, D)), whole((1, D))],
        [whole((length, D))] * 2,
        [jax.ShapeDtypeStruct((length, D), t) for t in (F32, BF16)],
        2 * length * D * BLOCK_COLS * count,
        [cols_in] + [gathered] * GROUP + [base, gain.reshape(1, D)],
    )


def back_grad_kernel(parts, own_ref, *rest):
    c_refs, rest = rest[:parts], rest[parts:]
    w_refs, rest = rest[:-8], rest[-8:]
    start_ref, x_ref, gain_ref, more_ref, o_ref, low_ref, dgain_ref, total = rest

    @pl.when(pl.program_id(0) == 0)
    def _():
        total[...] = start_ref[...]

    add_products(c_refs, w_refs, total)

    @pl.when(pl.program_id(0) == pl.num_programs(0) - 1)
    def _():
        dgain = jnp.zeros((1, D), F32)
        for part in row_parts(total.shape[0]):
            x, grad = x_ref[part, :].astype(F32), total[part, :]
            inv = lax.rsqrt(jnp.mean(x * x, axis=-1, keepdims=True) + 1e-05)
            unit = x * inv
            dgain += jnp.sum(grad * unit, axis=0, keepdims=True)
            scaled = grad * gain_ref[...]
            back = inv * (scaled - unit * jnp.mean(scaled * unit, axis=-1, keepdims=True))
            result = more_ref[part, :] + back
            o_ref[part, :] = result
            low_ref[part, :] = result.astype(BF16)
        dgain_ref[...] = dgain


def back_through_norm(cols_in, gathered, owner, first, count, start, x, gain, more):
    parts, length, _ = cols_in.shape
    group = GROUP // parts
    every = count // parts
    return pl.pallas_call(
        functools.partial(back_grad_kernel, parts),
        grid_spec=pltpu.PrefetchScalarGridSpec(
            num_scalar_prefetch=1,
            grid=(every // group,),
            in_specs=[
                pl.BlockSpec(
                    (1, length, group * BLOCK_COLS), lambda k, own, part=part: (part, 0, k)
                )
                for part in range(parts)
            ]
            + [
                slot_spec(gathered, first + part * every + g, group)
                for part in range(parts)
                for g in range(group)
            ]
            + [whole((length, D)), whole((length, D)), whole((1, D)), whole((length, D))],
            out_specs=[whole((length, D)), whole((length, D)), whole((1, D))],
            scratch_shapes=[pltpu.VMEM((length, D), F32)],
        ),
        out_shape=[
            jax.ShapeDtypeStruct((length, D), F32),
            jax.ShapeDtypeStruct((length, D), BF16),
            jax.ShapeDtypeStruct((1, D), F32),
        ],
        compiler_params=params(),
        cost_estimate=cost(
            2 * length * D * BLOCK_COLS * count, count * BLOCK_COLS * (2 * D + 2 * length)
        ),
    )(owner, *[cols_in] * parts, *[gathered] * GROUP, start, x, gain.reshape(1, D), more)


def wgrad_kernel(own_ref, l_ref, r_ref, *rest):
    o_ref, turned = rest[-2], rest[-1]

    @pl.when(pl.program_id(0) == 0)
    def _():
        turned[...] = l_ref[...].T

    grad = dot_nn(turned[...], r_ref[0])
    o_ref[...] = grad.astype(BF16).reshape(o_ref.shape)


def weight_grad(left_rows, right_cols, owner, first, like, into):
    rows, nslots, depth, _ = like
    length = left_rows.shape[0]
    each = right_cols.shape[2] // BLOCK_COLS
    count = right_cols.shape[0] * each
    in_specs = [
        pl.BlockSpec((length, D), lambda k, own: (0, 0)),
        pl.BlockSpec((1, length, BLOCK_COLS), lambda k, own: (k // each, 0, k % each)),
    ]
    operands = [owner, left_rows, right_cols]
    aliases = {}
    if into is not None:
        in_specs.append(pl.BlockSpec(memory_space=pl.ANY))
        operands.append(into)
        aliases = {3: 0}
    return pl.pallas_call(
        wgrad_kernel,
        grid_spec=pltpu.PrefetchScalarGridSpec(
            num_scalar_prefetch=1,
            grid=(count,),
            in_specs=in_specs,
            out_specs=pl.BlockSpec(
                (rows, 1, depth, BLOCK_COLS), lambda k, own: (0, own[first + k], 0, 0)
            ),
            scratch_shapes=[pltpu.VMEM((D, length), BF16)],
        ),
        out_shape=jax.ShapeDtypeStruct(like, BF16),
        input_output_aliases=aliases,
        compiler_params=params(),
        cost_estimate=cost(
            2 * length * D * BLOCK_COLS * count, count * BLOCK_COLS * (2 * D + 2 * length)
        ),
    )(*operands)


def rope_tables(length):
    half_dim = HEAD_DIM // 2
    frequency = rope_base ** (-jnp.arange(half_dim, dtype=F32) * 2.0 / HEAD_DIM)
    angles = jnp.arange(length, dtype=F32)[:, None] * frequency[None, :]
    cosine, sine = jnp.cos(angles), jnp.sin(angles)
    wide_cos = jnp.concatenate([cosine] * 4, axis=1)
    wide_sin = jnp.concatenate([-sine, sine, -sine, sine], axis=1)
    return wide_cos, wide_sin


def lane_iota():
    return lax.broadcasted_iota(jnp.int32, (1, LANES), 1)


def swap_halves(values):
    low_half = (lane_iota() % HEAD_DIM) < HEAD_DIM // 2
    return jnp.where(
        low_half,
        pltpu.roll(values, LANES - HEAD_DIM // 2, 1),
        pltpu.roll(values, HEAD_DIM // 2, 1),
    )


def turn(values, cosine, sine):
    return values * cosine + swap_halves(values) * sine


def turn_back(values, cosine, sine):
    return values * cosine - swap_halves(values) * sine


def doubled(values, group):
    moved = pltpu.roll(values, HEAD_DIM, 1)
    keep = (lane_iota() < HEAD_DIM) == (group == 0)
    return jnp.where(keep, values, moved)


def attention_mask(segc_ref, segr_ref, low_row, low_col, wide):
    doc_rows = segc_ref[low_row : low_row + QROWS, :]
    doc_cols = segr_ref[:, low_col : low_col + wide]
    row_pos = low_row + lax.broadcasted_iota(jnp.int32, (QROWS, wide), 0)
    col_pos = low_col + lax.broadcasted_iota(jnp.int32, (QROWS, wide), 1)
    return (doc_rows == doc_cols) & (row_pos >= col_pos)


def attention_probs(query, key, allowed):
    scores = jnp.where(allowed, dot_nt(query, key), -1e30)
    row_top = jnp.max(scores, axis=-1, keepdims=True)
    weights = jnp.exp(scores - row_top)
    return weights, jnp.sum(weights, axis=-1, keepdims=True)


def halves(values):
    high = values.astype(BF16).astype(F32)
    return high, values - high


def fold(values):
    return values + pltpu.roll(values, HEAD_DIM, 1)


def head_operands(values):
    low = lane_iota() < HEAD_DIM
    high, rest = halves(values)
    high_moved, rest_moved = pltpu.roll(high, HEAD_DIM, 1), pltpu.roll(rest, HEAD_DIM, 1)
    head_a = [jnp.where(low, high, rest_moved), jnp.where(low, high, 0.0)]
    head_b = [jnp.where(low, high_moved, rest), jnp.where(low, high_moved, 0.0)]
    return [jnp.concatenate(h, axis=1).astype(BF16) for h in (head_a, head_b)]


def group_operands(values):
    low = lane_iota() < HEAD_DIM
    high, rest = halves(values)
    inner = jnp.concatenate([high, rest], axis=1).astype(BF16)
    return inner, jnp.where(low, high, rest).astype(BF16)


def attn_fwd_kernel(
    q_ref, k_ref, v_ref, segc_ref, segr_ref, cos_ref, sin_ref, mixed_ref, o_ref
):
    group = pl.program_id(0) // 2
    low = lane_iota() < HEAD_DIM
    cosine, sine = cos_ref[...], sin_ref[...]
    length = cosine.shape[0]
    query_h = head_operands(turn(q_ref[...], cosine, sine) * HEAD_DIM ** (-0.5))
    key, _ = group_operands(doubled(turn(k_ref[...], cosine, sine), group))
    _, value = group_operands(doubled(v_ref[...], group))
    for block in range(length // QROWS):
        low_row = block * QROWS
        low_col = max(0, low_row - 2 * QROWS)
        wide = low_row + QROWS - low_col
        rows, cols = slice(low_row, low_row + QROWS), slice(low_col, low_col + wide)
        allowed = attention_mask(segc_ref, segr_ref, low_row, low_col, wide)
        outs = []
        for h in range(2):
            weights, total = attention_probs(query_h[h][rows], key[cols], allowed)
            weights_high, weights_rest = split(weights)
            mixed = dot_nn(weights_high, value[cols]) + dot_nn(weights_rest, value[cols])
            outs.append(fold(mixed) / total)
        o_ref[rows, :] = jnp.where(low, outs[0], outs[1]).astype(BF16)


def attn_bwd_kernel(
    q_ref, k_ref, v_ref, segc_ref, segr_ref, cos_ref, sin_ref, g_ref, into_ref, o_ref, dk_s, dv_s
):
    step = pl.program_id(0)
    pairs = HEADS // 2

    @pl.when(step < pairs)
    def _():
        attn_bwd_pair(
            q_ref, k_ref, v_ref, segc_ref, segr_ref, cos_ref, sin_ref, g_ref, o_ref, dk_s, dv_s
        )

    low = lane_iota() < HEAD_DIM

    @pl.when(step == pairs)
    def _():
        dk = jnp.where(low, fold(dk_s[0]), fold(dk_s[1]))
        o_ref[...] = turn_back(dk, cos_ref[...], sin_ref[...]).astype(BF16)

    @pl.when(step == pairs + 1)
    def _():
        o_ref[...] = jnp.where(low, fold(dv_s[0]), fold(dv_s[1])).astype(BF16)


def attn_bwd_pair(
    q_ref, k_ref, v_ref, segc_ref, segr_ref, cos_ref, sin_ref, g_ref, dq_ref, dk_s, dv_s
):
    step = pl.program_id(0)
    group = step // 2
    low = lane_iota() < HEAD_DIM
    cosine, sine = cos_ref[...], sin_ref[...]
    length = cosine.shape[0]

    @pl.when(step == 0)
    def _():
        dk_s[...] = jnp.zeros_like(dk_s)
        dv_s[...] = jnp.zeros_like(dv_s)

    scale = HEAD_DIM ** (-0.5)
    query_h = head_operands(turn(q_ref[...], cosine, sine) * scale)
    grad_h = head_operands(g_ref[...])
    key, key_out = group_operands(doubled(turn(k_ref[...], cosine, sine), group))
    value, _ = group_operands(doubled(v_ref[...], group))
    for block in range(length // QROWS):
        low_row = block * QROWS
        low_col = max(0, low_row - 2 * QROWS)
        wide = low_row + QROWS - low_col
        rows, cols = slice(low_row, low_row + QROWS), slice(low_col, low_col + wide)
        allowed = attention_mask(segc_ref, segr_ref, low_row, low_col, wide)
        dqs, ps, dss = [], [], []
        for h in range(2):
            weights, total = attention_probs(query_h[h][rows], key[cols], allowed)
            probs = weights * (1.0 / total)
            dprobs = dot_nt(grad_h[h][rows], value[cols])
            delta = jnp.sum(probs * dprobs, axis=-1, keepdims=True)
            dscores = split(probs * (dprobs - delta))
            dqs.append(fold(dot_nn(dscores[0], key_out[cols]) + dot_nn(dscores[1], key_out[cols])))
            ps.append(probs.astype(BF16))
            dss.append(dscores[0])
        both_p = jnp.concatenate(ps, axis=0)
        both_d = jnp.concatenate(dss, axis=0)
        both_g = jnp.concatenate([grad_h[h][rows, :LANES] for h in range(2)], axis=0)
        both_q = jnp.concatenate([query_h[h][rows, :LANES] for h in range(2)], axis=0)
        dv_s[group, cols, :] += dot_tn(both_p, both_g)
        dk_s[group, cols, :] += dot_tn(both_d, both_q)
        dq = jnp.where(low, dqs[0], dqs[1]) * scale
        dq_ref[rows, :] = turn_back(dq, cosine[rows], sine[rows]).astype(BF16)


def attention_specs(length, base):
    return [
        pl.BlockSpec((length, LANES), lambda p: (0, base + jnp.minimum(p, 3))),
        pl.BlockSpec((length, LANES), lambda p: (0, base + 4)),
        pl.BlockSpec((length, LANES), lambda p: (0, base + 5)),
        pl.BlockSpec((length, 1), lambda p: (0, 0)),
        pl.BlockSpec((1, length), lambda p: (0, 0)),
        pl.BlockSpec((length, LANES), lambda p: (0, 0)),
        pl.BlockSpec((length, LANES), lambda p: (0, 0)),
    ]


def attention_forward(both_proj, segc, segr, cosine, sine, mixed):
    length = both_proj.shape[0]
    base = (SSM_INNER + XBC_WIDTH) // LANES
    pairs = HEADS // 2
    at = SSM_INNER // LANES
    return pl.pallas_call(
        attn_fwd_kernel,
        grid=(pairs,),
        in_specs=attention_specs(length, base) + [pl.BlockSpec(memory_space=pl.ANY)],
        out_specs=pl.BlockSpec((length, LANES), lambda p: (0, at + p)),
        out_shape=jax.ShapeDtypeStruct(mixed.shape, BF16),
        input_output_aliases={7: 0},
        compiler_params=params(),
        cost_estimate=cost(
            4 * HEADS * length * length * HEAD_DIM, 6 * length * D, HEADS * length * length // 2
        ),
    )(both_proj, both_proj, both_proj, segc, segr, cosine, sine, mixed)


def attention_backward(both_proj, segc, segr, cosine, sine, grads, into):
    length = both_proj.shape[0]
    base = (SSM_INNER + XBC_WIDTH) // LANES
    at = SSM_INNER // LANES
    pairs = HEADS // 2
    return pl.pallas_call(
        attn_bwd_kernel,
        grid=(pairs + 2,),
        in_specs=attention_specs(length, base)
        + [
            pl.BlockSpec((length, LANES), lambda p: (0, at + jnp.minimum(p, 3))),
            pl.BlockSpec(memory_space=pl.ANY),
        ],
        out_specs=pl.BlockSpec((length, LANES), lambda p: (0, base + p)),
        out_shape=jax.ShapeDtypeStruct(into.shape, BF16),
        input_output_aliases={8: 0},
        scratch_shapes=[pltpu.VMEM((2, length, LANES), F32)] * 2,
        compiler_params=params(),
        cost_estimate=cost(
            10 * HEADS * length * length * HEAD_DIM, 10 * length * D, HEADS * length * length // 2
        ),
    )(both_proj, both_proj, both_proj, segc, segr, cosine, sine, grads, into)


def chunk_masks(segc_ref, segr_ref, last_ref, chunk):
    doc_rows, doc_cols = segc_ref[...], segr_ref[...]
    row_pos = lax.broadcasted_iota(jnp.int32, (CHUNK, CHUNK), 0)
    col_pos = lax.broadcasted_iota(jnp.int32, (CHUNK, CHUNK), 1)
    same = (doc_rows == doc_cols) & (row_pos >= col_pos)
    madd = jnp.where(same, 0.0, -1e30)
    last = last_ref[chunk]
    previous = jnp.where(chunk > 0, last_ref[jnp.maximum(chunk - 1, 0)], -1)
    carried = jnp.where(doc_rows == previous, 1.0, 0.0)
    tail = jnp.where(doc_rows == last, 1.0, 0.0)
    keep = jnp.where(last == previous, 1.0, 0.0)
    return madd, carried, tail, keep


def spread(low, columns, a):
    return jnp.where(low, columns[:, a : a + 1], columns[:, a + 1 : a + 2])


def split(values):
    high = values.astype(BF16)
    return high, (values - high.astype(F32)).astype(BF16)


def wide_split(values):
    return jnp.concatenate(split(values), axis=1)


def both_sides(values):
    return values[:, :LANES] + values[:, LANES:]


def ssm_fwd_kernel(
    last_ref, proj_ref, near_ref, cw_ref, cb_ref, gain_ref, dt_ref, cum_ref, cumt_ref, skip_ref,
    segc_ref, segr_ref, y_ref, s_ref, xbc_ref, slope_ref, mix_ref, state, ext,
):
    chunk = pl.program_id(0)

    @pl.when(chunk == 0)
    def _():
        state[...] = jnp.zeros_like(state)
        ext[:8, :] = jnp.zeros((8, XBC_WIDTH), F32)

    ext[8:, :] = proj_ref[:, SSM_INNER : SSM_INNER + XBC_WIDTH]
    for k in range(XBC_WIDTH // BLOCK_COLS):
        cols = cols_of(k)
        total = ext[8:, cols] * cw_ref[CONV - 1 :, cols] + cb_ref[:, cols]
        for d in range(1, CONV):
            taken = ext[8 - d : 8 - d + CHUNK, cols] * near_ref[:, d : d + 1]
            total += taken * cw_ref[CONV - 1 - d : CONV - d, cols]
        sig = sigmoid(total)
        silu = total * sig
        xbc_ref[:, cols] = silu
        slope_ref[:, cols] = sig + silu * (1.0 - sig)
    ext[:8, :] = ext[CHUNK:, :]
    s_ref[...] = state[...].reshape(s_ref.shape)
    low = lane_iota() < SSM_HEAD_DIM
    madd, carried, tail, keep = chunk_masks(segc_ref, segr_ref, last_ref, chunk)
    dt, cum, cumt = dt_ref[...], cum_ref[...], cumt_ref[...]
    last_cum = cum[CHUNK - 1 : CHUNK, :]
    ecum = jnp.exp(cum) * carried
    tails = jnp.exp(last_cum - cum) * tail
    keeps = jnp.exp(last_cum) * keep
    into = xbc_ref[:, SSM_INNER : SSM_INNER + STATE]
    into_t = into.T
    into_high, into_rest = split(into_t)
    out_high, out_rest = split(xbc_ref[:, SSM_INNER + STATE :])
    out_both = jnp.concatenate([out_high, out_rest], axis=1)
    into_both = jnp.concatenate([into_high, into_rest], axis=1)
    gram = dot_nn(out_both, jnp.concatenate([into_high, into_high], axis=0)) + dot_nn(
        out_high, into_rest
    )
    for p in range(SSM_HEADS // 2):
        a, cols = 2 * p, slice(p * LANES, (p + 1) * LANES)
        heads = xbc_ref[:, cols]
        scaled = heads * spread(low, dt, a)
        decay_a = jnp.exp(cum[:, a : a + 1] - cumt[a : a + 1, :] + madd)
        decay_b = jnp.exp(cum[:, a + 1 : a + 2] - cumt[a + 1 : a + 2, :] + madd)
        mixing = wide_split(jnp.concatenate([decay_a * gram, decay_b * gram], axis=1))
        stacked_wide = wide_split(
            jnp.concatenate([jnp.where(low, scaled, 0.0), jnp.where(low, 0.0, scaled)], axis=0)
        )
        old = state[:, cols]
        old_wide = wide_split(old)
        carry_in = both_sides(dot_nn(out_both, jnp.concatenate([old_wide, old_wide], axis=0)))
        y_ref[:, cols] = (
            both_sides(dot_nn(mixing, jnp.concatenate([stacked_wide, stacked_wide], axis=0)))
            + spread(low, ecum, a) * carry_in
            + spread(low, skip_ref[...], a) * heads
        )
        tail_in = wide_split(scaled * spread(low, tails, a))
        fresh = both_sides(dot_nn(into_both, jnp.concatenate([tail_in, tail_in], axis=0)))
        state[:, cols] = spread(low, keeps, a) * old + fresh
    squares = jnp.zeros((CHUNK, 1), F32)
    for k in range(SSM_INNER // BLOCK_COLS):
        gate = proj_ref[:, cols_of(k)]
        gated = y_ref[:, cols_of(k)] * (gate * sigmoid(gate))
        squares += jnp.sum(gated * gated, axis=-1, keepdims=True)
    inv = lax.rsqrt(squares / SSM_INNER + 1e-05)
    for k in range(SSM_INNER // BLOCK_COLS):
        gate = proj_ref[:, cols_of(k)]
        gated = y_ref[:, cols_of(k)] * (gate * sigmoid(gate))
        mix_ref[:, cols_of(k)] = (gated * inv * gain_ref[:, cols_of(k)]).astype(BF16)


def ssm_bwd_kernel(
    last_ref, proj_ref, near_ref, cw_ref, gain_ref, xbc_ref, slope_ref, dt_ref, cum_ref, cumt_ref,
    skip_ref, segc_ref, segr_ref, s_ref, n_ref, y_ref, out_ref, grad_ref, sums_ref, ends_ref,
    vec_ref, dstate, g_ref, dext,
):
    chunk = pl.num_programs(0) - 1 - pl.program_id(0)

    @pl.when(pl.program_id(0) == 0)
    def _():
        dstate[...] = jnp.zeros_like(dstate)
        dext[CHUNK:, :] = jnp.zeros((8, XBC_WIDTH), F32)
        vec_ref[...] = jnp.zeros_like(vec_ref)

    squares = jnp.zeros((CHUNK, 1), F32)
    along = jnp.zeros((CHUNK, 1), F32)
    for k in range(SSM_INNER // BLOCK_COLS):
        cols = cols_of(k)
        gate = proj_ref[:, cols]
        gated = y_ref[:, cols] * (gate * sigmoid(gate))
        squares += jnp.sum(gated * gated, axis=-1, keepdims=True)
        along += jnp.sum(gated * out_ref[:, cols] * gain_ref[:, cols], axis=-1, keepdims=True)
    inv = lax.rsqrt(squares / SSM_INNER + 1e-05)
    along = along * inv / SSM_INNER
    for k in range(SSM_INNER // BLOCK_COLS):
        cols = cols_of(k)
        gate = proj_ref[:, cols]
        sig = sigmoid(gate)
        silu = gate * sig
        unit = y_ref[:, cols] * silu * inv
        vec_ref[5:6, cols] += jnp.sum(out_ref[:, cols] * unit, axis=0, keepdims=True)
        gated_grad = inv * (out_ref[:, cols] * gain_ref[:, cols] - unit * along)
        g_ref[:, cols] = gated_grad * silu
        gate_grad = gated_grad * y_ref[:, cols] * (sig + silu * (1.0 - sig))
        grad_ref[:, cols] = gate_grad.astype(BF16)
    low = lane_iota() < SSM_HEAD_DIM
    madd, carried, tail, keep = chunk_masks(segc_ref, segr_ref, last_ref, chunk)
    dt, cum, cumt = dt_ref[...], cum_ref[...], cumt_ref[...]
    last_cum = cum[CHUNK - 1 : CHUNK, :]
    ecum = jnp.exp(cum) * carried
    tails = jnp.exp(last_cum - cum) * tail
    keeps = jnp.exp(last_cum) * keep
    into, into_rest = split(xbc_ref[:, SSM_INNER : SSM_INNER + STATE])
    outof, outof_rest = split(xbc_ref[:, SSM_INNER + STATE :])
    outof_t = outof.T
    into_both = jnp.concatenate([into, into_rest], axis=1)
    gram = dot_nt(
        jnp.concatenate([outof, outof_rest], axis=1), jnp.concatenate([into, into], axis=1)
    ) + dot_nt(outof, into_rest)
    dgram = jnp.zeros((CHUNK, CHUNK), F32)
    d_into = jnp.zeros((CHUNK, STATE), F32)
    d_outof = jnp.zeros((CHUNK, STATE), F32)
    sum_y = jnp.zeros((CHUNK, LANES), F32)
    sum_x = jnp.zeros((CHUNK, LANES), F32)
    sum_k = jnp.zeros((CHUNK, LANES), F32)
    ends = jnp.zeros((8, LANES), F32)
    lane_pos = lax.broadcasted_iota(jnp.int32, (LANES, LANES), 0) // SSM_HEAD_DIM
    head_pos = lax.broadcasted_iota(jnp.int32, (LANES, LANES), 1)

    def by_head(values, pick):
        high = values.astype(BF16)
        rest = (values - high.astype(F32)).astype(BF16)
        return dot_nn(jnp.concatenate([high, rest], axis=1), pick)

    for p in range(SSM_HEADS // 2):
        a, cols = 2 * p, slice(p * LANES, (p + 1) * LANES)
        pick = jnp.where(lane_pos + a == head_pos, 1.0, 0.0).astype(BF16)
        pick = jnp.concatenate([pick, pick], axis=0)
        heads, grad = xbc_ref[:, cols], g_ref[:, cols]
        dt_wide = spread(low, dt, a)
        skip_wide = spread(low, skip_ref[...], a)
        tail_wide = spread(low, tails, a)
        keep_wide = spread(low, keeps, a)
        scaled = heads * dt_wide
        scaled_low = scaled.astype(BF16)
        decay_a = jnp.exp(cum[:, a : a + 1] - cumt[a : a + 1, :] + madd)
        decay_b = jnp.exp(cum[:, a + 1 : a + 2] - cumt[a + 1 : a + 2, :] + madd)
        grads = wide_split(
            jnp.concatenate([jnp.where(low, grad, 0.0), jnp.where(low, 0.0, grad)], axis=0)
        )
        dmix = dot_nt(grads, jnp.concatenate([scaled_low, scaled_low], axis=1))
        dgram += decay_a * dmix[:CHUNK] + decay_b * dmix[CHUNK:]
        mixing = split(jnp.concatenate([decay_a * gram, decay_b * gram], axis=0))
        d_new = dstate[:, cols]
        d_new_wide = wide_split(d_new)
        d_new_low = d_new_wide[:, :LANES]
        d_inner = dot_tn(jnp.concatenate(mixing, axis=0), jnp.concatenate([grads, grads], axis=0))
        d_scaled = both_sides(d_inner) + tail_wide * both_sides(
            dot_nn(into_both, jnp.concatenate([d_new_wide, d_new_wide], axis=0))
        )
        old = s_ref[0, :, cols]
        d_carry = (spread(low, ecum, a) * grad).astype(BF16)
        d_outof += dot_nt(d_carry, old.astype(BF16))
        d_into += dot_nt((scaled * tail_wide).astype(BF16), d_new_low)
        ends += jnp.sum((d_new * n_ref[0, :, cols]).reshape(STATE // 8, 8, LANES), axis=0) @ pick[
            :LANES
        ].astype(F32)
        dstate[:, cols] = keep_wide * d_new + dot_nn(outof_t, d_carry)
        dext[:CHUNK, cols] = (d_scaled * dt_wide + skip_wide * grad) * slope_ref[:, cols]
        both = grad * heads
        sum_y += by_head(grad * y_ref[:, cols] - skip_wide * both - scaled * d_scaled, pick)
        sum_x += by_head(heads * d_scaled, pick)
        sum_k += by_head(both, pick)
    dgram_low = dgram.astype(BF16)
    cols = slice(SSM_INNER, SSM_INNER + STATE)
    dext[:CHUNK, cols] = (d_into + dot_tn(dgram_low, outof)) * slope_ref[:, cols]
    cols = slice(SSM_INNER + STATE, XBC_WIDTH)
    dext[:CHUNK, cols] = (d_outof + dot_nn(dgram_low, into)) * slope_ref[:, cols]
    for k in range(XBC_WIDTH // BLOCK_COLS):
        cols = cols_of(k)
        at = slice(SSM_INNER + k * BLOCK_COLS, SSM_INNER + (k + 1) * BLOCK_COLS)
        before = proj_ref[:, at]
        here = dext[:CHUNK, cols]
        total = here * cw_ref[CONV - 1 :, cols]
        vec_ref[CONV - 1 : CONV, cols] += jnp.sum(here * before, axis=0, keepdims=True)
        vec_ref[CONV : CONV + 1, cols] += jnp.sum(here, axis=0, keepdims=True)
        for d in range(1, CONV):
            later = dext[d : d + CHUNK, cols] * near_ref[:, CONV + d : CONV + d + 1]
            total += later * cw_ref[CONV - 1 - d : CONV - d, cols]
            vec_ref[CONV - 1 - d : CONV - d, cols] += jnp.sum(later * before, axis=0, keepdims=True)
        grad_ref[:, at] = total.astype(BF16)
    dext[CHUNK:, :] = dext[:8, :]
    sums_ref[:, :LANES] = sum_y
    sums_ref[:, LANES : 2 * LANES] = sum_x
    sums_ref[:, 2 * LANES :] = sum_k
    ends_ref[...] = ends.reshape(ends_ref.shape)


def scan_specs(at):
    here = lambda i, last: (at(i), 0)
    across = lambda i, last: (0, at(i))
    return dict(
        rows=lambda width: pl.BlockSpec((CHUNK, width), here),
        cols=lambda height: pl.BlockSpec((height, CHUNK), across),
        fixed=lambda *shape: pl.BlockSpec(shape, lambda i, last: (0,) * len(shape)),
    )


def ssm_forward(last, both_proj, near, conv_w, conv_b, gain, dt, cum, cumt, skip, segc, segr):
    length, width = both_proj.shape
    chunks = length // CHUNK
    spec = scan_specs(lambda i: i)
    return pl.pallas_call(
        ssm_fwd_kernel,
        grid_spec=pltpu.PrefetchScalarGridSpec(
            num_scalar_prefetch=1,
            grid=(chunks,),
            in_specs=[
                spec["rows"](width),
                spec["rows"](2 * CONV),
                spec["fixed"](CONV, XBC_WIDTH),
                spec["fixed"](1, XBC_WIDTH),
                spec["fixed"](1, SSM_INNER),
                spec["rows"](SSM_HEADS),
                spec["rows"](SSM_HEADS),
                spec["cols"](SSM_HEADS),
                spec["fixed"](1, SSM_HEADS),
                spec["rows"](1),
                spec["cols"](1),
            ],
            out_specs=[
                spec["rows"](SSM_INNER),
                pl.BlockSpec((1, STATE, SSM_INNER), lambda c, last: (c, 0, 0)),
                spec["rows"](XBC_WIDTH),
                spec["rows"](XBC_WIDTH),
                spec["rows"](SSM_INNER + HEADS * HEAD_DIM),
            ],
            scratch_shapes=[
                pltpu.VMEM((STATE, SSM_INNER), F32),
                pltpu.VMEM((CHUNK + 8, XBC_WIDTH), F32),
            ],
        ),
        out_shape=[
            jax.ShapeDtypeStruct((length, SSM_INNER), F32),
            jax.ShapeDtypeStruct((chunks, STATE, SSM_INNER), F32),
            jax.ShapeDtypeStruct((length, XBC_WIDTH), F32),
            jax.ShapeDtypeStruct((length, XBC_WIDTH), F32),
            jax.ShapeDtypeStruct((length, SSM_INNER + HEADS * HEAD_DIM), BF16),
        ],
        compiler_params=params(),
        cost_estimate=cost(
            8 * length * SSM_INNER * STATE, 40 * length * SSM_INNER, length * CHUNK * SSM_HEADS
        ),
    )(last, both_proj, near, conv_w, conv_b, gain, dt, cum, cumt, skip, segc, segr)


def ssm_backward(
    last, both_proj, near, conv_w, gain, xbc, slope, dt, cum, cumt, skip, segc, segr, states, outputs,
    grads,
):
    length, width = both_proj.shape
    chunks = length // CHUNK
    end = chunks - 1
    spec = scan_specs(lambda i: end - i)
    return pl.pallas_call(
        ssm_bwd_kernel,
        grid_spec=pltpu.PrefetchScalarGridSpec(
            num_scalar_prefetch=1,
            grid=(chunks,),
            in_specs=[
                spec["rows"](width),
                spec["rows"](2 * CONV),
                spec["fixed"](CONV, XBC_WIDTH),
                spec["fixed"](1, SSM_INNER),
                spec["rows"](XBC_WIDTH),
                spec["rows"](XBC_WIDTH),
                spec["rows"](SSM_HEADS),
                spec["rows"](SSM_HEADS),
                spec["cols"](SSM_HEADS),
                spec["fixed"](1, SSM_HEADS),
                spec["rows"](1),
                spec["cols"](1),
                pl.BlockSpec((1, STATE, SSM_INNER), lambda i, last: (end - i, 0, 0)),
                pl.BlockSpec(
                    (1, STATE, SSM_INNER), lambda i, last: (jnp.minimum(end - i + 1, end), 0, 0)
                ),
                spec["rows"](SSM_INNER),
                spec["rows"](grads.shape[1]),
            ],
            out_specs=[
                spec["rows"](width),
                spec["rows"](3 * LANES),
                pl.BlockSpec((1, 8, LANES), lambda i, last: (end - i, 0, 0)),
                spec["fixed"](8, XBC_WIDTH),
            ],
            scratch_shapes=[
                pltpu.VMEM((STATE, SSM_INNER), F32),
                pltpu.VMEM((CHUNK, SSM_INNER), F32),
                pltpu.VMEM((CHUNK + 8, XBC_WIDTH), F32),
            ],
        ),
        out_shape=[
            jax.ShapeDtypeStruct((length, width), BF16),
            jax.ShapeDtypeStruct((length, 3 * LANES), F32),
            jax.ShapeDtypeStruct((chunks, 8, LANES), F32),
            jax.ShapeDtypeStruct((8, XBC_WIDTH), F32),
        ],
        compiler_params=params(),
        cost_estimate=cost(
            24 * length * SSM_INNER * STATE, 60 * length * SSM_INNER, length * CHUNK * SSM_HEADS
        ),
    )(
        last, both_proj, near, conv_w, gain, xbc, slope, dt, cum, cumt, skip, segc, segr, states, states,
        outputs, grads,
    )


def neighbours(segment):
    length = segment.shape[0]
    columns = []
    for d in range(CONV):
        earlier = jnp.pad(segment, (d, 0), constant_values=-1)[:length]
        columns.append(earlier == segment)
    for d in range(CONV):
        later = jnp.pad(segment, (0, d), constant_values=-1)[d:]
        columns.append(later == segment)
    return jnp.stack(columns, axis=1).astype(F32)


def rows_kernel(counts, lo_ref, hi_ref, ids_ref, *rest):
    step = pl.program_id(0)
    g_refs, (o_ref, wide) = rest[:-2], rest[-2:]
    group = wide.shape[0]

    @pl.when(step == 0)
    def _():
        o_ref[...] = jnp.zeros_like(o_ref)

    before = 0
    for count, g_ref in zip(counts, g_refs):

        @pl.when((step >= before) & (step < before + count))
        def _(g_ref=g_ref):
            wide[...] = g_ref[...].astype(F32)

        before = before + count
    low, high = lo_ref[step], hi_ref[step]

    def one(j):
        o_ref[pl.ds(ids_ref[step * group + j], 1), :] += wide[pl.ds(j, 1), :]

    def eight(k, carry):
        for u in range(8):
            one(low + 8 * k + u)
        return carry

    def rest_of(j, carry):
        one(j)
        return carry

    eights = (high - low) // 8
    lax.fori_loop(0, eights, eight, 0)
    lax.fori_loop(low + 8 * eights, high, rest_of, 0)


def rows_by_token(local_ids, grads, shard_rows, group):
    width = grads[0].shape[1]
    counts = [g.shape[0] // group for g in grads]
    lists = local_ids.reshape(-1, group)
    low = jnp.sum((lists < 0).astype(jnp.int32), axis=1)
    high = jnp.sum((lists < shard_rows).astype(jnp.int32), axis=1)
    specs, before = [], 0
    for count in counts:
        specs.append(
            pl.BlockSpec(
                (group, width),
                lambda i, lo, hi, ids, before=before, count=count: (
                    jnp.clip(i - before, 0, count - 1),
                    0,
                ),
            )
        )
        before = before + count
    return pl.pallas_call(
        functools.partial(rows_kernel, counts),
        grid_spec=pltpu.PrefetchScalarGridSpec(
            num_scalar_prefetch=3,
            grid=(before,),
            in_specs=specs,
            out_specs=pl.BlockSpec((shard_rows, width), lambda i, lo, hi, ids: (0, 0)),
            scratch_shapes=[pltpu.VMEM((group, width), F32)],
        ),
        out_shape=jax.ShapeDtypeStruct((shard_rows, width), F32),
        compiler_params=params(),
        cost_estimate=cost(before * group * width * LANES, before * group * width * 2),
    )(low, high, local_ids, *grads)


def split_nn(left, right):
    left_high, left_rest = split(left)
    right_high, right_rest = split(right)
    return dot_nn(left_high, right_high) + dot_nn(left_rest, right_high) + dot_nn(left_high, right_rest)


def rotate_kernel(l_ref, g_ref, r_ref, o_ref):
    grad = g_ref[...].reshape(D, BLOCK_COLS)
    left_high, left_rest = split(l_ref[0])
    part = dot_nn(left_high, grad) + dot_nn(left_rest, grad)
    o_ref[0] = split_nn(part, r_ref[0])


def rotate_blocks(left_basis, grad_whole, right_basis):
    slots, depth, _ = left_basis.shape
    rows = grad_whole.shape[0]
    return pl.pallas_call(
        rotate_kernel,
        grid=(slots,),
        in_specs=[
            pl.BlockSpec((1, depth, D), lambda k: (k, 0, 0)),
            pl.BlockSpec((rows, 1, depth, BLOCK_COLS), lambda k: (0, k, 0, 0)),
            pl.BlockSpec((1, BLOCK_COLS, BLOCK_COLS), lambda k: (k, 0, 0)),
        ],
        out_specs=pl.BlockSpec((1, depth, BLOCK_COLS), lambda k: (k, 0, 0)),
        out_shape=jax.ShapeDtypeStruct((slots, depth, BLOCK_COLS), F32),
        compiler_params=params(),
        cost_estimate=cost(6 * slots * depth * D * BLOCK_COLS, slots * depth * D * 5),
    )(left_basis, grad_whole, right_basis)


def step_kernel(scale_ref, rot_ref, m_ref, v_ref, l_ref, r_ref, mo_ref, vo_ref, u_ref):
    rotated = rot_ref[0] * scale_ref[0]
    first_new = soap_first * m_ref[0] + (1.0 - soap_first) * rotated
    second_new = soap_second * v_ref[0] + (1.0 - soap_second) * rotated * rotated
    mo_ref[0], vo_ref[0] = first_new, second_new
    direction = (first_new / scale_ref[1]) / (jnp.sqrt(second_new / scale_ref[2]) + adam_eps)
    turned = split_nn(direction, r_ref[0].T).astype(BF16)
    left_high, left_rest = split(l_ref[0])
    update = dot_nn(left_high.T, turned) + dot_nn(left_rest.T, turned)
    u_ref[0] = update.astype(BF16)


def step_blocks(scales, rotated, block_first, block_second, left_basis, right_basis):
    slots, depth, _ = left_basis.shape
    own = pl.BlockSpec((1, depth, BLOCK_COLS), lambda k: (k, 0, 0))
    small = jax.ShapeDtypeStruct((slots, depth, BLOCK_COLS), F32)
    return pl.pallas_call(
        step_kernel,
        grid=(slots,),
        in_specs=[
            pl.BlockSpec(memory_space=pltpu.SMEM),
            own,
            own,
            own,
            pl.BlockSpec((1, depth, D), lambda k: (k, 0, 0)),
            pl.BlockSpec((1, BLOCK_COLS, BLOCK_COLS), lambda k: (k, 0, 0)),
        ],
        out_specs=[own, own, pl.BlockSpec((1, D, BLOCK_COLS), lambda k: (k, 0, 0))],
        out_shape=[small, small, jax.ShapeDtypeStruct((slots, D, BLOCK_COLS), BF16)],
        compiler_params=params(),
        cost_estimate=cost(6 * slots * depth * D * BLOCK_COLS, slots * depth * D * 7),
    )(scales, rotated, block_first, block_second, left_basis, right_basis)


def to_peers(axis, extent, place, src, box, send_sem, recv_sem):
    copies = []
    for k in range(1, extent):
        peer = list(place)
        peer[axis] = lax.rem(place[axis] + k, extent)
        copies.append(
            pltpu.make_async_remote_copy(
                src_ref=src,
                dst_ref=box.at[place[axis]],
                send_sem=send_sem.at[k],
                recv_sem=recv_sem.at[k],
                device_id=tuple(peer),
                device_id_type=MESH,
            )
        )
    return copies


def greet_peers(axes, place):
    barrier = pltpu.get_barrier_semaphore()
    count = 0
    for axis, extent in axes:
        for k in range(1, extent):
            peer = list(place)
            peer[axis] = lax.rem(place[axis] + k, extent)
            pl.semaphore_signal(barrier, inc=1, device_id=tuple(peer), device_id_type=MESH)
            count += 1
    pl.semaphore_wait(barrier, count)


def total_kernel(rows, cols, x_ref, o_ref, col_box, row_box, col_send, col_recv, row_send, row_recv):
    place = (lax.axis_index("row"), lax.axis_index("col"))
    greet_peers(((0, rows), (1, cols)), place)
    total = x_ref[...]
    for axis, extent, box, send_sem, recv_sem in (
        (1, cols, col_box, col_send, col_recv),
        (0, rows, row_box, row_send, row_recv),
    ):
        o_ref[...] = total
        box[place[axis]] = total
        copies = to_peers(axis, extent, place, o_ref, box, send_sem, recv_sem)
        for copy in copies:
            copy.start()
        for copy in copies:
            copy.wait()
        total = jnp.sum(box[...], axis=0)
    o_ref[...] = total


def total_over_all(values, rows, cols, collective_id):
    dma = pltpu.SemaphoreType.DMA
    return pl.pallas_call(
        functools.partial(total_kernel, rows, cols),
        in_specs=[pl.BlockSpec(memory_space=pltpu.VMEM)],
        out_specs=pl.BlockSpec(memory_space=pltpu.VMEM),
        out_shape=jax.ShapeDtypeStruct(values.shape, F32),
        scratch_shapes=[
            pltpu.VMEM((cols,) + values.shape, F32),
            pltpu.VMEM((rows,) + values.shape, F32),
            dma((cols,)),
            dma((cols,)),
            dma((rows,)),
            dma((rows,)),
        ],
        compiler_params=params(collective_id=collective_id, has_side_effects=True),
        cost_estimate=cost(rows * cols * values.size, rows * cols * values.size * 4),
    )(values)


def ring_bits(rows, cols):
    bits = []
    for axis, extent in ((0, rows), (1, cols)):
        bit = extent // 2
        while bit >= 1:
            bits.append((axis, bit))
            bit = bit // 2
    return bits


def scatter_orders(rows, cols):
    bits = ring_bits(rows, cols)
    row_bits = [b for b in reversed(bits) if b[0] == 0]
    col_bits = [b for b in reversed(bits) if b[0] == 1]
    return col_bits + row_bits, col_bits[:1] + col_bits[1:][::-1] + row_bits


def tail_kernel(rows, cols, slots, g_ref, p_ref, v_ref, whole_ref, tok_ref, vec_ref, own, *rest):
    bits = ring_bits(rows, cols)
    stages = len(bits)
    row_bits = [b for b in bits if b[0] == 0]
    col_bits = [b for b in bits if b[0] == 1]
    boxes, rest = rest[:stages], rest[stages:]
    vec_box, vec_sum, send_sem, recv_sem, own_sem = rest[:5]
    join_send, join_recv, tok_send, tok_recv, tok_own, vec_send, vec_recv = rest[5:]
    place = (lax.axis_index("row"), lax.axis_index("col"))
    half = whole_ref.shape[-2] // 2
    orders = scatter_orders(rows, cols)

    def side(which):
        axis, bit = which
        return place[axis] // bit % 2

    def partner(which):
        axis, bit = which
        moved = place[axis] + bit - 2 * bit * side(which)
        return (moved, place[1]) if axis == 0 else (place[0], moved)

    def remote(src, dst, send, recv, which):
        return pltpu.make_async_remote_copy(
            src_ref=src,
            dst_ref=dst,
            send_sem=send,
            recv_sem=recv,
            device_id=partner(which),
            device_id_type=MESH,
        )

    barrier = pltpu.get_barrier_semaphore()
    for which in bits:
        pl.semaphore_signal(barrier, inc=1, device_id=partner(which), device_id_type=MESH)
    pl.semaphore_wait(barrier, stages)
    units = [(slot, h) for slot in range(slots) for h in range(2)]

    def pick(ref, before, which, side_of, after):
        at = before.index(which)
        return ref.at[(slice(None),) * at + (side_of,) + (slice(None),) * (len(before) - at - 1) + after]

    def part(slot, h, side_of):
        return pick(g_ref, bits, orders[h][0], side_of, (slot, slice(h * half, (h + 1) * half)))

    def cut(stage, u, side_of):
        order = orders[units[u][1]]
        left = [b for b in bits if b not in order[: stage + 1]]
        return pick(boxes[stage].at[u], left, order[stage + 1], side_of, ())

    def send(stage, u):
        slot, h = units[u]
        which = orders[h][stage]
        other = 1 - side(which)
        return remote(
            part(slot, h, other) if stage == 0 else cut(stage - 1, u, other),
            boxes[stage].at[u],
            send_sem.at[stage, u],
            recv_sem.at[stage, u],
            which,
        )

    def keep(u):
        slot, h = units[u]
        return pltpu.make_async_copy(part(slot, h, side(orders[h][0])), own.at[u], own_sem.at[u])

    def joined(ref, order, of_bits, stage, after):
        at = tuple(slice(None) if b in order[:stage] else side(b) for b in of_bits)
        return ref.at[at + after]

    def join(stage, u):
        slot, h = units[u]
        region = joined(whole_ref, row_bits, row_bits, stage, (slot, slice(h * half, (h + 1) * half)))
        return remote(region, region, join_send.at[stage, u], join_recv.at[stage, u], row_bits[stage])

    def tok(stage, h):
        order = (orders[h][1 : len(col_bits)] + orders[h][:1])
        region = joined(tok_ref, order, col_bits, stage, (h,))
        return remote(
            p_ref.at[h] if stage == 0 else region, region, tok_send.at[stage, h],
            tok_recv.at[stage, h], order[stage],
        )

    def tok_keep():
        region = joined(tok_ref, [], col_bits, 0, ())
        return pltpu.make_async_copy(p_ref, region, tok_own)

    def vec(stage):
        return remote(
            vec_sum.at[stage], vec_box.at[stage], vec_send.at[stage], vec_recv.at[stage], bits[stage]
        )

    sent = []

    def start(copy):
        copy.start()
        sent.append(copy)
        return copy

    flying = {}
    vec_sum[0] = v_ref[...]
    flying["vec", 0] = start(vec(0))
    for u in range(len(units)):
        flying[0, u] = start(send(0, u))
        keep(u).start()
        if u == 1:
            tok_keep().start()
            for h in range(2):
                flying["tok", 0, h] = start(tok(0, h))
    steps = slots + stages + len(row_bits) - 1
    tok_at = [(k + 1) * steps // (len(col_bits) + 1) for k in range(len(col_bits))]
    for t in range(steps):
        if t < stages:
            flying["vec", t].wait_recv()
            if t + 1 < stages:
                vec_sum[t + 1] = vec_sum[t] + vec_box[t]
                flying["vec", t + 1] = start(vec(t + 1))
            else:
                vec_ref[...] = vec_sum[t] + vec_box[t]
        for k, at in enumerate(tok_at):
            if at == t:
                if k == 0:
                    tok_keep().wait()
                for h in range(2):
                    flying["tok", k, h].wait_recv()
                    if k + 1 < len(col_bits):
                        flying["tok", k + 1, h] = start(tok(k + 1, h))
        for stage in reversed(range(stages + len(row_bits))):
            slot = t - stage
            if not 0 <= slot < slots:
                continue
            for h in range(2):
                u = 2 * slot + h
                if stage >= stages:
                    flying["join", stage - stages, u].wait_recv()
                    if stage - stages + 1 < len(row_bits):
                        flying["join", stage - stages + 1, u] = start(join(stage - stages + 1, u))
                    continue
                flying[stage, u].wait_recv()
                box = boxes[stage].at[u]
                if stage == 0:
                    keep(u).wait()
                    held = own.at[u]
                else:
                    held = cut(stage - 1, u, side(orders[h][stage]))
                if stage == stages - 1:
                    total = held[...].astype(F32) + box[...].astype(F32)
                    mine = joined(
                        whole_ref, [], row_bits, 0, (slot, slice(h * half, (h + 1) * half))
                    )
                    mine[...] = total.astype(BF16)
                    flying["join", 0, u] = start(join(0, u))
                    continue
                extents = box.shape[:-2]

                def add(k, carry, box=box, held=held, extents=extents):
                    at = []
                    for extent in reversed(extents):
                        at.append(k % extent)
                        k = k // extent
                    at = tuple(reversed(at))
                    box[at] = (held[at].astype(F32) + box[at].astype(F32)).astype(BF16)
                    return carry

                lax.fori_loop(0, 2 ** len(extents), add, 0)
                flying[stage + 1, u] = start(send(stage + 1, u))
    for copy in sent:
        copy.wait_send()


def tail_exchange(grads, pieces, vectors, rows, cols, collective_id):
    _, nslots, depth, _ = grads.shape
    slots = nslots // cols
    bits = ring_bits(rows, cols)
    stages = len(bits)
    row_stages, col_stages = (rows - 1).bit_length(), (cols - 1).bit_length()
    units, half = 2 * slots, depth // 2
    count, width = pieces.shape
    boxes = [
        pltpu.VMEM((units,) + (2,) * (stages - s - 1) + (half, BLOCK_COLS), BF16)
        for s in range(stages)
    ]
    vec_shape = (stages,) + vectors.shape
    whole, tokens, total = pl.pallas_call(
        functools.partial(tail_kernel, rows, cols, slots),
        in_specs=[
            pl.BlockSpec(memory_space=pl.ANY),
            pl.BlockSpec(memory_space=pl.ANY),
            pl.BlockSpec(memory_space=pltpu.VMEM),
        ],
        out_specs=[
            pl.BlockSpec(memory_space=pltpu.VMEM),
            pl.BlockSpec(memory_space=pl.ANY),
            pl.BlockSpec(memory_space=pltpu.VMEM),
        ],
        out_shape=[
            jax.ShapeDtypeStruct((2,) * row_stages + (slots, depth, BLOCK_COLS), BF16),
            jax.ShapeDtypeStruct((2,) * col_stages + (2, count // 2, width), BF16),
            jax.ShapeDtypeStruct(vectors.shape, F32),
        ],
        scratch_shapes=[pltpu.VMEM(boxes[0].shape, BF16)]
        + boxes
        + [
            pltpu.VMEM(vec_shape, F32),
            pltpu.VMEM(vec_shape, F32),
            pltpu.SemaphoreType.DMA((stages, units)),
            pltpu.SemaphoreType.DMA((stages, units)),
            pltpu.SemaphoreType.DMA((units,)),
            pltpu.SemaphoreType.DMA((row_stages, units)),
            pltpu.SemaphoreType.DMA((row_stages, units)),
            pltpu.SemaphoreType.DMA((col_stages, 2)),
            pltpu.SemaphoreType.DMA((col_stages, 2)),
            pltpu.SemaphoreType.DMA,
            pltpu.SemaphoreType.DMA((stages,)),
            pltpu.SemaphoreType.DMA((stages,)),
        ],
        compiler_params=params(collective_id=collective_id, has_side_effects=True),
        cost_estimate=cost(rows * nslots * depth * BLOCK_COLS, rows * nslots * depth * BLOCK_COLS * 6),
    )(
        grads.reshape((2,) * stages + (slots, depth, BLOCK_COLS)),
        pieces.reshape(2, count // 2, width),
        vectors,
    )
    return whole.reshape(rows, slots, depth, BLOCK_COLS), tokens.reshape(cols * count, width), total


def doubling(place, bits):
    def side(which):
        axis, bit = which
        return place[axis] // bit % 2

    def partner(which):
        axis, bit = which
        moved = place[axis] + bit - 2 * bit * side(which)
        return (moved, place[1]) if axis == 0 else (place[0], moved)

    return side, partner


def greet(bits, partner):
    barrier = pltpu.get_barrier_semaphore()
    for which in bits:
        pl.semaphore_signal(barrier, inc=1, device_id=partner(which), device_id_type=MESH)
    pl.semaphore_wait(barrier, len(bits))


def joiner(side, partner, src, out, of_bits, order, after, send_sem, recv_sem):
    def copy(k):
        at = tuple(slice(None) if b in order[:k] else side(b) for b in of_bits)
        region = out.at[at + after]
        return pltpu.make_async_remote_copy(
            src_ref=src if k == 0 else region,
            dst_ref=region,
            send_sem=send_sem.at[k],
            recv_sem=recv_sem.at[k],
            device_id=partner(order[k]),
            device_id_type=MESH,
        )

    return copy


def front_kernel(rows, cols, i_ref, t_ref, w_ref, io_ref, to_ref, wo_ref, *sems):
    bits = ring_bits(rows, cols)
    row_bits = [b for b in bits if b[0] == 0]
    col_bits = [b for b in bits if b[0] == 1]
    place = (lax.axis_index("row"), lax.axis_index("col"))
    side, partner = doubling(place, bits)
    i_send, i_recv, t_send, t_recv, w_send, w_recv, keep_sem = sems
    greet(bits, partner)
    own_row, own_col = tuple(side(b) for b in row_bits), tuple(side(b) for b in col_bits)
    keeps = [
        pltpu.make_async_copy(i_ref, io_ref.at[own_row + own_col], keep_sem.at[0]),
        pltpu.make_async_copy(t_ref, to_ref.at[own_col], keep_sem.at[1]),
        pltpu.make_async_copy(w_ref, wo_ref.at[own_row], keep_sem.at[2]),
    ]
    orders = [o[1 : len(col_bits)] + o[:1] for o in scatter_orders(rows, cols)]
    jobs = {}
    jobs["i", 0] = (joiner(side, partner, i_ref, io_ref, bits, bits[::-1], (), i_send, i_recv), 0, 1)
    for p in range(t_ref.shape[0]):
        copy = joiner(
            side, partner, t_ref.at[p], to_ref, col_bits, orders[p % 2], (p,), t_send.at[p], t_recv.at[p]
        )
        jobs["t", p] = (copy, 2 + p // 2, 2)
    for p in range(w_ref.shape[0]):
        copy = joiner(
            side, partner, w_ref.at[p], wo_ref, row_bits, row_bits, (p,), w_send.at[p], w_recv.at[p]
        )
        jobs["w", p] = (copy, 1 + p, 1)
    run_joins(jobs, {"i": len(bits), "t": len(col_bits), "w": len(row_bits)}, keeps)


def run_joins(jobs, stages, keeps, done=None):
    for copy in keeps:
        copy.start()
    sent = []
    for copy, _, _ in jobs.values():
        sent.append(copy(0))
        sent[-1].start()
    for copy in keeps:
        copy.wait()
    ends = [at + every * (stages[name[0]] - 1) for name, (_, at, every) in jobs.items()]
    for t in range(max(ends) + 1):
        for name, (copy, at, every) in jobs.items():
            k = (t - at) // every
            if t < at or (t - at) % every or k >= stages[name[0]]:
                continue
            copy(k).wait_recv()
            if k + 1 < stages[name[0]]:
                sent.append(copy(k + 1))
                sent[-1].start()
            elif done is not None:
                done(name[1])
    for copy in sent:
        copy.wait_send()


def front_exchange(ints, table_low, weights_low, rows, cols, collective_id):
    row_stages, col_stages = (rows - 1).bit_length(), (cols - 1).bit_length()
    parts = TABLE_PARTS
    shard, width = table_low.shape
    slots = weights_low.shape[0]
    dma = pltpu.SemaphoreType.DMA
    ints = ints.reshape(-1, LANES)
    outs = pl.pallas_call(
        functools.partial(front_kernel, rows, cols),
        in_specs=[pl.BlockSpec(memory_space=pl.ANY)] * 3,
        out_specs=[pl.BlockSpec(memory_space=pltpu.VMEM)] * 3,
        out_shape=[
            jax.ShapeDtypeStruct((2,) * (row_stages + col_stages) + ints.shape, jnp.int32),
            jax.ShapeDtypeStruct((2,) * col_stages + (parts, shard // parts, width), BF16),
            jax.ShapeDtypeStruct((2,) * row_stages + weights_low.shape, BF16),
        ],
        scratch_shapes=[
            dma((row_stages + col_stages,)),
            dma((row_stages + col_stages,)),
            dma((parts, col_stages)),
            dma((parts, col_stages)),
            dma((slots, row_stages)),
            dma((slots, row_stages)),
            dma((3,)),
        ],
        compiler_params=params(collective_id=collective_id, has_side_effects=True),
        cost_estimate=cost(1 << 20, cols * shard * width * 4),
    )(ints, table_low.reshape(parts, shard // parts, width), weights_low)
    return (
        outs[0].reshape(rows, cols, -1),
        outs[1].reshape(cols * shard, width),
        outs[2].reshape((rows,) + weights_low.shape),
    )


def weights_kernel(rows, cols, w_ref, o_ref, box, send_sem, recv_sem, keep_sem, out_sem):
    bits = ring_bits(rows, cols)
    col_bits = [b for b in bits if b[0] == 1]
    place = (lax.axis_index("row"), lax.axis_index("col"))
    side, partner = doubling(place, bits)
    greet(col_bits, partner)
    own = tuple(side(b) for b in col_bits)
    slots, half = w_ref.shape[1], w_ref.shape[2] // 2
    orders = [o[1 : len(col_bits)] + o[:1] for o in scatter_orders(rows, cols)]
    keeps = [
        pltpu.make_async_copy(w_ref, box.at[(slice(None),) + own], keep_sem),
    ]
    jobs = {}
    outs = []

    def done(u):
        part = (slice(None),) * (1 + len(col_bits)) + parts[u]
        outs.append(pltpu.make_async_copy(box.at[part], o_ref.at[part], out_sem.at[u]))
        outs[-1].start()

    parts = [(slot, slice(h * half, (h + 1) * half)) for slot in range(slots) for h in range(2)]
    for slot in range(slots):
        for h in range(2):
            part = (slot, slice(h * half, (h + 1) * half))
            u = 2 * slot + h

            def copy(k, part=part, order=orders[h], u=u):
                at = tuple(slice(None) if b in order[:k] else side(b) for b in col_bits)
                region = box.at[(slice(None),) + at + part]
                return pltpu.make_async_remote_copy(
                    src_ref=w_ref.at[(slice(None),) + part] if k == 0 else region,
                    dst_ref=region,
                    send_sem=send_sem.at[u, k],
                    recv_sem=recv_sem.at[u, k],
                    device_id=partner(order[k]),
                    device_id_type=MESH,
                )

            jobs["w", u] = (copy, slot, 1)
    run_joins(jobs, {"w": len(col_bits)}, keeps, done)
    for copy in outs:
        copy.wait()


def gather_weights(weights, rows, cols, collective_id):
    _, slots, depth, width = weights.shape
    col_stages = (cols - 1).bit_length()
    dma = pltpu.SemaphoreType.DMA
    shape = (rows,) + (2,) * col_stages + (slots, depth, width)
    out = pl.pallas_call(
        functools.partial(weights_kernel, rows, cols),
        in_specs=[pl.BlockSpec(memory_space=pl.ANY)],
        out_specs=pl.BlockSpec(memory_space=pl.ANY),
        out_shape=jax.ShapeDtypeStruct(shape, BF16),
        scratch_shapes=[
            pltpu.VMEM(shape, BF16),
            dma((2 * slots, col_stages)),
            dma((2 * slots, col_stages)),
            dma,
            dma((2 * slots,)),
        ],
        compiler_params=params(collective_id=collective_id, has_side_effects=True),
        cost_estimate=cost(1 << 20, 4 * cols * weights.size),
    )(weights)
    return out.reshape(rows, cols * slots, depth, width)


def columns_kernel(cols, x_ref, o_ref, send_sem, recv_sem):
    place = (lax.axis_index("row"), lax.axis_index("col"))
    greet_peers(((1, cols),), place)
    o_ref[place[1]] = x_ref[...]
    copies = to_peers(1, cols, place, x_ref, o_ref, send_sem, recv_sem)
    for copy in copies:
        copy.start()
    for copy in copies:
        copy.wait()


def gather_columns(values, cols, collective_id):
    dma = pltpu.SemaphoreType.DMA
    return pl.pallas_call(
        functools.partial(columns_kernel, cols),
        in_specs=[pl.BlockSpec(memory_space=pltpu.VMEM)],
        out_specs=pl.BlockSpec(memory_space=pltpu.VMEM),
        out_shape=jax.ShapeDtypeStruct((cols,) + values.shape, values.dtype),
        scratch_shapes=[dma((cols,)), dma((cols,))],
        compiler_params=params(collective_id=collective_id, has_side_effects=True),
        cost_estimate=cost(1024, cols * values.size * 4),
    )(values)


def piece_order(rows):
    order = [0] + [k for pair in range(1, rows // 2 + 1) for k in (pair, rows - pair)][: rows - 1]
    return order[: rows // 2], order[rows // 2 :]


def exchange_rows(values, rows):
    row = lax.axis_index("row")
    width = values.shape[1] // rows
    arrived = []
    for group in piece_order(rows):
        parts = []
        for k in group:
            part = lax.dynamic_slice_in_dim(values, (row + k) % rows * width, width, 1)
            if k > 0:
                part = lax.ppermute(part, "row", [(r, (r + k) % rows) for r in range(rows)])
            parts.append(part)
        arrived.append(jnp.concatenate(parts, axis=0))
    return arrived


def adam_step(weights, grads, first, second, steps_done, decay, rate):
    first_new = adam_first * first + (1.0 - adam_first) * grads
    second_new = adam_second * second + (1.0 - adam_second) * grads * grads
    direction = (
        first_new
        / (1.0 - adam_first**steps_done)
        / (jnp.sqrt(second_new / (1.0 - adam_second**steps_done)) + adam_eps)
    )
    return (weights - rate * (direction + decay * weights), first_new, second_new)


def body(
    rows,
    cols,
    token_ids,
    segment_ids,
    loss_positions,
    loss_targets,
    loss_valid,
    block_owner,
    step_count,
    block_weights,
    block_first,
    block_second,
    left_basis,
    right_basis,
    table,
    table_first,
    table_second,
    vector_params,
    vector_first,
    vector_second,
):
    col_index = lax.axis_index("col")
    tokens = token_ids[0]
    segment = segment_ids[0]
    length = tokens.shape[0]
    in_cols = 2 * SSM_INNER + 2 * STATE
    in_blocks = (in_cols + (HEADS + 2 * KV_HEADS) * HEAD_DIM) // BLOCK_COLS
    branch_blocks = (SSM_INNER + HEADS * HEAD_DIM) // BLOCK_COLS
    gate_blocks = 2 * FF // BLOCK_COLS
    down_blocks = FF // BLOCK_COLS
    branch_at = in_blocks
    gate_at = branch_at + branch_blocks
    down_at = gate_at + gate_blocks
    nblocks = block_owner.shape[0]
    depth = block_weights.shape[1]
    shard_rows = table.shape[0]

    row_index = lax.axis_index("row")
    devices = rows * cols
    count_rows = loss_positions.shape[1]
    table_low = table.astype(BF16)
    shard_padded = -(-shard_rows // PAD_ROWS) * PAD_ROWS
    padded = jnp.pad(table_low, ((0, shard_padded - shard_rows), (0, 0)))
    order = jnp.argsort(tokens)
    sent = jnp.concatenate([tokens, jnp.sort(tokens), loss_targets[0], loss_valid[0]])
    ints, table_cols, weight_rows = front_exchange(
        sent, padded, block_weights.astype(BF16), rows, cols, 2
    )
    padded, weight_rows, table_cols = lax.optimization_barrier((padded, weight_rows, table_cols))
    table_rows = lax.all_gather(padded, "row", axis=1, tiled=True)
    token_list = lax.dynamic_index_in_dim(ints, col_index, 1, False)[:, :length].reshape(-1)
    owners = token_list // shard_rows
    looked_up = jnp.take(
        table_cols, token_list + owners * (shard_padded - shard_rows), axis=0, mode="clip"
    )
    looked_up, weight_rows = lax.optimization_barrier((looked_up, weight_rows))
    embedded = lax.all_to_all(looked_up, "row", split_axis=0, concat_axis=1, tiled=True)
    gathered = gather_weights(weight_rows, rows, cols, 3)
    sorted_ints = ints[:, :, length : 2 * length]
    sorted_all = [
        jnp.stack(
            [
                lax.dynamic_index_in_dim(sorted_ints, (row_index - k) % rows, 0, False)
                for k in part
            ],
            axis=1,
        ).reshape(-1)
        for part in piece_order(rows)
    ]
    sorted_all = jnp.concatenate(sorted_all)
    labels_all = lax.dynamic_index_in_dim(ints, row_index, 0, False)[:, 2 * length :]
    targets_all = labels_all[:, :count_rows].reshape(-1)
    valid_all = labels_all[:, count_rows:].reshape(-1)
    valid_count = jnp.sum(ints[:, :, 2 * length + count_rows :]).astype(F32)

    conv_weight, conv_bias, time_bias, decay_log, skip_gain, mixer_gain, norm_gains, time_proj = (
        unpack(vector_params)
    )
    gain_rows = norm_gains.reshape(3, D)
    time_low = time_proj.reshape(D, SSM_HEADS).astype(BF16)
    segc, segr = segment[:, None], segment[None, :]
    chunks = length // CHUNK
    last_docs = segment.reshape(chunks, CHUNK)[:, CHUNK - 1]
    cosine, sine = rope_tables(length)

    normed = rms_gain(embedded.astype(F32), gain_rows[0]).astype(BF16)
    both_proj = project(normed, gathered, block_owner, 0, in_blocks)
    time_raw = jnp.dot(normed, time_low, preferred_element_type=F32)

    def steps_of(time_in, bias_in, decay_in):
        step_size = jax.nn.softplus(time_in + bias_in[None, :])
        return step_size, step_size * -jnp.exp(decay_in)[None, :]

    (step_size, decays), steps_back = jax.vjp(steps_of, time_raw, time_bias, decay_log)
    earlier = jnp.tril(jnp.ones((CHUNK, CHUNK), F32))
    decays_cut = decays.reshape(chunks, CHUNK, SSM_HEADS)
    cum = jnp.einsum("ts,csh->cth", earlier, decays_cut, precision=highest).reshape(
        length, SSM_HEADS
    )
    cumt = cum.T
    near = neighbours(segment)
    conv_rows = conv_weight.reshape(CONV, XBC_WIDTH)
    gain_row = mixer_gain.reshape(1, SSM_INNER)
    times = (step_size, cum, cumt, skip_gain[None, :], segc, segr)
    scan_out, states, act_xbc, slope, mixed = ssm_forward(
        last_docs, both_proj, near, conv_rows, conv_bias[None, :], gain_row, *times
    )
    branch_in = attention_forward(both_proj, segc, segr, cosine, sine, mixed)
    hidden_one, normed_two = back_then_norm(
        branch_in, gathered, block_owner, branch_at, branch_blocks, embedded, gain_rows[1]
    )
    gate_val, up_val, act_low = project_gate_up(
        normed_two, gathered, block_owner, gate_at, down_blocks
    )
    hidden_two, final_out = back_then_norm(
        act_low, gathered, block_owner, down_at, down_blocks, hidden_one, gain_rows[2]
    )
    positions = loss_positions[0]
    chosen = (positions[:, None] == jnp.arange(length, dtype=jnp.int32)[None, :]).astype(BF16)
    picked_rows = jnp.dot(chosen, final_out, preferred_element_type=F32).astype(BF16)
    rows_all = gather_columns(picked_rows, cols, 4).reshape(-1, D)

    logits = jnp.einsum("rd,vd->rv", rows_all, table_rows, preferred_element_type=F32)
    local_target = targets_all - col_index * shard_rows
    places = jnp.arange(shard_padded, dtype=jnp.int32)[None, :]
    onehot = (places == local_target[:, None]) & (places < shard_rows)
    logits = jnp.where(places < shard_rows, logits, -1e30)
    row_top = jnp.max(logits, axis=1)
    row_total = jnp.sum(jnp.exp(logits - row_top[:, None]), axis=1)
    target_logit = jnp.sum(jnp.where(onehot, logits, 0.0), axis=1)
    no_part = jnp.zeros_like(row_top)
    parts = gather_columns(
        jnp.stack([row_top, row_total, target_logit] + [no_part] * 5), cols, 5
    )
    top_all = jnp.max(parts[:, 0], axis=0)
    total_all = jnp.sum(parts[:, 1] * jnp.exp(parts[:, 0] - top_all[None, :]), axis=0)
    target_all = jnp.sum(parts[:, 2], axis=0)
    log_total = top_all + jnp.log(total_all)
    valid_wide = valid_all.astype(F32)
    own_loss = lax.dynamic_slice_in_dim(
        (log_total - target_all) * valid_wide, col_index * count_rows, count_rows
    )
    logit_grad = (
        (jnp.exp(logits - log_total[:, None]) - onehot.astype(F32))
        * (valid_wide / valid_count)[:, None]
    ).astype(BF16)
    rows_grad = lax.psum_scatter(
        jnp.einsum("rv,vd->rd", logit_grad, table_rows, preferred_element_type=F32),
        "col",
        scatter_dimension=0,
        tiled=True,
    )
    table_loss_grad = jnp.einsum("rv,rd->vd", logit_grad, rows_all, preferred_element_type=F32)
    table_loss_low, rows_grad = lax.optimization_barrier((table_loss_grad.astype(BF16), rows_grad))
    table_loss_mine = lax.psum_scatter(table_loss_low, "row", scatter_dimension=1, tiled=True)
    final_grad = jnp.zeros((length, D), F32).at[positions].add(rows_grad)
    _, final_norm_back = jax.vjp(rms_gain, hidden_two, gain_rows[2])
    hidden_two_grad, gain_final_grad = final_norm_back(final_grad)
    down_in = hidden_two_grad.astype(BF16)
    like = (rows, nblocks, depth, BLOCK_COLS)
    gate_up_grad = project_act_back(
        down_in, gate_val, up_val, gathered, block_owner, down_at, down_blocks
    )
    hidden_one_grad, branch_grad_low, gain_ff_grad = back_through_norm(
        gate_up_grad,
        gathered,
        block_owner,
        gate_at,
        gate_blocks,
        jnp.zeros((length, D), F32),
        hidden_one,
        gain_rows[1],
        hidden_two_grad,
    )
    branch_out_grad = project(branch_grad_low, gathered, block_owner, branch_at, branch_blocks)

    in_grad_low, sums, ends, mixer_vectors = ssm_backward(
        last_docs,
        both_proj,
        near,
        conv_rows,
        gain_row,
        act_xbc,
        slope,
        *times,
        states,
        scan_out,
        branch_out_grad,
    )
    in_grad_low = attention_backward(
        both_proj, segc, segr, cosine, sine, branch_out_grad, in_grad_low
    )
    sum_y, sum_x, sum_k = (
        sums[:, i * LANES : i * LANES + SSM_HEADS] for i in range(3)
    )
    skip_grad = jnp.sum(sum_k, axis=0)
    cum_grad = sum_y.reshape(chunks, CHUNK, SSM_HEADS)
    decays_grad = jnp.einsum("ts,cth->csh", earlier, cum_grad, precision=highest)
    decays_grad = decays_grad + jnp.sum(ends, axis=1)[:, None, :SSM_HEADS]
    time_grad, time_bias_grad, decay_log_grad = steps_back(
        (sum_x, decays_grad.reshape(length, SSM_HEADS))
    )
    in_grad_low, table_loss_mine = lax.optimization_barrier((in_grad_low, table_loss_mine))
    time_grad_low = time_grad.astype(BF16)
    grad_time = jnp.einsum("td,th->dh", normed, time_grad_low, preferred_element_type=F32)
    time_part = jnp.einsum("th,dh->td", time_grad_low, time_low, preferred_element_type=F32)
    _, embed_grad, gain_in_grad = back_through_norm(
        in_grad_low[None],
        gathered,
        block_owner,
        0,
        in_blocks,
        time_part,
        embedded,
        gain_rows[0],
        hidden_one_grad,
    )
    placed = (order[:, None] == jnp.arange(length, dtype=jnp.int32)[None, :]).astype(BF16)
    embed_sorted = jnp.dot(placed, embed_grad, preferred_element_type=F32).astype(BF16)
    embed_sorted, down_in, normed_two, branch_grad_low, normed = lax.optimization_barrier(
        (embed_sorted, down_in, normed_two, branch_grad_low, normed)
    )
    early, late = exchange_rows(embed_sorted, rows)
    grad_slots = weight_grad(down_in, act_low[None], block_owner, down_at, like, None)
    grad_slots = weight_grad(normed_two, gate_up_grad, block_owner, gate_at, like, grad_slots)
    early_tokens = lax.all_gather(early, "col", axis=0, tiled=True)
    grad_slots = weight_grad(
        branch_grad_low, branch_in[None], block_owner, branch_at, like, grad_slots
    )
    grad_slots = weight_grad(normed, in_grad_low[None], block_owner, 0, like, grad_slots)
    early_tokens, late, grad_slots = lax.optimization_barrier((early_tokens, late, grad_slots))
    vector_grad = jnp.concatenate(
        [
            mixer_vectors[:CONV].reshape(-1),
            mixer_vectors[CONV],
            time_bias_grad,
            decay_log_grad,
            skip_grad,
            mixer_vectors[CONV + 1, :SSM_INNER],
            gain_in_grad[0],
            gain_ff_grad[0],
            gain_final_grad,
            grad_time.reshape(-1),
            jnp.sum(own_loss)[None],
        ]
    )
    nvec = vector_params.shape[0]
    packed_len = -(-(nvec + 1) // (8 * LANES)) * 8 * LANES
    to_sum = jnp.pad(vector_grad, (0, packed_len - nvec - 1)).reshape(-1, LANES)
    grad_whole, late_tokens, summed = tail_exchange(grad_slots, late, to_sum, rows, cols, 1)
    summed = summed.reshape(-1)
    vector_total, loss_sum = summed[:nvec], summed[nvec]
    table_input_grad = rows_by_token(
        sorted_all - col_index * shard_rows, (early_tokens, late_tokens), shard_rows, length
    )
    table_grad = table_loss_mine[:shard_rows].astype(F32) + table_input_grad
    grad_mine_wide = lax.dynamic_index_in_dim(grad_whole, row_index, 0, False).astype(F32)
    square_part = jnp.sum(grad_mine_wide * grad_mine_wide) + jnp.sum(table_grad * table_grad)
    square_total = total_over_all(jnp.full((8, LANES), square_part), rows, cols, 0)[0, 0]
    rotated = rotate_blocks(left_basis, grad_whole, right_basis)
    mean_loss = loss_sum / valid_count
    grad_norm = jnp.sqrt(square_total + jnp.sum(vector_total * vector_total))
    clip_scale = jnp.minimum(1.0, clip_limit / (grad_norm + 1e-06))
    steps_done = step_count[0].astype(F32)
    scales = jnp.stack(
        [clip_scale, 1.0 - soap_first**steps_done, 1.0 - soap_second**steps_done]
    )
    first_new, second_new, partial_update = step_blocks(
        scales, rotated, block_first, block_second, left_basis, right_basis
    )
    update = lax.psum_scatter(
        partial_update, "row", scatter_dimension=1, tiled=True
    ).astype(F32)
    new_blocks = block_weights - learn_rate * (update + weight_decay * block_weights)
    new_table, table_first_new, table_second_new = adam_step(
        table,
        table_grad * clip_scale,
        table_first,
        table_second,
        steps_done,
        weight_decay,
        learn_rate,
    )
    new_vectors, vector_first_new, vector_second_new = adam_step(
        vector_params,
        vector_total * clip_scale,
        vector_first,
        vector_second,
        steps_done,
        0.0,
        vector_rate,
    )
    return (
        mean_loss,
        grad_norm,
        new_blocks,
        first_new,
        second_new,
        new_table,
        table_first_new,
        table_second_new,
        new_vectors,
        vector_first_new,
        vector_second_new,
    )


def solution(mesh):
    rows, cols = mesh.shape["row"], mesh.shape["col"]
    placed = (
        P(("row", "col"), None),
        P(("row", "col"), None),
        P(("row", "col"), None),
        P(("row", "col"), None),
        P(("row", "col"), None),
        P(),
        P(),
        P("col", "row", None),
        P("col", "row", None),
        P("col", "row", None),
        P("col", "row", None),
        P("col", None, None),
        P("col", "row"),
        P("col", "row"),
        P("col", "row"),
        P(),
        P(),
        P(),
    )
    return jax.shard_map(
        functools.partial(body, rows, cols),
        mesh=mesh,
        in_specs=placed,
        out_specs=(
            P(),
            P(),
            P("col", "row", None),
            P("col", "row", None),
            P("col", "row", None),
            P("col", "row"),
            P("col", "row"),
            P("col", "row"),
            P(),
            P(),
            P(),
        ),
        check_vma=False,
    )
```

```python
import functools

import jax
import jax.numpy as jnp
from jax import lax
from jax.experimental import pallas as pl
from jax.experimental.pallas import tpu as pltpu
from jax.sharding import PartitionSpec as P

D = 1024
HEADS = 8
KV_HEADS = 2
HEAD_DIM = 64
SSM_HEADS = 24
SSM_HEAD_DIM = 64
STATE = 128
CONV = 4
FF = 2048
BLOCK_COLS = 256
SSM_INNER = 1536
XBC_WIDTH = 1792
CHUNK = 128
QROWS = 256
LANES = 128
NO_TOKEN = 1 << 30
TABLE_PARTS = 4
PAD_ROWS = 16 * TABLE_PARTS
GROUP = 4
ROW_PART = 64

BF16 = jnp.bfloat16
F32 = jnp.float32
MESH = pl.DeviceIdType.MESH
highest = lax.Precision.HIGHEST
rope_base = 100000000000.0
clip_limit = 1.0
learn_rate = 0.01
vector_rate = 0.08
weight_decay = 0.1
soap_first = 0.95
soap_second = 0.95
adam_first = 0.9
adam_second = 0.95
adam_eps = 1e-08
vmem_bytes = 56 * 1024 * 1024


def params(**more):
    return pltpu.CompilerParams(vmem_limit_bytes=vmem_bytes, **more)


def cost(flops, nbytes, exps=0):
    return pl.CostEstimate(flops=int(flops), bytes_accessed=int(nbytes), transcendentals=int(exps))


def rms_gain(values, gain_vec):
    inv_scale = lax.rsqrt(jnp.mean(values * values, axis=-1, keepdims=True) + 1e-05)
    return values * inv_scale * gain_vec


def unpack(flattened):
    piece_sizes = [
        CONV * XBC_WIDTH,
        XBC_WIDTH,
        SSM_HEADS,
        SSM_HEADS,
        SSM_HEADS,
        SSM_INNER,
        3 * D,
        D * SSM_HEADS,
    ]
    pieces = []
    offset = 0
    for length in piece_sizes:
        pieces.append(flattened[offset : offset + length])
        offset = offset + length
    return pieces


def dot_nt(left, right):
    return lax.dot_general(left, right, (((1,), (1,)), ((), ())), preferred_element_type=F32)


def dot_tn(left, right):
    return lax.dot_general(left, right, (((0,), (0,)), ((), ())), preferred_element_type=F32)


def dot_nn(left, right):
    return jnp.dot(left, right, preferred_element_type=F32)


def slot_spec(gathered, at, every):
    rows, _, depth, _ = gathered.shape
    return pl.BlockSpec(
        (rows, 1, depth, BLOCK_COLS), lambda k, own: (0, own[at + every * k], 0, 0)
    )


def whole(shape):
    return pl.BlockSpec(shape, lambda k, own: (0,) * len(shape))


def block_of(w_ref):
    return w_ref[...].reshape(D, BLOCK_COLS)


def slot_call(kernel, owner, steps, in_specs, out_specs, out_shape, flops, operands):
    nbytes = sum(o.size * o.dtype.itemsize for o in operands[:1])
    return pl.pallas_call(
        kernel,
        grid_spec=pltpu.PrefetchScalarGridSpec(
            num_scalar_prefetch=1, grid=(steps,), in_specs=in_specs, out_specs=out_specs
        ),
        out_shape=out_shape,
        compiler_params=params(),
        cost_estimate=cost(flops, flops // 512 + nbytes),
    )(owner, *operands)


def cols_of(k):
    return slice(k * BLOCK_COLS, (k + 1) * BLOCK_COLS)


def project_kernel(own_ref, x_ref, *rest):
    o_ref = rest[-1]
    for g, w_ref in enumerate(rest[:-1]):
        o_ref[:, cols_of(g)] = dot_nn(x_ref[...], block_of(w_ref))


def project(rows_in, gathered, owner, first, count):
    length = rows_in.shape[0]
    return slot_call(
        project_kernel,
        owner,
        count // GROUP,
        [whole((length, D))] + [slot_spec(gathered, first + g, GROUP) for g in range(GROUP)],
        pl.BlockSpec((length, GROUP * BLOCK_COLS), lambda k, own: (0, k)),
        jax.ShapeDtypeStruct((length, count * BLOCK_COLS), F32),
        2 * length * D * BLOCK_COLS * count,
        [rows_in] + [gathered] * GROUP,
    )


def sigmoid(values):
    return 1.0 / (1.0 + jnp.exp(-values))


def gate_up_kernel(own_ref, x_ref, *rest):
    w_refs, (gate_ref, up_ref, act_ref) = rest[:-3], rest[-3:]
    half = len(w_refs) // 2
    for g in range(half):
        gate = dot_nn(x_ref[...], block_of(w_refs[g]))
        up = dot_nn(x_ref[...], block_of(w_refs[half + g]))
        gate_ref[:, cols_of(g)] = gate
        up_ref[:, cols_of(g)] = up
        act_ref[:, cols_of(g)] = (gate * sigmoid(gate) * up).astype(BF16)


def project_gate_up(rows_in, gathered, owner, first, count):
    length = rows_in.shape[0]
    pairs = GROUP // 2
    wide = pl.BlockSpec((length, pairs * BLOCK_COLS), lambda k, own: (0, k))
    shapes = [jax.ShapeDtypeStruct((length, count * BLOCK_COLS), t) for t in (F32, F32, BF16)]
    return slot_call(
        gate_up_kernel,
        owner,
        count // pairs,
        [whole((length, D))]
        + [slot_spec(gathered, first + g, pairs) for g in range(pairs)]
        + [slot_spec(gathered, first + count + g, pairs) for g in range(pairs)],
        [wide] * 3,
        shapes,
        4 * length * D * BLOCK_COLS * count,
        [rows_in] + [gathered] * (2 * pairs),
    )


def act_back_kernel(own_ref, x_ref, gate_ref, up_ref, *rest):
    o_ref = rest[-1]
    for g, w_ref in enumerate(rest[:-1]):
        act_grad = dot_nn(x_ref[...], block_of(w_ref))
        gate, up = gate_ref[:, cols_of(g)], up_ref[:, cols_of(g)]
        sig = sigmoid(gate)
        silu = gate * sig
        o_ref[0, :, cols_of(g)] = (act_grad * up * (sig + silu * (1.0 - sig))).astype(BF16)
        o_ref[1, :, cols_of(g)] = (act_grad * silu).astype(BF16)


def project_act_back(rows_in, gate, up, gathered, owner, first, count):
    length = rows_in.shape[0]
    pairs = GROUP // 2
    wide = pl.BlockSpec((length, pairs * BLOCK_COLS), lambda k, own: (0, k))
    return slot_call(
        act_back_kernel,
        owner,
        count // pairs,
        [whole((length, D)), wide, wide]
        + [slot_spec(gathered, first + g, pairs) for g in range(pairs)],
        pl.BlockSpec((2, length, pairs * BLOCK_COLS), lambda k, own: (0, 0, k)),
        jax.ShapeDtypeStruct((2, length, count * BLOCK_COLS), BF16),
        2 * length * D * BLOCK_COLS * count,
        [rows_in, gate, up] + [gathered] * pairs,
    )


def add_products(c_refs, w_refs, o_ref):
    cols = [c_ref[...].reshape(-1, c_ref.shape[-1]) for c_ref in c_refs]
    cols = cols[0] if len(cols) == 1 else jnp.concatenate(cols, axis=1)
    o_ref[...] += dot_nt(cols, jnp.concatenate([block_of(w) for w in w_refs], axis=1))


def row_parts(length):
    return [slice(i, i + ROW_PART) for i in range(0, length, ROW_PART)]


def back_norm_kernel(own_ref, c_ref, *rest):
    w_refs, (base_ref, gain_ref, o_ref, n_ref) = rest[:-4], rest[-4:]

    @pl.when(pl.program_id(0) == 0)
    def _():
        o_ref[...] = base_ref[...].astype(F32)

    add_products([c_ref], w_refs, o_ref)

    @pl.when(pl.program_id(0) == pl.num_programs(0) - 1)
    def _():
        for part in row_parts(o_ref.shape[0]):
            n_ref[part, :] = rms_gain(o_ref[part, :], gain_ref[...]).astype(BF16)


def back_then_norm(cols_in, gathered, owner, first, count, base, gain):
    length = cols_in.shape[0]
    return slot_call(
        back_norm_kernel,
        owner,
        count // GROUP,
        [pl.BlockSpec((length, GROUP * BLOCK_COLS), lambda k, own: (0, k))]
        + [slot_spec(gathered, first + g, GROUP) for g in range(GROUP)]
        + [whole((length, D)), whole((1, D))],
        [whole((length, D))] * 2,
        [jax.ShapeDtypeStruct((length, D), t) for t in (F32, BF16)],
        2 * length * D * BLOCK_COLS * count,
        [cols_in] + [gathered] * GROUP + [base, gain.reshape(1, D)],
    )


def back_grad_kernel(parts, own_ref, *rest):
    c_refs, rest = rest[:parts], rest[parts:]
    w_refs, rest = rest[:-8], rest[-8:]
    start_ref, x_ref, gain_ref, more_ref, o_ref, low_ref, dgain_ref, total = rest

    @pl.when(pl.program_id(0) == 0)
    def _():
        total[...] = start_ref[...]

    add_products(c_refs, w_refs, total)

    @pl.when(pl.program_id(0) == pl.num_programs(0) - 1)
    def _():
        dgain = jnp.zeros((1, D), F32)
        for part in row_parts(total.shape[0]):
            x, grad = x_ref[part, :].astype(F32), total[part, :]
            inv = lax.rsqrt(jnp.mean(x * x, axis=-1, keepdims=True) + 1e-05)
            unit = x * inv
            dgain += jnp.sum(grad * unit, axis=0, keepdims=True)
            scaled = grad * gain_ref[...]
            back = inv * (scaled - unit * jnp.mean(scaled * unit, axis=-1, keepdims=True))
            result = more_ref[part, :] + back
            o_ref[part, :] = result
            low_ref[part, :] = result.astype(BF16)
        dgain_ref[...] = dgain


def back_through_norm(cols_in, gathered, owner, first, count, start, x, gain, more):
    parts, length, _ = cols_in.shape
    group = GROUP // parts
    every = count // parts
    return pl.pallas_call(
        functools.partial(back_grad_kernel, parts),
        grid_spec=pltpu.PrefetchScalarGridSpec(
            num_scalar_prefetch=1,
            grid=(every // group,),
            in_specs=[
                pl.BlockSpec(
                    (1, length, group * BLOCK_COLS), lambda k, own, part=part: (part, 0, k)
                )
                for part in range(parts)
            ]
            + [
                slot_spec(gathered, first + part * every + g, group)
                for part in range(parts)
                for g in range(group)
            ]
            + [whole((length, D)), whole((length, D)), whole((1, D)), whole((length, D))],
            out_specs=[whole((length, D)), whole((length, D)), whole((1, D))],
            scratch_shapes=[pltpu.VMEM((length, D), F32)],
        ),
        out_shape=[
            jax.ShapeDtypeStruct((length, D), F32),
            jax.ShapeDtypeStruct((length, D), BF16),
            jax.ShapeDtypeStruct((1, D), F32),
        ],
        compiler_params=params(),
        cost_estimate=cost(
            2 * length * D * BLOCK_COLS * count, count * BLOCK_COLS * (2 * D + 2 * length)
        ),
    )(owner, *[cols_in] * parts, *[gathered] * GROUP, start, x, gain.reshape(1, D), more)


def wgrad_kernel(own_ref, l_ref, r_ref, *rest):
    o_ref, turned = rest[-2], rest[-1]

    @pl.when(pl.program_id(0) == 0)
    def _():
        turned[...] = l_ref[...].T

    grad = dot_nn(turned[...], r_ref[0])
    o_ref[...] = grad.astype(BF16).reshape(o_ref.shape)


def weight_grad(left_rows, right_cols, owner, first, like, into):
    rows, nslots, depth, _ = like
    length = left_rows.shape[0]
    each = right_cols.shape[2] // BLOCK_COLS
    count = right_cols.shape[0] * each
    in_specs = [
        pl.BlockSpec((length, D), lambda k, own: (0, 0)),
        pl.BlockSpec((1, length, BLOCK_COLS), lambda k, own: (k // each, 0, k % each)),
    ]
    operands = [owner, left_rows, right_cols]
    aliases = {}
    if into is not None:
        in_specs.append(pl.BlockSpec(memory_space=pl.ANY))
        operands.append(into)
        aliases = {3: 0}
    return pl.pallas_call(
        wgrad_kernel,
        grid_spec=pltpu.PrefetchScalarGridSpec(
            num_scalar_prefetch=1,
            grid=(count,),
            in_specs=in_specs,
            out_specs=pl.BlockSpec(
                (rows, 1, depth, BLOCK_COLS), lambda k, own: (0, own[first + k], 0, 0)
            ),
            scratch_shapes=[pltpu.VMEM((D, length), BF16)],
        ),
        out_shape=jax.ShapeDtypeStruct(like, BF16),
        input_output_aliases=aliases,
        compiler_params=params(),
        cost_estimate=cost(
            2 * length * D * BLOCK_COLS * count, count * BLOCK_COLS * (2 * D + 2 * length)
        ),
    )(*operands)


def rope_tables(length):
    half_dim = HEAD_DIM // 2
    frequency = rope_base ** (-jnp.arange(half_dim, dtype=F32) * 2.0 / HEAD_DIM)
    angles = jnp.arange(length, dtype=F32)[:, None] * frequency[None, :]
    cosine, sine = jnp.cos(angles), jnp.sin(angles)
    wide_cos = jnp.concatenate([cosine] * 4, axis=1)
    wide_sin = jnp.concatenate([-sine, sine, -sine, sine], axis=1)
    return wide_cos, wide_sin


def lane_iota():
    return lax.broadcasted_iota(jnp.int32, (1, LANES), 1)


def swap_halves(values):
    low_half = (lane_iota() % HEAD_DIM) < HEAD_DIM // 2
    return jnp.where(
        low_half,
        pltpu.roll(values, LANES - HEAD_DIM // 2, 1),
        pltpu.roll(values, HEAD_DIM // 2, 1),
    )


def turn(values, cosine, sine):
    return values * cosine + swap_halves(values) * sine


def turn_back(values, cosine, sine):
    return values * cosine - swap_halves(values) * sine


def doubled(values, group):
    moved = pltpu.roll(values, HEAD_DIM, 1)
    keep = (lane_iota() < HEAD_DIM) == (group == 0)
    return jnp.where(keep, values, moved)


def attention_probs(query, key, allowed):
    scores = jnp.where(allowed, dot_nt(query, key), -1e30)
    row_top = jnp.max(scores, axis=-1, keepdims=True)
    weights = jnp.exp(scores - row_top)
    return weights, jnp.sum(weights, axis=-1, keepdims=True)


def halves(values):
    high = values.astype(BF16).astype(F32)
    return high, values - high


def fold(values):
    return values + pltpu.roll(values, HEAD_DIM, 1)


def head_operands(values):
    low = lane_iota() < HEAD_DIM
    high, rest = halves(values)
    high_moved, rest_moved = pltpu.roll(high, HEAD_DIM, 1), pltpu.roll(rest, HEAD_DIM, 1)
    head_a = [jnp.where(low, high, rest_moved), jnp.where(low, high, 0.0)]
    head_b = [jnp.where(low, high_moved, rest), jnp.where(low, high_moved, 0.0)]
    return [jnp.concatenate(h, axis=1).astype(BF16) for h in (head_a, head_b)]


def group_operands(values):
    low = lane_iota() < HEAD_DIM
    high, rest = halves(values)
    inner = jnp.concatenate([high, rest], axis=1).astype(BF16)
    return inner, jnp.where(low, high, rest).astype(BF16)


def picked_queries(pos_ref, q_ref, cos_ref, sin_ref, rows):
    count = rows.shape[1]
    for i in range(count):
        at = pl.ds(pos_ref[i], 1)
        for k, ref in enumerate((q_ref, cos_ref, sin_ref)):
            rows[k, i : i + 1, :] = ref[at, :]
    cosine, sine = rows[1], rows[2]
    turned = turn(rows[0], cosine, sine) * HEAD_DIM ** (-0.5)
    return jnp.concatenate(head_operands(turned), axis=0), cosine, sine


def picked_mask(pos_col_ref, seg_col_ref, segr_ref):
    positions = lax.broadcasted_iota(jnp.int32, (1, segr_ref.shape[1]), 1)
    allowed = (seg_col_ref[...] == segr_ref[...]) & (pos_col_ref[...] >= positions)
    return jnp.concatenate([allowed.astype(F32)] * 2, axis=0) > 0.5


def attn_fwd_kernel(
    pos_ref, q_ref, k_ref, v_ref, pos_col_ref, seg_col_ref, segr_ref, cos_ref, sin_ref, o_ref, rows
):
    group = pl.program_id(0) // 2
    low = lane_iota() < HEAD_DIM
    count = o_ref.shape[0]
    query, _, _ = picked_queries(pos_ref, q_ref, cos_ref, sin_ref, rows)
    key, _ = group_operands(doubled(turn(k_ref[...], cos_ref[...], sin_ref[...]), group))
    _, value = group_operands(doubled(v_ref[...], group))
    allowed = picked_mask(pos_col_ref, seg_col_ref, segr_ref)
    weights, total = attention_probs(query, key, allowed)
    high, rest = split(weights)
    out = fold(dot_nn(high, value) + dot_nn(rest, value)) / total
    o_ref[...] = jnp.where(low, out[:count], out[count:]).astype(BF16)


def attn_bwd_kernel(
    pos_ref, q_ref, k_ref, v_ref, pos_col_ref, seg_col_ref, segr_ref, cos_ref, sin_ref, g_ref,
    place_ref, into_ref, o_ref, rows, dk_s, dv_s,
):
    step = pl.program_id(0)
    pairs = HEADS // 2
    low = lane_iota() < HEAD_DIM

    @pl.when(step == 0)
    def _():
        dk_s[...] = jnp.zeros_like(dk_s)
        dv_s[...] = jnp.zeros_like(dv_s)

    @pl.when(step < pairs)
    def _():
        group = step // 2
        count = g_ref.shape[0]
        query, cosine, sine = picked_queries(pos_ref, q_ref, cos_ref, sin_ref, rows)
        grad = jnp.concatenate(head_operands(g_ref[...]), axis=0)
        key, key_out = group_operands(doubled(turn(k_ref[...], cos_ref[...], sin_ref[...]), group))
        value, _ = group_operands(doubled(v_ref[...], group))
        allowed = picked_mask(pos_col_ref, seg_col_ref, segr_ref)
        weights, total = attention_probs(query, key, allowed)
        probs = weights * (1.0 / total)
        dprobs = dot_nt(grad, value)
        delta = jnp.sum(probs * dprobs, axis=-1, keepdims=True)
        dscores = jnp.concatenate(split(probs * (dprobs - delta)), axis=0)
        dq = fold(dot_nn(dscores[: 2 * count], key_out) + dot_nn(dscores[2 * count :], key_out))
        dq = jnp.where(low, dq[:count], dq[count:]) * HEAD_DIM ** (-0.5)
        dq_low = turn_back(dq, cosine, sine).astype(BF16)
        o_ref[...] = dot_nn(place_ref[...], dq_low).astype(BF16)
        inner_q, inner_g = query[:, :LANES], grad[:, :LANES]
        dv_s[group] += dot_tn(
            jnp.concatenate(split(probs), axis=0), jnp.concatenate([inner_g, inner_g], axis=0)
        )
        dk_s[group] += dot_tn(dscores, jnp.concatenate([inner_q, inner_q], axis=0))

    @pl.when(step == pairs)
    def _():
        dk = jnp.where(low, fold(dk_s[0]), fold(dk_s[1]))
        o_ref[...] = turn_back(dk, cos_ref[...], sin_ref[...]).astype(BF16)

    @pl.when(step == pairs + 1)
    def _():
        o_ref[...] = jnp.where(low, fold(dv_s[0]), fold(dv_s[1])).astype(BF16)


def attention_specs(length, count, base):
    fixed = lambda *shape: pl.BlockSpec(shape, lambda p, pos: (0, 0))
    return [
        pl.BlockSpec((length, LANES), lambda p, pos: (0, base + jnp.minimum(p, 3))),
        pl.BlockSpec((length, LANES), lambda p, pos: (0, base + 4)),
        pl.BlockSpec((length, LANES), lambda p, pos: (0, base + 5)),
        fixed(count, 1),
        fixed(count, 1),
        fixed(1, length),
        fixed(length, LANES),
        fixed(length, LANES),
    ]


def attention_forward(both_proj, positions, pos_col, seg_col, segr, cosine, sine):
    length, count = both_proj.shape[0], positions.shape[0]
    base = (SSM_INNER + XBC_WIDTH) // LANES
    return pl.pallas_call(
        attn_fwd_kernel,
        grid_spec=pltpu.PrefetchScalarGridSpec(
            num_scalar_prefetch=1,
            grid=(HEADS // 2,),
            in_specs=attention_specs(length, count, base),
            out_specs=pl.BlockSpec((count, LANES), lambda p, pos: (0, p)),
            scratch_shapes=[pltpu.VMEM((3, count, LANES), F32)],
        ),
        out_shape=jax.ShapeDtypeStruct((count, HEADS * HEAD_DIM), BF16),
        compiler_params=params(),
        cost_estimate=cost(
            4 * HEADS * count * length * HEAD_DIM, 6 * length * D, HEADS * length * count
        ),
    )(positions, both_proj, both_proj, both_proj, pos_col, seg_col, segr, cosine, sine)


def attention_backward(
    both_proj, positions, pos_col, seg_col, segr, cosine, sine, grads, place, into
):
    length, count = both_proj.shape[0], positions.shape[0]
    base = (SSM_INNER + XBC_WIDTH) // LANES
    at = SSM_INNER // LANES
    pairs = HEADS // 2
    return pl.pallas_call(
        attn_bwd_kernel,
        grid_spec=pltpu.PrefetchScalarGridSpec(
            num_scalar_prefetch=1,
            grid=(pairs + 2,),
            in_specs=attention_specs(length, count, base)
            + [
                pl.BlockSpec((count, LANES), lambda p, pos: (0, at + jnp.minimum(p, 3))),
                pl.BlockSpec((length, count), lambda p, pos: (0, 0)),
                pl.BlockSpec(memory_space=pl.ANY),
            ],
            out_specs=pl.BlockSpec((length, LANES), lambda p, pos: (0, base + p)),
            scratch_shapes=[pltpu.VMEM((3, count, LANES), F32)]
            + [pltpu.VMEM((2, length, LANES), F32)] * 2,
        ),
        out_shape=jax.ShapeDtypeStruct(into.shape, BF16),
        input_output_aliases={11: 0},
        compiler_params=params(),
        cost_estimate=cost(
            10 * HEADS * count * length * HEAD_DIM, 10 * length * D, HEADS * length * count
        ),
    )(positions, both_proj, both_proj, both_proj, pos_col, seg_col, segr, cosine, sine, grads, place, into)


def chunk_masks(segc_ref, segr_ref, last_ref, chunk):
    doc_rows, doc_cols = segc_ref[...], segr_ref[...]
    row_pos = lax.broadcasted_iota(jnp.int32, (CHUNK, CHUNK), 0)
    col_pos = lax.broadcasted_iota(jnp.int32, (CHUNK, CHUNK), 1)
    same = (doc_rows == doc_cols) & (row_pos >= col_pos)
    madd = jnp.where(same, 0.0, -1e30)
    last = last_ref[chunk]
    previous = jnp.where(chunk > 0, last_ref[jnp.maximum(chunk - 1, 0)], -1)
    carried = jnp.where(doc_rows == previous, 1.0, 0.0)
    tail = jnp.where(doc_rows == last, 1.0, 0.0)
    keep = jnp.where(last == previous, 1.0, 0.0)
    return madd, carried, tail, keep


def spread(low, columns, a):
    return jnp.where(low, columns[:, a : a + 1], columns[:, a + 1 : a + 2])


def split(values):
    high = values.astype(BF16)
    return high, (values - high.astype(F32)).astype(BF16)


def wide_split(values):
    return jnp.concatenate(split(values), axis=1)


def both_sides(values):
    return values[:, :LANES] + values[:, LANES:]


def ssm_fwd_kernel(
    last_ref, proj_ref, near_ref, cw_ref, cb_ref, gain_ref, dt_ref, cum_ref, cumt_ref, skip_ref,
    segc_ref, segr_ref, y_ref, s_ref, xbc_ref, slope_ref, mix_ref, state, ext,
):
    chunk = pl.program_id(0)

    @pl.when(chunk == 0)
    def _():
        state[...] = jnp.zeros_like(state)
        ext[:8, :] = jnp.zeros((8, XBC_WIDTH), F32)

    ext[8:, :] = proj_ref[:, SSM_INNER : SSM_INNER + XBC_WIDTH]
    for k in range(XBC_WIDTH // BLOCK_COLS):
        cols = cols_of(k)
        total = ext[8:, cols] * cw_ref[CONV - 1 :, cols] + cb_ref[:, cols]
        for d in range(1, CONV):
            taken = ext[8 - d : 8 - d + CHUNK, cols] * near_ref[:, d : d + 1]
            total += taken * cw_ref[CONV - 1 - d : CONV - d, cols]
        sig = sigmoid(total)
        silu = total * sig
        xbc_ref[:, cols] = silu
        slope_ref[:, cols] = sig + silu * (1.0 - sig)
    ext[:8, :] = ext[CHUNK:, :]
    s_ref[...] = state[...].reshape(s_ref.shape)
    low = lane_iota() < SSM_HEAD_DIM
    madd, carried, tail, keep = chunk_masks(segc_ref, segr_ref, last_ref, chunk)
    dt, cum, cumt = dt_ref[...], cum_ref[...], cumt_ref[...]
    last_cum = cum[CHUNK - 1 : CHUNK, :]
    ecum = jnp.exp(cum) * carried
    tails = jnp.exp(last_cum - cum) * tail
    keeps = jnp.exp(last_cum) * keep
    into = xbc_ref[:, SSM_INNER : SSM_INNER + STATE]
    into_t = into.T
    into_high, into_rest = split(into_t)
    out_high, out_rest = split(xbc_ref[:, SSM_INNER + STATE :])
    out_both = jnp.concatenate([out_high, out_rest], axis=1)
    into_both = jnp.concatenate([into_high, into_rest], axis=1)
    gram = dot_nn(out_both, jnp.concatenate([into_high, into_high], axis=0)) + dot_nn(
        out_high, into_rest
    )
    for p in range(SSM_HEADS // 2):
        a, cols = 2 * p, slice(p * LANES, (p + 1) * LANES)
        heads = xbc_ref[:, cols]
        scaled = heads * spread(low, dt, a)
        decay_a = jnp.exp(cum[:, a : a + 1] - cumt[a : a + 1, :] + madd)
        decay_b = jnp.exp(cum[:, a + 1 : a + 2] - cumt[a + 1 : a + 2, :] + madd)
        mixing = wide_split(jnp.concatenate([decay_a * gram, decay_b * gram], axis=1))
        stacked_wide = wide_split(
            jnp.concatenate([jnp.where(low, scaled, 0.0), jnp.where(low, 0.0, scaled)], axis=0)
        )
        old = state[:, cols]
        old_wide = wide_split(old)
        carry_in = both_sides(dot_nn(out_both, jnp.concatenate([old_wide, old_wide], axis=0)))
        y_ref[:, cols] = (
            both_sides(dot_nn(mixing, jnp.concatenate([stacked_wide, stacked_wide], axis=0)))
            + spread(low, ecum, a) * carry_in
            + spread(low, skip_ref[...], a) * heads
        )
        tail_in = wide_split(scaled * spread(low, tails, a))
        fresh = both_sides(dot_nn(into_both, jnp.concatenate([tail_in, tail_in], axis=0)))
        state[:, cols] = spread(low, keeps, a) * old + fresh
    squares = jnp.zeros((CHUNK, 1), F32)
    for k in range(SSM_INNER // BLOCK_COLS):
        gate = proj_ref[:, cols_of(k)]
        gated = y_ref[:, cols_of(k)] * (gate * sigmoid(gate))
        squares += jnp.sum(gated * gated, axis=-1, keepdims=True)
    inv = lax.rsqrt(squares / SSM_INNER + 1e-05)
    for k in range(SSM_INNER // BLOCK_COLS):
        gate = proj_ref[:, cols_of(k)]
        gated = y_ref[:, cols_of(k)] * (gate * sigmoid(gate))
        mix_ref[:, cols_of(k)] = (gated * inv * gain_ref[:, cols_of(k)]).astype(BF16)


def ssm_bwd_kernel(
    last_ref, proj_ref, near_ref, cw_ref, gain_ref, xbc_ref, slope_ref, dt_ref, cum_ref, cumt_ref,
    skip_ref, segc_ref, segr_ref, s_ref, n_ref, y_ref, out_ref, grad_ref, sums_ref, ends_ref,
    vec_ref, dstate, g_ref, dext,
):
    chunk = pl.num_programs(0) - 1 - pl.program_id(0)

    @pl.when(pl.program_id(0) == 0)
    def _():
        dstate[...] = jnp.zeros_like(dstate)
        dext[CHUNK:, :] = jnp.zeros((8, XBC_WIDTH), F32)
        vec_ref[...] = jnp.zeros_like(vec_ref)

    squares = jnp.zeros((CHUNK, 1), F32)
    along = jnp.zeros((CHUNK, 1), F32)
    for k in range(SSM_INNER // BLOCK_COLS):
        cols = cols_of(k)
        gate = proj_ref[:, cols]
        gated = y_ref[:, cols] * (gate * sigmoid(gate))
        squares += jnp.sum(gated * gated, axis=-1, keepdims=True)
        along += jnp.sum(gated * out_ref[:, cols] * gain_ref[:, cols], axis=-1, keepdims=True)
    inv = lax.rsqrt(squares / SSM_INNER + 1e-05)
    along = along * inv / SSM_INNER
    for k in range(SSM_INNER // BLOCK_COLS):
        cols = cols_of(k)
        gate = proj_ref[:, cols]
        sig = sigmoid(gate)
        silu = gate * sig
        unit = y_ref[:, cols] * silu * inv
        vec_ref[5:6, cols] += jnp.sum(out_ref[:, cols] * unit, axis=0, keepdims=True)
        gated_grad = inv * (out_ref[:, cols] * gain_ref[:, cols] - unit * along)
        g_ref[:, cols] = gated_grad * silu
        gate_grad = gated_grad * y_ref[:, cols] * (sig + silu * (1.0 - sig))
        grad_ref[:, cols] = gate_grad.astype(BF16)
    low = lane_iota() < SSM_HEAD_DIM
    madd, carried, tail, keep = chunk_masks(segc_ref, segr_ref, last_ref, chunk)
    dt, cum, cumt = dt_ref[...], cum_ref[...], cumt_ref[...]
    last_cum = cum[CHUNK - 1 : CHUNK, :]
    ecum = jnp.exp(cum) * carried
    tails = jnp.exp(last_cum - cum) * tail
    keeps = jnp.exp(last_cum) * keep
    into, into_rest = split(xbc_ref[:, SSM_INNER : SSM_INNER + STATE])
    outof, outof_rest = split(xbc_ref[:, SSM_INNER + STATE :])
    outof_t = outof.T
    into_both = jnp.concatenate([into, into_rest], axis=1)
    gram = dot_nt(
        jnp.concatenate([outof, outof_rest], axis=1), jnp.concatenate([into, into], axis=1)
    ) + dot_nt(outof, into_rest)
    dgram = jnp.zeros((CHUNK, CHUNK), F32)
    d_into = jnp.zeros((CHUNK, STATE), F32)
    d_outof = jnp.zeros((CHUNK, STATE), F32)
    sum_y = jnp.zeros((CHUNK, LANES), F32)
    sum_x = jnp.zeros((CHUNK, LANES), F32)
    sum_k = jnp.zeros((CHUNK, LANES), F32)
    ends = jnp.zeros((8, LANES), F32)
    lane_pos = lax.broadcasted_iota(jnp.int32, (LANES, LANES), 0) // SSM_HEAD_DIM
    head_pos = lax.broadcasted_iota(jnp.int32, (LANES, LANES), 1)

    def by_head(values, pick):
        high = values.astype(BF16)
        rest = (values - high.astype(F32)).astype(BF16)
        return dot_nn(jnp.concatenate([high, rest], axis=1), pick)

    for p in range(SSM_HEADS // 2):
        a, cols = 2 * p, slice(p * LANES, (p + 1) * LANES)
        pick = jnp.where(lane_pos + a == head_pos, 1.0, 0.0).astype(BF16)
        pick = jnp.concatenate([pick, pick], axis=0)
        heads, grad = xbc_ref[:, cols], g_ref[:, cols]
        dt_wide = spread(low, dt, a)
        skip_wide = spread(low, skip_ref[...], a)
        tail_wide = spread(low, tails, a)
        keep_wide = spread(low, keeps, a)
        scaled = heads * dt_wide
        scaled_low = scaled.astype(BF16)
        decay_a = jnp.exp(cum[:, a : a + 1] - cumt[a : a + 1, :] + madd)
        decay_b = jnp.exp(cum[:, a + 1 : a + 2] - cumt[a + 1 : a + 2, :] + madd)
        grads = wide_split(
            jnp.concatenate([jnp.where(low, grad, 0.0), jnp.where(low, 0.0, grad)], axis=0)
        )
        dmix = dot_nt(grads, jnp.concatenate([scaled_low, scaled_low], axis=1))
        dgram += decay_a * dmix[:CHUNK] + decay_b * dmix[CHUNK:]
        mixing = split(jnp.concatenate([decay_a * gram, decay_b * gram], axis=0))
        d_new = dstate[:, cols]
        d_new_wide = wide_split(d_new)
        d_new_low = d_new_wide[:, :LANES]
        d_inner = dot_tn(jnp.concatenate(mixing, axis=0), jnp.concatenate([grads, grads], axis=0))
        d_scaled = both_sides(d_inner) + tail_wide * both_sides(
            dot_nn(into_both, jnp.concatenate([d_new_wide, d_new_wide], axis=0))
        )
        old = s_ref[0, :, cols]
        d_carry = (spread(low, ecum, a) * grad).astype(BF16)
        d_outof += dot_nt(d_carry, old.astype(BF16))
        d_into += dot_nt((scaled * tail_wide).astype(BF16), d_new_low)
        ends += jnp.sum((d_new * n_ref[0, :, cols]).reshape(STATE // 8, 8, LANES), axis=0) @ pick[
            :LANES
        ].astype(F32)
        dstate[:, cols] = keep_wide * d_new + dot_nn(outof_t, d_carry)
        dext[:CHUNK, cols] = (d_scaled * dt_wide + skip_wide * grad) * slope_ref[:, cols]
        both = grad * heads
        sum_y += by_head(grad * y_ref[:, cols] - skip_wide * both - scaled * d_scaled, pick)
        sum_x += by_head(heads * d_scaled, pick)
        sum_k += by_head(both, pick)
    dgram_low = dgram.astype(BF16)
    cols = slice(SSM_INNER, SSM_INNER + STATE)
    dext[:CHUNK, cols] = (d_into + dot_tn(dgram_low, outof)) * slope_ref[:, cols]
    cols = slice(SSM_INNER + STATE, XBC_WIDTH)
    dext[:CHUNK, cols] = (d_outof + dot_nn(dgram_low, into)) * slope_ref[:, cols]
    for k in range(XBC_WIDTH // BLOCK_COLS):
        cols = cols_of(k)
        at = slice(SSM_INNER + k * BLOCK_COLS, SSM_INNER + (k + 1) * BLOCK_COLS)
        before = proj_ref[:, at]
        here = dext[:CHUNK, cols]
        total = here * cw_ref[CONV - 1 :, cols]
        vec_ref[CONV - 1 : CONV, cols] += jnp.sum(here * before, axis=0, keepdims=True)
        vec_ref[CONV : CONV + 1, cols] += jnp.sum(here, axis=0, keepdims=True)
        for d in range(1, CONV):
            later = dext[d : d + CHUNK, cols] * near_ref[:, CONV + d : CONV + d + 1]
            total += later * cw_ref[CONV - 1 - d : CONV - d, cols]
            vec_ref[CONV - 1 - d : CONV - d, cols] += jnp.sum(later * before, axis=0, keepdims=True)
        grad_ref[:, at] = total.astype(BF16)
    dext[CHUNK:, :] = dext[:8, :]
    sums_ref[:, :LANES] = sum_y
    sums_ref[:, LANES : 2 * LANES] = sum_x
    sums_ref[:, 2 * LANES :] = sum_k
    ends_ref[...] = ends.reshape(ends_ref.shape)


def scan_specs(at):
    here = lambda i, last: (at(i), 0)
    across = lambda i, last: (0, at(i))
    return dict(
        rows=lambda width: pl.BlockSpec((CHUNK, width), here),
        cols=lambda height: pl.BlockSpec((height, CHUNK), across),
        fixed=lambda *shape: pl.BlockSpec(shape, lambda i, last: (0,) * len(shape)),
    )


def ssm_forward(last, both_proj, near, conv_w, conv_b, gain, dt, cum, cumt, skip, segc, segr):
    length, width = both_proj.shape
    chunks = length // CHUNK
    spec = scan_specs(lambda i: i)
    return pl.pallas_call(
        ssm_fwd_kernel,
        grid_spec=pltpu.PrefetchScalarGridSpec(
            num_scalar_prefetch=1,
            grid=(chunks,),
            in_specs=[
                spec["rows"](width),
                spec["rows"](2 * CONV),
                spec["fixed"](CONV, XBC_WIDTH),
                spec["fixed"](1, XBC_WIDTH),
                spec["fixed"](1, SSM_INNER),
                spec["rows"](SSM_HEADS),
                spec["rows"](SSM_HEADS),
                spec["cols"](SSM_HEADS),
                spec["fixed"](1, SSM_HEADS),
                spec["rows"](1),
                spec["cols"](1),
            ],
            out_specs=[
                spec["rows"](SSM_INNER),
                pl.BlockSpec((1, STATE, SSM_INNER), lambda c, last: (c, 0, 0)),
                spec["rows"](XBC_WIDTH),
                spec["rows"](XBC_WIDTH),
                spec["rows"](SSM_INNER),
            ],
            scratch_shapes=[
                pltpu.VMEM((STATE, SSM_INNER), F32),
                pltpu.VMEM((CHUNK + 8, XBC_WIDTH), F32),
            ],
        ),
        out_shape=[
            jax.ShapeDtypeStruct((length, SSM_INNER), F32),
            jax.ShapeDtypeStruct((chunks, STATE, SSM_INNER), F32),
            jax.ShapeDtypeStruct((length, XBC_WIDTH), F32),
            jax.ShapeDtypeStruct((length, XBC_WIDTH), F32),
            jax.ShapeDtypeStruct((length, SSM_INNER), BF16),
        ],
        compiler_params=params(),
        cost_estimate=cost(
            8 * length * SSM_INNER * STATE, 40 * length * SSM_INNER, length * CHUNK * SSM_HEADS
        ),
    )(last, both_proj, near, conv_w, conv_b, gain, dt, cum, cumt, skip, segc, segr)


def ssm_backward(
    last, both_proj, near, conv_w, gain, xbc, slope, dt, cum, cumt, skip, segc, segr, states, outputs,
    grads,
):
    length, width = both_proj.shape
    chunks = length // CHUNK
    end = chunks - 1
    spec = scan_specs(lambda i: end - i)
    return pl.pallas_call(
        ssm_bwd_kernel,
        grid_spec=pltpu.PrefetchScalarGridSpec(
            num_scalar_prefetch=1,
            grid=(chunks,),
            in_specs=[
                spec["rows"](width),
                spec["rows"](2 * CONV),
                spec["fixed"](CONV, XBC_WIDTH),
                spec["fixed"](1, SSM_INNER),
                spec["rows"](XBC_WIDTH),
                spec["rows"](XBC_WIDTH),
                spec["rows"](SSM_HEADS),
                spec["rows"](SSM_HEADS),
                spec["cols"](SSM_HEADS),
                spec["fixed"](1, SSM_HEADS),
                spec["rows"](1),
                spec["cols"](1),
                pl.BlockSpec((1, STATE, SSM_INNER), lambda i, last: (end - i, 0, 0)),
                pl.BlockSpec(
                    (1, STATE, SSM_INNER), lambda i, last: (jnp.minimum(end - i + 1, end), 0, 0)
                ),
                spec["rows"](SSM_INNER),
                spec["rows"](grads.shape[1]),
            ],
            out_specs=[
                spec["rows"](width),
                spec["rows"](3 * LANES),
                pl.BlockSpec((1, 8, LANES), lambda i, last: (end - i, 0, 0)),
                spec["fixed"](8, XBC_WIDTH),
            ],
            scratch_shapes=[
                pltpu.VMEM((STATE, SSM_INNER), F32),
                pltpu.VMEM((CHUNK, SSM_INNER), F32),
                pltpu.VMEM((CHUNK + 8, XBC_WIDTH), F32),
            ],
        ),
        out_shape=[
            jax.ShapeDtypeStruct((length, width), BF16),
            jax.ShapeDtypeStruct((length, 3 * LANES), F32),
            jax.ShapeDtypeStruct((chunks, 8, LANES), F32),
            jax.ShapeDtypeStruct((8, XBC_WIDTH), F32),
        ],
        compiler_params=params(),
        cost_estimate=cost(
            24 * length * SSM_INNER * STATE, 60 * length * SSM_INNER, length * CHUNK * SSM_HEADS
        ),
    )(
        last, both_proj, near, conv_w, gain, xbc, slope, dt, cum, cumt, skip, segc, segr, states, states,
        outputs, grads,
    )


def neighbours(segment):
    length = segment.shape[0]
    columns = []
    for d in range(CONV):
        earlier = jnp.pad(segment, (d, 0), constant_values=-1)[:length]
        columns.append(earlier == segment)
    for d in range(CONV):
        later = jnp.pad(segment, (0, d), constant_values=-1)[d:]
        columns.append(later == segment)
    return jnp.stack(columns, axis=1).astype(F32)


def rows_kernel(counts, lo_ref, hi_ref, ids_ref, *rest):
    step = pl.program_id(0)
    g_refs, (o_ref, wide) = rest[:-2], rest[-2:]
    group = wide.shape[0]

    @pl.when(step == 0)
    def _():
        o_ref[...] = jnp.zeros_like(o_ref)

    before = 0
    for count, g_ref in zip(counts, g_refs):

        @pl.when((step >= before) & (step < before + count))
        def _(g_ref=g_ref):
            wide[...] = g_ref[...].astype(F32)

        before = before + count
    low, high = lo_ref[step], hi_ref[step]

    def one(j):
        o_ref[pl.ds(ids_ref[step * group + j], 1), :] += wide[pl.ds(j, 1), :]

    def eight(k, carry):
        for u in range(8):
            one(low + 8 * k + u)
        return carry

    def rest_of(j, carry):
        one(j)
        return carry

    eights = (high - low) // 8
    lax.fori_loop(0, eights, eight, 0)
    lax.fori_loop(low + 8 * eights, high, rest_of, 0)


def rows_by_token(local_ids, grads, shard_rows, group):
    width = grads[0].shape[1]
    counts = [g.shape[0] // group for g in grads]
    lists = local_ids.reshape(-1, group)
    low = jnp.sum((lists < 0).astype(jnp.int32), axis=1)
    high = jnp.sum((lists < shard_rows).astype(jnp.int32), axis=1)
    specs, before = [], 0
    for count in counts:
        specs.append(
            pl.BlockSpec(
                (group, width),
                lambda i, lo, hi, ids, before=before, count=count: (
                    jnp.clip(i - before, 0, count - 1),
                    0,
                ),
            )
        )
        before = before + count
    return pl.pallas_call(
        functools.partial(rows_kernel, counts),
        grid_spec=pltpu.PrefetchScalarGridSpec(
            num_scalar_prefetch=3,
            grid=(before,),
            in_specs=specs,
            out_specs=pl.BlockSpec((shard_rows, width), lambda i, lo, hi, ids: (0, 0)),
            scratch_shapes=[pltpu.VMEM((group, width), F32)],
        ),
        out_shape=jax.ShapeDtypeStruct((shard_rows, width), F32),
        compiler_params=params(),
        cost_estimate=cost(before * group * width * LANES, before * group * width * 2),
    )(low, high, local_ids, *grads)


def split_nn(left, right):
    left_high, left_rest = split(left)
    right_high, right_rest = split(right)
    return dot_nn(left_high, right_high) + dot_nn(left_rest, right_high) + dot_nn(left_high, right_rest)


def rotate_kernel(l_ref, g_ref, r_ref, o_ref):
    grad = g_ref[...].reshape(D, BLOCK_COLS)
    left_high, left_rest = split(l_ref[0])
    part = dot_nn(left_high, grad) + dot_nn(left_rest, grad)
    o_ref[0] = split_nn(part, r_ref[0])


def rotate_blocks(left_basis, grad_whole, right_basis):
    slots, depth, _ = left_basis.shape
    rows = grad_whole.shape[0]
    return pl.pallas_call(
        rotate_kernel,
        grid=(slots,),
        in_specs=[
            pl.BlockSpec((1, depth, D), lambda k: (k, 0, 0)),
            pl.BlockSpec((rows, 1, depth, BLOCK_COLS), lambda k: (0, k, 0, 0)),
            pl.BlockSpec((1, BLOCK_COLS, BLOCK_COLS), lambda k: (k, 0, 0)),
        ],
        out_specs=pl.BlockSpec((1, depth, BLOCK_COLS), lambda k: (k, 0, 0)),
        out_shape=jax.ShapeDtypeStruct((slots, depth, BLOCK_COLS), F32),
        compiler_params=params(),
        cost_estimate=cost(6 * slots * depth * D * BLOCK_COLS, slots * depth * D * 5),
    )(left_basis, grad_whole, right_basis)


def step_kernel(scale_ref, rot_ref, m_ref, v_ref, l_ref, r_ref, mo_ref, vo_ref, u_ref):
    rotated = rot_ref[0] * scale_ref[0]
    first_new = soap_first * m_ref[0] + (1.0 - soap_first) * rotated
    second_new = soap_second * v_ref[0] + (1.0 - soap_second) * rotated * rotated
    mo_ref[0], vo_ref[0] = first_new, second_new
    direction = (first_new / scale_ref[1]) / (jnp.sqrt(second_new / scale_ref[2]) + adam_eps)
    turned = split_nn(direction, r_ref[0].T).astype(BF16)
    left_high, left_rest = split(l_ref[0])
    update = dot_nn(left_high.T, turned) + dot_nn(left_rest.T, turned)
    u_ref[0] = update.astype(BF16)


def step_blocks(scales, rotated, block_first, block_second, left_basis, right_basis):
    slots, depth, _ = left_basis.shape
    own = pl.BlockSpec((1, depth, BLOCK_COLS), lambda k: (k, 0, 0))
    small = jax.ShapeDtypeStruct((slots, depth, BLOCK_COLS), F32)
    return pl.pallas_call(
        step_kernel,
        grid=(slots,),
        in_specs=[
            pl.BlockSpec(memory_space=pltpu.SMEM),
            own,
            own,
            own,
            pl.BlockSpec((1, depth, D), lambda k: (k, 0, 0)),
            pl.BlockSpec((1, BLOCK_COLS, BLOCK_COLS), lambda k: (k, 0, 0)),
        ],
        out_specs=[own, own, pl.BlockSpec((1, D, BLOCK_COLS), lambda k: (k, 0, 0))],
        out_shape=[small, small, jax.ShapeDtypeStruct((slots, D, BLOCK_COLS), BF16)],
        compiler_params=params(),
        cost_estimate=cost(6 * slots * depth * D * BLOCK_COLS, slots * depth * D * 7),
    )(scales, rotated, block_first, block_second, left_basis, right_basis)


def to_peers(axis, extent, place, src, box, send_sem, recv_sem):
    copies = []
    for k in range(1, extent):
        peer = list(place)
        peer[axis] = lax.rem(place[axis] + k, extent)
        copies.append(
            pltpu.make_async_remote_copy(
                src_ref=src,
                dst_ref=box.at[place[axis]],
                send_sem=send_sem.at[k],
                recv_sem=recv_sem.at[k],
                device_id=tuple(peer),
                device_id_type=MESH,
            )
        )
    return copies


def greet_peers(axes, place):
    barrier = pltpu.get_barrier_semaphore()
    count = 0
    for axis, extent in axes:
        for k in range(1, extent):
            peer = list(place)
            peer[axis] = lax.rem(place[axis] + k, extent)
            pl.semaphore_signal(barrier, inc=1, device_id=tuple(peer), device_id_type=MESH)
            count += 1
    pl.semaphore_wait(barrier, count)


def total_kernel(rows, cols, x_ref, o_ref, col_box, row_box, col_send, col_recv, row_send, row_recv):
    place = (lax.axis_index("row"), lax.axis_index("col"))
    greet_peers(((0, rows), (1, cols)), place)
    total = x_ref[...]
    for axis, extent, box, send_sem, recv_sem in (
        (1, cols, col_box, col_send, col_recv),
        (0, rows, row_box, row_send, row_recv),
    ):
        o_ref[...] = total
        box[place[axis]] = total
        copies = to_peers(axis, extent, place, o_ref, box, send_sem, recv_sem)
        for copy in copies:
            copy.start()
        for copy in copies:
            copy.wait()
        total = jnp.sum(box[...], axis=0)
    o_ref[...] = total


def total_over_all(values, rows, cols, collective_id):
    dma = pltpu.SemaphoreType.DMA
    return pl.pallas_call(
        functools.partial(total_kernel, rows, cols),
        in_specs=[pl.BlockSpec(memory_space=pltpu.VMEM)],
        out_specs=pl.BlockSpec(memory_space=pltpu.VMEM),
        out_shape=jax.ShapeDtypeStruct(values.shape, F32),
        scratch_shapes=[
            pltpu.VMEM((cols,) + values.shape, F32),
            pltpu.VMEM((rows,) + values.shape, F32),
            dma((cols,)),
            dma((cols,)),
            dma((rows,)),
            dma((rows,)),
        ],
        compiler_params=params(collective_id=collective_id, has_side_effects=True),
        cost_estimate=cost(rows * cols * values.size, rows * cols * values.size * 4),
    )(values)


def ring_bits(rows, cols):
    bits = []
    for axis, extent in ((0, rows), (1, cols)):
        bit = extent // 2
        while bit >= 1:
            bits.append((axis, bit))
            bit = bit // 2
    return bits


def scatter_orders(rows, cols):
    bits = ring_bits(rows, cols)
    row_bits = [b for b in reversed(bits) if b[0] == 0]
    col_bits = [b for b in reversed(bits) if b[0] == 1]
    return col_bits + row_bits, col_bits[:1] + col_bits[1:][::-1] + row_bits


def tail_kernel(rows, cols, slots, g_ref, p_ref, v_ref, whole_ref, tok_ref, vec_ref, own, *rest):
    bits = ring_bits(rows, cols)
    stages = len(bits)
    row_bits = [b for b in bits if b[0] == 0]
    col_bits = [b for b in bits if b[0] == 1]
    boxes, rest = rest[:stages], rest[stages:]
    vec_box, vec_sum, send_sem, recv_sem, own_sem = rest[:5]
    join_send, join_recv, tok_send, tok_recv, tok_own, vec_send, vec_recv = rest[5:]
    place = (lax.axis_index("row"), lax.axis_index("col"))
    half = whole_ref.shape[-2] // 2
    orders = scatter_orders(rows, cols)

    def side(which):
        axis, bit = which
        return place[axis] // bit % 2

    def partner(which):
        axis, bit = which
        moved = place[axis] + bit - 2 * bit * side(which)
        return (moved, place[1]) if axis == 0 else (place[0], moved)

    def remote(src, dst, send, recv, which):
        return pltpu.make_async_remote_copy(
            src_ref=src,
            dst_ref=dst,
            send_sem=send,
            recv_sem=recv,
            device_id=partner(which),
            device_id_type=MESH,
        )

    barrier = pltpu.get_barrier_semaphore()
    for which in bits:
        pl.semaphore_signal(barrier, inc=1, device_id=partner(which), device_id_type=MESH)
    pl.semaphore_wait(barrier, stages)
    units = [(slot, h) for slot in range(slots) for h in range(2)]

    def pick(ref, before, which, side_of, after):
        at = before.index(which)
        return ref.at[(slice(None),) * at + (side_of,) + (slice(None),) * (len(before) - at - 1) + after]

    def part(slot, h, side_of):
        return pick(g_ref, bits, orders[h][0], side_of, (slot, slice(h * half, (h + 1) * half)))

    def cut(stage, u, side_of):
        order = orders[units[u][1]]
        left = [b for b in bits if b not in order[: stage + 1]]
        return pick(boxes[stage].at[u], left, order[stage + 1], side_of, ())

    def send(stage, u):
        slot, h = units[u]
        which = orders[h][stage]
        other = 1 - side(which)
        return remote(
            part(slot, h, other) if stage == 0 else cut(stage - 1, u, other),
            boxes[stage].at[u],
            send_sem.at[stage, u],
            recv_sem.at[stage, u],
            which,
        )

    def keep(u):
        slot, h = units[u]
        return pltpu.make_async_copy(part(slot, h, side(orders[h][0])), own.at[u], own_sem.at[u])

    def joined(ref, order, of_bits, stage, after):
        at = tuple(slice(None) if b in order[:stage] else side(b) for b in of_bits)
        return ref.at[at + after]

    def join(stage, u):
        slot, h = units[u]
        region = joined(whole_ref, row_bits, row_bits, stage, (slot, slice(h * half, (h + 1) * half)))
        return remote(region, region, join_send.at[stage, u], join_recv.at[stage, u], row_bits[stage])

    def tok(stage, h):
        order = (orders[h][1 : len(col_bits)] + orders[h][:1])
        region = joined(tok_ref, order, col_bits, stage, (h,))
        return remote(
            p_ref.at[h] if stage == 0 else region, region, tok_send.at[stage, h],
            tok_recv.at[stage, h], order[stage],
        )

    def tok_keep():
        region = joined(tok_ref, [], col_bits, 0, ())
        return pltpu.make_async_copy(p_ref, region, tok_own)

    def vec(stage):
        return remote(
            vec_sum.at[stage], vec_box.at[stage], vec_send.at[stage], vec_recv.at[stage], bits[stage]
        )

    sent = []

    def start(copy):
        copy.start()
        sent.append(copy)
        return copy

    flying = {}
    vec_sum[0] = v_ref[...]
    flying["vec", 0] = start(vec(0))
    for u in range(len(units)):
        flying[0, u] = start(send(0, u))
        keep(u).start()
        if u == 1:
            tok_keep().start()
            for h in range(2):
                flying["tok", 0, h] = start(tok(0, h))
    steps = slots + stages + len(row_bits) - 1
    tok_at = [(k + 1) * steps // (len(col_bits) + 1) for k in range(len(col_bits))]
    for t in range(steps):
        if t < stages:
            flying["vec", t].wait_recv()
            if t + 1 < stages:
                vec_sum[t + 1] = vec_sum[t] + vec_box[t]
                flying["vec", t + 1] = start(vec(t + 1))
            else:
                vec_ref[...] = vec_sum[t] + vec_box[t]
        for k, at in enumerate(tok_at):
            if at == t:
                if k == 0:
                    tok_keep().wait()
                for h in range(2):
                    flying["tok", k, h].wait_recv()
                    if k + 1 < len(col_bits):
                        flying["tok", k + 1, h] = start(tok(k + 1, h))
        for stage in reversed(range(stages + len(row_bits))):
            slot = t - stage
            if not 0 <= slot < slots:
                continue
            for h in range(2):
                u = 2 * slot + h
                if stage >= stages:
                    flying["join", stage - stages, u].wait_recv()
                    if stage - stages + 1 < len(row_bits):
                        flying["join", stage - stages + 1, u] = start(join(stage - stages + 1, u))
                    continue
                flying[stage, u].wait_recv()
                box = boxes[stage].at[u]
                if stage == 0:
                    keep(u).wait()
                    held = own.at[u]
                else:
                    held = cut(stage - 1, u, side(orders[h][stage]))
                if stage == stages - 1:
                    total = held[...].astype(F32) + box[...].astype(F32)
                    mine = joined(
                        whole_ref, [], row_bits, 0, (slot, slice(h * half, (h + 1) * half))
                    )
                    mine[...] = total.astype(BF16)
                    flying["join", 0, u] = start(join(0, u))
                    continue
                extents = box.shape[:-2]

                def add(k, carry, box=box, held=held, extents=extents):
                    at = []
                    for extent in reversed(extents):
                        at.append(k % extent)
                        k = k // extent
                    at = tuple(reversed(at))
                    box[at] = (held[at].astype(F32) + box[at].astype(F32)).astype(BF16)
                    return carry

                lax.fori_loop(0, 2 ** len(extents), add, 0)
                flying[stage + 1, u] = start(send(stage + 1, u))
    for copy in sent:
        copy.wait_send()


def tail_exchange(grads, pieces, vectors, rows, cols, collective_id):
    _, nslots, depth, _ = grads.shape
    slots = nslots // cols
    bits = ring_bits(rows, cols)
    stages = len(bits)
    row_stages, col_stages = (rows - 1).bit_length(), (cols - 1).bit_length()
    units, half = 2 * slots, depth // 2
    count, width = pieces.shape
    boxes = [
        pltpu.VMEM((units,) + (2,) * (stages - s - 1) + (half, BLOCK_COLS), BF16)
        for s in range(stages)
    ]
    vec_shape = (stages,) + vectors.shape
    whole, tokens, total = pl.pallas_call(
        functools.partial(tail_kernel, rows, cols, slots),
        in_specs=[
            pl.BlockSpec(memory_space=pl.ANY),
            pl.BlockSpec(memory_space=pl.ANY),
            pl.BlockSpec(memory_space=pltpu.VMEM),
        ],
        out_specs=[
            pl.BlockSpec(memory_space=pltpu.VMEM),
            pl.BlockSpec(memory_space=pl.ANY),
            pl.BlockSpec(memory_space=pltpu.VMEM),
        ],
        out_shape=[
            jax.ShapeDtypeStruct((2,) * row_stages + (slots, depth, BLOCK_COLS), BF16),
            jax.ShapeDtypeStruct((2,) * col_stages + (2, count // 2, width), BF16),
            jax.ShapeDtypeStruct(vectors.shape, F32),
        ],
        scratch_shapes=[pltpu.VMEM(boxes[0].shape, BF16)]
        + boxes
        + [
            pltpu.VMEM(vec_shape, F32),
            pltpu.VMEM(vec_shape, F32),
            pltpu.SemaphoreType.DMA((stages, units)),
            pltpu.SemaphoreType.DMA((stages, units)),
            pltpu.SemaphoreType.DMA((units,)),
            pltpu.SemaphoreType.DMA((row_stages, units)),
            pltpu.SemaphoreType.DMA((row_stages, units)),
            pltpu.SemaphoreType.DMA((col_stages, 2)),
            pltpu.SemaphoreType.DMA((col_stages, 2)),
            pltpu.SemaphoreType.DMA,
            pltpu.SemaphoreType.DMA((stages,)),
            pltpu.SemaphoreType.DMA((stages,)),
        ],
        compiler_params=params(collective_id=collective_id, has_side_effects=True),
        cost_estimate=cost(rows * nslots * depth * BLOCK_COLS, rows * nslots * depth * BLOCK_COLS * 6),
    )(
        grads.reshape((2,) * stages + (slots, depth, BLOCK_COLS)),
        pieces.reshape(2, count // 2, width),
        vectors,
    )
    return whole.reshape(rows, slots, depth, BLOCK_COLS), tokens.reshape(cols * count, width), total


def doubling(place, bits):
    def side(which):
        axis, bit = which
        return place[axis] // bit % 2

    def partner(which):
        axis, bit = which
        moved = place[axis] + bit - 2 * bit * side(which)
        return (moved, place[1]) if axis == 0 else (place[0], moved)

    return side, partner


def greet(bits, partner):
    barrier = pltpu.get_barrier_semaphore()
    for which in bits:
        pl.semaphore_signal(barrier, inc=1, device_id=partner(which), device_id_type=MESH)
    pl.semaphore_wait(barrier, len(bits))


def joiner(side, partner, src, out, of_bits, order, after, send_sem, recv_sem):
    def copy(k):
        at = tuple(slice(None) if b in order[:k] else side(b) for b in of_bits)
        region = out.at[at + after]
        return pltpu.make_async_remote_copy(
            src_ref=src if k == 0 else region,
            dst_ref=region,
            send_sem=send_sem.at[k],
            recv_sem=recv_sem.at[k],
            device_id=partner(order[k]),
            device_id_type=MESH,
        )

    return copy


def front_kernel(rows, cols, i_ref, t_ref, w_ref, io_ref, to_ref, wo_ref, *sems):
    bits = ring_bits(rows, cols)
    row_bits = [b for b in bits if b[0] == 0]
    col_bits = [b for b in bits if b[0] == 1]
    place = (lax.axis_index("row"), lax.axis_index("col"))
    side, partner = doubling(place, bits)
    i_send, i_recv, t_send, t_recv, w_send, w_recv, keep_sem = sems
    greet(bits, partner)
    own_row, own_col = tuple(side(b) for b in row_bits), tuple(side(b) for b in col_bits)
    keeps = [
        pltpu.make_async_copy(i_ref, io_ref.at[own_row + own_col], keep_sem.at[0]),
        pltpu.make_async_copy(t_ref, to_ref.at[own_col], keep_sem.at[1]),
        pltpu.make_async_copy(w_ref, wo_ref.at[own_row], keep_sem.at[2]),
    ]
    orders = [o[1 : len(col_bits)] + o[:1] for o in scatter_orders(rows, cols)]
    jobs = {}
    jobs["i", 0] = (joiner(side, partner, i_ref, io_ref, bits, bits[::-1], (), i_send, i_recv), 0, 1)
    for p in range(t_ref.shape[0]):
        copy = joiner(
            side, partner, t_ref.at[p], to_ref, col_bits, orders[p % 2], (p,), t_send.at[p], t_recv.at[p]
        )
        jobs["t", p] = (copy, 2 + p // 2, 2)
    for p in range(w_ref.shape[0]):
        copy = joiner(
            side, partner, w_ref.at[p], wo_ref, row_bits, row_bits, (p,), w_send.at[p], w_recv.at[p]
        )
        jobs["w", p] = (copy, 1 + p, 1)
    run_joins(jobs, {"i": len(bits), "t": len(col_bits), "w": len(row_bits)}, keeps)


def run_joins(jobs, stages, keeps, done=None):
    for copy in keeps:
        copy.start()
    sent = []
    for copy, _, _ in jobs.values():
        sent.append(copy(0))
        sent[-1].start()
    for copy in keeps:
        copy.wait()
    ends = [at + every * (stages[name[0]] - 1) for name, (_, at, every) in jobs.items()]
    for t in range(max(ends) + 1):
        for name, (copy, at, every) in jobs.items():
            k = (t - at) // every
            if t < at or (t - at) % every or k >= stages[name[0]]:
                continue
            copy(k).wait_recv()
            if k + 1 < stages[name[0]]:
                sent.append(copy(k + 1))
                sent[-1].start()
            elif done is not None:
                done(name[1])
    for copy in sent:
        copy.wait_send()


def front_exchange(ints, table_low, weights_low, rows, cols, collective_id):
    row_stages, col_stages = (rows - 1).bit_length(), (cols - 1).bit_length()
    parts = TABLE_PARTS
    shard, width = table_low.shape
    slots = weights_low.shape[0]
    dma = pltpu.SemaphoreType.DMA
    ints = ints.reshape(-1, LANES)
    outs = pl.pallas_call(
        functools.partial(front_kernel, rows, cols),
        in_specs=[pl.BlockSpec(memory_space=pl.ANY)] * 3,
        out_specs=[pl.BlockSpec(memory_space=pltpu.VMEM)] * 3,
        out_shape=[
            jax.ShapeDtypeStruct((2,) * (row_stages + col_stages) + ints.shape, jnp.int32),
            jax.ShapeDtypeStruct((2,) * col_stages + (parts, shard // parts, width), BF16),
            jax.ShapeDtypeStruct((2,) * row_stages + weights_low.shape, BF16),
        ],
        scratch_shapes=[
            dma((row_stages + col_stages,)),
            dma((row_stages + col_stages,)),
            dma((parts, col_stages)),
            dma((parts, col_stages)),
            dma((slots, row_stages)),
            dma((slots, row_stages)),
            dma((3,)),
        ],
        compiler_params=params(collective_id=collective_id, has_side_effects=True),
        cost_estimate=cost(1 << 20, cols * shard * width * 4),
    )(ints, table_low.reshape(parts, shard // parts, width), weights_low)
    return (
        outs[0].reshape(rows, cols, -1),
        outs[1].reshape(cols * shard, width),
        outs[2].reshape((rows,) + weights_low.shape),
    )


def weights_kernel(rows, cols, w_ref, o_ref, box, send_sem, recv_sem, keep_sem, out_sem):
    bits = ring_bits(rows, cols)
    col_bits = [b for b in bits if b[0] == 1]
    place = (lax.axis_index("row"), lax.axis_index("col"))
    side, partner = doubling(place, bits)
    greet(col_bits, partner)
    own = tuple(side(b) for b in col_bits)
    slots, half = w_ref.shape[1], w_ref.shape[2] // 2
    orders = [o[1 : len(col_bits)] + o[:1] for o in scatter_orders(rows, cols)]
    keeps = [
        pltpu.make_async_copy(w_ref, box.at[(slice(None),) + own], keep_sem),
    ]
    jobs = {}
    outs = []

    def done(u):
        part = (slice(None),) * (1 + len(col_bits)) + parts[u]
        outs.append(pltpu.make_async_copy(box.at[part], o_ref.at[part], out_sem.at[u]))
        outs[-1].start()

    parts = [(slot, slice(h * half, (h + 1) * half)) for slot in range(slots) for h in range(2)]
    for slot in range(slots):
        for h in range(2):
            part = (slot, slice(h * half, (h + 1) * half))
            u = 2 * slot + h

            def copy(k, part=part, order=orders[h], u=u):
                at = tuple(slice(None) if b in order[:k] else side(b) for b in col_bits)
                region = box.at[(slice(None),) + at + part]
                return pltpu.make_async_remote_copy(
                    src_ref=w_ref.at[(slice(None),) + part] if k == 0 else region,
                    dst_ref=region,
                    send_sem=send_sem.at[u, k],
                    recv_sem=recv_sem.at[u, k],
                    device_id=partner(order[k]),
                    device_id_type=MESH,
                )

            jobs["w", u] = (copy, slot, 1)
    run_joins(jobs, {"w": len(col_bits)}, keeps, done)
    for copy in outs:
        copy.wait()


def gather_weights(weights, rows, cols, collective_id):
    _, slots, depth, width = weights.shape
    col_stages = (cols - 1).bit_length()
    dma = pltpu.SemaphoreType.DMA
    shape = (rows,) + (2,) * col_stages + (slots, depth, width)
    out = pl.pallas_call(
        functools.partial(weights_kernel, rows, cols),
        in_specs=[pl.BlockSpec(memory_space=pl.ANY)],
        out_specs=pl.BlockSpec(memory_space=pl.ANY),
        out_shape=jax.ShapeDtypeStruct(shape, BF16),
        scratch_shapes=[
            pltpu.VMEM(shape, BF16),
            dma((2 * slots, col_stages)),
            dma((2 * slots, col_stages)),
            dma,
            dma((2 * slots,)),
        ],
        compiler_params=params(collective_id=collective_id, has_side_effects=True),
        cost_estimate=cost(1 << 20, 4 * cols * weights.size),
    )(weights)
    return out.reshape(rows, cols * slots, depth, width)


def columns_kernel(cols, x_ref, o_ref, send_sem, recv_sem):
    place = (lax.axis_index("row"), lax.axis_index("col"))
    greet_peers(((1, cols),), place)
    o_ref[place[1]] = x_ref[...]
    copies = to_peers(1, cols, place, x_ref, o_ref, send_sem, recv_sem)
    for copy in copies:
        copy.start()
    for copy in copies:
        copy.wait()


def gather_columns(values, cols, collective_id):
    dma = pltpu.SemaphoreType.DMA
    return pl.pallas_call(
        functools.partial(columns_kernel, cols),
        in_specs=[pl.BlockSpec(memory_space=pltpu.VMEM)],
        out_specs=pl.BlockSpec(memory_space=pltpu.VMEM),
        out_shape=jax.ShapeDtypeStruct((cols,) + values.shape, values.dtype),
        scratch_shapes=[dma((cols,)), dma((cols,))],
        compiler_params=params(collective_id=collective_id, has_side_effects=True),
        cost_estimate=cost(1024, cols * values.size * 4),
    )(values)


def scatter_columns_kernel(rows, cols, x_ref, o_ref, *rest):
    bits = [b for b in ring_bits(rows, cols) if b[0] == 1]
    stages = len(bits)
    boxes, (send_sem, recv_sem) = rest[:stages], rest[stages:]
    place = (lax.axis_index("row"), lax.axis_index("col"))
    side, partner = doubling(place, bits)
    orders = [o[:stages] for o in scatter_orders(rows, cols)]
    greet(bits, partner)

    def held(stage, h, side_of):
        left = [b for b in bits if b not in orders[h][:stage]]
        at = tuple(side_of if b == orders[h][stage] else slice(None) for b in left)
        return x_ref.at[at + (h,)] if stage == 0 else boxes[stage - 1].at[(h,) + at]

    def send(stage, h):
        which = orders[h][stage]
        return pltpu.make_async_remote_copy(
            src_ref=held(stage, h, 1 - side(which)),
            dst_ref=boxes[stage].at[h],
            send_sem=send_sem.at[stage, h],
            recv_sem=recv_sem.at[stage, h],
            device_id=partner(which),
            device_id_type=MESH,
        )

    sent = []
    for stage in range(stages + 1):
        for h in range(2):
            if stage > 0:
                sent[2 * (stage - 1) + h].wait_recv()
                total = held(stage - 1, h, side(orders[h][stage - 1]))[...] + boxes[stage - 1][h]
                if stage == stages:
                    o_ref[h] = total
                else:
                    boxes[stage - 1][h] = total
            if stage < stages:
                sent.append(send(stage, h))
                sent[-1].start()
    for copy in sent:
        copy.wait_send()


def scatter_columns(values, rows, cols, collective_id):
    count, width = values.shape[0] // cols, values.shape[1]
    stages = (cols - 1).bit_length()
    dma = pltpu.SemaphoreType.DMA
    out = pl.pallas_call(
        functools.partial(scatter_columns_kernel, rows, cols),
        in_specs=[pl.BlockSpec(memory_space=pltpu.VMEM)],
        out_specs=pl.BlockSpec(memory_space=pltpu.VMEM),
        out_shape=jax.ShapeDtypeStruct((2, count // 2, width), F32),
        scratch_shapes=[
            pltpu.VMEM((2,) + (2,) * (stages - s - 1) + (count // 2, width), F32)
            for s in range(stages)
        ]
        + [dma((stages, 2)), dma((stages, 2))],
        compiler_params=params(collective_id=collective_id, has_side_effects=True),
        cost_estimate=cost(values.size, values.size * 8),
    )(values.reshape((2,) * stages + (2, count // 2, width)))
    return out.reshape(count, width)


def piece_order(rows):
    order = [0] + [k for pair in range(1, rows // 2 + 1) for k in (pair, rows - pair)][: rows - 1]
    return order[: rows // 2], order[rows // 2 :]


def exchange_rows(values, rows):
    row = lax.axis_index("row")
    width = values.shape[1] // rows
    arrived = []
    for group in piece_order(rows):
        parts = []
        for k in group:
            part = lax.dynamic_slice_in_dim(values, (row + k) % rows * width, width, 1)
            if k > 0:
                part = lax.ppermute(part, "row", [(r, (r + k) % rows) for r in range(rows)])
            parts.append(part)
        arrived.append(jnp.concatenate(parts, axis=0))
    return arrived


def adam_step(weights, grads, first, second, steps_done, decay, rate):
    first_new = adam_first * first + (1.0 - adam_first) * grads
    second_new = adam_second * second + (1.0 - adam_second) * grads * grads
    direction = (
        first_new
        / (1.0 - adam_first**steps_done)
        / (jnp.sqrt(second_new / (1.0 - adam_second**steps_done)) + adam_eps)
    )
    return (weights - rate * (direction + decay * weights), first_new, second_new)


def body(
    rows,
    cols,
    token_ids,
    segment_ids,
    loss_positions,
    loss_targets,
    loss_valid,
    block_owner,
    step_count,
    block_weights,
    block_first,
    block_second,
    left_basis,
    right_basis,
    table,
    table_first,
    table_second,
    vector_params,
    vector_first,
    vector_second,
):
    col_index = lax.axis_index("col")
    tokens = token_ids[0]
    segment = segment_ids[0]
    length = tokens.shape[0]
    in_cols = 2 * SSM_INNER + 2 * STATE
    in_blocks = (in_cols + (HEADS + 2 * KV_HEADS) * HEAD_DIM) // BLOCK_COLS
    branch_blocks = (SSM_INNER + HEADS * HEAD_DIM) // BLOCK_COLS
    gate_blocks = 2 * FF // BLOCK_COLS
    down_blocks = FF // BLOCK_COLS
    branch_at = in_blocks
    gate_at = branch_at + branch_blocks
    down_at = gate_at + gate_blocks
    nblocks = block_owner.shape[0]
    depth = block_weights.shape[1]
    shard_rows = table.shape[0]

    row_index = lax.axis_index("row")
    devices = rows * cols
    count_rows = loss_positions.shape[1]
    table_low = table.astype(BF16)
    shard_padded = -(-shard_rows // PAD_ROWS) * PAD_ROWS
    padded = jnp.pad(table_low, ((0, shard_padded - shard_rows), (0, 0)))
    in_order = jnp.sort(tokens)
    repeats = jnp.pad(in_order[1:] == in_order[:-1], (1, 0))
    different = jnp.sort(jnp.where(repeats, NO_TOKEN, in_order))
    token_place = jnp.sum((different[:, None] < tokens[None, :]).astype(jnp.int32), axis=0)
    sent = jnp.concatenate([tokens, different, loss_targets[0], loss_valid[0]])
    ints, table_cols, weight_rows = front_exchange(
        sent, padded, block_weights.astype(BF16), rows, cols, 2
    )
    padded, weight_rows, table_cols = lax.optimization_barrier((padded, weight_rows, table_cols))
    table_rows = lax.all_gather(padded, "row", axis=1, tiled=True)
    token_list = lax.dynamic_index_in_dim(ints, col_index, 1, False)[:, :length].reshape(-1)
    owners = token_list // shard_rows
    looked_up = jnp.take(
        table_cols, token_list + owners * (shard_padded - shard_rows), axis=0, mode="clip"
    )
    looked_up, weight_rows = lax.optimization_barrier((looked_up, weight_rows))
    embedded = lax.all_to_all(looked_up, "row", split_axis=0, concat_axis=1, tiled=True)
    gathered = gather_weights(weight_rows, rows, cols, 3)
    sorted_ints = ints[:, :, length : 2 * length]
    sorted_all = [
        jnp.stack(
            [
                lax.dynamic_index_in_dim(sorted_ints, (row_index - k) % rows, 0, False)
                for k in part
            ],
            axis=1,
        ).reshape(-1)
        for part in piece_order(rows)
    ]
    sorted_all = jnp.concatenate(sorted_all)
    labels_all = lax.dynamic_index_in_dim(ints, row_index, 0, False)[:, 2 * length :]
    targets_all = labels_all[:, :count_rows].reshape(-1)
    valid_all = labels_all[:, count_rows:].reshape(-1)
    valid_count = jnp.sum(ints[:, :, 2 * length + count_rows :]).astype(F32)

    conv_weight, conv_bias, time_bias, decay_log, skip_gain, mixer_gain, norm_gains, time_proj = (
        unpack(vector_params)
    )
    gain_rows = norm_gains.reshape(3, D)
    time_low = time_proj.reshape(D, SSM_HEADS).astype(BF16)
    segc, segr = segment[:, None], segment[None, :]
    chunks = length // CHUNK
    last_docs = segment.reshape(chunks, CHUNK)[:, CHUNK - 1]
    cosine, sine = rope_tables(length)

    normed = rms_gain(embedded.astype(F32), gain_rows[0]).astype(BF16)
    both_proj = project(normed, gathered, block_owner, 0, in_blocks)
    time_raw = jnp.dot(normed, time_low, preferred_element_type=F32)

    def steps_of(time_in, bias_in, decay_in):
        step_size = jax.nn.softplus(time_in + bias_in[None, :])
        return step_size, step_size * -jnp.exp(decay_in)[None, :]

    (step_size, decays), steps_back = jax.vjp(steps_of, time_raw, time_bias, decay_log)
    earlier = jnp.tril(jnp.ones((CHUNK, CHUNK), F32))
    decays_cut = decays.reshape(chunks, CHUNK, SSM_HEADS)
    cum = jnp.einsum("ts,csh->cth", earlier, decays_cut, precision=highest).reshape(
        length, SSM_HEADS
    )
    cumt = cum.T
    near = neighbours(segment)
    conv_rows = conv_weight.reshape(CONV, XBC_WIDTH)
    gain_row = mixer_gain.reshape(1, SSM_INNER)
    times = (step_size, cum, cumt, skip_gain[None, :], segc, segr)
    scan_out, states, act_xbc, slope, mixed = ssm_forward(
        last_docs, both_proj, near, conv_rows, conv_bias[None, :], gain_row, *times
    )
    positions = loss_positions[0]
    pos_col = positions[:, None]
    hits = pos_col == jnp.arange(length, dtype=jnp.int32)[None, :]
    chosen, place = hits.astype(BF16), hits.T.astype(BF16)
    seg_col = jnp.sum(jnp.where(hits, segr, 0), axis=1, keepdims=True)
    choose = lambda values: jnp.dot(chosen, values, preferred_element_type=F32).astype(BF16)
    spread_rows = lambda values: jnp.dot(hits.T.astype(F32), values, precision=highest)
    picked_in = (positions, pos_col, seg_col, segr, cosine, sine)
    context = attention_forward(both_proj, *picked_in)
    branch_in = jnp.concatenate([choose(mixed), context], axis=1)
    hidden_one, normed_two = back_then_norm(
        branch_in, gathered, block_owner, branch_at, branch_blocks, choose(embedded), gain_rows[1]
    )
    gate_val, up_val, act_low = project_gate_up(
        normed_two, gathered, block_owner, gate_at, down_blocks
    )
    hidden_two, picked_rows = back_then_norm(
        act_low, gathered, block_owner, down_at, down_blocks, hidden_one, gain_rows[2]
    )
    rows_all = gather_columns(picked_rows, cols, 4).reshape(-1, D)

    logits = jnp.einsum("rd,vd->rv", rows_all, table_rows, preferred_element_type=F32)
    local_target = targets_all - col_index * shard_rows
    places = jnp.arange(shard_padded, dtype=jnp.int32)[None, :]
    onehot = (places == local_target[:, None]) & (places < shard_rows)
    logits = jnp.where(places < shard_rows, logits, -1e30)
    row_top = jnp.max(logits, axis=1)
    row_total = jnp.sum(jnp.exp(logits - row_top[:, None]), axis=1)
    target_logit = jnp.sum(jnp.where(onehot, logits, 0.0), axis=1)
    no_part = jnp.zeros_like(row_top)
    parts = gather_columns(
        jnp.stack([row_top, row_total, target_logit] + [no_part] * 5), cols, 5
    )
    top_all = jnp.max(parts[:, 0], axis=0)
    total_all = jnp.sum(parts[:, 1] * jnp.exp(parts[:, 0] - top_all[None, :]), axis=0)
    target_all = jnp.sum(parts[:, 2], axis=0)
    log_total = top_all + jnp.log(total_all)
    valid_wide = valid_all.astype(F32)
    own_loss = lax.dynamic_slice_in_dim(
        (log_total - target_all) * valid_wide, col_index * count_rows, count_rows
    )
    logit_grad = (
        (jnp.exp(logits - log_total[:, None]) - onehot.astype(F32))
        * (valid_wide / valid_count)[:, None]
    ).astype(BF16)
    rows_part = jnp.einsum("rv,vd->rd", logit_grad, table_rows, preferred_element_type=F32)
    table_loss_grad = jnp.einsum("rv,rd->vd", logit_grad, rows_all, preferred_element_type=F32)
    table_loss_low, rows_part = lax.optimization_barrier((table_loss_grad.astype(BF16), rows_part))
    rows_grad = scatter_columns(rows_part, rows, cols, 6)
    table_loss_mine = lax.psum_scatter(table_loss_low, "row", scatter_dimension=1, tiled=True)
    equal = pos_col == positions[None, :]
    numbers = jnp.arange(count_rows, dtype=jnp.int32)
    again = jnp.any(equal & (numbers[None, :] < numbers[:, None]), axis=1)
    adds = jnp.where(again[:, None], 0.0, equal.astype(F32))
    final_grad = jnp.dot(adds, rows_grad, precision=highest)
    _, final_norm_back = jax.vjp(rms_gain, hidden_two, gain_rows[2])
    hidden_two_grad, gain_final_grad = final_norm_back(final_grad)
    down_in = hidden_two_grad.astype(BF16)
    like = (rows, nblocks, depth, BLOCK_COLS)
    gate_up_grad = project_act_back(
        down_in, gate_val, up_val, gathered, block_owner, down_at, down_blocks
    )
    hidden_one_grad, branch_grad_low, gain_ff_grad = back_through_norm(
        gate_up_grad,
        gathered,
        block_owner,
        gate_at,
        gate_blocks,
        jnp.zeros((count_rows, D), F32),
        hidden_one,
        gain_rows[1],
        hidden_two_grad,
    )
    branch_out_grad = project(branch_grad_low, gathered, block_owner, branch_at, branch_blocks)

    in_grad_low, sums, ends, mixer_vectors = ssm_backward(
        last_docs,
        both_proj,
        near,
        conv_rows,
        gain_row,
        act_xbc,
        slope,
        *times,
        states,
        scan_out,
        spread_rows(branch_out_grad[:, :SSM_INNER]),
    )
    in_grad_low = attention_backward(
        both_proj, *picked_in, branch_out_grad, place, in_grad_low
    )
    sum_y, sum_x, sum_k = (
        sums[:, i * LANES : i * LANES + SSM_HEADS] for i in range(3)
    )
    skip_grad = jnp.sum(sum_k, axis=0)
    cum_grad = sum_y.reshape(chunks, CHUNK, SSM_HEADS)
    decays_grad = jnp.einsum("ts,cth->csh", earlier, cum_grad, precision=highest)
    decays_grad = decays_grad + jnp.sum(ends, axis=1)[:, None, :SSM_HEADS]
    time_grad, time_bias_grad, decay_log_grad = steps_back(
        (sum_x, decays_grad.reshape(length, SSM_HEADS))
    )
    time_grad_low = time_grad.astype(BF16)
    grad_time = jnp.einsum("td,th->dh", normed, time_grad_low, preferred_element_type=F32)
    time_part = jnp.einsum("th,dh->td", time_grad_low, time_low, preferred_element_type=F32)
    _, embed_grad, gain_in_grad = back_through_norm(
        in_grad_low[None],
        gathered,
        block_owner,
        0,
        in_blocks,
        time_part,
        embedded,
        gain_rows[0],
        spread_rows(hidden_one_grad),
    )
    placed = (jnp.arange(length, dtype=jnp.int32)[:, None] == token_place[None, :]).astype(BF16)
    embed_sorted = jnp.dot(placed, embed_grad, preferred_element_type=F32).astype(BF16)
    embed_sorted, table_loss_mine, down_in, normed_two, branch_grad_low, normed = (
        lax.optimization_barrier(
            (embed_sorted, table_loss_mine, down_in, normed_two, branch_grad_low, normed)
        )
    )
    early, late = exchange_rows(embed_sorted, rows)
    grad_slots = weight_grad(down_in, act_low[None], block_owner, down_at, like, None)
    grad_slots = weight_grad(normed_two, gate_up_grad, block_owner, gate_at, like, grad_slots)
    early_tokens = lax.all_gather(early, "col", axis=0, tiled=True)
    grad_slots = weight_grad(
        branch_grad_low, branch_in[None], block_owner, branch_at, like, grad_slots
    )
    grad_slots = weight_grad(normed, in_grad_low[None], block_owner, 0, like, grad_slots)
    early_tokens, late, grad_slots = lax.optimization_barrier((early_tokens, late, grad_slots))
    vector_grad = jnp.concatenate(
        [
            mixer_vectors[:CONV].reshape(-1),
            mixer_vectors[CONV],
            time_bias_grad,
            decay_log_grad,
            skip_grad,
            mixer_vectors[CONV + 1, :SSM_INNER],
            gain_in_grad[0],
            gain_ff_grad[0],
            gain_final_grad,
            grad_time.reshape(-1),
            jnp.sum(own_loss)[None],
        ]
    )
    nvec = vector_params.shape[0]
    packed_len = -(-(nvec + 1) // (8 * LANES)) * 8 * LANES
    to_sum = jnp.pad(vector_grad, (0, packed_len - nvec - 1)).reshape(-1, LANES)
    grad_whole, late_tokens, summed = tail_exchange(grad_slots, late, to_sum, rows, cols, 1)
    summed = summed.reshape(-1)
    vector_total, loss_sum = summed[:nvec], summed[nvec]
    table_input_grad = rows_by_token(
        sorted_all - col_index * shard_rows, (early_tokens, late_tokens), shard_rows, length
    )
    table_grad = table_loss_mine[:shard_rows].astype(F32) + table_input_grad
    grad_mine_wide = lax.dynamic_index_in_dim(grad_whole, row_index, 0, False).astype(F32)
    square_part = jnp.sum(grad_mine_wide * grad_mine_wide) + jnp.sum(table_grad * table_grad)
    square_total = total_over_all(jnp.full((8, LANES), square_part), rows, cols, 0)[0, 0]
    rotated = rotate_blocks(left_basis, grad_whole, right_basis)
    mean_loss = loss_sum / valid_count
    grad_norm = jnp.sqrt(square_total + jnp.sum(vector_total * vector_total))
    clip_scale = jnp.minimum(1.0, clip_limit / (grad_norm + 1e-06))
    steps_done = step_count[0].astype(F32)
    scales = jnp.stack(
        [clip_scale, 1.0 - soap_first**steps_done, 1.0 - soap_second**steps_done]
    )
    first_new, second_new, partial_update = step_blocks(
        scales, rotated, block_first, block_second, left_basis, right_basis
    )
    update = lax.psum_scatter(
        partial_update, "row", scatter_dimension=1, tiled=True
    ).astype(F32)
    new_blocks = block_weights - learn_rate * (update + weight_decay * block_weights)
    new_table, table_first_new, table_second_new = adam_step(
        table,
        table_grad * clip_scale,
        table_first,
        table_second,
        steps_done,
        weight_decay,
        learn_rate,
    )
    new_vectors, vector_first_new, vector_second_new = adam_step(
        vector_params,
        vector_total * clip_scale,
        vector_first,
        vector_second,
        steps_done,
        0.0,
        vector_rate,
    )
    return (
        mean_loss,
        grad_norm,
        new_blocks,
        first_new,
        second_new,
        new_table,
        table_first_new,
        table_second_new,
        new_vectors,
        vector_first_new,
        vector_second_new,
    )


def solution(mesh):
    rows, cols = mesh.shape["row"], mesh.shape["col"]
    placed = (
        P(("row", "col"), None),
        P(("row", "col"), None),
        P(("row", "col"), None),
        P(("row", "col"), None),
        P(("row", "col"), None),
        P(),
        P(),
        P("col", "row", None),
        P("col", "row", None),
        P("col", "row", None),
        P("col", "row", None),
        P("col", None, None),
        P("col", "row"),
        P("col", "row"),
        P("col", "row"),
        P(),
        P(),
        P(),
    )
    return jax.shard_map(
        functools.partial(body, rows, cols),
        mesh=mesh,
        in_specs=placed,
        out_specs=(
            P(),
            P(),
            P("col", "row", None),
            P("col", "row", None),
            P("col", "row", None),
            P("col", "row"),
            P("col", "row"),
            P("col", "row"),
            P(),
            P(),
            P(),
        ),
        check_vma=False,
    )
```

```python
import functools

import jax
import jax.numpy as jnp
from jax import lax
from jax.experimental import pallas as pl
from jax.experimental.pallas import tpu as pltpu
from jax.sharding import PartitionSpec as P

D = 1024
HEADS = 8
KV_HEADS = 2
HEAD_DIM = 64
SSM_HEADS = 24
SSM_HEAD_DIM = 64
STATE = 128
CONV = 4
FF = 2048
BLOCK_COLS = 256
SSM_INNER = 1536
XBC_WIDTH = 1792
CHUNK = 128
QROWS = 256
LANES = 128
NO_TOKEN = 1 << 30
TABLE_PARTS = 4
PAD_ROWS = 16 * TABLE_PARTS
GROUP = 4
ROW_PART = 64

BF16 = jnp.bfloat16
F32 = jnp.float32
MESH = pl.DeviceIdType.MESH
highest = lax.Precision.HIGHEST
rope_base = 100000000000.0
clip_limit = 1.0
learn_rate = 0.01
vector_rate = 0.08
weight_decay = 0.1
soap_first = 0.95
soap_second = 0.95
adam_first = 0.9
adam_second = 0.95
adam_eps = 1e-08
vmem_bytes = 56 * 1024 * 1024


def params(**more):
    return pltpu.CompilerParams(vmem_limit_bytes=vmem_bytes, **more)


def cost(flops, nbytes, exps=0):
    return pl.CostEstimate(flops=int(flops), bytes_accessed=int(nbytes), transcendentals=int(exps))


def rms_gain(values, gain_vec):
    inv_scale = lax.rsqrt(jnp.mean(values * values, axis=-1, keepdims=True) + 1e-05)
    return values * inv_scale * gain_vec


def unpack(flattened):
    piece_sizes = [
        CONV * XBC_WIDTH,
        XBC_WIDTH,
        SSM_HEADS,
        SSM_HEADS,
        SSM_HEADS,
        SSM_INNER,
        3 * D,
        D * SSM_HEADS,
    ]
    pieces = []
    offset = 0
    for length in piece_sizes:
        pieces.append(flattened[offset : offset + length])
        offset = offset + length
    return pieces


def dot_nt(left, right):
    return lax.dot_general(left, right, (((1,), (1,)), ((), ())), preferred_element_type=F32)


def dot_tn(left, right):
    return lax.dot_general(left, right, (((0,), (0,)), ((), ())), preferred_element_type=F32)


def dot_nn(left, right):
    return jnp.dot(left, right, preferred_element_type=F32)


def slot_spec(gathered, at, every):
    rows, _, depth, _ = gathered.shape
    return pl.BlockSpec(
        (rows, 1, depth, BLOCK_COLS), lambda k, own: (0, own[at + every * k], 0, 0)
    )


def whole(shape):
    return pl.BlockSpec(shape, lambda k, own: (0,) * len(shape))


def block_of(w_ref):
    return w_ref[...].reshape(D, BLOCK_COLS)


def slot_call(kernel, owner, steps, in_specs, out_specs, out_shape, flops, operands):
    nbytes = sum(o.size * o.dtype.itemsize for o in operands[:1])
    return pl.pallas_call(
        kernel,
        grid_spec=pltpu.PrefetchScalarGridSpec(
            num_scalar_prefetch=1, grid=(steps,), in_specs=in_specs, out_specs=out_specs
        ),
        out_shape=out_shape,
        compiler_params=params(),
        cost_estimate=cost(flops, flops // 512 + nbytes),
    )(owner, *operands)


def cols_of(k):
    return slice(k * BLOCK_COLS, (k + 1) * BLOCK_COLS)


def project_kernel(own_ref, x_ref, *rest):
    o_ref = rest[-1]
    for g, w_ref in enumerate(rest[:-1]):
        o_ref[:, cols_of(g)] = dot_nn(x_ref[...], block_of(w_ref))


def project(rows_in, gathered, owner, first, count):
    length = rows_in.shape[0]
    return slot_call(
        project_kernel,
        owner,
        count // GROUP,
        [whole((length, D))] + [slot_spec(gathered, first + g, GROUP) for g in range(GROUP)],
        pl.BlockSpec((length, GROUP * BLOCK_COLS), lambda k, own: (0, k)),
        jax.ShapeDtypeStruct((length, count * BLOCK_COLS), F32),
        2 * length * D * BLOCK_COLS * count,
        [rows_in] + [gathered] * GROUP,
    )


def sigmoid(values):
    return 1.0 / (1.0 + jnp.exp(-values))


def gate_up_kernel(own_ref, x_ref, *rest):
    w_refs, (gate_ref, up_ref, act_ref) = rest[:-3], rest[-3:]
    half = len(w_refs) // 2
    for g in range(half):
        gate = dot_nn(x_ref[...], block_of(w_refs[g]))
        up = dot_nn(x_ref[...], block_of(w_refs[half + g]))
        gate_ref[:, cols_of(g)] = gate
        up_ref[:, cols_of(g)] = up
        act_ref[:, cols_of(g)] = (gate * sigmoid(gate) * up).astype(BF16)


def project_gate_up(rows_in, gathered, owner, first, count):
    length = rows_in.shape[0]
    pairs = GROUP // 2
    wide = pl.BlockSpec((length, pairs * BLOCK_COLS), lambda k, own: (0, k))
    shapes = [jax.ShapeDtypeStruct((length, count * BLOCK_COLS), t) for t in (F32, F32, BF16)]
    return slot_call(
        gate_up_kernel,
        owner,
        count // pairs,
        [whole((length, D))]
        + [slot_spec(gathered, first + g, pairs) for g in range(pairs)]
        + [slot_spec(gathered, first + count + g, pairs) for g in range(pairs)],
        [wide] * 3,
        shapes,
        4 * length * D * BLOCK_COLS * count,
        [rows_in] + [gathered] * (2 * pairs),
    )


def act_back_kernel(own_ref, x_ref, gate_ref, up_ref, *rest):
    o_ref = rest[-1]
    for g, w_ref in enumerate(rest[:-1]):
        act_grad = dot_nn(x_ref[...], block_of(w_ref))
        gate, up = gate_ref[:, cols_of(g)], up_ref[:, cols_of(g)]
        sig = sigmoid(gate)
        silu = gate * sig
        o_ref[0, :, cols_of(g)] = (act_grad * up * (sig + silu * (1.0 - sig))).astype(BF16)
        o_ref[1, :, cols_of(g)] = (act_grad * silu).astype(BF16)


def project_act_back(rows_in, gate, up, gathered, owner, first, count):
    length = rows_in.shape[0]
    pairs = GROUP // 2
    wide = pl.BlockSpec((length, pairs * BLOCK_COLS), lambda k, own: (0, k))
    return slot_call(
        act_back_kernel,
        owner,
        count // pairs,
        [whole((length, D)), wide, wide]
        + [slot_spec(gathered, first + g, pairs) for g in range(pairs)],
        pl.BlockSpec((2, length, pairs * BLOCK_COLS), lambda k, own: (0, 0, k)),
        jax.ShapeDtypeStruct((2, length, count * BLOCK_COLS), BF16),
        2 * length * D * BLOCK_COLS * count,
        [rows_in, gate, up] + [gathered] * pairs,
    )


def add_products(c_refs, w_refs, o_ref):
    cols = [c_ref[...].reshape(-1, c_ref.shape[-1]) for c_ref in c_refs]
    cols = cols[0] if len(cols) == 1 else jnp.concatenate(cols, axis=1)
    o_ref[...] += dot_nt(cols, jnp.concatenate([block_of(w) for w in w_refs], axis=1))


def row_parts(length):
    return [slice(i, i + ROW_PART) for i in range(0, length, ROW_PART)]


def back_norm_kernel(own_ref, c_ref, *rest):
    w_refs, (base_ref, gain_ref, o_ref, n_ref) = rest[:-4], rest[-4:]

    @pl.when(pl.program_id(0) == 0)
    def _():
        o_ref[...] = base_ref[...].astype(F32)

    add_products([c_ref], w_refs, o_ref)

    @pl.when(pl.program_id(0) == pl.num_programs(0) - 1)
    def _():
        for part in row_parts(o_ref.shape[0]):
            n_ref[part, :] = rms_gain(o_ref[part, :], gain_ref[...]).astype(BF16)


def back_then_norm(cols_in, gathered, owner, first, count, base, gain):
    length = cols_in.shape[0]
    return slot_call(
        back_norm_kernel,
        owner,
        count // GROUP,
        [pl.BlockSpec((length, GROUP * BLOCK_COLS), lambda k, own: (0, k))]
        + [slot_spec(gathered, first + g, GROUP) for g in range(GROUP)]
        + [whole((length, D)), whole((1, D))],
        [whole((length, D))] * 2,
        [jax.ShapeDtypeStruct((length, D), t) for t in (F32, BF16)],
        2 * length * D * BLOCK_COLS * count,
        [cols_in] + [gathered] * GROUP + [base, gain.reshape(1, D)],
    )


def back_grad_kernel(parts, own_ref, *rest):
    c_refs, rest = rest[:parts], rest[parts:]
    w_refs, rest = rest[:-8], rest[-8:]
    start_ref, x_ref, gain_ref, more_ref, o_ref, low_ref, dgain_ref, total = rest

    @pl.when(pl.program_id(0) == 0)
    def _():
        total[...] = start_ref[...]

    add_products(c_refs, w_refs, total)

    @pl.when(pl.program_id(0) == pl.num_programs(0) - 1)
    def _():
        dgain = jnp.zeros((1, D), F32)
        for part in row_parts(total.shape[0]):
            x, grad = x_ref[part, :].astype(F32), total[part, :]
            inv = lax.rsqrt(jnp.mean(x * x, axis=-1, keepdims=True) + 1e-05)
            unit = x * inv
            dgain += jnp.sum(grad * unit, axis=0, keepdims=True)
            scaled = grad * gain_ref[...]
            back = inv * (scaled - unit * jnp.mean(scaled * unit, axis=-1, keepdims=True))
            result = more_ref[part, :] + back
            o_ref[part, :] = result
            low_ref[part, :] = result.astype(BF16)
        dgain_ref[...] = dgain


def back_through_norm(cols_in, gathered, owner, first, count, start, x, gain, more):
    parts, length, _ = cols_in.shape
    group = GROUP // parts
    every = count // parts
    return pl.pallas_call(
        functools.partial(back_grad_kernel, parts),
        grid_spec=pltpu.PrefetchScalarGridSpec(
            num_scalar_prefetch=1,
            grid=(every // group,),
            in_specs=[
                pl.BlockSpec(
                    (1, length, group * BLOCK_COLS), lambda k, own, part=part: (part, 0, k)
                )
                for part in range(parts)
            ]
            + [
                slot_spec(gathered, first + part * every + g, group)
                for part in range(parts)
                for g in range(group)
            ]
            + [whole((length, D)), whole((length, D)), whole((1, D)), whole((length, D))],
            out_specs=[whole((length, D)), whole((length, D)), whole((1, D))],
            scratch_shapes=[pltpu.VMEM((length, D), F32)],
        ),
        out_shape=[
            jax.ShapeDtypeStruct((length, D), F32),
            jax.ShapeDtypeStruct((length, D), BF16),
            jax.ShapeDtypeStruct((1, D), F32),
        ],
        compiler_params=params(),
        cost_estimate=cost(
            2 * length * D * BLOCK_COLS * count, count * BLOCK_COLS * (2 * D + 2 * length)
        ),
    )(owner, *[cols_in] * parts, *[gathered] * GROUP, start, x, gain.reshape(1, D), more)


def wgrad_kernel(own_ref, l_ref, r_ref, *rest):
    o_ref, turned = rest[-2], rest[-1]

    @pl.when(pl.program_id(0) == 0)
    def _():
        turned[...] = l_ref[...].T

    grad = dot_nn(turned[...], r_ref[0])
    o_ref[...] = grad.astype(BF16).reshape(o_ref.shape)


def weight_grad(left_rows, right_cols, owner, first, like, into):
    rows, nslots, depth, _ = like
    length = left_rows.shape[0]
    each = right_cols.shape[2] // BLOCK_COLS
    count = right_cols.shape[0] * each
    in_specs = [
        pl.BlockSpec((length, D), lambda k, own: (0, 0)),
        pl.BlockSpec((1, length, BLOCK_COLS), lambda k, own: (k // each, 0, k % each)),
    ]
    operands = [owner, left_rows, right_cols]
    aliases = {}
    if into is not None:
        in_specs.append(pl.BlockSpec(memory_space=pl.ANY))
        operands.append(into)
        aliases = {3: 0}
    return pl.pallas_call(
        wgrad_kernel,
        grid_spec=pltpu.PrefetchScalarGridSpec(
            num_scalar_prefetch=1,
            grid=(count,),
            in_specs=in_specs,
            out_specs=pl.BlockSpec(
                (rows, 1, depth, BLOCK_COLS), lambda k, own: (0, own[first + k], 0, 0)
            ),
            scratch_shapes=[pltpu.VMEM((D, length), BF16)],
        ),
        out_shape=jax.ShapeDtypeStruct(like, BF16),
        input_output_aliases=aliases,
        compiler_params=params(),
        cost_estimate=cost(
            2 * length * D * BLOCK_COLS * count, count * BLOCK_COLS * (2 * D + 2 * length)
        ),
    )(*operands)


def embed_kernel(x_ref, gain_ref, e_ref, n_ref):
    rows = jnp.concatenate([x_ref[r] for r in range(x_ref.shape[0])], axis=1)
    e_ref[...] = rows
    n_ref[...] = rms_gain(rows.astype(F32), gain_ref[...]).astype(BF16)


def embed_and_norm(column_parts, gain):
    parts, length, width = column_parts.shape
    step = 2 * CHUNK
    return pl.pallas_call(
        embed_kernel,
        grid=(length // step,),
        in_specs=[
            pl.BlockSpec((parts, step, width), lambda i: (0, i, 0)),
            pl.BlockSpec((1, D), lambda i: (0, 0)),
        ],
        out_specs=[pl.BlockSpec((step, D), lambda i: (i, 0))] * 2,
        out_shape=[jax.ShapeDtypeStruct((length, D), BF16)] * 2,
        compiler_params=params(),
        cost_estimate=cost(8 * length * D, 6 * length * D),
    )(column_parts, gain.reshape(1, D))


def rope_tables(length):
    half_dim = HEAD_DIM // 2
    frequency = rope_base ** (-jnp.arange(half_dim, dtype=F32) * 2.0 / HEAD_DIM)
    angles = jnp.arange(length, dtype=F32)[:, None] * frequency[None, :]
    cosine, sine = jnp.cos(angles), jnp.sin(angles)
    wide_cos = jnp.concatenate([cosine] * 4, axis=1)
    wide_sin = jnp.concatenate([-sine, sine, -sine, sine], axis=1)
    return wide_cos, wide_sin


def lane_iota():
    return lax.broadcasted_iota(jnp.int32, (1, LANES), 1)


def swap_halves(values):
    low_half = (lane_iota() % HEAD_DIM) < HEAD_DIM // 2
    return jnp.where(
        low_half,
        pltpu.roll(values, LANES - HEAD_DIM // 2, 1),
        pltpu.roll(values, HEAD_DIM // 2, 1),
    )


def turn(values, cosine, sine):
    return values * cosine + swap_halves(values) * sine


def turn_back(values, cosine, sine):
    return values * cosine - swap_halves(values) * sine


def doubled(values, group):
    moved = pltpu.roll(values, HEAD_DIM, 1)
    keep = (lane_iota() < HEAD_DIM) == (group == 0)
    return jnp.where(keep, values, moved)


def attention_probs(query, key, allowed):
    scores = jnp.where(allowed, dot_nt(query, key), -1e30)
    row_top = jnp.max(scores, axis=-1, keepdims=True)
    weights = jnp.exp(scores - row_top)
    return weights, jnp.sum(weights, axis=-1, keepdims=True)


def halves(values):
    high = values.astype(BF16).astype(F32)
    return high, values - high


def fold(values):
    return values + pltpu.roll(values, HEAD_DIM, 1)


def head_operands(values):
    low = lane_iota() < HEAD_DIM
    high, rest = halves(values)
    high_moved, rest_moved = pltpu.roll(high, HEAD_DIM, 1), pltpu.roll(rest, HEAD_DIM, 1)
    head_a = [jnp.where(low, high, rest_moved), jnp.where(low, high, 0.0)]
    head_b = [jnp.where(low, high_moved, rest), jnp.where(low, high_moved, 0.0)]
    return [jnp.concatenate(h, axis=1).astype(BF16) for h in (head_a, head_b)]


def group_operands(values):
    low = lane_iota() < HEAD_DIM
    high, rest = halves(values)
    inner = jnp.concatenate([high, rest], axis=1).astype(BF16)
    return inner, jnp.where(low, high, rest).astype(BF16)


def picked_queries(pos_ref, q_ref, cos_ref, sin_ref, rows):
    count = rows.shape[1]
    for i in range(count):
        at = pl.ds(pos_ref[i], 1)
        for k, ref in enumerate((q_ref, cos_ref, sin_ref)):
            rows[k, i : i + 1, :] = ref[at, :]
    cosine, sine = rows[1], rows[2]
    turned = turn(rows[0], cosine, sine) * HEAD_DIM ** (-0.5)
    return jnp.concatenate(head_operands(turned), axis=0), cosine, sine


def picked_mask(pos_col_ref, seg_col_ref, segr_ref):
    positions = lax.broadcasted_iota(jnp.int32, (1, segr_ref.shape[1]), 1)
    allowed = (seg_col_ref[...] == segr_ref[...]) & (pos_col_ref[...] >= positions)
    return jnp.concatenate([allowed.astype(F32)] * 2, axis=0) > 0.5


def attn_fwd_kernel(
    pos_ref, q_ref, k_ref, v_ref, pos_col_ref, seg_col_ref, segr_ref, cos_ref, sin_ref, o_ref, rows
):
    group = pl.program_id(0) // 2
    low = lane_iota() < HEAD_DIM
    count = o_ref.shape[0]
    query, _, _ = picked_queries(pos_ref, q_ref, cos_ref, sin_ref, rows)
    key, _ = group_operands(doubled(turn(k_ref[...], cos_ref[...], sin_ref[...]), group))
    _, value = group_operands(doubled(v_ref[...], group))
    allowed = picked_mask(pos_col_ref, seg_col_ref, segr_ref)
    weights, total = attention_probs(query, key, allowed)
    high, rest = split(weights)
    out = fold(dot_nn(high, value) + dot_nn(rest, value)) / total
    o_ref[...] = jnp.where(low, out[:count], out[count:]).astype(BF16)


def attn_bwd_kernel(
    pos_ref, q_ref, k_ref, v_ref, pos_col_ref, seg_col_ref, segr_ref, cos_ref, sin_ref, g_ref,
    place_ref, into_ref, o_ref, rows, dk_s, dv_s,
):
    step = pl.program_id(0)
    pairs = HEADS // 2
    low = lane_iota() < HEAD_DIM

    @pl.when(step == 0)
    def _():
        dk_s[...] = jnp.zeros_like(dk_s)
        dv_s[...] = jnp.zeros_like(dv_s)

    @pl.when(step < pairs)
    def _():
        group = step // 2
        count = g_ref.shape[0]
        query, cosine, sine = picked_queries(pos_ref, q_ref, cos_ref, sin_ref, rows)
        grad = jnp.concatenate(head_operands(g_ref[...]), axis=0)
        key, key_out = group_operands(doubled(turn(k_ref[...], cos_ref[...], sin_ref[...]), group))
        value, _ = group_operands(doubled(v_ref[...], group))
        allowed = picked_mask(pos_col_ref, seg_col_ref, segr_ref)
        weights, total = attention_probs(query, key, allowed)
        probs = weights * (1.0 / total)
        dprobs = dot_nt(grad, value)
        delta = jnp.sum(probs * dprobs, axis=-1, keepdims=True)
        dscores = jnp.concatenate(split(probs * (dprobs - delta)), axis=0)
        dq = fold(dot_nn(dscores[: 2 * count], key_out) + dot_nn(dscores[2 * count :], key_out))
        dq = jnp.where(low, dq[:count], dq[count:]) * HEAD_DIM ** (-0.5)
        dq_low = turn_back(dq, cosine, sine).astype(BF16)
        o_ref[...] = dot_nn(place_ref[...], dq_low).astype(BF16)
        inner_q, inner_g = query[:, :LANES], grad[:, :LANES]
        dv_s[group] += dot_tn(
            jnp.concatenate(split(probs), axis=0), jnp.concatenate([inner_g, inner_g], axis=0)
        )
        dk_s[group] += dot_tn(dscores, jnp.concatenate([inner_q, inner_q], axis=0))

    @pl.when(step == pairs)
    def _():
        dk = jnp.where(low, fold(dk_s[0]), fold(dk_s[1]))
        o_ref[...] = turn_back(dk, cos_ref[...], sin_ref[...]).astype(BF16)

    @pl.when(step == pairs + 1)
    def _():
        o_ref[...] = jnp.where(low, fold(dv_s[0]), fold(dv_s[1])).astype(BF16)


def attention_specs(length, count, base):
    fixed = lambda *shape: pl.BlockSpec(shape, lambda p, pos: (0, 0))
    return [
        pl.BlockSpec((length, LANES), lambda p, pos: (0, base + jnp.minimum(p, 3))),
        pl.BlockSpec((length, LANES), lambda p, pos: (0, base + 4)),
        pl.BlockSpec((length, LANES), lambda p, pos: (0, base + 5)),
        fixed(count, 1),
        fixed(count, 1),
        fixed(1, length),
        fixed(length, LANES),
        fixed(length, LANES),
    ]


def attention_forward(both_proj, positions, pos_col, seg_col, segr, cosine, sine):
    length, count = both_proj.shape[0], positions.shape[0]
    base = (SSM_INNER + XBC_WIDTH) // LANES
    return pl.pallas_call(
        attn_fwd_kernel,
        grid_spec=pltpu.PrefetchScalarGridSpec(
            num_scalar_prefetch=1,
            grid=(HEADS // 2,),
            in_specs=attention_specs(length, count, base),
            out_specs=pl.BlockSpec((count, LANES), lambda p, pos: (0, p)),
            scratch_shapes=[pltpu.VMEM((3, count, LANES), F32)],
        ),
        out_shape=jax.ShapeDtypeStruct((count, HEADS * HEAD_DIM), BF16),
        compiler_params=params(),
        cost_estimate=cost(
            4 * HEADS * count * length * HEAD_DIM, 6 * length * D, HEADS * length * count
        ),
    )(positions, both_proj, both_proj, both_proj, pos_col, seg_col, segr, cosine, sine)


def attention_backward(
    both_proj, positions, pos_col, seg_col, segr, cosine, sine, grads, place, into
):
    length, count = both_proj.shape[0], positions.shape[0]
    base = (SSM_INNER + XBC_WIDTH) // LANES
    at = SSM_INNER // LANES
    pairs = HEADS // 2
    return pl.pallas_call(
        attn_bwd_kernel,
        grid_spec=pltpu.PrefetchScalarGridSpec(
            num_scalar_prefetch=1,
            grid=(pairs + 2,),
            in_specs=attention_specs(length, count, base)
            + [
                pl.BlockSpec((count, LANES), lambda p, pos: (0, at + jnp.minimum(p, 3))),
                pl.BlockSpec((length, count), lambda p, pos: (0, 0)),
                pl.BlockSpec(memory_space=pl.ANY),
            ],
            out_specs=pl.BlockSpec((length, LANES), lambda p, pos: (0, base + p)),
            scratch_shapes=[pltpu.VMEM((3, count, LANES), F32)]
            + [pltpu.VMEM((2, length, LANES), F32)] * 2,
        ),
        out_shape=jax.ShapeDtypeStruct(into.shape, BF16),
        input_output_aliases={11: 0},
        compiler_params=params(),
        cost_estimate=cost(
            10 * HEADS * count * length * HEAD_DIM, 10 * length * D, HEADS * length * count
        ),
    )(positions, both_proj, both_proj, both_proj, pos_col, seg_col, segr, cosine, sine, grads, place, into)


def chunk_masks(segc_ref, segr_ref, last_ref, chunk):
    doc_rows, doc_cols = segc_ref[...], segr_ref[...]
    row_pos = lax.broadcasted_iota(jnp.int32, (CHUNK, CHUNK), 0)
    col_pos = lax.broadcasted_iota(jnp.int32, (CHUNK, CHUNK), 1)
    same = (doc_rows == doc_cols) & (row_pos >= col_pos)
    madd = jnp.where(same, 0.0, -1e30)
    last = last_ref[chunk]
    previous = jnp.where(chunk > 0, last_ref[jnp.maximum(chunk - 1, 0)], -1)
    carried = jnp.where(doc_rows == previous, 1.0, 0.0)
    tail = jnp.where(doc_rows == last, 1.0, 0.0)
    keep = jnp.where(last == previous, 1.0, 0.0)
    return madd, carried, tail, keep


def spread(low, columns, a):
    return jnp.where(low, columns[:, a : a + 1], columns[:, a + 1 : a + 2])


def split(values):
    high = values.astype(BF16)
    return high, (values - high.astype(F32)).astype(BF16)


def wide_split(values):
    return jnp.concatenate(split(values), axis=1)


def both_sides(values):
    return values[:, :LANES] + values[:, LANES:]


def ssm_fwd_kernel(
    last_ref, proj_ref, near_ref, cw_ref, cb_ref, gain_ref, dt_ref, cum_ref, cumt_ref, skip_ref,
    segc_ref, segr_ref, y_ref, s_ref, xbc_ref, slope_ref, mix_ref, state, ext,
):
    chunk = pl.program_id(0)

    @pl.when(chunk == 0)
    def _():
        state[...] = jnp.zeros_like(state)
        ext[:8, :] = jnp.zeros((8, XBC_WIDTH), F32)

    ext[8:, :] = proj_ref[:, SSM_INNER : SSM_INNER + XBC_WIDTH]
    for k in range(XBC_WIDTH // BLOCK_COLS):
        cols = cols_of(k)
        total = ext[8:, cols] * cw_ref[CONV - 1 :, cols] + cb_ref[:, cols]
        for d in range(1, CONV):
            taken = ext[8 - d : 8 - d + CHUNK, cols] * near_ref[:, d : d + 1]
            total += taken * cw_ref[CONV - 1 - d : CONV - d, cols]
        sig = sigmoid(total)
        silu = total * sig
        xbc_ref[:, cols] = silu
        slope_ref[:, cols] = sig + silu * (1.0 - sig)
    ext[:8, :] = ext[CHUNK:, :]
    s_ref[...] = state[...].reshape(s_ref.shape)
    low = lane_iota() < SSM_HEAD_DIM
    madd, carried, tail, keep = chunk_masks(segc_ref, segr_ref, last_ref, chunk)
    dt, cum, cumt = dt_ref[...], cum_ref[...], cumt_ref[...]
    last_cum = cum[CHUNK - 1 : CHUNK, :]
    ecum = jnp.exp(cum) * carried
    tails = jnp.exp(last_cum - cum) * tail
    keeps = jnp.exp(last_cum) * keep
    into = xbc_ref[:, SSM_INNER : SSM_INNER + STATE]
    into_t = into.T
    into_high, into_rest = split(into_t)
    out_high, out_rest = split(xbc_ref[:, SSM_INNER + STATE :])
    out_both = jnp.concatenate([out_high, out_rest], axis=1)
    into_both = jnp.concatenate([into_high, into_rest], axis=1)
    gram = dot_nn(out_both, jnp.concatenate([into_high, into_high], axis=0)) + dot_nn(
        out_high, into_rest
    )
    for p in range(SSM_HEADS // 2):
        a, cols = 2 * p, slice(p * LANES, (p + 1) * LANES)
        heads = xbc_ref[:, cols]
        scaled = heads * spread(low, dt, a)
        decay_a = jnp.exp(cum[:, a : a + 1] - cumt[a : a + 1, :] + madd)
        decay_b = jnp.exp(cum[:, a + 1 : a + 2] - cumt[a + 1 : a + 2, :] + madd)
        mixing = wide_split(jnp.concatenate([decay_a * gram, decay_b * gram], axis=1))
        stacked_wide = wide_split(
            jnp.concatenate([jnp.where(low, scaled, 0.0), jnp.where(low, 0.0, scaled)], axis=0)
        )
        old = state[:, cols]
        old_wide = wide_split(old)
        carry_in = both_sides(dot_nn(out_both, jnp.concatenate([old_wide, old_wide], axis=0)))
        y_ref[:, cols] = (
            both_sides(dot_nn(mixing, jnp.concatenate([stacked_wide, stacked_wide], axis=0)))
            + spread(low, ecum, a) * carry_in
            + spread(low, skip_ref[...], a) * heads
        )
        tail_in = wide_split(scaled * spread(low, tails, a))
        fresh = both_sides(dot_nn(into_both, jnp.concatenate([tail_in, tail_in], axis=0)))
        state[:, cols] = spread(low, keeps, a) * old + fresh
    squares = jnp.zeros((CHUNK, 1), F32)
    for k in range(SSM_INNER // BLOCK_COLS):
        gate = proj_ref[:, cols_of(k)]
        gated = y_ref[:, cols_of(k)] * (gate * sigmoid(gate))
        squares += jnp.sum(gated * gated, axis=-1, keepdims=True)
    inv = lax.rsqrt(squares / SSM_INNER + 1e-05)
    for k in range(SSM_INNER // BLOCK_COLS):
        gate = proj_ref[:, cols_of(k)]
        gated = y_ref[:, cols_of(k)] * (gate * sigmoid(gate))
        mix_ref[:, cols_of(k)] = (gated * inv * gain_ref[:, cols_of(k)]).astype(BF16)


def ssm_bwd_kernel(
    last_ref, proj_ref, near_ref, cw_ref, gain_ref, xbc_ref, slope_ref, dt_ref, cum_ref, cumt_ref,
    skip_ref, segc_ref, segr_ref, s_ref, n_ref, y_ref, out_ref, grad_ref, sums_ref, ends_ref,
    vec_ref, dstate, g_ref, dext,
):
    chunk = pl.num_programs(0) - 1 - pl.program_id(0)

    @pl.when(pl.program_id(0) == 0)
    def _():
        dstate[...] = jnp.zeros_like(dstate)
        dext[CHUNK:, :] = jnp.zeros((8, XBC_WIDTH), F32)
        vec_ref[...] = jnp.zeros_like(vec_ref)

    squares = jnp.zeros((CHUNK, 1), F32)
    along = jnp.zeros((CHUNK, 1), F32)
    for k in range(SSM_INNER // BLOCK_COLS):
        cols = cols_of(k)
        gate = proj_ref[:, cols]
        gated = y_ref[:, cols] * (gate * sigmoid(gate))
        squares += jnp.sum(gated * gated, axis=-1, keepdims=True)
        along += jnp.sum(gated * out_ref[:, cols] * gain_ref[:, cols], axis=-1, keepdims=True)
    inv = lax.rsqrt(squares / SSM_INNER + 1e-05)
    along = along * inv / SSM_INNER
    for k in range(SSM_INNER // BLOCK_COLS):
        cols = cols_of(k)
        gate = proj_ref[:, cols]
        sig = sigmoid(gate)
        silu = gate * sig
        unit = y_ref[:, cols] * silu * inv
        vec_ref[5:6, cols] += jnp.sum(out_ref[:, cols] * unit, axis=0, keepdims=True)
        gated_grad = inv * (out_ref[:, cols] * gain_ref[:, cols] - unit * along)
        g_ref[:, cols] = gated_grad * silu
        gate_grad = gated_grad * y_ref[:, cols] * (sig + silu * (1.0 - sig))
        grad_ref[:, cols] = gate_grad.astype(BF16)
    low = lane_iota() < SSM_HEAD_DIM
    madd, carried, tail, keep = chunk_masks(segc_ref, segr_ref, last_ref, chunk)
    dt, cum, cumt = dt_ref[...], cum_ref[...], cumt_ref[...]
    last_cum = cum[CHUNK - 1 : CHUNK, :]
    ecum = jnp.exp(cum) * carried
    tails = jnp.exp(last_cum - cum) * tail
    keeps = jnp.exp(last_cum) * keep
    into, into_rest = split(xbc_ref[:, SSM_INNER : SSM_INNER + STATE])
    outof, outof_rest = split(xbc_ref[:, SSM_INNER + STATE :])
    outof_t = outof.T
    into_both = jnp.concatenate([into, into_rest], axis=1)
    gram = dot_nt(
        jnp.concatenate([outof, outof_rest], axis=1), jnp.concatenate([into, into], axis=1)
    ) + dot_nt(outof, into_rest)
    dgram = jnp.zeros((CHUNK, CHUNK), F32)
    d_into = jnp.zeros((CHUNK, STATE), F32)
    d_outof = jnp.zeros((CHUNK, STATE), F32)
    sum_y = jnp.zeros((CHUNK, LANES), F32)
    sum_xk = jnp.zeros((CHUNK, LANES), F32)
    ends = jnp.zeros((8, LANES), F32)
    lane_pos = lax.broadcasted_iota(jnp.int32, (LANES, LANES), 0) // SSM_HEAD_DIM
    head_pos = lax.broadcasted_iota(jnp.int32, (LANES, LANES), 1)

    def by_head(values, pick):
        high = values.astype(BF16)
        rest = (values - high.astype(F32)).astype(BF16)
        return dot_nn(jnp.concatenate([high, rest], axis=1), pick)

    for p in range(SSM_HEADS // 2):
        a, cols = 2 * p, slice(p * LANES, (p + 1) * LANES)
        pick = jnp.where(lane_pos + a == head_pos, 1.0, 0.0).astype(BF16)
        pick_next = jnp.where(lane_pos + a + SSM_HEADS == head_pos, 1.0, 0.0).astype(BF16)
        pick_two = jnp.concatenate([pick, pick_next], axis=0)
        pick = jnp.concatenate([pick, pick], axis=0)
        heads, grad = xbc_ref[:, cols], g_ref[:, cols]
        dt_wide = spread(low, dt, a)
        skip_wide = spread(low, skip_ref[...], a)
        tail_wide = spread(low, tails, a)
        keep_wide = spread(low, keeps, a)
        scaled = heads * dt_wide
        scaled_low = scaled.astype(BF16)
        decay_a = jnp.exp(cum[:, a : a + 1] - cumt[a : a + 1, :] + madd)
        decay_b = jnp.exp(cum[:, a + 1 : a + 2] - cumt[a + 1 : a + 2, :] + madd)
        grads = wide_split(
            jnp.concatenate([jnp.where(low, grad, 0.0), jnp.where(low, 0.0, grad)], axis=0)
        )
        dmix = dot_nt(grads, jnp.concatenate([scaled_low, scaled_low], axis=1))
        dgram += decay_a * dmix[:CHUNK] + decay_b * dmix[CHUNK:]
        mixing = split(jnp.concatenate([decay_a * gram, decay_b * gram], axis=0))
        d_new = dstate[:, cols]
        d_new_wide = wide_split(d_new)
        d_new_low = d_new_wide[:, :LANES]
        d_inner = dot_tn(jnp.concatenate(mixing, axis=0), jnp.concatenate([grads, grads], axis=0))
        d_scaled = both_sides(d_inner) + tail_wide * both_sides(
            dot_nn(into_both, jnp.concatenate([d_new_wide, d_new_wide], axis=0))
        )
        old = s_ref[0, :, cols]
        d_carry = (spread(low, ecum, a) * grad).astype(BF16)
        d_outof += dot_nt(d_carry, old.astype(BF16))
        d_into += dot_nt((scaled * tail_wide).astype(BF16), d_new_low)
        ends += jnp.sum((d_new * n_ref[0, :, cols]).reshape(STATE // 8, 8, LANES), axis=0) @ pick[
            :LANES
        ].astype(F32)
        dstate[:, cols] = keep_wide * d_new + dot_nn(outof_t, d_carry)
        dext[:CHUNK, cols] = (d_scaled * dt_wide + skip_wide * grad) * slope_ref[:, cols]
        both = grad * heads
        sum_y += by_head(grad * y_ref[:, cols] - skip_wide * both - scaled * d_scaled, pick)
        pair = jnp.concatenate([heads * d_scaled, both], axis=1).astype(BF16)
        sum_xk += dot_nn(pair, pick_two)
    dgram_low = dgram.astype(BF16)
    cols = slice(SSM_INNER, SSM_INNER + STATE)
    dext[:CHUNK, cols] = (d_into + dot_tn(dgram_low, outof)) * slope_ref[:, cols]
    cols = slice(SSM_INNER + STATE, XBC_WIDTH)
    dext[:CHUNK, cols] = (d_outof + dot_nn(dgram_low, into)) * slope_ref[:, cols]
    for k in range(XBC_WIDTH // BLOCK_COLS):
        cols = cols_of(k)
        at = slice(SSM_INNER + k * BLOCK_COLS, SSM_INNER + (k + 1) * BLOCK_COLS)
        before = proj_ref[:, at]
        here = dext[:CHUNK, cols]
        total = here * cw_ref[CONV - 1 :, cols]
        vec_ref[CONV - 1 : CONV, cols] += jnp.sum(here * before, axis=0, keepdims=True)
        vec_ref[CONV : CONV + 1, cols] += jnp.sum(here, axis=0, keepdims=True)
        for d in range(1, CONV):
            later = dext[d : d + CHUNK, cols] * near_ref[:, CONV + d : CONV + d + 1]
            total += later * cw_ref[CONV - 1 - d : CONV - d, cols]
            vec_ref[CONV - 1 - d : CONV - d, cols] += jnp.sum(later * before, axis=0, keepdims=True)
        grad_ref[:, at] = total.astype(BF16)
    dext[CHUNK:, :] = dext[:8, :]
    sums_ref[:, :LANES] = sum_y
    sums_ref[:, LANES:] = sum_xk
    ends_ref[...] = ends.reshape(ends_ref.shape)


def scan_specs(at):
    here = lambda i, last: (at(i), 0)
    across = lambda i, last: (0, at(i))
    return dict(
        rows=lambda width: pl.BlockSpec((CHUNK, width), here),
        cols=lambda height: pl.BlockSpec((height, CHUNK), across),
        fixed=lambda *shape: pl.BlockSpec(shape, lambda i, last: (0,) * len(shape)),
    )


def ssm_forward(last, both_proj, near, conv_w, conv_b, gain, dt, cum, cumt, skip, segc, segr):
    length, width = both_proj.shape
    chunks = length // CHUNK
    spec = scan_specs(lambda i: i)
    return pl.pallas_call(
        ssm_fwd_kernel,
        grid_spec=pltpu.PrefetchScalarGridSpec(
            num_scalar_prefetch=1,
            grid=(chunks,),
            in_specs=[
                spec["rows"](width),
                spec["rows"](2 * CONV),
                spec["fixed"](CONV, XBC_WIDTH),
                spec["fixed"](1, XBC_WIDTH),
                spec["fixed"](1, SSM_INNER),
                spec["rows"](SSM_HEADS),
                spec["rows"](SSM_HEADS),
                spec["cols"](SSM_HEADS),
                spec["fixed"](1, SSM_HEADS),
                spec["rows"](1),
                spec["cols"](1),
            ],
            out_specs=[
                spec["rows"](SSM_INNER),
                pl.BlockSpec((1, STATE, SSM_INNER), lambda c, last: (c, 0, 0)),
                spec["rows"](XBC_WIDTH),
                spec["rows"](XBC_WIDTH),
                spec["rows"](SSM_INNER),
            ],
            scratch_shapes=[
                pltpu.VMEM((STATE, SSM_INNER), F32),
                pltpu.VMEM((CHUNK + 8, XBC_WIDTH), F32),
            ],
        ),
        out_shape=[
            jax.ShapeDtypeStruct((length, SSM_INNER), F32),
            jax.ShapeDtypeStruct((chunks, STATE, SSM_INNER), F32),
            jax.ShapeDtypeStruct((length, XBC_WIDTH), F32),
            jax.ShapeDtypeStruct((length, XBC_WIDTH), F32),
            jax.ShapeDtypeStruct((length, SSM_INNER), BF16),
        ],
        compiler_params=params(),
        cost_estimate=cost(
            8 * length * SSM_INNER * STATE, 40 * length * SSM_INNER, length * CHUNK * SSM_HEADS
        ),
    )(last, both_proj, near, conv_w, conv_b, gain, dt, cum, cumt, skip, segc, segr)


def ssm_backward(
    last, both_proj, near, conv_w, gain, xbc, slope, dt, cum, cumt, skip, segc, segr, states, outputs,
    grads,
):
    length, width = both_proj.shape
    chunks = length // CHUNK
    end = chunks - 1
    spec = scan_specs(lambda i: end - i)
    return pl.pallas_call(
        ssm_bwd_kernel,
        grid_spec=pltpu.PrefetchScalarGridSpec(
            num_scalar_prefetch=1,
            grid=(chunks,),
            in_specs=[
                spec["rows"](width),
                spec["rows"](2 * CONV),
                spec["fixed"](CONV, XBC_WIDTH),
                spec["fixed"](1, SSM_INNER),
                spec["rows"](XBC_WIDTH),
                spec["rows"](XBC_WIDTH),
                spec["rows"](SSM_HEADS),
                spec["rows"](SSM_HEADS),
                spec["cols"](SSM_HEADS),
                spec["fixed"](1, SSM_HEADS),
                spec["rows"](1),
                spec["cols"](1),
                pl.BlockSpec((1, STATE, SSM_INNER), lambda i, last: (end - i, 0, 0)),
                pl.BlockSpec(
                    (1, STATE, SSM_INNER), lambda i, last: (jnp.minimum(end - i + 1, end), 0, 0)
                ),
                spec["rows"](SSM_INNER),
                spec["rows"](grads.shape[1]),
            ],
            out_specs=[
                spec["rows"](width),
                spec["rows"](2 * LANES),
                pl.BlockSpec((1, 8, LANES), lambda i, last: (end - i, 0, 0)),
                spec["fixed"](8, XBC_WIDTH),
            ],
            scratch_shapes=[
                pltpu.VMEM((STATE, SSM_INNER), F32),
                pltpu.VMEM((CHUNK, SSM_INNER), F32),
                pltpu.VMEM((CHUNK + 8, XBC_WIDTH), F32),
            ],
        ),
        out_shape=[
            jax.ShapeDtypeStruct((length, width), BF16),
            jax.ShapeDtypeStruct((length, 2 * LANES), F32),
            jax.ShapeDtypeStruct((chunks, 8, LANES), F32),
            jax.ShapeDtypeStruct((8, XBC_WIDTH), F32),
        ],
        compiler_params=params(),
        cost_estimate=cost(
            24 * length * SSM_INNER * STATE, 60 * length * SSM_INNER, length * CHUNK * SSM_HEADS
        ),
    )(
        last, both_proj, near, conv_w, gain, xbc, slope, dt, cum, cumt, skip, segc, segr, states, states,
        outputs, grads,
    )


def neighbours(segment):
    length = segment.shape[0]
    columns = []
    for d in range(CONV):
        earlier = jnp.pad(segment, (d, 0), constant_values=-1)[:length]
        columns.append(earlier == segment)
    for d in range(CONV):
        later = jnp.pad(segment, (0, d), constant_values=-1)[d:]
        columns.append(later == segment)
    return jnp.stack(columns, axis=1).astype(F32)


def rows_kernel(counts, lo_ref, hi_ref, ids_ref, *rest):
    step = pl.program_id(0)
    g_refs, (o_ref, wide) = rest[:-2], rest[-2:]
    group = wide.shape[0]

    @pl.when(step == 0)
    def _():
        o_ref[...] = jnp.zeros_like(o_ref)

    before = 0
    for count, g_ref in zip(counts, g_refs):

        @pl.when((step >= before) & (step < before + count))
        def _(g_ref=g_ref):
            wide[...] = g_ref[...].astype(F32)

        before = before + count
    low, high = lo_ref[step], hi_ref[step]

    def one(j):
        o_ref[pl.ds(ids_ref[step * group + j], 1), :] += wide[pl.ds(j, 1), :]

    def eight(k, carry):
        for u in range(8):
            one(low + 8 * k + u)
        return carry

    def rest_of(j, carry):
        one(j)
        return carry

    eights = (high - low) // 8
    lax.fori_loop(0, eights, eight, 0)
    lax.fori_loop(low + 8 * eights, high, rest_of, 0)


def rows_by_token(local_ids, grads, shard_rows, group):
    width = grads[0].shape[1]
    counts = [g.shape[0] // group for g in grads]
    lists = local_ids.reshape(-1, group)
    low = jnp.sum((lists < 0).astype(jnp.int32), axis=1)
    high = jnp.sum((lists < shard_rows).astype(jnp.int32), axis=1)
    specs, before = [], 0
    for count in counts:
        specs.append(
            pl.BlockSpec(
                (group, width),
                lambda i, lo, hi, ids, before=before, count=count: (
                    jnp.clip(i - before, 0, count - 1),
                    0,
                ),
            )
        )
        before = before + count
    return pl.pallas_call(
        functools.partial(rows_kernel, counts),
        grid_spec=pltpu.PrefetchScalarGridSpec(
            num_scalar_prefetch=3,
            grid=(before,),
            in_specs=specs,
            out_specs=pl.BlockSpec((shard_rows, width), lambda i, lo, hi, ids: (0, 0)),
            scratch_shapes=[pltpu.VMEM((group, width), F32)],
        ),
        out_shape=jax.ShapeDtypeStruct((shard_rows, width), F32),
        compiler_params=params(),
        cost_estimate=cost(before * group * width * LANES, before * group * width * 2),
    )(low, high, local_ids, *grads)


def split_nn(left, right):
    left_high, left_rest = split(left)
    right_high, right_rest = split(right)
    return dot_nn(left_high, right_high) + dot_nn(left_rest, right_high) + dot_nn(left_high, right_rest)


def rotate_kernel(l_ref, g_ref, r_ref, o_ref):
    grad = g_ref[...].reshape(D, BLOCK_COLS)
    left_high, left_rest = split(l_ref[0])
    part = dot_nn(left_high, grad) + dot_nn(left_rest, grad)
    o_ref[0] = split_nn(part, r_ref[0])


def rotate_blocks(left_basis, grad_whole, right_basis):
    slots, depth, _ = left_basis.shape
    rows = grad_whole.shape[0]
    return pl.pallas_call(
        rotate_kernel,
        grid=(slots,),
        in_specs=[
            pl.BlockSpec((1, depth, D), lambda k: (k, 0, 0)),
            pl.BlockSpec((rows, 1, depth, BLOCK_COLS), lambda k: (0, k, 0, 0)),
            pl.BlockSpec((1, BLOCK_COLS, BLOCK_COLS), lambda k: (k, 0, 0)),
        ],
        out_specs=pl.BlockSpec((1, depth, BLOCK_COLS), lambda k: (k, 0, 0)),
        out_shape=jax.ShapeDtypeStruct((slots, depth, BLOCK_COLS), F32),
        compiler_params=params(),
        cost_estimate=cost(6 * slots * depth * D * BLOCK_COLS, slots * depth * D * 5),
    )(left_basis, grad_whole, right_basis)


def step_kernel(scale_ref, rot_ref, m_ref, v_ref, l_ref, r_ref, mo_ref, vo_ref, u_ref):
    rotated = rot_ref[0] * scale_ref[0]
    first_new = soap_first * m_ref[0] + (1.0 - soap_first) * rotated
    second_new = soap_second * v_ref[0] + (1.0 - soap_second) * rotated * rotated
    mo_ref[0], vo_ref[0] = first_new, second_new
    direction = (first_new / scale_ref[1]) / (jnp.sqrt(second_new / scale_ref[2]) + adam_eps)
    turned = split_nn(direction, r_ref[0].T).astype(BF16)
    left_high, left_rest = split(l_ref[0])
    update = dot_nn(left_high.T, turned) + dot_nn(left_rest.T, turned)
    u_ref[0] = update.astype(BF16)


def step_blocks(scales, rotated, block_first, block_second, left_basis, right_basis):
    slots, depth, _ = left_basis.shape
    own = pl.BlockSpec((1, depth, BLOCK_COLS), lambda k: (k, 0, 0))
    small = jax.ShapeDtypeStruct((slots, depth, BLOCK_COLS), F32)
    return pl.pallas_call(
        step_kernel,
        grid=(slots,),
        in_specs=[
            pl.BlockSpec(memory_space=pltpu.SMEM),
            own,
            own,
            own,
            pl.BlockSpec((1, depth, D), lambda k: (k, 0, 0)),
            pl.BlockSpec((1, BLOCK_COLS, BLOCK_COLS), lambda k: (k, 0, 0)),
        ],
        out_specs=[own, own, pl.BlockSpec((1, D, BLOCK_COLS), lambda k: (k, 0, 0))],
        out_shape=[small, small, jax.ShapeDtypeStruct((slots, D, BLOCK_COLS), BF16)],
        compiler_params=params(),
        cost_estimate=cost(6 * slots * depth * D * BLOCK_COLS, slots * depth * D * 7),
    )(scales, rotated, block_first, block_second, left_basis, right_basis)


def to_peers(axis, extent, place, src, box, send_sem, recv_sem):
    copies = []
    for k in range(1, extent):
        peer = list(place)
        peer[axis] = lax.rem(place[axis] + k, extent)
        copies.append(
            pltpu.make_async_remote_copy(
                src_ref=src,
                dst_ref=box.at[place[axis]],
                send_sem=send_sem.at[k],
                recv_sem=recv_sem.at[k],
                device_id=tuple(peer),
                device_id_type=MESH,
            )
        )
    return copies


def greet_peers(axes, place):
    barrier = pltpu.get_barrier_semaphore()
    count = 0
    for axis, extent in axes:
        for k in range(1, extent):
            peer = list(place)
            peer[axis] = lax.rem(place[axis] + k, extent)
            pl.semaphore_signal(barrier, inc=1, device_id=tuple(peer), device_id_type=MESH)
            count += 1
    pl.semaphore_wait(barrier, count)


def total_kernel(rows, cols, x_ref, o_ref, col_box, row_box, col_send, col_recv, row_send, row_recv):
    place = (lax.axis_index("row"), lax.axis_index("col"))
    greet_peers(((0, rows), (1, cols)), place)
    total = x_ref[...]
    for axis, extent, box, send_sem, recv_sem in (
        (1, cols, col_box, col_send, col_recv),
        (0, rows, row_box, row_send, row_recv),
    ):
        o_ref[...] = total
        box[place[axis]] = total
        copies = to_peers(axis, extent, place, o_ref, box, send_sem, recv_sem)
        for copy in copies:
            copy.start()
        for copy in copies:
            copy.wait()
        total = jnp.sum(box[...], axis=0)
    o_ref[...] = total


def total_over_all(values, rows, cols, collective_id):
    dma = pltpu.SemaphoreType.DMA
    return pl.pallas_call(
        functools.partial(total_kernel, rows, cols),
        in_specs=[pl.BlockSpec(memory_space=pltpu.VMEM)],
        out_specs=pl.BlockSpec(memory_space=pltpu.VMEM),
        out_shape=jax.ShapeDtypeStruct(values.shape, F32),
        scratch_shapes=[
            pltpu.VMEM((cols,) + values.shape, F32),
            pltpu.VMEM((rows,) + values.shape, F32),
            dma((cols,)),
            dma((cols,)),
            dma((rows,)),
            dma((rows,)),
        ],
        compiler_params=params(collective_id=collective_id, has_side_effects=True),
        cost_estimate=cost(rows * cols * values.size, rows * cols * values.size * 4),
    )(values)


def ring_bits(rows, cols):
    bits = []
    for axis, extent in ((0, rows), (1, cols)):
        bit = extent // 2
        while bit >= 1:
            bits.append((axis, bit))
            bit = bit // 2
    return bits


def scatter_orders(rows, cols):
    bits = ring_bits(rows, cols)
    row_bits = [b for b in reversed(bits) if b[0] == 0]
    col_bits = [b for b in reversed(bits) if b[0] == 1]
    return col_bits + row_bits, col_bits[:1] + col_bits[1:][::-1] + row_bits


def tail_kernel(rows, cols, slots, g_ref, p_ref, v_ref, whole_ref, tok_ref, vec_ref, own, *rest):
    bits = ring_bits(rows, cols)
    stages = len(bits)
    row_bits = [b for b in bits if b[0] == 0]
    col_bits = [b for b in bits if b[0] == 1]
    boxes, rest = rest[:stages], rest[stages:]
    vec_box, vec_sum, send_sem, recv_sem, own_sem = rest[:5]
    join_send, join_recv, tok_send, tok_recv, tok_own, vec_send, vec_recv = rest[5:]
    place = (lax.axis_index("row"), lax.axis_index("col"))
    half = whole_ref.shape[-2] // 2
    orders = scatter_orders(rows, cols)

    def side(which):
        axis, bit = which
        return place[axis] // bit % 2

    def partner(which):
        axis, bit = which
        moved = place[axis] + bit - 2 * bit * side(which)
        return (moved, place[1]) if axis == 0 else (place[0], moved)

    def remote(src, dst, send, recv, which):
        return pltpu.make_async_remote_copy(
            src_ref=src,
            dst_ref=dst,
            send_sem=send,
            recv_sem=recv,
            device_id=partner(which),
            device_id_type=MESH,
        )

    barrier = pltpu.get_barrier_semaphore()
    for which in bits:
        pl.semaphore_signal(barrier, inc=1, device_id=partner(which), device_id_type=MESH)
    pl.semaphore_wait(barrier, stages)
    units = [(slot, h) for slot in range(slots) for h in range(2)]

    def pick(ref, before, which, side_of, after):
        at = before.index(which)
        return ref.at[(slice(None),) * at + (side_of,) + (slice(None),) * (len(before) - at - 1) + after]

    def part(slot, h, side_of):
        return pick(g_ref, bits, orders[h][0], side_of, (slot, slice(h * half, (h + 1) * half)))

    def cut(stage, u, side_of):
        order = orders[units[u][1]]
        left = [b for b in bits if b not in order[: stage + 1]]
        return pick(boxes[stage].at[u], left, order[stage + 1], side_of, ())

    def send(stage, u):
        slot, h = units[u]
        which = orders[h][stage]
        other = 1 - side(which)
        return remote(
            part(slot, h, other) if stage == 0 else cut(stage - 1, u, other),
            boxes[stage].at[u],
            send_sem.at[stage, u],
            recv_sem.at[stage, u],
            which,
        )

    def keep(u):
        slot, h = units[u]
        return pltpu.make_async_copy(part(slot, h, side(orders[h][0])), own.at[u], own_sem.at[u])

    def joined(ref, order, of_bits, stage, after):
        at = tuple(slice(None) if b in order[:stage] else side(b) for b in of_bits)
        return ref.at[at + after]

    def join(stage, u):
        slot, h = units[u]
        region = joined(whole_ref, row_bits, row_bits, stage, (slot, slice(h * half, (h + 1) * half)))
        return remote(region, region, join_send.at[stage, u], join_recv.at[stage, u], row_bits[stage])

    def tok(stage, h):
        order = (orders[h][1 : len(col_bits)] + orders[h][:1])
        region = joined(tok_ref, order, col_bits, stage, (h,))
        return remote(
            p_ref.at[h] if stage == 0 else region, region, tok_send.at[stage, h],
            tok_recv.at[stage, h], order[stage],
        )

    def tok_keep():
        region = joined(tok_ref, [], col_bits, 0, ())
        return pltpu.make_async_copy(p_ref, region, tok_own)

    def vec(stage):
        return remote(
            vec_sum.at[stage], vec_box.at[stage], vec_send.at[stage], vec_recv.at[stage], bits[stage]
        )

    sent = []

    def start(copy):
        copy.start()
        sent.append(copy)
        return copy

    flying = {}
    vec_sum[0] = v_ref[...]
    flying["vec", 0] = start(vec(0))
    for u in range(len(units)):
        flying[0, u] = start(send(0, u))
        keep(u).start()
        if u == 1:
            tok_keep().start()
            for h in range(2):
                flying["tok", 0, h] = start(tok(0, h))
    steps = slots + stages + len(row_bits) - 1
    tok_at = [steps - 1 - 2 * (len(col_bits) - 1 - k) for k in range(len(col_bits))]
    for t in range(steps):
        if t < stages:
            flying["vec", t].wait_recv()
            if t + 1 < stages:
                vec_sum[t + 1] = vec_sum[t] + vec_box[t]
                flying["vec", t + 1] = start(vec(t + 1))
            else:
                vec_ref[...] = vec_sum[t] + vec_box[t]
        for k, at in enumerate(tok_at):
            if at == t:
                if k == 0:
                    tok_keep().wait()
                for h in range(2):
                    flying["tok", k, h].wait_recv()
                    if k + 1 < len(col_bits):
                        flying["tok", k + 1, h] = start(tok(k + 1, h))
        for stage in reversed(range(stages + len(row_bits))):
            slot = t - stage
            if not 0 <= slot < slots:
                continue
            for h in range(2):
                u = 2 * slot + h
                if stage >= stages:
                    flying["join", stage - stages, u].wait_recv()
                    if stage - stages + 1 < len(row_bits):
                        flying["join", stage - stages + 1, u] = start(join(stage - stages + 1, u))
                    continue
                flying[stage, u].wait_recv()
                box = boxes[stage].at[u]
                if stage == 0:
                    keep(u).wait()
                    held = own.at[u]
                else:
                    held = cut(stage - 1, u, side(orders[h][stage]))
                if stage == stages - 1:
                    total = held[...].astype(F32) + box[...].astype(F32)
                    mine = joined(
                        whole_ref, [], row_bits, 0, (slot, slice(h * half, (h + 1) * half))
                    )
                    mine[...] = total.astype(BF16)
                    flying["join", 0, u] = start(join(0, u))
                    continue
                extents = box.shape[:-2]

                def add(k, carry, box=box, held=held, extents=extents):
                    at = []
                    for extent in reversed(extents):
                        at.append(k % extent)
                        k = k // extent
                    at = tuple(reversed(at))
                    box[at] = (held[at].astype(F32) + box[at].astype(F32)).astype(BF16)
                    return carry

                lax.fori_loop(0, 2 ** len(extents), add, 0)
                flying[stage + 1, u] = start(send(stage + 1, u))
    for copy in sent:
        copy.wait_send()


def tail_exchange(grads, pieces, vectors, rows, cols, collective_id):
    _, nslots, depth, _ = grads.shape
    slots = nslots // cols
    bits = ring_bits(rows, cols)
    stages = len(bits)
    row_stages, col_stages = (rows - 1).bit_length(), (cols - 1).bit_length()
    units, half = 2 * slots, depth // 2
    count, width = pieces.shape
    boxes = [
        pltpu.VMEM((units,) + (2,) * (stages - s - 1) + (half, BLOCK_COLS), BF16)
        for s in range(stages)
    ]
    vec_shape = (stages,) + vectors.shape
    whole, tokens, total = pl.pallas_call(
        functools.partial(tail_kernel, rows, cols, slots),
        in_specs=[
            pl.BlockSpec(memory_space=pl.ANY),
            pl.BlockSpec(memory_space=pl.ANY),
            pl.BlockSpec(memory_space=pltpu.VMEM),
        ],
        out_specs=[
            pl.BlockSpec(memory_space=pltpu.VMEM),
            pl.BlockSpec(memory_space=pl.ANY),
            pl.BlockSpec(memory_space=pltpu.VMEM),
        ],
        out_shape=[
            jax.ShapeDtypeStruct((2,) * row_stages + (slots, depth, BLOCK_COLS), BF16),
            jax.ShapeDtypeStruct((2,) * col_stages + (2, count // 2, width), BF16),
            jax.ShapeDtypeStruct(vectors.shape, F32),
        ],
        scratch_shapes=[pltpu.VMEM(boxes[0].shape, BF16)]
        + boxes
        + [
            pltpu.VMEM(vec_shape, F32),
            pltpu.VMEM(vec_shape, F32),
            pltpu.SemaphoreType.DMA((stages, units)),
            pltpu.SemaphoreType.DMA((stages, units)),
            pltpu.SemaphoreType.DMA((units,)),
            pltpu.SemaphoreType.DMA((row_stages, units)),
            pltpu.SemaphoreType.DMA((row_stages, units)),
            pltpu.SemaphoreType.DMA((col_stages, 2)),
            pltpu.SemaphoreType.DMA((col_stages, 2)),
            pltpu.SemaphoreType.DMA,
            pltpu.SemaphoreType.DMA((stages,)),
            pltpu.SemaphoreType.DMA((stages,)),
        ],
        compiler_params=params(collective_id=collective_id, has_side_effects=True),
        cost_estimate=cost(rows * nslots * depth * BLOCK_COLS, rows * nslots * depth * BLOCK_COLS * 6),
    )(
        grads.reshape((2,) * stages + (slots, depth, BLOCK_COLS)),
        pieces.reshape(2, count // 2, width),
        vectors,
    )
    return whole.reshape(rows, slots, depth, BLOCK_COLS), tokens.reshape(cols * count, width), total


def doubling(place, bits):
    def side(which):
        axis, bit = which
        return place[axis] // bit % 2

    def partner(which):
        axis, bit = which
        moved = place[axis] + bit - 2 * bit * side(which)
        return (moved, place[1]) if axis == 0 else (place[0], moved)

    return side, partner


def greet(bits, partner):
    barrier = pltpu.get_barrier_semaphore()
    for which in bits:
        pl.semaphore_signal(barrier, inc=1, device_id=partner(which), device_id_type=MESH)
    pl.semaphore_wait(barrier, len(bits))


def joiner(side, partner, src, out, of_bits, order, after, send_sem, recv_sem):
    def copy(k):
        at = tuple(slice(None) if b in order[:k] else side(b) for b in of_bits)
        region = out.at[at + after]
        return pltpu.make_async_remote_copy(
            src_ref=src if k == 0 else region,
            dst_ref=region,
            send_sem=send_sem.at[k],
            recv_sem=recv_sem.at[k],
            device_id=partner(order[k]),
            device_id_type=MESH,
        )

    return copy


def front_kernel(rows, cols, i_ref, t_ref, w_ref, io_ref, to_ref, wo_ref, *sems):
    bits = ring_bits(rows, cols)
    row_bits = [b for b in bits if b[0] == 0]
    col_bits = [b for b in bits if b[0] == 1]
    place = (lax.axis_index("row"), lax.axis_index("col"))
    side, partner = doubling(place, bits)
    i_send, i_recv, t_send, t_recv, w_send, w_recv, keep_sem = sems
    greet(bits, partner)
    own_row, own_col = tuple(side(b) for b in row_bits), tuple(side(b) for b in col_bits)
    keeps = [
        pltpu.make_async_copy(i_ref, io_ref.at[own_row + own_col], keep_sem.at[0]),
        pltpu.make_async_copy(t_ref, to_ref.at[own_col], keep_sem.at[1]),
        pltpu.make_async_copy(w_ref, wo_ref.at[own_row], keep_sem.at[2]),
    ]
    orders = [o[1 : len(col_bits)] + o[:1] for o in scatter_orders(rows, cols)]
    jobs = {}
    jobs["i", 0] = (joiner(side, partner, i_ref, io_ref, bits, bits[::-1], (), i_send, i_recv), 0, 1)
    for p in range(t_ref.shape[0]):
        copy = joiner(
            side, partner, t_ref.at[p], to_ref, col_bits, orders[p % 2], (p,), t_send.at[p], t_recv.at[p]
        )
        jobs["t", p] = (copy, 2 + p // 2, 2)
    for p in range(w_ref.shape[0]):
        copy = joiner(
            side, partner, w_ref.at[p], wo_ref, row_bits, row_bits, (p,), w_send.at[p], w_recv.at[p]
        )
        jobs["w", p] = (copy, 1 + p, 1)
    run_joins(jobs, {"i": len(bits), "t": len(col_bits), "w": len(row_bits)}, keeps)


def run_joins(jobs, stages, keeps, done=None):
    for copy in keeps:
        copy.start()
    sent = []
    for copy, _, _ in jobs.values():
        sent.append(copy(0))
        sent[-1].start()
    for copy in keeps:
        copy.wait()
    ends = [at + every * (stages[name[0]] - 1) for name, (_, at, every) in jobs.items()]
    for t in range(max(ends) + 1):
        for name, (copy, at, every) in jobs.items():
            k = (t - at) // every
            if t < at or (t - at) % every or k >= stages[name[0]]:
                continue
            copy(k).wait_recv()
            if k + 1 < stages[name[0]]:
                sent.append(copy(k + 1))
                sent[-1].start()
            elif done is not None:
                done(name[1])
    for copy in sent:
        copy.wait_send()


def front_exchange(ints, table_low, weights_low, rows, cols, collective_id):
    row_stages, col_stages = (rows - 1).bit_length(), (cols - 1).bit_length()
    parts = TABLE_PARTS
    shard, width = table_low.shape
    slots = weights_low.shape[0]
    dma = pltpu.SemaphoreType.DMA
    ints = ints.reshape(-1, LANES)
    outs = pl.pallas_call(
        functools.partial(front_kernel, rows, cols),
        in_specs=[pl.BlockSpec(memory_space=pl.ANY)] * 3,
        out_specs=[pl.BlockSpec(memory_space=pltpu.VMEM)] * 3,
        out_shape=[
            jax.ShapeDtypeStruct((2,) * (row_stages + col_stages) + ints.shape, jnp.int32),
            jax.ShapeDtypeStruct((2,) * col_stages + (parts, shard // parts, width), BF16),
            jax.ShapeDtypeStruct((2,) * row_stages + weights_low.shape, BF16),
        ],
        scratch_shapes=[
            dma((row_stages + col_stages,)),
            dma((row_stages + col_stages,)),
            dma((parts, col_stages)),
            dma((parts, col_stages)),
            dma((slots, row_stages)),
            dma((slots, row_stages)),
            dma((3,)),
        ],
        compiler_params=params(collective_id=collective_id, has_side_effects=True),
        cost_estimate=cost(1 << 20, cols * shard * width * 4),
    )(ints, table_low.reshape(parts, shard // parts, width), weights_low)
    return (
        outs[0].reshape(rows, cols, -1),
        outs[1].reshape(cols * shard, width),
        outs[2].reshape((rows,) + weights_low.shape),
    )


def weights_kernel(rows, cols, w_ref, o_ref, box, send_sem, recv_sem, keep_sem, out_sem):
    bits = ring_bits(rows, cols)
    col_bits = [b for b in bits if b[0] == 1]
    place = (lax.axis_index("row"), lax.axis_index("col"))
    side, partner = doubling(place, bits)
    greet(col_bits, partner)
    own = tuple(side(b) for b in col_bits)
    slots, half = w_ref.shape[1], w_ref.shape[2] // 2
    orders = [o[1 : len(col_bits)] + o[:1] for o in scatter_orders(rows, cols)]
    keeps = [
        pltpu.make_async_copy(w_ref, box.at[(slice(None),) + own], keep_sem),
    ]
    jobs = {}
    outs = []

    def done(u):
        part = (slice(None),) * (1 + len(col_bits)) + parts[u]
        outs.append(pltpu.make_async_copy(box.at[part], o_ref.at[part], out_sem.at[u]))
        outs[-1].start()

    parts = [(slot, slice(h * half, (h + 1) * half)) for slot in range(slots) for h in range(2)]
    for slot in range(slots):
        for h in range(2):
            part = (slot, slice(h * half, (h + 1) * half))
            u = 2 * slot + h

            def copy(k, part=part, order=orders[h], u=u):
                at = tuple(slice(None) if b in order[:k] else side(b) for b in col_bits)
                region = box.at[(slice(None),) + at + part]
                return pltpu.make_async_remote_copy(
                    src_ref=w_ref.at[(slice(None),) + part] if k == 0 else region,
                    dst_ref=region,
                    send_sem=send_sem.at[u, k],
                    recv_sem=recv_sem.at[u, k],
                    device_id=partner(order[k]),
                    device_id_type=MESH,
                )

            jobs["w", u] = (copy, slot, 1)
    run_joins(jobs, {"w": len(col_bits)}, keeps, done)
    for copy in outs:
        copy.wait()


def gather_weights(weights, rows, cols, collective_id):
    _, slots, depth, width = weights.shape
    col_stages = (cols - 1).bit_length()
    dma = pltpu.SemaphoreType.DMA
    shape = (rows,) + (2,) * col_stages + (slots, depth, width)
    out = pl.pallas_call(
        functools.partial(weights_kernel, rows, cols),
        in_specs=[pl.BlockSpec(memory_space=pl.ANY)],
        out_specs=pl.BlockSpec(memory_space=pl.ANY),
        out_shape=jax.ShapeDtypeStruct(shape, BF16),
        scratch_shapes=[
            pltpu.VMEM(shape, BF16),
            dma((2 * slots, col_stages)),
            dma((2 * slots, col_stages)),
            dma,
            dma((2 * slots,)),
        ],
        compiler_params=params(collective_id=collective_id, has_side_effects=True),
        cost_estimate=cost(1 << 20, 4 * cols * weights.size),
    )(weights)
    return out.reshape(rows, cols * slots, depth, width)


def columns_kernel(cols, x_ref, o_ref, send_sem, recv_sem):
    place = (lax.axis_index("row"), lax.axis_index("col"))
    greet_peers(((1, cols),), place)
    o_ref[place[1]] = x_ref[...]
    copies = to_peers(1, cols, place, x_ref, o_ref, send_sem, recv_sem)
    for copy in copies:
        copy.start()
    for copy in copies:
        copy.wait()


def gather_columns(values, cols, collective_id):
    dma = pltpu.SemaphoreType.DMA
    return pl.pallas_call(
        functools.partial(columns_kernel, cols),
        in_specs=[pl.BlockSpec(memory_space=pltpu.VMEM)],
        out_specs=pl.BlockSpec(memory_space=pltpu.VMEM),
        out_shape=jax.ShapeDtypeStruct((cols,) + values.shape, values.dtype),
        scratch_shapes=[dma((cols,)), dma((cols,))],
        compiler_params=params(collective_id=collective_id, has_side_effects=True),
        cost_estimate=cost(1024, cols * values.size * 4),
    )(values)


def rows_gather_kernel(rows, cols, x_ref, o_ref, send_sem, recv_sem):
    col_bits = [b for b in ring_bits(rows, cols) if b[0] == 1]
    place = (lax.axis_index("row"), lax.axis_index("col"))
    side, partner = doubling(place, col_bits)
    orders = [o[1 : len(col_bits)] + o[:1] for o in scatter_orders(rows, cols)]
    greet(col_bits, partner)
    own = tuple(side(b) for b in col_bits)
    jobs = {}
    for h in range(2):
        o_ref[own + (h,)] = x_ref[h]
        copy = joiner(
            side, partner, x_ref.at[h], o_ref, col_bits, orders[h], (h,), send_sem.at[h], recv_sem.at[h]
        )
        jobs["x", h] = (copy, 0, 1)
    run_joins(jobs, {"x": len(col_bits)}, [])


def gather_rows(values, rows, cols, collective_id):
    count, width = values.shape
    stages = (cols - 1).bit_length()
    dma = pltpu.SemaphoreType.DMA
    out = pl.pallas_call(
        functools.partial(rows_gather_kernel, rows, cols),
        in_specs=[pl.BlockSpec(memory_space=pltpu.VMEM)],
        out_specs=pl.BlockSpec(memory_space=pltpu.VMEM),
        out_shape=jax.ShapeDtypeStruct((2,) * stages + (2, count // 2, width), values.dtype),
        scratch_shapes=[dma((2, stages)), dma((2, stages))],
        compiler_params=params(collective_id=collective_id, has_side_effects=True),
        cost_estimate=cost(1024, cols * values.size * 4),
    )(values.reshape(2, count // 2, width))
    return out.reshape(cols * count, width)


def scatter_columns_kernel(rows, cols, x_ref, o_ref, *rest):
    bits = [b for b in ring_bits(rows, cols) if b[0] == 1]
    stages = len(bits)
    boxes, (send_sem, recv_sem) = rest[:stages], rest[stages:]
    place = (lax.axis_index("row"), lax.axis_index("col"))
    side, partner = doubling(place, bits)
    orders = [o[:stages] for o in scatter_orders(rows, cols)]
    greet(bits, partner)

    def held(stage, h, side_of):
        left = [b for b in bits if b not in orders[h][:stage]]
        at = tuple(side_of if b == orders[h][stage] else slice(None) for b in left)
        return x_ref.at[at + (h,)] if stage == 0 else boxes[stage - 1].at[(h,) + at]

    def send(stage, h):
        which = orders[h][stage]
        return pltpu.make_async_remote_copy(
            src_ref=held(stage, h, 1 - side(which)),
            dst_ref=boxes[stage].at[h],
            send_sem=send_sem.at[stage, h],
            recv_sem=recv_sem.at[stage, h],
            device_id=partner(which),
            device_id_type=MESH,
        )

    sent = []
    for stage in range(stages + 1):
        for h in range(2):
            if stage > 0:
                sent[2 * (stage - 1) + h].wait_recv()
                total = held(stage - 1, h, side(orders[h][stage - 1]))[...] + boxes[stage - 1][h]
                if stage == stages:
                    o_ref[h] = total
                else:
                    boxes[stage - 1][h] = total
            if stage < stages:
                sent.append(send(stage, h))
                sent[-1].start()
    for copy in sent:
        copy.wait_send()


def scatter_columns(values, rows, cols, collective_id):
    count, width = values.shape[0] // cols, values.shape[1]
    stages = (cols - 1).bit_length()
    dma = pltpu.SemaphoreType.DMA
    out = pl.pallas_call(
        functools.partial(scatter_columns_kernel, rows, cols),
        in_specs=[pl.BlockSpec(memory_space=pltpu.VMEM)],
        out_specs=pl.BlockSpec(memory_space=pltpu.VMEM),
        out_shape=jax.ShapeDtypeStruct((2, count // 2, width), F32),
        scratch_shapes=[
            pltpu.VMEM((2,) + (2,) * (stages - s - 1) + (count // 2, width), F32)
            for s in range(stages)
        ]
        + [dma((stages, 2)), dma((stages, 2))],
        compiler_params=params(collective_id=collective_id, has_side_effects=True),
        cost_estimate=cost(values.size, values.size * 8),
    )(values.reshape((2,) * stages + (2, count // 2, width)))
    return out.reshape(count, width)


def piece_order(rows):
    order = [0] + [k for pair in range(1, rows // 2 + 1) for k in (pair, rows - pair)][: rows - 1]
    return order[: rows // 4], order[rows // 4 :]


def exchange_rows(values, rows):
    row = lax.axis_index("row")
    width = values.shape[1] // rows
    arrived = []
    for group in piece_order(rows):
        parts = []
        for k in group:
            part = lax.dynamic_slice_in_dim(values, (row + k) % rows * width, width, 1)
            if k > 0:
                part = lax.ppermute(part, "row", [(r, (r + k) % rows) for r in range(rows)])
            parts.append(part)
        arrived.append(jnp.concatenate(parts, axis=0))
    return arrived


def adam_step(weights, grads, first, second, steps_done, decay, rate):
    first_new = adam_first * first + (1.0 - adam_first) * grads
    second_new = adam_second * second + (1.0 - adam_second) * grads * grads
    direction = (
        first_new
        / (1.0 - adam_first**steps_done)
        / (jnp.sqrt(second_new / (1.0 - adam_second**steps_done)) + adam_eps)
    )
    return (weights - rate * (direction + decay * weights), first_new, second_new)


def body(
    rows,
    cols,
    token_ids,
    segment_ids,
    loss_positions,
    loss_targets,
    loss_valid,
    block_owner,
    step_count,
    block_weights,
    block_first,
    block_second,
    left_basis,
    right_basis,
    table,
    table_first,
    table_second,
    vector_params,
    vector_first,
    vector_second,
):
    col_index = lax.axis_index("col")
    tokens = token_ids[0]
    segment = segment_ids[0]
    length = tokens.shape[0]
    in_cols = 2 * SSM_INNER + 2 * STATE
    in_blocks = (in_cols + (HEADS + 2 * KV_HEADS) * HEAD_DIM) // BLOCK_COLS
    branch_blocks = (SSM_INNER + HEADS * HEAD_DIM) // BLOCK_COLS
    gate_blocks = 2 * FF // BLOCK_COLS
    down_blocks = FF // BLOCK_COLS
    branch_at = in_blocks
    gate_at = branch_at + branch_blocks
    down_at = gate_at + gate_blocks
    nblocks = block_owner.shape[0]
    depth = block_weights.shape[1]
    shard_rows = table.shape[0]

    row_index = lax.axis_index("row")
    devices = rows * cols
    count_rows = loss_positions.shape[1]
    table_low = table.astype(BF16)
    shard_padded = -(-shard_rows // PAD_ROWS) * PAD_ROWS
    padded = jnp.pad(table_low, ((0, shard_padded - shard_rows), (0, 0)))
    in_order = jnp.sort(tokens)
    repeats = jnp.pad(in_order[1:] == in_order[:-1], (1, 0))
    different = jnp.sort(jnp.where(repeats, NO_TOKEN, in_order))
    token_place = jnp.sum((different[:, None] < tokens[None, :]).astype(jnp.int32), axis=0)
    sent = jnp.concatenate([tokens, different, loss_targets[0], loss_valid[0]])
    ints, table_cols, weight_rows = front_exchange(
        sent, padded, block_weights.astype(BF16), rows, cols, 2
    )
    padded, weight_rows, table_cols = lax.optimization_barrier((padded, weight_rows, table_cols))
    table_rows = lax.all_gather(padded, "row", axis=1, tiled=True)
    token_list = lax.dynamic_index_in_dim(ints, col_index, 1, False)[:, :length].reshape(-1)
    owners = token_list // shard_rows
    looked_up = jnp.take(
        table_cols, token_list + owners * (shard_padded - shard_rows), axis=0, mode="clip"
    )
    looked_up, weight_rows = lax.optimization_barrier((looked_up, weight_rows))
    arrived = lax.all_to_all(
        looked_up.reshape(rows, length, -1), "row", split_axis=0, concat_axis=0, tiled=True
    )
    gathered = gather_weights(weight_rows, rows, cols, 3)
    sorted_ints = ints[:, :, length : 2 * length]
    sorted_all = [
        jnp.stack(
            [
                lax.dynamic_index_in_dim(sorted_ints, (row_index - k) % rows, 0, False)
                for k in part
            ],
            axis=1,
        ).reshape(-1)
        for part in piece_order(rows)
    ]
    sorted_all = jnp.concatenate(sorted_all)
    labels_all = lax.dynamic_index_in_dim(ints, row_index, 0, False)[:, 2 * length :]
    targets_all = labels_all[:, :count_rows].reshape(-1)
    valid_all = labels_all[:, count_rows:].reshape(-1)
    valid_count = jnp.sum(ints[:, :, 2 * length + count_rows :]).astype(F32)

    conv_weight, conv_bias, time_bias, decay_log, skip_gain, mixer_gain, norm_gains, time_proj = (
        unpack(vector_params)
    )
    gain_rows = norm_gains.reshape(3, D)
    time_low = time_proj.reshape(D, SSM_HEADS).astype(BF16)
    segc, segr = segment[:, None], segment[None, :]
    chunks = length // CHUNK
    last_docs = segment.reshape(chunks, CHUNK)[:, CHUNK - 1]
    cosine, sine = rope_tables(length)

    embedded, normed = embed_and_norm(arrived, gain_rows[0])
    both_proj = project(normed, gathered, block_owner, 0, in_blocks)
    time_raw = jnp.dot(normed, time_low, preferred_element_type=F32)

    def steps_of(time_in, bias_in, decay_in):
        step_size = jax.nn.softplus(time_in + bias_in[None, :])
        return step_size, step_size * -jnp.exp(decay_in)[None, :]

    (step_size, decays), steps_back = jax.vjp(steps_of, time_raw, time_bias, decay_log)
    earlier = jnp.tril(jnp.ones((CHUNK, CHUNK), F32))
    decays_cut = decays.reshape(chunks, CHUNK, SSM_HEADS)
    cum = jnp.einsum("ts,csh->cth", earlier, decays_cut, precision=highest).reshape(
        length, SSM_HEADS
    )
    cumt = cum.T
    near = neighbours(segment)
    conv_rows = conv_weight.reshape(CONV, XBC_WIDTH)
    gain_row = mixer_gain.reshape(1, SSM_INNER)
    times = (step_size, cum, cumt, skip_gain[None, :], segc, segr)
    scan_out, states, act_xbc, slope, mixed = ssm_forward(
        last_docs, both_proj, near, conv_rows, conv_bias[None, :], gain_row, *times
    )
    positions = loss_positions[0]
    pos_col = positions[:, None]
    hits = pos_col == jnp.arange(length, dtype=jnp.int32)[None, :]
    chosen, place = hits.astype(BF16), hits.T.astype(BF16)
    seg_col = jnp.sum(jnp.where(hits, segr, 0), axis=1, keepdims=True)
    choose = lambda values: jnp.dot(chosen, values, preferred_element_type=F32).astype(BF16)
    spread_rows = lambda values: jnp.dot(hits.T.astype(F32), values, precision=highest)
    picked_in = (positions, pos_col, seg_col, segr, cosine, sine)
    context = attention_forward(both_proj, *picked_in)
    branch_in = jnp.concatenate([choose(mixed), context], axis=1)
    hidden_one, normed_two = back_then_norm(
        branch_in, gathered, block_owner, branch_at, branch_blocks, choose(embedded), gain_rows[1]
    )
    gate_val, up_val, act_low = project_gate_up(
        normed_two, gathered, block_owner, gate_at, down_blocks
    )
    hidden_two, picked_rows = back_then_norm(
        act_low, gathered, block_owner, down_at, down_blocks, hidden_one, gain_rows[2]
    )
    rows_all = gather_rows(picked_rows, rows, cols, 4)

    logits = jnp.einsum("rd,vd->rv", rows_all, table_rows, preferred_element_type=F32)
    local_target = targets_all - col_index * shard_rows
    places = jnp.arange(shard_padded, dtype=jnp.int32)[None, :]
    onehot = (places == local_target[:, None]) & (places < shard_rows)
    logits = jnp.where(places < shard_rows, logits, -1e30)
    row_top = jnp.max(logits, axis=1)
    row_total = jnp.sum(jnp.exp(logits - row_top[:, None]), axis=1)
    target_logit = jnp.sum(jnp.where(onehot, logits, 0.0), axis=1)
    no_part = jnp.zeros_like(row_top)
    parts = gather_columns(
        jnp.stack([row_top, row_total, target_logit] + [no_part] * 5), cols, 5
    )
    top_all = jnp.max(parts[:, 0], axis=0)
    total_all = jnp.sum(parts[:, 1] * jnp.exp(parts[:, 0] - top_all[None, :]), axis=0)
    target_all = jnp.sum(parts[:, 2], axis=0)
    log_total = top_all + jnp.log(total_all)
    valid_wide = valid_all.astype(F32)
    own_loss = lax.dynamic_slice_in_dim(
        (log_total - target_all) * valid_wide, col_index * count_rows, count_rows
    )
    logit_grad = (
        (jnp.exp(logits - log_total[:, None]) - onehot.astype(F32))
        * (valid_wide / valid_count)[:, None]
    ).astype(BF16)
    rows_part = jnp.einsum("rv,vd->rd", logit_grad, table_rows, preferred_element_type=F32)
    table_loss_grad = jnp.einsum("rv,rd->vd", logit_grad, rows_all, preferred_element_type=F32)
    table_loss_low, rows_part = lax.optimization_barrier((table_loss_grad.astype(BF16), rows_part))
    rows_grad = scatter_columns(rows_part, rows, cols, 6)
    table_loss_mine = lax.psum_scatter(table_loss_low, "row", scatter_dimension=1, tiled=True)
    equal = pos_col == positions[None, :]
    numbers = jnp.arange(count_rows, dtype=jnp.int32)
    again = jnp.any(equal & (numbers[None, :] < numbers[:, None]), axis=1)
    adds = jnp.where(again[:, None], 0.0, equal.astype(F32))
    final_grad = jnp.dot(adds, rows_grad, precision=highest)
    _, final_norm_back = jax.vjp(rms_gain, hidden_two, gain_rows[2])
    hidden_two_grad, gain_final_grad = final_norm_back(final_grad)
    down_in = hidden_two_grad.astype(BF16)
    like = (rows, nblocks, depth, BLOCK_COLS)
    gate_up_grad = project_act_back(
        down_in, gate_val, up_val, gathered, block_owner, down_at, down_blocks
    )
    hidden_one_grad, branch_grad_low, gain_ff_grad = back_through_norm(
        gate_up_grad,
        gathered,
        block_owner,
        gate_at,
        gate_blocks,
        jnp.zeros((count_rows, D), F32),
        hidden_one,
        gain_rows[1],
        hidden_two_grad,
    )
    branch_out_grad = project(branch_grad_low, gathered, block_owner, branch_at, branch_blocks)

    in_grad_low, sums, ends, mixer_vectors = ssm_backward(
        last_docs,
        both_proj,
        near,
        conv_rows,
        gain_row,
        act_xbc,
        slope,
        *times,
        states,
        scan_out,
        spread_rows(branch_out_grad[:, :SSM_INNER]),
    )
    in_grad_low = attention_backward(
        both_proj, *picked_in, branch_out_grad, place, in_grad_low
    )
    sum_y, sum_x, sum_k = (
        sums[:, at : at + SSM_HEADS] for at in (0, LANES, LANES + SSM_HEADS)
    )
    skip_grad = jnp.sum(sum_k, axis=0)
    cum_grad = sum_y.reshape(chunks, CHUNK, SSM_HEADS)
    decays_grad = jnp.einsum("ts,cth->csh", earlier, cum_grad, precision=highest)
    decays_grad = decays_grad + jnp.sum(ends, axis=1)[:, None, :SSM_HEADS]
    time_grad, time_bias_grad, decay_log_grad = steps_back(
        (sum_x, decays_grad.reshape(length, SSM_HEADS))
    )
    time_grad_low = time_grad.astype(BF16)
    grad_time = jnp.einsum("td,th->dh", normed, time_grad_low, preferred_element_type=F32)
    time_part = jnp.einsum("th,dh->td", time_grad_low, time_low, preferred_element_type=F32)
    _, embed_grad, gain_in_grad = back_through_norm(
        in_grad_low[None],
        gathered,
        block_owner,
        0,
        in_blocks,
        time_part,
        embedded,
        gain_rows[0],
        spread_rows(hidden_one_grad),
    )
    placed = (jnp.arange(length, dtype=jnp.int32)[:, None] == token_place[None, :]).astype(BF16)
    embed_sorted = jnp.dot(placed, embed_grad, preferred_element_type=F32).astype(BF16)
    embed_sorted, table_loss_mine, down_in, normed_two, branch_grad_low, normed = (
        lax.optimization_barrier(
            (embed_sorted, table_loss_mine, down_in, normed_two, branch_grad_low, normed)
        )
    )
    early, late = exchange_rows(embed_sorted, rows)
    grad_slots = weight_grad(down_in, act_low[None], block_owner, down_at, like, None)
    grad_slots = weight_grad(normed_two, gate_up_grad, block_owner, gate_at, like, grad_slots)
    early_tokens = lax.all_gather(early, "col", axis=0, tiled=True)
    grad_slots = weight_grad(
        branch_grad_low, branch_in[None], block_owner, branch_at, like, grad_slots
    )
    grad_slots = weight_grad(normed, in_grad_low[None], block_owner, 0, like, grad_slots)
    early_tokens, late, grad_slots = lax.optimization_barrier((early_tokens, late, grad_slots))
    vector_grad = jnp.concatenate(
        [
            mixer_vectors[:CONV].reshape(-1),
            mixer_vectors[CONV],
            time_bias_grad,
            decay_log_grad,
            skip_grad,
            mixer_vectors[CONV + 1, :SSM_INNER],
            gain_in_grad[0],
            gain_ff_grad[0],
            gain_final_grad,
            grad_time.reshape(-1),
            jnp.sum(own_loss)[None],
        ]
    )
    nvec = vector_params.shape[0]
    packed_len = -(-(nvec + 1) // (8 * LANES)) * 8 * LANES
    to_sum = jnp.pad(vector_grad, (0, packed_len - nvec - 1)).reshape(-1, LANES)
    grad_whole, late_tokens, summed = tail_exchange(grad_slots, late, to_sum, rows, cols, 1)
    summed = summed.reshape(-1)
    vector_total, loss_sum = summed[:nvec], summed[nvec]
    table_input_grad = rows_by_token(
        sorted_all - col_index * shard_rows, (early_tokens, late_tokens), shard_rows, length
    )
    table_grad = table_loss_mine[:shard_rows].astype(F32) + table_input_grad
    grad_mine_wide = lax.dynamic_index_in_dim(grad_whole, row_index, 0, False).astype(F32)
    square_part = jnp.sum(grad_mine_wide * grad_mine_wide) + jnp.sum(table_grad * table_grad)
    square_total = total_over_all(jnp.full((8, LANES), square_part), rows, cols, 0)[0, 0]
    rotated = rotate_blocks(left_basis, grad_whole, right_basis)
    mean_loss = loss_sum / valid_count
    grad_norm = jnp.sqrt(square_total + jnp.sum(vector_total * vector_total))
    clip_scale = jnp.minimum(1.0, clip_limit / (grad_norm + 1e-06))
    steps_done = step_count[0].astype(F32)
    scales = jnp.stack(
        [clip_scale, 1.0 - soap_first**steps_done, 1.0 - soap_second**steps_done]
    )
    first_new, second_new, partial_update = step_blocks(
        scales, rotated, block_first, block_second, left_basis, right_basis
    )
    update = lax.psum_scatter(
        partial_update, "row", scatter_dimension=1, tiled=True
    ).astype(F32)
    new_blocks = block_weights - learn_rate * (update + weight_decay * block_weights)
    new_table, table_first_new, table_second_new = adam_step(
        table,
        table_grad * clip_scale,
        table_first,
        table_second,
        steps_done,
        weight_decay,
        learn_rate,
    )
    new_vectors, vector_first_new, vector_second_new = adam_step(
        vector_params,
        vector_total * clip_scale,
        vector_first,
        vector_second,
        steps_done,
        0.0,
        vector_rate,
    )
    return (
        mean_loss,
        grad_norm,
        new_blocks,
        first_new,
        second_new,
        new_table,
        table_first_new,
        table_second_new,
        new_vectors,
        vector_first_new,
        vector_second_new,
    )


def solution(mesh):
    rows, cols = mesh.shape["row"], mesh.shape["col"]
    placed = (
        P(("row", "col"), None),
        P(("row", "col"), None),
        P(("row", "col"), None),
        P(("row", "col"), None),
        P(("row", "col"), None),
        P(),
        P(),
        P("col", "row", None),
        P("col", "row", None),
        P("col", "row", None),
        P("col", "row", None),
        P("col", None, None),
        P("col", "row"),
        P("col", "row"),
        P("col", "row"),
        P(),
        P(),
        P(),
    )
    return jax.shard_map(
        functools.partial(body, rows, cols),
        mesh=mesh,
        in_specs=placed,
        out_specs=(
            P(),
            P(),
            P("col", "row", None),
            P("col", "row", None),
            P("col", "row", None),
            P("col", "row"),
            P("col", "row"),
            P("col", "row"),
            P(),
            P(),
            P(),
        ),
        check_vma=False,
    )
```

```python
import functools

import jax
import jax.numpy as jnp
from jax import lax
from jax.experimental import pallas as pl
from jax.experimental.pallas import tpu as pltpu
from jax.sharding import PartitionSpec as P

D = 1024
HEADS = 8
KV_HEADS = 2
HEAD_DIM = 64
SSM_HEADS = 24
SSM_HEAD_DIM = 64
STATE = 128
CONV = 4
FF = 2048
BLOCK_COLS = 256
SSM_INNER = 1536
XBC_WIDTH = 1792
CHUNK = 128
QROWS = 256
LANES = 128
NO_TOKEN = 1 << 30
LISTS = 4
TABLE_PARTS = 4
PAD_ROWS = 16 * TABLE_PARTS
GROUP = 4
ROW_PART = 64

BF16 = jnp.bfloat16
F32 = jnp.float32
MESH = pl.DeviceIdType.MESH
highest = lax.Precision.HIGHEST
rope_base = 100000000000.0
clip_limit = 1.0
learn_rate = 0.01
vector_rate = 0.08
weight_decay = 0.1
soap_first = 0.95
soap_second = 0.95
adam_first = 0.9
adam_second = 0.95
adam_eps = 1e-08
vmem_bytes = 56 * 1024 * 1024


def params(**more):
    return pltpu.CompilerParams(vmem_limit_bytes=vmem_bytes, **more)


def cost(flops, nbytes, exps=0):
    return pl.CostEstimate(flops=int(flops), bytes_accessed=int(nbytes), transcendentals=int(exps))


def rms_gain(values, gain_vec):
    inv_scale = lax.rsqrt(jnp.mean(values * values, axis=-1, keepdims=True) + 1e-05)
    return values * inv_scale * gain_vec


def unpack(flattened):
    piece_sizes = [
        CONV * XBC_WIDTH,
        XBC_WIDTH,
        SSM_HEADS,
        SSM_HEADS,
        SSM_HEADS,
        SSM_INNER,
        3 * D,
        D * SSM_HEADS,
    ]
    pieces = []
    offset = 0
    for length in piece_sizes:
        pieces.append(flattened[offset : offset + length])
        offset = offset + length
    return pieces


def dot_nt(left, right):
    return lax.dot_general(left, right, (((1,), (1,)), ((), ())), preferred_element_type=F32)


def dot_tn(left, right):
    return lax.dot_general(left, right, (((0,), (0,)), ((), ())), preferred_element_type=F32)


def dot_nn(left, right):
    return jnp.dot(left, right, preferred_element_type=F32)


def slot_spec(gathered, at, every):
    rows, _, depth, _ = gathered.shape
    return pl.BlockSpec(
        (rows, 1, depth, BLOCK_COLS), lambda k, own: (0, own[at + every * k], 0, 0)
    )


def whole(shape):
    return pl.BlockSpec(shape, lambda k, own: (0,) * len(shape))


def block_of(w_ref):
    return w_ref[...].reshape(D, BLOCK_COLS)


def slot_call(kernel, owner, steps, in_specs, out_specs, out_shape, flops, operands):
    nbytes = sum(o.size * o.dtype.itemsize for o in operands[:1])
    return pl.pallas_call(
        kernel,
        grid_spec=pltpu.PrefetchScalarGridSpec(
            num_scalar_prefetch=1, grid=(steps,), in_specs=in_specs, out_specs=out_specs
        ),
        out_shape=out_shape,
        compiler_params=params(),
        cost_estimate=cost(flops, flops // 512 + nbytes),
    )(owner, *operands)


def cols_of(k):
    return slice(k * BLOCK_COLS, (k + 1) * BLOCK_COLS)


def project_kernel(own_ref, x_ref, *rest):
    o_ref = rest[-1]
    for g, w_ref in enumerate(rest[:-1]):
        o_ref[:, cols_of(g)] = dot_nn(x_ref[...], block_of(w_ref))


def project(rows_in, gathered, owner, first, count):
    length = rows_in.shape[0]
    return slot_call(
        project_kernel,
        owner,
        count // GROUP,
        [whole((length, D))] + [slot_spec(gathered, first + g, GROUP) for g in range(GROUP)],
        pl.BlockSpec((length, GROUP * BLOCK_COLS), lambda k, own: (0, k)),
        jax.ShapeDtypeStruct((length, count * BLOCK_COLS), F32),
        2 * length * D * BLOCK_COLS * count,
        [rows_in] + [gathered] * GROUP,
    )


def sigmoid(values):
    return 1.0 / (1.0 + jnp.exp(-values))


def gate_up_kernel(own_ref, x_ref, *rest):
    w_refs, (gate_ref, up_ref, act_ref) = rest[:-3], rest[-3:]
    half = len(w_refs) // 2
    for g in range(half):
        gate = dot_nn(x_ref[...], block_of(w_refs[g]))
        up = dot_nn(x_ref[...], block_of(w_refs[half + g]))
        gate_ref[:, cols_of(g)] = gate
        up_ref[:, cols_of(g)] = up
        act_ref[:, cols_of(g)] = (gate * sigmoid(gate) * up).astype(BF16)


def project_gate_up(rows_in, gathered, owner, first, count):
    length = rows_in.shape[0]
    pairs = GROUP // 2
    wide = pl.BlockSpec((length, pairs * BLOCK_COLS), lambda k, own: (0, k))
    shapes = [jax.ShapeDtypeStruct((length, count * BLOCK_COLS), t) for t in (F32, F32, BF16)]
    return slot_call(
        gate_up_kernel,
        owner,
        count // pairs,
        [whole((length, D))]
        + [slot_spec(gathered, first + g, pairs) for g in range(pairs)]
        + [slot_spec(gathered, first + count + g, pairs) for g in range(pairs)],
        [wide] * 3,
        shapes,
        4 * length * D * BLOCK_COLS * count,
        [rows_in] + [gathered] * (2 * pairs),
    )


def act_back_kernel(own_ref, x_ref, gate_ref, up_ref, *rest):
    o_ref = rest[-1]
    for g, w_ref in enumerate(rest[:-1]):
        act_grad = dot_nn(x_ref[...], block_of(w_ref))
        gate, up = gate_ref[:, cols_of(g)], up_ref[:, cols_of(g)]
        sig = sigmoid(gate)
        silu = gate * sig
        o_ref[0, :, cols_of(g)] = (act_grad * up * (sig + silu * (1.0 - sig))).astype(BF16)
        o_ref[1, :, cols_of(g)] = (act_grad * silu).astype(BF16)


def project_act_back(rows_in, gate, up, gathered, owner, first, count):
    length = rows_in.shape[0]
    pairs = GROUP // 2
    wide = pl.BlockSpec((length, pairs * BLOCK_COLS), lambda k, own: (0, k))
    return slot_call(
        act_back_kernel,
        owner,
        count // pairs,
        [whole((length, D)), wide, wide]
        + [slot_spec(gathered, first + g, pairs) for g in range(pairs)],
        pl.BlockSpec((2, length, pairs * BLOCK_COLS), lambda k, own: (0, 0, k)),
        jax.ShapeDtypeStruct((2, length, count * BLOCK_COLS), BF16),
        2 * length * D * BLOCK_COLS * count,
        [rows_in, gate, up] + [gathered] * pairs,
    )


def add_products(c_refs, w_refs, o_ref):
    cols = [c_ref[...].reshape(-1, c_ref.shape[-1]) for c_ref in c_refs]
    cols = cols[0] if len(cols) == 1 else jnp.concatenate(cols, axis=1)
    o_ref[...] += dot_nt(cols, jnp.concatenate([block_of(w) for w in w_refs], axis=1))


def row_parts(length):
    return [slice(i, i + ROW_PART) for i in range(0, length, ROW_PART)]


def back_norm_kernel(own_ref, c_ref, *rest):
    w_refs, (base_ref, gain_ref, o_ref, n_ref) = rest[:-4], rest[-4:]

    @pl.when(pl.program_id(0) == 0)
    def _():
        o_ref[...] = base_ref[...].astype(F32)

    add_products([c_ref], w_refs, o_ref)

    @pl.when(pl.program_id(0) == pl.num_programs(0) - 1)
    def _():
        for part in row_parts(o_ref.shape[0]):
            n_ref[part, :] = rms_gain(o_ref[part, :], gain_ref[...]).astype(BF16)


def back_then_norm(cols_in, gathered, owner, first, count, base, gain):
    length = cols_in.shape[0]
    return slot_call(
        back_norm_kernel,
        owner,
        count // GROUP,
        [pl.BlockSpec((length, GROUP * BLOCK_COLS), lambda k, own: (0, k))]
        + [slot_spec(gathered, first + g, GROUP) for g in range(GROUP)]
        + [whole((length, D)), whole((1, D))],
        [whole((length, D))] * 2,
        [jax.ShapeDtypeStruct((length, D), t) for t in (F32, BF16)],
        2 * length * D * BLOCK_COLS * count,
        [cols_in] + [gathered] * GROUP + [base, gain.reshape(1, D)],
    )


def back_grad_kernel(parts, own_ref, *rest):
    c_refs, rest = rest[:parts], rest[parts:]
    w_refs, rest = rest[:-8], rest[-8:]
    start_ref, x_ref, gain_ref, more_ref, o_ref, low_ref, dgain_ref, total = rest

    @pl.when(pl.program_id(0) == 0)
    def _():
        total[...] = start_ref[...]

    add_products(c_refs, w_refs, total)

    @pl.when(pl.program_id(0) == pl.num_programs(0) - 1)
    def _():
        dgain = jnp.zeros((1, D), F32)
        for part in row_parts(total.shape[0]):
            x, grad = x_ref[part, :].astype(F32), total[part, :]
            inv = lax.rsqrt(jnp.mean(x * x, axis=-1, keepdims=True) + 1e-05)
            unit = x * inv
            dgain += jnp.sum(grad * unit, axis=0, keepdims=True)
            scaled = grad * gain_ref[...]
            back = inv * (scaled - unit * jnp.mean(scaled * unit, axis=-1, keepdims=True))
            result = more_ref[part, :] + back
            o_ref[part, :] = result
            low_ref[part, :] = result.astype(BF16)
        dgain_ref[...] = dgain


def back_through_norm(cols_in, gathered, owner, first, count, start, x, gain, more):
    parts, length, _ = cols_in.shape
    group = GROUP // parts
    every = count // parts
    return pl.pallas_call(
        functools.partial(back_grad_kernel, parts),
        grid_spec=pltpu.PrefetchScalarGridSpec(
            num_scalar_prefetch=1,
            grid=(every // group,),
            in_specs=[
                pl.BlockSpec(
                    (1, length, group * BLOCK_COLS), lambda k, own, part=part: (part, 0, k)
                )
                for part in range(parts)
            ]
            + [
                slot_spec(gathered, first + part * every + g, group)
                for part in range(parts)
                for g in range(group)
            ]
            + [whole((length, D)), whole((length, D)), whole((1, D)), whole((length, D))],
            out_specs=[whole((length, D)), whole((length, D)), whole((1, D))],
            scratch_shapes=[pltpu.VMEM((length, D), F32)],
        ),
        out_shape=[
            jax.ShapeDtypeStruct((length, D), F32),
            jax.ShapeDtypeStruct((length, D), BF16),
            jax.ShapeDtypeStruct((1, D), F32),
        ],
        compiler_params=params(),
        cost_estimate=cost(
            2 * length * D * BLOCK_COLS * count, count * BLOCK_COLS * (2 * D + 2 * length)
        ),
    )(owner, *[cols_in] * parts, *[gathered] * GROUP, start, x, gain.reshape(1, D), more)


def wgrad_kernel(own_ref, l_ref, r_ref, *rest):
    o_ref, turned = rest[-2], rest[-1]

    @pl.when(pl.program_id(0) == 0)
    def _():
        turned[...] = l_ref[...].T

    grad = dot_nn(turned[...], r_ref[0])
    o_ref[...] = grad.astype(BF16).reshape(o_ref.shape)


def weight_grad(left_rows, right_cols, owner, first, like, into):
    rows, nslots, depth, _ = like
    length = left_rows.shape[0]
    each = right_cols.shape[2] // BLOCK_COLS
    count = right_cols.shape[0] * each
    in_specs = [
        pl.BlockSpec((length, D), lambda k, own: (0, 0)),
        pl.BlockSpec((1, length, BLOCK_COLS), lambda k, own: (k // each, 0, k % each)),
    ]
    operands = [owner, left_rows, right_cols]
    aliases = {}
    if into is not None:
        in_specs.append(pl.BlockSpec(memory_space=pl.ANY))
        operands.append(into)
        aliases = {3: 0}
    return pl.pallas_call(
        wgrad_kernel,
        grid_spec=pltpu.PrefetchScalarGridSpec(
            num_scalar_prefetch=1,
            grid=(count,),
            in_specs=in_specs,
            out_specs=pl.BlockSpec(
                (rows, 1, depth, BLOCK_COLS), lambda k, own: (0, own[first + k], 0, 0)
            ),
            scratch_shapes=[pltpu.VMEM((D, length), BF16)],
        ),
        out_shape=jax.ShapeDtypeStruct(like, BF16),
        input_output_aliases=aliases,
        compiler_params=params(),
        cost_estimate=cost(
            2 * length * D * BLOCK_COLS * count, count * BLOCK_COLS * (2 * D + 2 * length)
        ),
    )(*operands)


def embed_kernel(x_ref, gain_ref, e_ref, n_ref):
    rows = jnp.concatenate([x_ref[r] for r in range(x_ref.shape[0])], axis=1)
    e_ref[...] = rows
    n_ref[...] = rms_gain(rows.astype(F32), gain_ref[...]).astype(BF16)


def embed_and_norm(column_parts, gain):
    parts, length, width = column_parts.shape
    step = 2 * CHUNK
    return pl.pallas_call(
        embed_kernel,
        grid=(length // step,),
        in_specs=[
            pl.BlockSpec((parts, step, width), lambda i: (0, i, 0)),
            pl.BlockSpec((1, D), lambda i: (0, 0)),
        ],
        out_specs=[pl.BlockSpec((step, D), lambda i: (i, 0))] * 2,
        out_shape=[jax.ShapeDtypeStruct((length, D), BF16)] * 2,
        compiler_params=params(),
        cost_estimate=cost(8 * length * D, 6 * length * D),
    )(column_parts, gain.reshape(1, D))


def rope_tables(length):
    half_dim = HEAD_DIM // 2
    frequency = rope_base ** (-jnp.arange(half_dim, dtype=F32) * 2.0 / HEAD_DIM)
    angles = jnp.arange(length, dtype=F32)[:, None] * frequency[None, :]
    cosine, sine = jnp.cos(angles), jnp.sin(angles)
    wide_cos = jnp.concatenate([cosine] * 4, axis=1)
    wide_sin = jnp.concatenate([-sine, sine, -sine, sine], axis=1)
    return wide_cos, wide_sin


def lane_iota():
    return lax.broadcasted_iota(jnp.int32, (1, LANES), 1)


def swap_halves(values):
    low_half = (lane_iota() % HEAD_DIM) < HEAD_DIM // 2
    return jnp.where(
        low_half,
        pltpu.roll(values, LANES - HEAD_DIM // 2, 1),
        pltpu.roll(values, HEAD_DIM // 2, 1),
    )


def turn(values, cosine, sine):
    return values * cosine + swap_halves(values) * sine


def turn_back(values, cosine, sine):
    return values * cosine - swap_halves(values) * sine


def doubled(values, group):
    moved = pltpu.roll(values, HEAD_DIM, 1)
    keep = (lane_iota() < HEAD_DIM) == (group == 0)
    return jnp.where(keep, values, moved)


def attention_probs(query, key, allowed):
    scores = jnp.where(allowed, dot_nt(query, key), -1e30)
    row_top = jnp.max(scores, axis=-1, keepdims=True)
    weights = jnp.exp(scores - row_top)
    return weights, jnp.sum(weights, axis=-1, keepdims=True)


def halves(values):
    high = values.astype(BF16).astype(F32)
    return high, values - high


def fold(values):
    return values + pltpu.roll(values, HEAD_DIM, 1)


def head_operands(values):
    low = lane_iota() < HEAD_DIM
    high, rest = halves(values)
    high_moved, rest_moved = pltpu.roll(high, HEAD_DIM, 1), pltpu.roll(rest, HEAD_DIM, 1)
    head_a = [jnp.where(low, high, rest_moved), jnp.where(low, high, 0.0)]
    head_b = [jnp.where(low, high_moved, rest), jnp.where(low, high_moved, 0.0)]
    return [jnp.concatenate(h, axis=1).astype(BF16) for h in (head_a, head_b)]


def group_operands(values):
    low = lane_iota() < HEAD_DIM
    high, rest = halves(values)
    inner = jnp.concatenate([high, rest], axis=1).astype(BF16)
    return inner, jnp.where(low, high, rest).astype(BF16)


def picked_queries(pos_ref, q_ref, cos_ref, sin_ref, rows):
    count = rows.shape[1]
    for i in range(count):
        at = pl.ds(pos_ref[i], 1)
        for k, ref in enumerate((q_ref, cos_ref, sin_ref)):
            rows[k, i : i + 1, :] = ref[at, :]
    cosine, sine = rows[1], rows[2]
    turned = turn(rows[0], cosine, sine) * HEAD_DIM ** (-0.5)
    return jnp.concatenate(head_operands(turned), axis=0), cosine, sine


def picked_mask(pos_col_ref, seg_col_ref, segr_ref):
    positions = lax.broadcasted_iota(jnp.int32, (1, segr_ref.shape[1]), 1)
    allowed = (seg_col_ref[...] == segr_ref[...]) & (pos_col_ref[...] >= positions)
    return jnp.concatenate([allowed.astype(F32)] * 2, axis=0) > 0.5


def attn_fwd_kernel(
    pos_ref, q_ref, k_ref, v_ref, pos_col_ref, seg_col_ref, segr_ref, cos_ref, sin_ref, o_ref, rows
):
    group = pl.program_id(0) // 2
    low = lane_iota() < HEAD_DIM
    count = o_ref.shape[0]
    query, _, _ = picked_queries(pos_ref, q_ref, cos_ref, sin_ref, rows)
    key, _ = group_operands(doubled(turn(k_ref[...], cos_ref[...], sin_ref[...]), group))
    _, value = group_operands(doubled(v_ref[...], group))
    allowed = picked_mask(pos_col_ref, seg_col_ref, segr_ref)
    weights, total = attention_probs(query, key, allowed)
    high, rest = split(weights)
    out = fold(dot_nn(high, value) + dot_nn(rest, value)) / total
    o_ref[...] = jnp.where(low, out[:count], out[count:]).astype(BF16)


def attn_bwd_kernel(
    pos_ref, q_ref, k_ref, v_ref, pos_col_ref, seg_col_ref, segr_ref, cos_ref, sin_ref, g_ref,
    place_ref, into_ref, o_ref, rows, dk_s, dv_s,
):
    step = pl.program_id(0)
    pairs = HEADS // 2
    low = lane_iota() < HEAD_DIM

    @pl.when(step == 0)
    def _():
        dk_s[...] = jnp.zeros_like(dk_s)
        dv_s[...] = jnp.zeros_like(dv_s)

    @pl.when(step < pairs)
    def _():
        group = step // 2
        count = g_ref.shape[0]
        query, cosine, sine = picked_queries(pos_ref, q_ref, cos_ref, sin_ref, rows)
        grad = jnp.concatenate(head_operands(g_ref[...]), axis=0)
        key, key_out = group_operands(doubled(turn(k_ref[...], cos_ref[...], sin_ref[...]), group))
        value, _ = group_operands(doubled(v_ref[...], group))
        allowed = picked_mask(pos_col_ref, seg_col_ref, segr_ref)
        weights, total = attention_probs(query, key, allowed)
        probs = weights * (1.0 / total)
        dprobs = dot_nt(grad, value)
        delta = jnp.sum(probs * dprobs, axis=-1, keepdims=True)
        dscores = jnp.concatenate(split(probs * (dprobs - delta)), axis=0)
        dq = fold(dot_nn(dscores[: 2 * count], key_out) + dot_nn(dscores[2 * count :], key_out))
        dq = jnp.where(low, dq[:count], dq[count:]) * HEAD_DIM ** (-0.5)
        dq_low = turn_back(dq, cosine, sine).astype(BF16)
        o_ref[...] = dot_nn(place_ref[...], dq_low).astype(BF16)
        inner_q, inner_g = query[:, :LANES], grad[:, :LANES]
        dv_s[group] += dot_tn(
            jnp.concatenate(split(probs), axis=0), jnp.concatenate([inner_g, inner_g], axis=0)
        )
        dk_s[group] += dot_tn(dscores, jnp.concatenate([inner_q, inner_q], axis=0))

    @pl.when(step == pairs)
    def _():
        dk = jnp.where(low, fold(dk_s[0]), fold(dk_s[1]))
        o_ref[...] = turn_back(dk, cos_ref[...], sin_ref[...]).astype(BF16)

    @pl.when(step == pairs + 1)
    def _():
        o_ref[...] = jnp.where(low, fold(dv_s[0]), fold(dv_s[1])).astype(BF16)


def attention_specs(length, count, base):
    fixed = lambda *shape: pl.BlockSpec(shape, lambda p, pos: (0, 0))
    return [
        pl.BlockSpec((length, LANES), lambda p, pos: (0, base + jnp.minimum(p, 3))),
        pl.BlockSpec((length, LANES), lambda p, pos: (0, base + 4)),
        pl.BlockSpec((length, LANES), lambda p, pos: (0, base + 5)),
        fixed(count, 1),
        fixed(count, 1),
        fixed(1, length),
        fixed(length, LANES),
        fixed(length, LANES),
    ]


def attention_forward(both_proj, positions, pos_col, seg_col, segr, cosine, sine):
    length, count = both_proj.shape[0], positions.shape[0]
    base = (SSM_INNER + XBC_WIDTH) // LANES
    return pl.pallas_call(
        attn_fwd_kernel,
        grid_spec=pltpu.PrefetchScalarGridSpec(
            num_scalar_prefetch=1,
            grid=(HEADS // 2,),
            in_specs=attention_specs(length, count, base),
            out_specs=pl.BlockSpec((count, LANES), lambda p, pos: (0, p)),
            scratch_shapes=[pltpu.VMEM((3, count, LANES), F32)],
        ),
        out_shape=jax.ShapeDtypeStruct((count, HEADS * HEAD_DIM), BF16),
        compiler_params=params(),
        cost_estimate=cost(
            4 * HEADS * count * length * HEAD_DIM, 6 * length * D, HEADS * length * count
        ),
    )(positions, both_proj, both_proj, both_proj, pos_col, seg_col, segr, cosine, sine)


def attention_backward(
    both_proj, positions, pos_col, seg_col, segr, cosine, sine, grads, place, into
):
    length, count = both_proj.shape[0], positions.shape[0]
    base = (SSM_INNER + XBC_WIDTH) // LANES
    at = SSM_INNER // LANES
    pairs = HEADS // 2
    return pl.pallas_call(
        attn_bwd_kernel,
        grid_spec=pltpu.PrefetchScalarGridSpec(
            num_scalar_prefetch=1,
            grid=(pairs + 2,),
            in_specs=attention_specs(length, count, base)
            + [
                pl.BlockSpec((count, LANES), lambda p, pos: (0, at + jnp.minimum(p, 3))),
                pl.BlockSpec((length, count), lambda p, pos: (0, 0)),
                pl.BlockSpec(memory_space=pl.ANY),
            ],
            out_specs=pl.BlockSpec((length, LANES), lambda p, pos: (0, base + p)),
            scratch_shapes=[pltpu.VMEM((3, count, LANES), F32)]
            + [pltpu.VMEM((2, length, LANES), F32)] * 2,
        ),
        out_shape=jax.ShapeDtypeStruct(into.shape, BF16),
        input_output_aliases={11: 0},
        compiler_params=params(),
        cost_estimate=cost(
            10 * HEADS * count * length * HEAD_DIM, 10 * length * D, HEADS * length * count
        ),
    )(positions, both_proj, both_proj, both_proj, pos_col, seg_col, segr, cosine, sine, grads, place, into)


def chunk_masks(segc_ref, segr_ref, last_ref, chunk):
    doc_rows, doc_cols = segc_ref[...], segr_ref[...]
    row_pos = lax.broadcasted_iota(jnp.int32, (CHUNK, CHUNK), 0)
    col_pos = lax.broadcasted_iota(jnp.int32, (CHUNK, CHUNK), 1)
    same = (doc_rows == doc_cols) & (row_pos >= col_pos)
    madd = jnp.where(same, 0.0, -1e30)
    last = last_ref[chunk]
    previous = jnp.where(chunk > 0, last_ref[jnp.maximum(chunk - 1, 0)], -1)
    carried = jnp.where(doc_rows == previous, 1.0, 0.0)
    tail = jnp.where(doc_rows == last, 1.0, 0.0)
    keep = jnp.where(last == previous, 1.0, 0.0)
    return madd, carried, tail, keep


def spread(low, columns, a):
    return jnp.where(low, columns[:, a : a + 1], columns[:, a + 1 : a + 2])


def split(values):
    high = values.astype(BF16)
    return high, (values - high.astype(F32)).astype(BF16)


def wide_split(values):
    return jnp.concatenate(split(values), axis=1)


def both_sides(values):
    return values[:, :LANES] + values[:, LANES:]


def ssm_fwd_kernel(
    last_ref, proj_ref, near_ref, cw_ref, cb_ref, gain_ref, dt_ref, cum_ref, cumt_ref, skip_ref,
    segc_ref, segr_ref, y_ref, s_ref, xbc_ref, slope_ref, mix_ref, state, ext,
):
    chunk = pl.program_id(0)

    @pl.when(chunk == 0)
    def _():
        state[...] = jnp.zeros_like(state)
        ext[:8, :] = jnp.zeros((8, XBC_WIDTH), F32)

    ext[8:, :] = proj_ref[:, SSM_INNER : SSM_INNER + XBC_WIDTH]
    for k in range(XBC_WIDTH // BLOCK_COLS):
        cols = cols_of(k)
        total = ext[8:, cols] * cw_ref[CONV - 1 :, cols] + cb_ref[:, cols]
        for d in range(1, CONV):
            taken = ext[8 - d : 8 - d + CHUNK, cols] * near_ref[:, d : d + 1]
            total += taken * cw_ref[CONV - 1 - d : CONV - d, cols]
        sig = sigmoid(total)
        silu = total * sig
        xbc_ref[:, cols] = silu
        slope_ref[:, cols] = sig + silu * (1.0 - sig)
    ext[:8, :] = ext[CHUNK:, :]
    s_ref[...] = state[...].reshape(s_ref.shape)
    low = lane_iota() < SSM_HEAD_DIM
    madd, carried, tail, keep = chunk_masks(segc_ref, segr_ref, last_ref, chunk)
    dt, cum, cumt = dt_ref[...], cum_ref[...], cumt_ref[...]
    last_cum = cum[CHUNK - 1 : CHUNK, :]
    ecum = jnp.exp(cum) * carried
    tails = jnp.exp(last_cum - cum) * tail
    keeps = jnp.exp(last_cum) * keep
    into = xbc_ref[:, SSM_INNER : SSM_INNER + STATE]
    into_t = into.T
    into_high, into_rest = split(into_t)
    out_high, out_rest = split(xbc_ref[:, SSM_INNER + STATE :])
    out_both = jnp.concatenate([out_high, out_rest], axis=1)
    into_both = jnp.concatenate([into_high, into_rest], axis=1)
    gram = dot_nn(out_both, jnp.concatenate([into_high, into_high], axis=0)) + dot_nn(
        out_high, into_rest
    )
    for p in range(SSM_HEADS // 2):
        a, cols = 2 * p, slice(p * LANES, (p + 1) * LANES)
        heads = xbc_ref[:, cols]
        scaled = heads * spread(low, dt, a)
        decay_a = jnp.exp(cum[:, a : a + 1] - cumt[a : a + 1, :] + madd)
        decay_b = jnp.exp(cum[:, a + 1 : a + 2] - cumt[a + 1 : a + 2, :] + madd)
        mixing = wide_split(jnp.concatenate([decay_a * gram, decay_b * gram], axis=1))
        stacked_wide = wide_split(
            jnp.concatenate([jnp.where(low, scaled, 0.0), jnp.where(low, 0.0, scaled)], axis=0)
        )
        old = state[:, cols]
        old_wide = wide_split(old)
        carry_in = both_sides(dot_nn(out_both, jnp.concatenate([old_wide, old_wide], axis=0)))
        y_ref[:, cols] = (
            both_sides(dot_nn(mixing, jnp.concatenate([stacked_wide, stacked_wide], axis=0)))
            + spread(low, ecum, a) * carry_in
            + spread(low, skip_ref[...], a) * heads
        )
        tail_in = wide_split(scaled * spread(low, tails, a))
        fresh = both_sides(dot_nn(into_both, jnp.concatenate([tail_in, tail_in], axis=0)))
        state[:, cols] = spread(low, keeps, a) * old + fresh
    squares = jnp.zeros((CHUNK, 1), F32)
    for k in range(SSM_INNER // BLOCK_COLS):
        gate = proj_ref[:, cols_of(k)]
        gated = y_ref[:, cols_of(k)] * (gate * sigmoid(gate))
        squares += jnp.sum(gated * gated, axis=-1, keepdims=True)
    inv = lax.rsqrt(squares / SSM_INNER + 1e-05)
    for k in range(SSM_INNER // BLOCK_COLS):
        gate = proj_ref[:, cols_of(k)]
        gated = y_ref[:, cols_of(k)] * (gate * sigmoid(gate))
        mix_ref[:, cols_of(k)] = (gated * inv * gain_ref[:, cols_of(k)]).astype(BF16)


def ssm_bwd_kernel(
    last_ref, proj_ref, near_ref, cw_ref, gain_ref, xbc_ref, slope_ref, dt_ref, cum_ref, cumt_ref,
    skip_ref, segc_ref, segr_ref, s_ref, n_ref, y_ref, out_ref, grad_ref, sums_ref, ends_ref,
    vec_ref, dstate, g_ref, dext,
):
    chunk = pl.num_programs(0) - 1 - pl.program_id(0)

    @pl.when(pl.program_id(0) == 0)
    def _():
        dstate[...] = jnp.zeros_like(dstate)
        dext[CHUNK:, :] = jnp.zeros((8, XBC_WIDTH), F32)
        vec_ref[...] = jnp.zeros_like(vec_ref)

    squares = jnp.zeros((CHUNK, 1), F32)
    along = jnp.zeros((CHUNK, 1), F32)
    for k in range(SSM_INNER // BLOCK_COLS):
        cols = cols_of(k)
        gate = proj_ref[:, cols]
        gated = y_ref[:, cols] * (gate * sigmoid(gate))
        squares += jnp.sum(gated * gated, axis=-1, keepdims=True)
        along += jnp.sum(gated * out_ref[:, cols] * gain_ref[:, cols], axis=-1, keepdims=True)
    inv = lax.rsqrt(squares / SSM_INNER + 1e-05)
    along = along * inv / SSM_INNER
    for k in range(SSM_INNER // BLOCK_COLS):
        cols = cols_of(k)
        gate = proj_ref[:, cols]
        sig = sigmoid(gate)
        silu = gate * sig
        unit = y_ref[:, cols] * silu * inv
        vec_ref[5:6, cols] += jnp.sum(out_ref[:, cols] * unit, axis=0, keepdims=True)
        gated_grad = inv * (out_ref[:, cols] * gain_ref[:, cols] - unit * along)
        g_ref[:, cols] = gated_grad * silu
        gate_grad = gated_grad * y_ref[:, cols] * (sig + silu * (1.0 - sig))
        grad_ref[:, cols] = gate_grad.astype(BF16)
    low = lane_iota() < SSM_HEAD_DIM
    madd, carried, tail, keep = chunk_masks(segc_ref, segr_ref, last_ref, chunk)
    dt, cum, cumt = dt_ref[...], cum_ref[...], cumt_ref[...]
    last_cum = cum[CHUNK - 1 : CHUNK, :]
    ecum = jnp.exp(cum) * carried
    tails = jnp.exp(last_cum - cum) * tail
    keeps = jnp.exp(last_cum) * keep
    into, into_rest = split(xbc_ref[:, SSM_INNER : SSM_INNER + STATE])
    outof, outof_rest = split(xbc_ref[:, SSM_INNER + STATE :])
    outof_t = outof.T
    into_both = jnp.concatenate([into, into_rest], axis=1)
    gram = dot_nt(
        jnp.concatenate([outof, outof_rest], axis=1), jnp.concatenate([into, into], axis=1)
    ) + dot_nt(outof, into_rest)
    dgram = jnp.zeros((CHUNK, CHUNK), F32)
    d_into = jnp.zeros((CHUNK, STATE), F32)
    d_outof = jnp.zeros((CHUNK, STATE), F32)
    sum_y = jnp.zeros((CHUNK, LANES), F32)
    sum_xk = jnp.zeros((CHUNK, LANES), F32)
    ends = jnp.zeros((8, LANES), F32)
    lane_pos = lax.broadcasted_iota(jnp.int32, (LANES, LANES), 0) // SSM_HEAD_DIM
    head_pos = lax.broadcasted_iota(jnp.int32, (LANES, LANES), 1)

    def by_head(values, pick):
        high = values.astype(BF16)
        rest = (values - high.astype(F32)).astype(BF16)
        return dot_nn(jnp.concatenate([high, rest], axis=1), pick)

    for p in range(SSM_HEADS // 2):
        a, cols = 2 * p, slice(p * LANES, (p + 1) * LANES)
        pick = jnp.where(lane_pos + a == head_pos, 1.0, 0.0).astype(BF16)
        pick_next = jnp.where(lane_pos + a + SSM_HEADS == head_pos, 1.0, 0.0).astype(BF16)
        pick_two = jnp.concatenate([pick, pick_next], axis=0)
        pick = jnp.concatenate([pick, pick], axis=0)
        heads, grad = xbc_ref[:, cols], g_ref[:, cols]
        dt_wide = spread(low, dt, a)
        skip_wide = spread(low, skip_ref[...], a)
        tail_wide = spread(low, tails, a)
        keep_wide = spread(low, keeps, a)
        scaled = heads * dt_wide
        scaled_low = scaled.astype(BF16)
        decay_a = jnp.exp(cum[:, a : a + 1] - cumt[a : a + 1, :] + madd)
        decay_b = jnp.exp(cum[:, a + 1 : a + 2] - cumt[a + 1 : a + 2, :] + madd)
        grads = wide_split(
            jnp.concatenate([jnp.where(low, grad, 0.0), jnp.where(low, 0.0, grad)], axis=0)
        )
        dmix = dot_nt(grads, jnp.concatenate([scaled_low, scaled_low], axis=1))
        dgram += decay_a * dmix[:CHUNK] + decay_b * dmix[CHUNK:]
        mixing = split(jnp.concatenate([decay_a * gram, decay_b * gram], axis=0))
        d_new = dstate[:, cols]
        d_new_wide = wide_split(d_new)
        d_new_low = d_new_wide[:, :LANES]
        d_inner = dot_tn(jnp.concatenate(mixing, axis=0), jnp.concatenate([grads, grads], axis=0))
        d_scaled = both_sides(d_inner) + tail_wide * both_sides(
            dot_nn(into_both, jnp.concatenate([d_new_wide, d_new_wide], axis=0))
        )
        old = s_ref[0, :, cols]
        d_carry = (spread(low, ecum, a) * grad).astype(BF16)
        d_outof += dot_nt(d_carry, old.astype(BF16))
        d_into += dot_nt((scaled * tail_wide).astype(BF16), d_new_low)
        ends += jnp.sum((d_new * n_ref[0, :, cols]).reshape(STATE // 8, 8, LANES), axis=0) @ pick[
            :LANES
        ].astype(F32)
        dstate[:, cols] = keep_wide * d_new + dot_nn(outof_t, d_carry)
        dext[:CHUNK, cols] = (d_scaled * dt_wide + skip_wide * grad) * slope_ref[:, cols]
        both = grad * heads
        sum_y += by_head(grad * y_ref[:, cols] - skip_wide * both - scaled * d_scaled, pick)
        pair = jnp.concatenate([heads * d_scaled, both], axis=1).astype(BF16)
        sum_xk += dot_nn(pair, pick_two)
    dgram_low = dgram.astype(BF16)
    cols = slice(SSM_INNER, SSM_INNER + STATE)
    dext[:CHUNK, cols] = (d_into + dot_tn(dgram_low, outof)) * slope_ref[:, cols]
    cols = slice(SSM_INNER + STATE, XBC_WIDTH)
    dext[:CHUNK, cols] = (d_outof + dot_nn(dgram_low, into)) * slope_ref[:, cols]
    for k in range(XBC_WIDTH // BLOCK_COLS):
        cols = cols_of(k)
        at = slice(SSM_INNER + k * BLOCK_COLS, SSM_INNER + (k + 1) * BLOCK_COLS)
        before = proj_ref[:, at]
        here = dext[:CHUNK, cols]
        total = here * cw_ref[CONV - 1 :, cols]
        vec_ref[CONV - 1 : CONV, cols] += jnp.sum(here * before, axis=0, keepdims=True)
        vec_ref[CONV : CONV + 1, cols] += jnp.sum(here, axis=0, keepdims=True)
        for d in range(1, CONV):
            later = dext[d : d + CHUNK, cols] * near_ref[:, CONV + d : CONV + d + 1]
            total += later * cw_ref[CONV - 1 - d : CONV - d, cols]
            vec_ref[CONV - 1 - d : CONV - d, cols] += jnp.sum(later * before, axis=0, keepdims=True)
        grad_ref[:, at] = total.astype(BF16)
    dext[CHUNK:, :] = dext[:8, :]
    sums_ref[:, :LANES] = sum_y
    sums_ref[:, LANES:] = sum_xk
    ends_ref[...] = ends.reshape(ends_ref.shape)


def scan_specs(at):
    here = lambda i, last: (at(i), 0)
    across = lambda i, last: (0, at(i))
    return dict(
        rows=lambda width: pl.BlockSpec((CHUNK, width), here),
        cols=lambda height: pl.BlockSpec((height, CHUNK), across),
        fixed=lambda *shape: pl.BlockSpec(shape, lambda i, last: (0,) * len(shape)),
    )


def ssm_forward(last, both_proj, near, conv_w, conv_b, gain, dt, cum, cumt, skip, segc, segr):
    length, width = both_proj.shape
    chunks = length // CHUNK
    spec = scan_specs(lambda i: i)
    return pl.pallas_call(
        ssm_fwd_kernel,
        grid_spec=pltpu.PrefetchScalarGridSpec(
            num_scalar_prefetch=1,
            grid=(chunks,),
            in_specs=[
                spec["rows"](width),
                spec["rows"](2 * CONV),
                spec["fixed"](CONV, XBC_WIDTH),
                spec["fixed"](1, XBC_WIDTH),
                spec["fixed"](1, SSM_INNER),
                spec["rows"](SSM_HEADS),
                spec["rows"](SSM_HEADS),
                spec["cols"](SSM_HEADS),
                spec["fixed"](1, SSM_HEADS),
                spec["rows"](1),
                spec["cols"](1),
            ],
            out_specs=[
                spec["rows"](SSM_INNER),
                pl.BlockSpec((1, STATE, SSM_INNER), lambda c, last: (c, 0, 0)),
                spec["rows"](XBC_WIDTH),
                spec["rows"](XBC_WIDTH),
                spec["rows"](SSM_INNER),
            ],
            scratch_shapes=[
                pltpu.VMEM((STATE, SSM_INNER), F32),
                pltpu.VMEM((CHUNK + 8, XBC_WIDTH), F32),
            ],
        ),
        out_shape=[
            jax.ShapeDtypeStruct((length, SSM_INNER), F32),
            jax.ShapeDtypeStruct((chunks, STATE, SSM_INNER), F32),
            jax.ShapeDtypeStruct((length, XBC_WIDTH), F32),
            jax.ShapeDtypeStruct((length, XBC_WIDTH), F32),
            jax.ShapeDtypeStruct((length, SSM_INNER), BF16),
        ],
        compiler_params=params(),
        cost_estimate=cost(
            8 * length * SSM_INNER * STATE, 40 * length * SSM_INNER, length * CHUNK * SSM_HEADS
        ),
    )(last, both_proj, near, conv_w, conv_b, gain, dt, cum, cumt, skip, segc, segr)


def ssm_backward(
    last, both_proj, near, conv_w, gain, xbc, slope, dt, cum, cumt, skip, segc, segr, states, outputs,
    grads,
):
    length, width = both_proj.shape
    chunks = length // CHUNK
    end = chunks - 1
    spec = scan_specs(lambda i: end - i)
    return pl.pallas_call(
        ssm_bwd_kernel,
        grid_spec=pltpu.PrefetchScalarGridSpec(
            num_scalar_prefetch=1,
            grid=(chunks,),
            in_specs=[
                spec["rows"](width),
                spec["rows"](2 * CONV),
                spec["fixed"](CONV, XBC_WIDTH),
                spec["fixed"](1, SSM_INNER),
                spec["rows"](XBC_WIDTH),
                spec["rows"](XBC_WIDTH),
                spec["rows"](SSM_HEADS),
                spec["rows"](SSM_HEADS),
                spec["cols"](SSM_HEADS),
                spec["fixed"](1, SSM_HEADS),
                spec["rows"](1),
                spec["cols"](1),
                pl.BlockSpec((1, STATE, SSM_INNER), lambda i, last: (end - i, 0, 0)),
                pl.BlockSpec(
                    (1, STATE, SSM_INNER), lambda i, last: (jnp.minimum(end - i + 1, end), 0, 0)
                ),
                spec["rows"](SSM_INNER),
                spec["rows"](grads.shape[1]),
            ],
            out_specs=[
                spec["rows"](width),
                spec["rows"](2 * LANES),
                pl.BlockSpec((1, 8, LANES), lambda i, last: (end - i, 0, 0)),
                spec["fixed"](8, XBC_WIDTH),
            ],
            scratch_shapes=[
                pltpu.VMEM((STATE, SSM_INNER), F32),
                pltpu.VMEM((CHUNK, SSM_INNER), F32),
                pltpu.VMEM((CHUNK + 8, XBC_WIDTH), F32),
            ],
        ),
        out_shape=[
            jax.ShapeDtypeStruct((length, width), BF16),
            jax.ShapeDtypeStruct((length, 2 * LANES), F32),
            jax.ShapeDtypeStruct((chunks, 8, LANES), F32),
            jax.ShapeDtypeStruct((8, XBC_WIDTH), F32),
        ],
        compiler_params=params(),
        cost_estimate=cost(
            24 * length * SSM_INNER * STATE, 60 * length * SSM_INNER, length * CHUNK * SSM_HEADS
        ),
    )(
        last, both_proj, near, conv_w, gain, xbc, slope, dt, cum, cumt, skip, segc, segr, states, states,
        outputs, grads,
    )


def neighbours(segment):
    length = segment.shape[0]
    columns = []
    for d in range(CONV):
        earlier = jnp.pad(segment, (d, 0), constant_values=-1)[:length]
        columns.append(earlier == segment)
    for d in range(CONV):
        later = jnp.pad(segment, (0, d), constant_values=-1)[d:]
        columns.append(later == segment)
    return jnp.stack(columns, axis=1).astype(F32)


def rows_kernel(counts, lo_ref, hi_ref, ids_ref, *rest):
    step = pl.program_id(0)
    g_refs, (o_ref, wide) = rest[:-2], rest[-2:]
    group = wide.shape[0] // LISTS

    @pl.when(step == 0)
    def _():
        o_ref[...] = jnp.zeros_like(o_ref)

    before = 0
    for count, g_ref in zip(counts, g_refs):

        @pl.when((step >= before) & (step < before + count))
        def _(g_ref=g_ref):
            wide[...] = g_ref[...].astype(F32)

        before = before + count
    for q in range(LISTS):
        at = step * LISTS + q
        low, high = lo_ref[at], hi_ref[at]

        def one(j, at=at, q=q):
            o_ref[pl.ds(ids_ref[at * group + j], 1), :] += wide[pl.ds(q * group + j, 1), :]

        def eight(k, carry, one=one, low=low):
            for u in range(8):
                one(low + 8 * k + u)
            return carry

        def rest_of(j, carry, one=one):
            one(j)
            return carry

        eights = (high - low) // 8
        lax.fori_loop(0, eights, eight, 0)
        lax.fori_loop(low + 8 * eights, high, rest_of, 0)


def rows_by_token(local_ids, grads, shard_rows, group):
    width = grads[0].shape[1]
    counts = [g.shape[0] // (LISTS * group) for g in grads]
    lists = local_ids.reshape(-1, group)
    low = jnp.sum((lists < 0).astype(jnp.int32), axis=1)
    high = jnp.sum((lists < shard_rows).astype(jnp.int32), axis=1)
    specs, before = [], 0
    for count in counts:
        specs.append(
            pl.BlockSpec(
                (LISTS * group, width),
                lambda i, lo, hi, ids, before=before, count=count: (
                    jnp.clip(i - before, 0, count - 1),
                    0,
                ),
            )
        )
        before = before + count
    return pl.pallas_call(
        functools.partial(rows_kernel, counts),
        grid_spec=pltpu.PrefetchScalarGridSpec(
            num_scalar_prefetch=3,
            grid=(before,),
            in_specs=specs,
            out_specs=pl.BlockSpec((shard_rows, width), lambda i, lo, hi, ids: (0, 0)),
            scratch_shapes=[pltpu.VMEM((LISTS * group, width), F32)],
        ),
        out_shape=jax.ShapeDtypeStruct((shard_rows, width), F32),
        compiler_params=params(),
        cost_estimate=cost(before * group * width * LANES, before * group * width * 8),
    )(low, high, local_ids, *grads)


def split_nn(left, right):
    left_high, left_rest = split(left)
    right_high, right_rest = split(right)
    return dot_nn(left_high, right_high) + dot_nn(left_rest, right_high) + dot_nn(left_high, right_rest)


def rotate_kernel(l_ref, g_ref, r_ref, o_ref):
    grad = g_ref[...].reshape(D, BLOCK_COLS)
    left_high, left_rest = split(l_ref[0])
    part = dot_nn(left_high, grad) + dot_nn(left_rest, grad)
    o_ref[0] = split_nn(part, r_ref[0])


def rotate_blocks(left_basis, grad_whole, right_basis):
    slots, depth, _ = left_basis.shape
    rows = grad_whole.shape[0]
    return pl.pallas_call(
        rotate_kernel,
        grid=(slots,),
        in_specs=[
            pl.BlockSpec((1, depth, D), lambda k: (k, 0, 0)),
            pl.BlockSpec((rows, 1, depth, BLOCK_COLS), lambda k: (0, k, 0, 0)),
            pl.BlockSpec((1, BLOCK_COLS, BLOCK_COLS), lambda k: (k, 0, 0)),
        ],
        out_specs=pl.BlockSpec((1, depth, BLOCK_COLS), lambda k: (k, 0, 0)),
        out_shape=jax.ShapeDtypeStruct((slots, depth, BLOCK_COLS), F32),
        compiler_params=params(),
        cost_estimate=cost(6 * slots * depth * D * BLOCK_COLS, slots * depth * D * 5),
    )(left_basis, grad_whole, right_basis)


def step_kernel(scale_ref, rot_ref, m_ref, v_ref, l_ref, r_ref, mo_ref, vo_ref, u_ref):
    rotated = rot_ref[0] * scale_ref[0]
    first_new = soap_first * m_ref[0] + (1.0 - soap_first) * rotated
    second_new = soap_second * v_ref[0] + (1.0 - soap_second) * rotated * rotated
    mo_ref[0], vo_ref[0] = first_new, second_new
    direction = (first_new / scale_ref[1]) / (jnp.sqrt(second_new / scale_ref[2]) + adam_eps)
    turned = split_nn(direction, r_ref[0].T).astype(BF16)
    left_high, left_rest = split(l_ref[0])
    update = dot_nn(left_high.T, turned) + dot_nn(left_rest.T, turned)
    u_ref[0] = update.astype(BF16)


def step_blocks(scales, rotated, block_first, block_second, left_basis, right_basis):
    slots, depth, _ = left_basis.shape
    own = pl.BlockSpec((1, depth, BLOCK_COLS), lambda k: (k, 0, 0))
    small = jax.ShapeDtypeStruct((slots, depth, BLOCK_COLS), F32)
    return pl.pallas_call(
        step_kernel,
        grid=(slots,),
        in_specs=[
            pl.BlockSpec(memory_space=pltpu.SMEM),
            own,
            own,
            own,
            pl.BlockSpec((1, depth, D), lambda k: (k, 0, 0)),
            pl.BlockSpec((1, BLOCK_COLS, BLOCK_COLS), lambda k: (k, 0, 0)),
        ],
        out_specs=[own, own, pl.BlockSpec((1, D, BLOCK_COLS), lambda k: (k, 0, 0))],
        out_shape=[small, small, jax.ShapeDtypeStruct((slots, D, BLOCK_COLS), BF16)],
        compiler_params=params(),
        cost_estimate=cost(6 * slots * depth * D * BLOCK_COLS, slots * depth * D * 7),
    )(scales, rotated, block_first, block_second, left_basis, right_basis)


def to_peers(axis, extent, place, src, box, send_sem, recv_sem):
    copies = []
    for k in range(1, extent):
        peer = list(place)
        peer[axis] = lax.rem(place[axis] + k, extent)
        copies.append(
            pltpu.make_async_remote_copy(
                src_ref=src,
                dst_ref=box.at[place[axis]],
                send_sem=send_sem.at[k],
                recv_sem=recv_sem.at[k],
                device_id=tuple(peer),
                device_id_type=MESH,
            )
        )
    return copies


def greet_peers(axes, place):
    barrier = pltpu.get_barrier_semaphore()
    count = 0
    for axis, extent in axes:
        for k in range(1, extent):
            peer = list(place)
            peer[axis] = lax.rem(place[axis] + k, extent)
            pl.semaphore_signal(barrier, inc=1, device_id=tuple(peer), device_id_type=MESH)
            count += 1
    pl.semaphore_wait(barrier, count)


def total_kernel(rows, cols, x_ref, o_ref, col_box, row_box, col_send, col_recv, row_send, row_recv):
    place = (lax.axis_index("row"), lax.axis_index("col"))
    greet_peers(((0, rows), (1, cols)), place)
    total = x_ref[...]
    for axis, extent, box, send_sem, recv_sem in (
        (1, cols, col_box, col_send, col_recv),
        (0, rows, row_box, row_send, row_recv),
    ):
        o_ref[...] = total
        box[place[axis]] = total
        copies = to_peers(axis, extent, place, o_ref, box, send_sem, recv_sem)
        for copy in copies:
            copy.start()
        for copy in copies:
            copy.wait()
        total = jnp.sum(box[...], axis=0)
    o_ref[...] = total


def total_over_all(values, rows, cols, collective_id):
    dma = pltpu.SemaphoreType.DMA
    return pl.pallas_call(
        functools.partial(total_kernel, rows, cols),
        in_specs=[pl.BlockSpec(memory_space=pltpu.VMEM)],
        out_specs=pl.BlockSpec(memory_space=pltpu.VMEM),
        out_shape=jax.ShapeDtypeStruct(values.shape, F32),
        scratch_shapes=[
            pltpu.VMEM((cols,) + values.shape, F32),
            pltpu.VMEM((rows,) + values.shape, F32),
            dma((cols,)),
            dma((cols,)),
            dma((rows,)),
            dma((rows,)),
        ],
        compiler_params=params(collective_id=collective_id, has_side_effects=True),
        cost_estimate=cost(rows * cols * values.size, rows * cols * values.size * 4),
    )(values)


def ring_bits(rows, cols):
    bits = []
    for axis, extent in ((0, rows), (1, cols)):
        bit = extent // 2
        while bit >= 1:
            bits.append((axis, bit))
            bit = bit // 2
    return bits


def scatter_orders(rows, cols):
    bits = ring_bits(rows, cols)
    row_bits = [b for b in reversed(bits) if b[0] == 0]
    col_bits = [b for b in reversed(bits) if b[0] == 1]
    return col_bits + row_bits, col_bits[:1] + col_bits[1:][::-1] + row_bits


def tail_kernel(rows, cols, slots, g_ref, p_ref, v_ref, whole_ref, tok_ref, vec_ref, own, *rest):
    bits = ring_bits(rows, cols)
    stages = len(bits)
    row_bits = [b for b in bits if b[0] == 0]
    col_bits = [b for b in bits if b[0] == 1]
    boxes, rest = rest[:stages], rest[stages:]
    vec_box, vec_sum, send_sem, recv_sem, own_sem = rest[:5]
    join_send, join_recv, tok_send, tok_recv, tok_own, vec_send, vec_recv = rest[5:]
    place = (lax.axis_index("row"), lax.axis_index("col"))
    half = whole_ref.shape[-2] // 2
    orders = scatter_orders(rows, cols)

    def side(which):
        axis, bit = which
        return place[axis] // bit % 2

    def partner(which):
        axis, bit = which
        moved = place[axis] + bit - 2 * bit * side(which)
        return (moved, place[1]) if axis == 0 else (place[0], moved)

    def remote(src, dst, send, recv, which):
        return pltpu.make_async_remote_copy(
            src_ref=src,
            dst_ref=dst,
            send_sem=send,
            recv_sem=recv,
            device_id=partner(which),
            device_id_type=MESH,
        )

    barrier = pltpu.get_barrier_semaphore()
    for which in bits:
        pl.semaphore_signal(barrier, inc=1, device_id=partner(which), device_id_type=MESH)
    pl.semaphore_wait(barrier, stages)
    units = [(slot, h) for slot in range(slots) for h in range(2)]

    def pick(ref, before, which, side_of, after):
        at = before.index(which)
        return ref.at[(slice(None),) * at + (side_of,) + (slice(None),) * (len(before) - at - 1) + after]

    def part(slot, h, side_of):
        return pick(g_ref, bits, orders[h][0], side_of, (slot, slice(h * half, (h + 1) * half)))

    def cut(stage, u, side_of):
        order = orders[units[u][1]]
        left = [b for b in bits if b not in order[: stage + 1]]
        return pick(boxes[stage].at[u], left, order[stage + 1], side_of, ())

    def send(stage, u):
        slot, h = units[u]
        which = orders[h][stage]
        other = 1 - side(which)
        return remote(
            part(slot, h, other) if stage == 0 else cut(stage - 1, u, other),
            boxes[stage].at[u],
            send_sem.at[stage, u],
            recv_sem.at[stage, u],
            which,
        )

    def keep(u):
        slot, h = units[u]
        return pltpu.make_async_copy(part(slot, h, side(orders[h][0])), own.at[u], own_sem.at[u])

    def joined(ref, order, of_bits, stage, after):
        at = tuple(slice(None) if b in order[:stage] else side(b) for b in of_bits)
        return ref.at[at + after]

    def join(stage, u):
        slot, h = units[u]
        region = joined(whole_ref, row_bits, row_bits, stage, (slot, slice(h * half, (h + 1) * half)))
        return remote(region, region, join_send.at[stage, u], join_recv.at[stage, u], row_bits[stage])

    def tok(stage, h):
        order = (orders[h][1 : len(col_bits)] + orders[h][:1])
        region = joined(tok_ref, order, col_bits, stage, (h,))
        return remote(
            p_ref.at[h] if stage == 0 else region, region, tok_send.at[stage, h],
            tok_recv.at[stage, h], order[stage],
        )

    def tok_keep():
        region = joined(tok_ref, [], col_bits, 0, ())
        return pltpu.make_async_copy(p_ref, region, tok_own)

    def vec(stage):
        return remote(
            vec_sum.at[stage], vec_box.at[stage], vec_send.at[stage], vec_recv.at[stage], bits[stage]
        )

    sent = []

    def start(copy):
        copy.start()
        sent.append(copy)
        return copy

    flying = {}
    vec_sum[0] = v_ref[...]
    flying["vec", 0] = start(vec(0))
    for u in range(len(units)):
        flying[0, u] = start(send(0, u))
        keep(u).start()
        if u == 1:
            tok_keep().start()
            for h in range(2):
                flying["tok", 0, h] = start(tok(0, h))
    steps = slots + stages + len(row_bits) - 1
    tok_at = [steps - 1 - 2 * (len(col_bits) - 1 - k) for k in range(len(col_bits))]
    for t in range(steps):
        if t < stages:
            flying["vec", t].wait_recv()
            if t + 1 < stages:
                vec_sum[t + 1] = vec_sum[t] + vec_box[t]
                flying["vec", t + 1] = start(vec(t + 1))
            else:
                vec_ref[...] = vec_sum[t] + vec_box[t]
        for k, at in enumerate(tok_at):
            if at == t:
                if k == 0:
                    tok_keep().wait()
                for h in range(2):
                    flying["tok", k, h].wait_recv()
                    if k + 1 < len(col_bits):
                        flying["tok", k + 1, h] = start(tok(k + 1, h))
        for stage in reversed(range(stages + len(row_bits))):
            slot = t - stage
            if not 0 <= slot < slots:
                continue
            for h in range(2):
                u = 2 * slot + h
                if stage >= stages:
                    flying["join", stage - stages, u].wait_recv()
                    if stage - stages + 1 < len(row_bits):
                        flying["join", stage - stages + 1, u] = start(join(stage - stages + 1, u))
                    continue
                flying[stage, u].wait_recv()
                box = boxes[stage].at[u]
                if stage == 0:
                    keep(u).wait()
                    held = own.at[u]
                else:
                    held = cut(stage - 1, u, side(orders[h][stage]))
                if stage == stages - 1:
                    total = held[...].astype(F32) + box[...].astype(F32)
                    mine = joined(
                        whole_ref, [], row_bits, 0, (slot, slice(h * half, (h + 1) * half))
                    )
                    mine[...] = total.astype(BF16)
                    flying["join", 0, u] = start(join(0, u))
                    continue
                extents = box.shape[:-2]

                def add(k, carry, box=box, held=held, extents=extents):
                    at = []
                    for extent in reversed(extents):
                        at.append(k % extent)
                        k = k // extent
                    at = tuple(reversed(at))
                    box[at] = (held[at].astype(F32) + box[at].astype(F32)).astype(BF16)
                    return carry

                lax.fori_loop(0, 2 ** len(extents), add, 0)
                flying[stage + 1, u] = start(send(stage + 1, u))
    for copy in sent:
        copy.wait_send()


def tail_exchange(grads, pieces, vectors, rows, cols, collective_id):
    _, nslots, depth, _ = grads.shape
    slots = nslots // cols
    bits = ring_bits(rows, cols)
    stages = len(bits)
    row_stages, col_stages = (rows - 1).bit_length(), (cols - 1).bit_length()
    units, half = 2 * slots, depth // 2
    count, width = pieces.shape
    boxes = [
        pltpu.VMEM((units,) + (2,) * (stages - s - 1) + (half, BLOCK_COLS), BF16)
        for s in range(stages)
    ]
    vec_shape = (stages,) + vectors.shape
    whole, tokens, total = pl.pallas_call(
        functools.partial(tail_kernel, rows, cols, slots),
        in_specs=[
            pl.BlockSpec(memory_space=pl.ANY),
            pl.BlockSpec(memory_space=pl.ANY),
            pl.BlockSpec(memory_space=pltpu.VMEM),
        ],
        out_specs=[
            pl.BlockSpec(memory_space=pltpu.VMEM),
            pl.BlockSpec(memory_space=pl.ANY),
            pl.BlockSpec(memory_space=pltpu.VMEM),
        ],
        out_shape=[
            jax.ShapeDtypeStruct((2,) * row_stages + (slots, depth, BLOCK_COLS), BF16),
            jax.ShapeDtypeStruct((2,) * col_stages + (2, count // 2, width), BF16),
            jax.ShapeDtypeStruct(vectors.shape, F32),
        ],
        scratch_shapes=[pltpu.VMEM(boxes[0].shape, BF16)]
        + boxes
        + [
            pltpu.VMEM(vec_shape, F32),
            pltpu.VMEM(vec_shape, F32),
            pltpu.SemaphoreType.DMA((stages, units)),
            pltpu.SemaphoreType.DMA((stages, units)),
            pltpu.SemaphoreType.DMA((units,)),
            pltpu.SemaphoreType.DMA((row_stages, units)),
            pltpu.SemaphoreType.DMA((row_stages, units)),
            pltpu.SemaphoreType.DMA((col_stages, 2)),
            pltpu.SemaphoreType.DMA((col_stages, 2)),
            pltpu.SemaphoreType.DMA,
            pltpu.SemaphoreType.DMA((stages,)),
            pltpu.SemaphoreType.DMA((stages,)),
        ],
        compiler_params=params(collective_id=collective_id, has_side_effects=True),
        cost_estimate=cost(rows * nslots * depth * BLOCK_COLS, rows * nslots * depth * BLOCK_COLS * 6),
    )(
        grads.reshape((2,) * stages + (slots, depth, BLOCK_COLS)),
        pieces.reshape(2, count // 2, width),
        vectors,
    )
    return whole.reshape(rows, slots, depth, BLOCK_COLS), tokens.reshape(cols * count, width), total


def doubling(place, bits):
    def side(which):
        axis, bit = which
        return place[axis] // bit % 2

    def partner(which):
        axis, bit = which
        moved = place[axis] + bit - 2 * bit * side(which)
        return (moved, place[1]) if axis == 0 else (place[0], moved)

    return side, partner


def greet(bits, partner):
    barrier = pltpu.get_barrier_semaphore()
    for which in bits:
        pl.semaphore_signal(barrier, inc=1, device_id=partner(which), device_id_type=MESH)
    pl.semaphore_wait(barrier, len(bits))


def joiner(side, partner, src, out, of_bits, order, after, send_sem, recv_sem):
    def copy(k):
        at = tuple(slice(None) if b in order[:k] else side(b) for b in of_bits)
        region = out.at[at + after]
        return pltpu.make_async_remote_copy(
            src_ref=src if k == 0 else region,
            dst_ref=region,
            send_sem=send_sem.at[k],
            recv_sem=recv_sem.at[k],
            device_id=partner(order[k]),
            device_id_type=MESH,
        )

    return copy


def front_kernel(rows, cols, i_ref, t_ref, w_ref, io_ref, to_ref, wo_ref, *sems):
    bits = ring_bits(rows, cols)
    row_bits = [b for b in bits if b[0] == 0]
    col_bits = [b for b in bits if b[0] == 1]
    place = (lax.axis_index("row"), lax.axis_index("col"))
    side, partner = doubling(place, bits)
    i_send, i_recv, t_send, t_recv, w_send, w_recv, keep_sem = sems
    greet(bits, partner)
    own_row, own_col = tuple(side(b) for b in row_bits), tuple(side(b) for b in col_bits)
    keeps = [
        pltpu.make_async_copy(i_ref, io_ref.at[own_row + own_col], keep_sem.at[0]),
        pltpu.make_async_copy(t_ref, to_ref.at[own_col], keep_sem.at[1]),
        pltpu.make_async_copy(w_ref, wo_ref.at[own_row], keep_sem.at[2]),
    ]
    orders = [o[1 : len(col_bits)] + o[:1] for o in scatter_orders(rows, cols)]
    jobs = {}
    jobs["i", 0] = (joiner(side, partner, i_ref, io_ref, bits, bits[::-1], (), i_send, i_recv), 0, 1)
    for p in range(t_ref.shape[0]):
        copy = joiner(
            side, partner, t_ref.at[p], to_ref, col_bits, orders[p % 2], (p,), t_send.at[p], t_recv.at[p]
        )
        jobs["t", p] = (copy, 1 + p // 2, 3)
    for p in range(w_ref.shape[0]):
        copy = joiner(
            side, partner, w_ref.at[p], wo_ref, row_bits, row_bits, (p,), w_send.at[p], w_recv.at[p]
        )
        jobs["w", p] = (copy, p, 1)
    run_joins(jobs, {"i": len(bits), "t": len(col_bits), "w": len(row_bits)}, keeps)


def run_joins(jobs, stages, keeps, done=None):
    for copy in keeps:
        copy.start()
    sent = []
    for copy, _, _ in jobs.values():
        sent.append(copy(0))
        sent[-1].start()
    for copy in keeps:
        copy.wait()
    ends = [at + every * (stages[name[0]] - 1) for name, (_, at, every) in jobs.items()]
    for t in range(max(ends) + 1):
        for name, (copy, at, every) in jobs.items():
            k = (t - at) // every
            if t < at or (t - at) % every or k >= stages[name[0]]:
                continue
            copy(k).wait_recv()
            if k + 1 < stages[name[0]]:
                sent.append(copy(k + 1))
                sent[-1].start()
            elif done is not None:
                done(name[1])
    for copy in sent:
        copy.wait_send()


def front_exchange(ints, table_low, weights_low, rows, cols, collective_id):
    row_stages, col_stages = (rows - 1).bit_length(), (cols - 1).bit_length()
    parts = TABLE_PARTS
    shard, width = table_low.shape
    slots = weights_low.shape[0]
    dma = pltpu.SemaphoreType.DMA
    ints = ints.reshape(-1, LANES)
    outs = pl.pallas_call(
        functools.partial(front_kernel, rows, cols),
        in_specs=[pl.BlockSpec(memory_space=pl.ANY)] * 3,
        out_specs=[pl.BlockSpec(memory_space=pltpu.VMEM)] * 3,
        out_shape=[
            jax.ShapeDtypeStruct((2,) * (row_stages + col_stages) + ints.shape, jnp.int32),
            jax.ShapeDtypeStruct((2,) * col_stages + (parts, shard // parts, width), BF16),
            jax.ShapeDtypeStruct((2,) * row_stages + weights_low.shape, BF16),
        ],
        scratch_shapes=[
            dma((row_stages + col_stages,)),
            dma((row_stages + col_stages,)),
            dma((parts, col_stages)),
            dma((parts, col_stages)),
            dma((slots, row_stages)),
            dma((slots, row_stages)),
            dma((3,)),
        ],
        compiler_params=params(collective_id=collective_id, has_side_effects=True),
        cost_estimate=cost(1 << 20, cols * shard * width * 4),
    )(ints, table_low.reshape(parts, shard // parts, width), weights_low)
    return (
        outs[0].reshape(rows, cols, -1),
        outs[1].reshape(cols * shard, width),
        outs[2].reshape((rows,) + weights_low.shape),
    )


def weights_kernel(rows, cols, w_ref, o_ref, box, send_sem, recv_sem, keep_sem, out_sem):
    bits = ring_bits(rows, cols)
    col_bits = [b for b in bits if b[0] == 1]
    place = (lax.axis_index("row"), lax.axis_index("col"))
    side, partner = doubling(place, bits)
    greet(col_bits, partner)
    own = tuple(side(b) for b in col_bits)
    slots, half = w_ref.shape[1], w_ref.shape[2] // 2
    orders = [o[1 : len(col_bits)] + o[:1] for o in scatter_orders(rows, cols)]
    keeps = [
        pltpu.make_async_copy(w_ref, box.at[(slice(None),) + own], keep_sem),
    ]
    jobs = {}
    outs = []

    def done(u):
        part = (slice(None),) * (1 + len(col_bits)) + parts[u]
        outs.append(pltpu.make_async_copy(box.at[part], o_ref.at[part], out_sem.at[u]))
        outs[-1].start()

    parts = [(slot, slice(h * half, (h + 1) * half)) for slot in range(slots) for h in range(2)]
    for slot in range(slots):
        for h in range(2):
            part = (slot, slice(h * half, (h + 1) * half))
            u = 2 * slot + h

            def copy(k, part=part, order=orders[h], u=u):
                at = tuple(slice(None) if b in order[:k] else side(b) for b in col_bits)
                region = box.at[(slice(None),) + at + part]
                return pltpu.make_async_remote_copy(
                    src_ref=w_ref.at[(slice(None),) + part] if k == 0 else region,
                    dst_ref=region,
                    send_sem=send_sem.at[u, k],
                    recv_sem=recv_sem.at[u, k],
                    device_id=partner(order[k]),
                    device_id_type=MESH,
                )

            jobs["w", u] = (copy, slot, 1)
    run_joins(jobs, {"w": len(col_bits)}, keeps, done)
    for copy in outs:
        copy.wait()


def gather_weights(weights, rows, cols, collective_id):
    _, slots, depth, width = weights.shape
    col_stages = (cols - 1).bit_length()
    dma = pltpu.SemaphoreType.DMA
    shape = (rows,) + (2,) * col_stages + (slots, depth, width)
    out = pl.pallas_call(
        functools.partial(weights_kernel, rows, cols),
        in_specs=[pl.BlockSpec(memory_space=pl.ANY)],
        out_specs=pl.BlockSpec(memory_space=pl.ANY),
        out_shape=jax.ShapeDtypeStruct(shape, BF16),
        scratch_shapes=[
            pltpu.VMEM(shape, BF16),
            dma((2 * slots, col_stages)),
            dma((2 * slots, col_stages)),
            dma,
            dma((2 * slots,)),
        ],
        compiler_params=params(collective_id=collective_id, has_side_effects=True),
        cost_estimate=cost(1 << 20, 4 * cols * weights.size),
    )(weights)
    return out.reshape(rows, cols * slots, depth, width)


def columns_kernel(cols, x_ref, o_ref, send_sem, recv_sem):
    place = (lax.axis_index("row"), lax.axis_index("col"))
    greet_peers(((1, cols),), place)
    o_ref[place[1]] = x_ref[...]
    copies = to_peers(1, cols, place, x_ref, o_ref, send_sem, recv_sem)
    for copy in copies:
        copy.start()
    for copy in copies:
        copy.wait()


def gather_columns(values, cols, collective_id):
    dma = pltpu.SemaphoreType.DMA
    return pl.pallas_call(
        functools.partial(columns_kernel, cols),
        in_specs=[pl.BlockSpec(memory_space=pltpu.VMEM)],
        out_specs=pl.BlockSpec(memory_space=pltpu.VMEM),
        out_shape=jax.ShapeDtypeStruct((cols,) + values.shape, values.dtype),
        scratch_shapes=[dma((cols,)), dma((cols,))],
        compiler_params=params(collective_id=collective_id, has_side_effects=True),
        cost_estimate=cost(1024, cols * values.size * 4),
    )(values)


def rows_gather_kernel(rows, cols, x_ref, o_ref, send_sem, recv_sem):
    col_bits = [b for b in ring_bits(rows, cols) if b[0] == 1]
    place = (lax.axis_index("row"), lax.axis_index("col"))
    side, partner = doubling(place, col_bits)
    orders = [o[1 : len(col_bits)] + o[:1] for o in scatter_orders(rows, cols)]
    greet(col_bits, partner)
    own = tuple(side(b) for b in col_bits)
    jobs = {}
    for h in range(2):
        o_ref[own + (h,)] = x_ref[h]
        copy = joiner(
            side, partner, x_ref.at[h], o_ref, col_bits, orders[h], (h,), send_sem.at[h], recv_sem.at[h]
        )
        jobs["x", h] = (copy, 0, 1)
    run_joins(jobs, {"x": len(col_bits)}, [])


def gather_rows(values, rows, cols, collective_id):
    count, width = values.shape
    stages = (cols - 1).bit_length()
    dma = pltpu.SemaphoreType.DMA
    out = pl.pallas_call(
        functools.partial(rows_gather_kernel, rows, cols),
        in_specs=[pl.BlockSpec(memory_space=pltpu.VMEM)],
        out_specs=pl.BlockSpec(memory_space=pltpu.VMEM),
        out_shape=jax.ShapeDtypeStruct((2,) * stages + (2, count // 2, width), values.dtype),
        scratch_shapes=[dma((2, stages)), dma((2, stages))],
        compiler_params=params(collective_id=collective_id, has_side_effects=True),
        cost_estimate=cost(1024, cols * values.size * 4),
    )(values.reshape(2, count // 2, width))
    return out.reshape(cols * count, width)


def scatter_columns_kernel(rows, cols, x_ref, o_ref, *rest):
    bits = [b for b in ring_bits(rows, cols) if b[0] == 1]
    stages = len(bits)
    boxes, (send_sem, recv_sem) = rest[:stages], rest[stages:]
    place = (lax.axis_index("row"), lax.axis_index("col"))
    side, partner = doubling(place, bits)
    orders = [o[:stages] for o in scatter_orders(rows, cols)]
    greet(bits, partner)

    def held(stage, h, side_of):
        left = [b for b in bits if b not in orders[h][:stage]]
        at = tuple(side_of if b == orders[h][stage] else slice(None) for b in left)
        return x_ref.at[at + (h,)] if stage == 0 else boxes[stage - 1].at[(h,) + at]

    def send(stage, h):
        which = orders[h][stage]
        return pltpu.make_async_remote_copy(
            src_ref=held(stage, h, 1 - side(which)),
            dst_ref=boxes[stage].at[h],
            send_sem=send_sem.at[stage, h],
            recv_sem=recv_sem.at[stage, h],
            device_id=partner(which),
            device_id_type=MESH,
        )

    sent = []
    for stage in range(stages + 1):
        for h in range(2):
            if stage > 0:
                sent[2 * (stage - 1) + h].wait_recv()
                total = held(stage - 1, h, side(orders[h][stage - 1]))[...] + boxes[stage - 1][h]
                if stage == stages:
                    o_ref[h] = total
                else:
                    boxes[stage - 1][h] = total
            if stage < stages:
                sent.append(send(stage, h))
                sent[-1].start()
    for copy in sent:
        copy.wait_send()


def scatter_columns(values, rows, cols, collective_id):
    count, width = values.shape[0] // cols, values.shape[1]
    stages = (cols - 1).bit_length()
    dma = pltpu.SemaphoreType.DMA
    out = pl.pallas_call(
        functools.partial(scatter_columns_kernel, rows, cols),
        in_specs=[pl.BlockSpec(memory_space=pltpu.VMEM)],
        out_specs=pl.BlockSpec(memory_space=pltpu.VMEM),
        out_shape=jax.ShapeDtypeStruct((2, count // 2, width), F32),
        scratch_shapes=[
            pltpu.VMEM((2,) + (2,) * (stages - s - 1) + (count // 2, width), F32)
            for s in range(stages)
        ]
        + [dma((stages, 2)), dma((stages, 2))],
        compiler_params=params(collective_id=collective_id, has_side_effects=True),
        cost_estimate=cost(values.size, values.size * 8),
    )(values.reshape((2,) * stages + (2, count // 2, width)))
    return out.reshape(count, width)


def piece_order(rows):
    order = [0] + [k for pair in range(1, rows // 2 + 1) for k in (pair, rows - pair)][: rows - 1]
    return order[: rows // 4], order[rows // 4 :]


def exchange_rows(values, rows):
    row = lax.axis_index("row")
    width = values.shape[1] // rows
    arrived = []
    for group in piece_order(rows):
        parts = []
        for k in group:
            part = lax.dynamic_slice_in_dim(values, (row + k) % rows * width, width, 1)
            if k > 0:
                part = lax.ppermute(part, "row", [(r, (r + k) % rows) for r in range(rows)])
            parts.append(part)
        arrived.append(jnp.concatenate(parts, axis=0))
    return arrived


def adam_step(weights, grads, first, second, steps_done, decay, rate):
    first_new = adam_first * first + (1.0 - adam_first) * grads
    second_new = adam_second * second + (1.0 - adam_second) * grads * grads
    direction = (
        first_new
        / (1.0 - adam_first**steps_done)
        / (jnp.sqrt(second_new / (1.0 - adam_second**steps_done)) + adam_eps)
    )
    return (weights - rate * (direction + decay * weights), first_new, second_new)


def body(
    rows,
    cols,
    token_ids,
    segment_ids,
    loss_positions,
    loss_targets,
    loss_valid,
    block_owner,
    step_count,
    block_weights,
    block_first,
    block_second,
    left_basis,
    right_basis,
    table,
    table_first,
    table_second,
    vector_params,
    vector_first,
    vector_second,
):
    col_index = lax.axis_index("col")
    tokens = token_ids[0]
    segment = segment_ids[0]
    length = tokens.shape[0]
    in_cols = 2 * SSM_INNER + 2 * STATE
    in_blocks = (in_cols + (HEADS + 2 * KV_HEADS) * HEAD_DIM) // BLOCK_COLS
    branch_blocks = (SSM_INNER + HEADS * HEAD_DIM) // BLOCK_COLS
    gate_blocks = 2 * FF // BLOCK_COLS
    down_blocks = FF // BLOCK_COLS
    branch_at = in_blocks
    gate_at = branch_at + branch_blocks
    down_at = gate_at + gate_blocks
    nblocks = block_owner.shape[0]
    depth = block_weights.shape[1]
    shard_rows = table.shape[0]

    row_index = lax.axis_index("row")
    devices = rows * cols
    count_rows = loss_positions.shape[1]
    table_low = table.astype(BF16)
    shard_padded = -(-shard_rows // PAD_ROWS) * PAD_ROWS
    padded = jnp.pad(table_low, ((0, shard_padded - shard_rows), (0, 0)))
    in_order = jnp.sort(tokens)
    repeats = jnp.pad(in_order[1:] == in_order[:-1], (1, 0))
    different = jnp.sort(jnp.where(repeats, NO_TOKEN, in_order))
    token_place = jnp.sum((different[:, None] < tokens[None, :]).astype(jnp.int32), axis=0)
    sent = jnp.concatenate([tokens, different, loss_targets[0], loss_valid[0]])
    ints, table_cols, weight_rows = front_exchange(
        sent, padded, block_weights.astype(BF16), rows, cols, 2
    )
    padded, weight_rows, table_cols = lax.optimization_barrier((padded, weight_rows, table_cols))
    table_rows = lax.all_gather(padded, "row", axis=1, tiled=True)
    token_list = lax.dynamic_index_in_dim(ints, col_index, 1, False)[:, :length].reshape(-1)
    owners = token_list // shard_rows
    looked_up = jnp.take(
        table_cols, token_list + owners * (shard_padded - shard_rows), axis=0, mode="clip"
    )
    looked_up, weight_rows = lax.optimization_barrier((looked_up, weight_rows))
    arrived = lax.all_to_all(
        looked_up.reshape(rows, length, -1), "row", split_axis=0, concat_axis=0, tiled=True
    )
    gathered = gather_weights(weight_rows, rows, cols, 3)
    sorted_ints = ints[:, :, length : 2 * length]
    sorted_all = [
        jnp.stack(
            [
                lax.dynamic_index_in_dim(sorted_ints, (row_index - k) % rows, 0, False)
                for k in part
            ],
            axis=1,
        ).reshape(-1)
        for part in piece_order(rows)
    ]
    sorted_all = jnp.concatenate(sorted_all)
    labels_all = lax.dynamic_index_in_dim(ints, row_index, 0, False)[:, 2 * length :]
    targets_all = labels_all[:, :count_rows].reshape(-1)
    valid_all = labels_all[:, count_rows:].reshape(-1)
    valid_count = jnp.sum(ints[:, :, 2 * length + count_rows :]).astype(F32)

    conv_weight, conv_bias, time_bias, decay_log, skip_gain, mixer_gain, norm_gains, time_proj = (
        unpack(vector_params)
    )
    gain_rows = norm_gains.reshape(3, D)
    time_low = time_proj.reshape(D, SSM_HEADS).astype(BF16)
    segc, segr = segment[:, None], segment[None, :]
    chunks = length // CHUNK
    last_docs = segment.reshape(chunks, CHUNK)[:, CHUNK - 1]
    cosine, sine = rope_tables(length)

    embedded, normed = embed_and_norm(arrived, gain_rows[0])
    both_proj = project(normed, gathered, block_owner, 0, in_blocks)
    time_raw = jnp.dot(normed, time_low, preferred_element_type=F32)

    def steps_of(time_in, bias_in, decay_in):
        step_size = jax.nn.softplus(time_in + bias_in[None, :])
        return step_size, step_size * -jnp.exp(decay_in)[None, :]

    (step_size, decays), steps_back = jax.vjp(steps_of, time_raw, time_bias, decay_log)
    earlier = jnp.tril(jnp.ones((CHUNK, CHUNK), F32))
    decays_cut = decays.reshape(chunks, CHUNK, SSM_HEADS)
    cum = jnp.einsum("ts,csh->cth", earlier, decays_cut, precision=highest).reshape(
        length, SSM_HEADS
    )
    cumt = cum.T
    near = neighbours(segment)
    conv_rows = conv_weight.reshape(CONV, XBC_WIDTH)
    gain_row = mixer_gain.reshape(1, SSM_INNER)
    times = (step_size, cum, cumt, skip_gain[None, :], segc, segr)
    scan_out, states, act_xbc, slope, mixed = ssm_forward(
        last_docs, both_proj, near, conv_rows, conv_bias[None, :], gain_row, *times
    )
    positions = loss_positions[0]
    pos_col = positions[:, None]
    hits = pos_col == jnp.arange(length, dtype=jnp.int32)[None, :]
    chosen, place = hits.astype(BF16), hits.T.astype(BF16)
    seg_col = jnp.sum(jnp.where(hits, segr, 0), axis=1, keepdims=True)
    choose = lambda values: jnp.dot(chosen, values, preferred_element_type=F32).astype(BF16)
    spread_rows = lambda values: jnp.dot(hits.T.astype(F32), values, precision=highest)
    picked_in = (positions, pos_col, seg_col, segr, cosine, sine)
    context = attention_forward(both_proj, *picked_in)
    branch_in = jnp.concatenate([choose(mixed), context], axis=1)
    hidden_one, normed_two = back_then_norm(
        branch_in, gathered, block_owner, branch_at, branch_blocks, choose(embedded), gain_rows[1]
    )
    gate_val, up_val, act_low = project_gate_up(
        normed_two, gathered, block_owner, gate_at, down_blocks
    )
    hidden_two, picked_rows = back_then_norm(
        act_low, gathered, block_owner, down_at, down_blocks, hidden_one, gain_rows[2]
    )
    rows_all = gather_rows(picked_rows, rows, cols, 4)

    logits = jnp.einsum("rd,vd->rv", rows_all, table_rows, preferred_element_type=F32)
    local_target = targets_all - col_index * shard_rows
    places = jnp.arange(shard_padded, dtype=jnp.int32)[None, :]
    onehot = (places == local_target[:, None]) & (places < shard_rows)
    logits = jnp.where(places < shard_rows, logits, -1e30)
    row_top = jnp.max(logits, axis=1)
    row_total = jnp.sum(jnp.exp(logits - row_top[:, None]), axis=1)
    target_logit = jnp.sum(jnp.where(onehot, logits, 0.0), axis=1)
    no_part = jnp.zeros_like(row_top)
    parts = gather_columns(
        jnp.stack([row_top, row_total, target_logit] + [no_part] * 5), cols, 5
    )
    top_all = jnp.max(parts[:, 0], axis=0)
    total_all = jnp.sum(parts[:, 1] * jnp.exp(parts[:, 0] - top_all[None, :]), axis=0)
    target_all = jnp.sum(parts[:, 2], axis=0)
    log_total = top_all + jnp.log(total_all)
    valid_wide = valid_all.astype(F32)
    own_loss = lax.dynamic_slice_in_dim(
        (log_total - target_all) * valid_wide, col_index * count_rows, count_rows
    )
    logit_grad = (
        (jnp.exp(logits - log_total[:, None]) - onehot.astype(F32))
        * (valid_wide / valid_count)[:, None]
    ).astype(BF16)
    rows_part = jnp.einsum("rv,vd->rd", logit_grad, table_rows, preferred_element_type=F32)
    table_loss_grad = jnp.einsum("rv,rd->vd", logit_grad, rows_all, preferred_element_type=F32)
    table_loss_low, rows_part = lax.optimization_barrier((table_loss_grad.astype(BF16), rows_part))
    rows_grad = scatter_columns(rows_part, rows, cols, 6)
    table_loss_mine = lax.psum_scatter(table_loss_low, "row", scatter_dimension=1, tiled=True)
    equal = pos_col == positions[None, :]
    numbers = jnp.arange(count_rows, dtype=jnp.int32)
    again = jnp.any(equal & (numbers[None, :] < numbers[:, None]), axis=1)
    adds = jnp.where(again[:, None], 0.0, equal.astype(F32))
    final_grad = jnp.dot(adds, rows_grad, precision=highest)
    _, final_norm_back = jax.vjp(rms_gain, hidden_two, gain_rows[2])
    hidden_two_grad, gain_final_grad = final_norm_back(final_grad)
    down_in = hidden_two_grad.astype(BF16)
    like = (rows, nblocks, depth, BLOCK_COLS)
    gate_up_grad = project_act_back(
        down_in, gate_val, up_val, gathered, block_owner, down_at, down_blocks
    )
    hidden_one_grad, branch_grad_low, gain_ff_grad = back_through_norm(
        gate_up_grad,
        gathered,
        block_owner,
        gate_at,
        gate_blocks,
        jnp.zeros((count_rows, D), F32),
        hidden_one,
        gain_rows[1],
        hidden_two_grad,
    )
    branch_out_grad = project(branch_grad_low, gathered, block_owner, branch_at, branch_blocks)

    in_grad_low, sums, ends, mixer_vectors = ssm_backward(
        last_docs,
        both_proj,
        near,
        conv_rows,
        gain_row,
        act_xbc,
        slope,
        *times,
        states,
        scan_out,
        spread_rows(branch_out_grad[:, :SSM_INNER]),
    )
    in_grad_low = attention_backward(
        both_proj, *picked_in, branch_out_grad, place, in_grad_low
    )
    sum_y, sum_x, sum_k = (
        sums[:, at : at + SSM_HEADS] for at in (0, LANES, LANES + SSM_HEADS)
    )
    skip_grad = jnp.sum(sum_k, axis=0)
    cum_grad = sum_y.reshape(chunks, CHUNK, SSM_HEADS)
    decays_grad = jnp.einsum("ts,cth->csh", earlier, cum_grad, precision=highest)
    decays_grad = decays_grad + jnp.sum(ends, axis=1)[:, None, :SSM_HEADS]
    time_grad, time_bias_grad, decay_log_grad = steps_back(
        (sum_x, decays_grad.reshape(length, SSM_HEADS))
    )
    time_grad_low = time_grad.astype(BF16)
    grad_time = jnp.einsum("td,th->dh", normed, time_grad_low, preferred_element_type=F32)
    time_part = jnp.einsum("th,dh->td", time_grad_low, time_low, preferred_element_type=F32)
    _, embed_grad, gain_in_grad = back_through_norm(
        in_grad_low[None],
        gathered,
        block_owner,
        0,
        in_blocks,
        time_part,
        embedded,
        gain_rows[0],
        spread_rows(hidden_one_grad),
    )
    placed = (jnp.arange(length, dtype=jnp.int32)[:, None] == token_place[None, :]).astype(BF16)
    embed_sorted = jnp.dot(placed, embed_grad, preferred_element_type=F32).astype(BF16)
    embed_sorted, table_loss_mine, down_in, normed_two, branch_grad_low, normed = (
        lax.optimization_barrier(
            (embed_sorted, table_loss_mine, down_in, normed_two, branch_grad_low, normed)
        )
    )
    early, late = exchange_rows(embed_sorted, rows)
    grad_slots = weight_grad(down_in, act_low[None], block_owner, down_at, like, None)
    grad_slots = weight_grad(normed_two, gate_up_grad, block_owner, gate_at, like, grad_slots)
    early_tokens = lax.all_gather(early, "col", axis=0, tiled=True)
    grad_slots = weight_grad(
        branch_grad_low, branch_in[None], block_owner, branch_at, like, grad_slots
    )
    grad_slots = weight_grad(normed, in_grad_low[None], block_owner, 0, like, grad_slots)
    early_tokens, late, grad_slots = lax.optimization_barrier((early_tokens, late, grad_slots))
    vector_grad = jnp.concatenate(
        [
            mixer_vectors[:CONV].reshape(-1),
            mixer_vectors[CONV],
            time_bias_grad,
            decay_log_grad,
            skip_grad,
            mixer_vectors[CONV + 1, :SSM_INNER],
            gain_in_grad[0],
            gain_ff_grad[0],
            gain_final_grad,
            grad_time.reshape(-1),
            jnp.sum(own_loss)[None],
        ]
    )
    nvec = vector_params.shape[0]
    packed_len = -(-(nvec + 1) // (8 * LANES)) * 8 * LANES
    to_sum = jnp.pad(vector_grad, (0, packed_len - nvec - 1)).reshape(-1, LANES)
    grad_whole, late_tokens, summed = tail_exchange(grad_slots, late, to_sum, rows, cols, 1)
    summed = summed.reshape(-1)
    vector_total, loss_sum = summed[:nvec], summed[nvec]
    table_input_grad = rows_by_token(
        sorted_all - col_index * shard_rows, (early_tokens, late_tokens), shard_rows, length
    )
    table_grad = table_loss_mine[:shard_rows].astype(F32) + table_input_grad
    grad_mine_wide = lax.dynamic_index_in_dim(grad_whole, row_index, 0, False).astype(F32)
    square_part = jnp.sum(grad_mine_wide * grad_mine_wide) + jnp.sum(table_grad * table_grad)
    square_total = total_over_all(jnp.full((8, LANES), square_part), rows, cols, 0)[0, 0]
    rotated = rotate_blocks(left_basis, grad_whole, right_basis)
    mean_loss = loss_sum / valid_count
    grad_norm = jnp.sqrt(square_total + jnp.sum(vector_total * vector_total))
    clip_scale = jnp.minimum(1.0, clip_limit / (grad_norm + 1e-06))
    steps_done = step_count[0].astype(F32)
    scales = jnp.stack(
        [clip_scale, 1.0 - soap_first**steps_done, 1.0 - soap_second**steps_done]
    )
    first_new, second_new, partial_update = step_blocks(
        scales, rotated, block_first, block_second, left_basis, right_basis
    )
    update = lax.psum_scatter(
        partial_update, "row", scatter_dimension=1, tiled=True
    ).astype(F32)
    new_blocks = block_weights - learn_rate * (update + weight_decay * block_weights)
    new_table, table_first_new, table_second_new = adam_step(
        table,
        table_grad * clip_scale,
        table_first,
        table_second,
        steps_done,
        weight_decay,
        learn_rate,
    )
    new_vectors, vector_first_new, vector_second_new = adam_step(
        vector_params,
        vector_total * clip_scale,
        vector_first,
        vector_second,
        steps_done,
        0.0,
        vector_rate,
    )
    return (
        mean_loss,
        grad_norm,
        new_blocks,
        first_new,
        second_new,
        new_table,
        table_first_new,
        table_second_new,
        new_vectors,
        vector_first_new,
        vector_second_new,
    )


def solution(mesh):
    rows, cols = mesh.shape["row"], mesh.shape["col"]
    placed = (
        P(("row", "col"), None),
        P(("row", "col"), None),
        P(("row", "col"), None),
        P(("row", "col"), None),
        P(("row", "col"), None),
        P(),
        P(),
        P("col", "row", None),
        P("col", "row", None),
        P("col", "row", None),
        P("col", "row", None),
        P("col", None, None),
        P("col", "row"),
        P("col", "row"),
        P("col", "row"),
        P(),
        P(),
        P(),
    )
    return jax.shard_map(
        functools.partial(body, rows, cols),
        mesh=mesh,
        in_specs=placed,
        out_specs=(
            P(),
            P(),
            P("col", "row", None),
            P("col", "row", None),
            P("col", "row", None),
            P("col", "row"),
            P("col", "row"),
            P("col", "row"),
            P(),
            P(),
            P(),
        ),
        check_vma=False,
    )
```

```python
import functools

import jax
import jax.numpy as jnp
from jax import lax
from jax.experimental import pallas as pl
from jax.experimental.pallas import tpu as pltpu
from jax.sharding import PartitionSpec as P

D = 1024
HEADS = 8
KV_HEADS = 2
HEAD_DIM = 64
SSM_HEADS = 24
SSM_HEAD_DIM = 64
STATE = 128
CONV = 4
FF = 2048
BLOCK_COLS = 256
SSM_INNER = 1536
XBC_WIDTH = 1792
CHUNK = 128
QROWS = 256
LANES = 128
NO_TOKEN = 1 << 30
LISTS = 8
TABLE_PARTS = 4
PAD_ROWS = 16 * TABLE_PARTS
GROUP = 4
ROW_PART = 64

BF16 = jnp.bfloat16
F32 = jnp.float32
MESH = pl.DeviceIdType.MESH
highest = lax.Precision.HIGHEST
rope_base = 100000000000.0
clip_limit = 1.0
learn_rate = 0.01
vector_rate = 0.08
weight_decay = 0.1
soap_first = 0.95
soap_second = 0.95
adam_first = 0.9
adam_second = 0.95
adam_eps = 1e-08
vmem_bytes = 56 * 1024 * 1024


def params(**more):
    return pltpu.CompilerParams(vmem_limit_bytes=vmem_bytes, **more)


def cost(flops, nbytes, exps=0):
    return pl.CostEstimate(flops=int(flops), bytes_accessed=int(nbytes), transcendentals=int(exps))


def rms_gain(values, gain_vec):
    inv_scale = lax.rsqrt(jnp.mean(values * values, axis=-1, keepdims=True) + 1e-05)
    return values * inv_scale * gain_vec


def unpack(flattened):
    piece_sizes = [
        CONV * XBC_WIDTH,
        XBC_WIDTH,
        SSM_HEADS,
        SSM_HEADS,
        SSM_HEADS,
        SSM_INNER,
        3 * D,
        D * SSM_HEADS,
    ]
    pieces = []
    offset = 0
    for length in piece_sizes:
        pieces.append(flattened[offset : offset + length])
        offset = offset + length
    return pieces


def dot_nt(left, right):
    return lax.dot_general(left, right, (((1,), (1,)), ((), ())), preferred_element_type=F32)


def dot_tn(left, right):
    return lax.dot_general(left, right, (((0,), (0,)), ((), ())), preferred_element_type=F32)


def dot_nn(left, right):
    return jnp.dot(left, right, preferred_element_type=F32)


def slot_spec(gathered, at, every):
    rows, _, depth, _ = gathered.shape
    return pl.BlockSpec(
        (rows, 1, depth, BLOCK_COLS), lambda k, own: (0, own[at + every * k], 0, 0)
    )


def whole(shape):
    return pl.BlockSpec(shape, lambda k, own: (0,) * len(shape))


def block_of(w_ref):
    return w_ref[...].reshape(D, BLOCK_COLS)


def slot_call(kernel, owner, steps, in_specs, out_specs, out_shape, flops, operands):
    nbytes = sum(o.size * o.dtype.itemsize for o in operands[:1])
    return pl.pallas_call(
        kernel,
        grid_spec=pltpu.PrefetchScalarGridSpec(
            num_scalar_prefetch=1, grid=(steps,), in_specs=in_specs, out_specs=out_specs
        ),
        out_shape=out_shape,
        compiler_params=params(),
        cost_estimate=cost(flops, flops // 512 + nbytes),
    )(owner, *operands)


def cols_of(k):
    return slice(k * BLOCK_COLS, (k + 1) * BLOCK_COLS)


def project_kernel(own_ref, x_ref, *rest):
    o_ref = rest[-1]
    for g, w_ref in enumerate(rest[:-1]):
        o_ref[:, cols_of(g)] = dot_nn(x_ref[...], block_of(w_ref))


def project(rows_in, gathered, owner, first, count):
    length = rows_in.shape[0]
    return slot_call(
        project_kernel,
        owner,
        count // GROUP,
        [whole((length, D))] + [slot_spec(gathered, first + g, GROUP) for g in range(GROUP)],
        pl.BlockSpec((length, GROUP * BLOCK_COLS), lambda k, own: (0, k)),
        jax.ShapeDtypeStruct((length, count * BLOCK_COLS), F32),
        2 * length * D * BLOCK_COLS * count,
        [rows_in] + [gathered] * GROUP,
    )


def sigmoid(values):
    return 0.5 + 0.5 * jnp.tanh(0.5 * values)


def gate_up_kernel(own_ref, x_ref, *rest):
    w_refs, (gate_ref, up_ref, act_ref) = rest[:-3], rest[-3:]
    half = len(w_refs) // 2
    for g in range(half):
        gate = dot_nn(x_ref[...], block_of(w_refs[g]))
        up = dot_nn(x_ref[...], block_of(w_refs[half + g]))
        gate_ref[:, cols_of(g)] = gate
        up_ref[:, cols_of(g)] = up
        act_ref[:, cols_of(g)] = (gate * sigmoid(gate) * up).astype(BF16)


def project_gate_up(rows_in, gathered, owner, first, count):
    length = rows_in.shape[0]
    pairs = GROUP // 2
    wide = pl.BlockSpec((length, pairs * BLOCK_COLS), lambda k, own: (0, k))
    shapes = [jax.ShapeDtypeStruct((length, count * BLOCK_COLS), t) for t in (F32, F32, BF16)]
    return slot_call(
        gate_up_kernel,
        owner,
        count // pairs,
        [whole((length, D))]
        + [slot_spec(gathered, first + g, pairs) for g in range(pairs)]
        + [slot_spec(gathered, first + count + g, pairs) for g in range(pairs)],
        [wide] * 3,
        shapes,
        4 * length * D * BLOCK_COLS * count,
        [rows_in] + [gathered] * (2 * pairs),
    )


def act_back_kernel(own_ref, x_ref, gate_ref, up_ref, *rest):
    o_ref = rest[-1]
    for g, w_ref in enumerate(rest[:-1]):
        act_grad = dot_nn(x_ref[...], block_of(w_ref))
        gate, up = gate_ref[:, cols_of(g)], up_ref[:, cols_of(g)]
        sig = sigmoid(gate)
        silu = gate * sig
        o_ref[0, :, cols_of(g)] = (act_grad * up * (sig + silu * (1.0 - sig))).astype(BF16)
        o_ref[1, :, cols_of(g)] = (act_grad * silu).astype(BF16)


def project_act_back(rows_in, gate, up, gathered, owner, first, count):
    length = rows_in.shape[0]
    pairs = GROUP // 2
    wide = pl.BlockSpec((length, pairs * BLOCK_COLS), lambda k, own: (0, k))
    return slot_call(
        act_back_kernel,
        owner,
        count // pairs,
        [whole((length, D)), wide, wide]
        + [slot_spec(gathered, first + g, pairs) for g in range(pairs)],
        pl.BlockSpec((2, length, pairs * BLOCK_COLS), lambda k, own: (0, 0, k)),
        jax.ShapeDtypeStruct((2, length, count * BLOCK_COLS), BF16),
        2 * length * D * BLOCK_COLS * count,
        [rows_in, gate, up] + [gathered] * pairs,
    )


def add_products(c_refs, w_refs, o_ref):
    cols = [c_ref[...].reshape(-1, c_ref.shape[-1]) for c_ref in c_refs]
    cols = cols[0] if len(cols) == 1 else jnp.concatenate(cols, axis=1)
    o_ref[...] += dot_nt(cols, jnp.concatenate([block_of(w) for w in w_refs], axis=1))


def row_parts(length):
    return [slice(i, i + ROW_PART) for i in range(0, length, ROW_PART)]


def back_norm_kernel(own_ref, c_ref, *rest):
    w_refs, (base_ref, gain_ref, o_ref, n_ref) = rest[:-4], rest[-4:]

    @pl.when(pl.program_id(0) == 0)
    def _():
        o_ref[...] = base_ref[...].astype(F32)

    add_products([c_ref], w_refs, o_ref)

    @pl.when(pl.program_id(0) == pl.num_programs(0) - 1)
    def _():
        for part in row_parts(o_ref.shape[0]):
            n_ref[part, :] = rms_gain(o_ref[part, :], gain_ref[...]).astype(BF16)


def back_then_norm(cols_in, gathered, owner, first, count, base, gain):
    length = cols_in.shape[0]
    return slot_call(
        back_norm_kernel,
        owner,
        count // GROUP,
        [pl.BlockSpec((length, GROUP * BLOCK_COLS), lambda k, own: (0, k))]
        + [slot_spec(gathered, first + g, GROUP) for g in range(GROUP)]
        + [whole((length, D)), whole((1, D))],
        [whole((length, D))] * 2,
        [jax.ShapeDtypeStruct((length, D), t) for t in (F32, BF16)],
        2 * length * D * BLOCK_COLS * count,
        [cols_in] + [gathered] * GROUP + [base, gain.reshape(1, D)],
    )


def back_grad_kernel(parts, own_ref, *rest):
    c_refs, rest = rest[:parts], rest[parts:]
    w_refs, rest = rest[:-8], rest[-8:]
    start_ref, x_ref, gain_ref, more_ref, o_ref, low_ref, dgain_ref, total = rest

    @pl.when(pl.program_id(0) == 0)
    def _():
        total[...] = start_ref[...]

    add_products(c_refs, w_refs, total)

    @pl.when(pl.program_id(0) == pl.num_programs(0) - 1)
    def _():
        dgain = jnp.zeros((1, D), F32)
        for part in row_parts(total.shape[0]):
            x, grad = x_ref[part, :].astype(F32), total[part, :]
            inv = lax.rsqrt(jnp.mean(x * x, axis=-1, keepdims=True) + 1e-05)
            unit = x * inv
            dgain += jnp.sum(grad * unit, axis=0, keepdims=True)
            scaled = grad * gain_ref[...]
            back = inv * (scaled - unit * jnp.mean(scaled * unit, axis=-1, keepdims=True))
            result = more_ref[part, :] + back
            o_ref[part, :] = result
            low_ref[part, :] = result.astype(BF16)
        dgain_ref[...] = dgain


def back_through_norm(cols_in, gathered, owner, first, count, start, x, gain, more):
    parts, length, _ = cols_in.shape
    group = GROUP // parts
    every = count // parts
    return pl.pallas_call(
        functools.partial(back_grad_kernel, parts),
        grid_spec=pltpu.PrefetchScalarGridSpec(
            num_scalar_prefetch=1,
            grid=(every // group,),
            in_specs=[
                pl.BlockSpec(
                    (1, length, group * BLOCK_COLS), lambda k, own, part=part: (part, 0, k)
                )
                for part in range(parts)
            ]
            + [
                slot_spec(gathered, first + part * every + g, group)
                for part in range(parts)
                for g in range(group)
            ]
            + [whole((length, D)), whole((length, D)), whole((1, D)), whole((length, D))],
            out_specs=[whole((length, D)), whole((length, D)), whole((1, D))],
            scratch_shapes=[pltpu.VMEM((length, D), F32)],
        ),
        out_shape=[
            jax.ShapeDtypeStruct((length, D), F32),
            jax.ShapeDtypeStruct((length, D), BF16),
            jax.ShapeDtypeStruct((1, D), F32),
        ],
        compiler_params=params(),
        cost_estimate=cost(
            2 * length * D * BLOCK_COLS * count, count * BLOCK_COLS * (2 * D + 2 * length)
        ),
    )(owner, *[cols_in] * parts, *[gathered] * GROUP, start, x, gain.reshape(1, D), more)


def wgrad_kernel(own_ref, l_ref, r_ref, *rest):
    o_ref, turned = rest[-2], rest[-1]

    @pl.when(pl.program_id(0) == 0)
    def _():
        turned[...] = l_ref[...].T

    grad = dot_nn(turned[...], r_ref[0])
    o_ref[...] = grad.astype(BF16).reshape(o_ref.shape)


def weight_grad(left_rows, right_cols, owner, first, like, into):
    rows, nslots, depth, _ = like
    length = left_rows.shape[0]
    each = right_cols.shape[2] // BLOCK_COLS
    count = right_cols.shape[0] * each
    in_specs = [
        pl.BlockSpec((length, D), lambda k, own: (0, 0)),
        pl.BlockSpec((1, length, BLOCK_COLS), lambda k, own: (k // each, 0, k % each)),
    ]
    operands = [owner, left_rows, right_cols]
    aliases = {}
    if into is not None:
        in_specs.append(pl.BlockSpec(memory_space=pl.ANY))
        operands.append(into)
        aliases = {3: 0}
    return pl.pallas_call(
        wgrad_kernel,
        grid_spec=pltpu.PrefetchScalarGridSpec(
            num_scalar_prefetch=1,
            grid=(count,),
            in_specs=in_specs,
            out_specs=pl.BlockSpec(
                (rows, 1, depth, BLOCK_COLS), lambda k, own: (0, own[first + k], 0, 0)
            ),
            scratch_shapes=[pltpu.VMEM((D, length), BF16)],
        ),
        out_shape=jax.ShapeDtypeStruct(like, BF16),
        input_output_aliases=aliases,
        compiler_params=params(),
        cost_estimate=cost(
            2 * length * D * BLOCK_COLS * count, count * BLOCK_COLS * (2 * D + 2 * length)
        ),
    )(*operands)


def embed_kernel(x_ref, gain_ref, e_ref, n_ref):
    rows = jnp.concatenate([x_ref[r] for r in range(x_ref.shape[0])], axis=1)
    e_ref[...] = rows
    n_ref[...] = rms_gain(rows.astype(F32), gain_ref[...]).astype(BF16)


def embed_and_norm(column_parts, gain):
    parts, length, width = column_parts.shape
    step = 2 * CHUNK
    return pl.pallas_call(
        embed_kernel,
        grid=(length // step,),
        in_specs=[
            pl.BlockSpec((parts, step, width), lambda i: (0, i, 0)),
            pl.BlockSpec((1, D), lambda i: (0, 0)),
        ],
        out_specs=[pl.BlockSpec((step, D), lambda i: (i, 0))] * 2,
        out_shape=[jax.ShapeDtypeStruct((length, D), BF16)] * 2,
        compiler_params=params(),
        cost_estimate=cost(8 * length * D, 6 * length * D),
    )(column_parts, gain.reshape(1, D))


def rope_tables(length):
    half_dim = HEAD_DIM // 2
    frequency = rope_base ** (-jnp.arange(half_dim, dtype=F32) * 2.0 / HEAD_DIM)
    angles = jnp.arange(length, dtype=F32)[:, None] * frequency[None, :]
    cosine, sine = jnp.cos(angles), jnp.sin(angles)
    wide_cos = jnp.concatenate([cosine] * 4, axis=1)
    wide_sin = jnp.concatenate([-sine, sine, -sine, sine], axis=1)
    return wide_cos, wide_sin


def lane_iota():
    return lax.broadcasted_iota(jnp.int32, (1, LANES), 1)


def swap_halves(values):
    low_half = (lane_iota() % HEAD_DIM) < HEAD_DIM // 2
    return jnp.where(
        low_half,
        pltpu.roll(values, LANES - HEAD_DIM // 2, 1),
        pltpu.roll(values, HEAD_DIM // 2, 1),
    )


def turn(values, cosine, sine):
    return values * cosine + swap_halves(values) * sine


def turn_back(values, cosine, sine):
    return values * cosine - swap_halves(values) * sine


def doubled(values, group):
    moved = pltpu.roll(values, HEAD_DIM, 1)
    keep = (lane_iota() < HEAD_DIM) == (group == 0)
    return jnp.where(keep, values, moved)


def attention_probs(query, key, allowed):
    scores = jnp.where(allowed, dot_nt(query, key), -1e30)
    row_top = jnp.max(scores, axis=-1, keepdims=True)
    weights = jnp.exp(scores - row_top)
    return weights, jnp.sum(weights, axis=-1, keepdims=True)


def halves(values):
    high = values.astype(BF16).astype(F32)
    return high, values - high


def fold(values):
    return values + pltpu.roll(values, HEAD_DIM, 1)


def head_operands(values):
    low = lane_iota() < HEAD_DIM
    high, rest = halves(values)
    high_moved, rest_moved = pltpu.roll(high, HEAD_DIM, 1), pltpu.roll(rest, HEAD_DIM, 1)
    head_a = [jnp.where(low, high, rest_moved), jnp.where(low, high, 0.0)]
    head_b = [jnp.where(low, high_moved, rest), jnp.where(low, high_moved, 0.0)]
    return [jnp.concatenate(h, axis=1).astype(BF16) for h in (head_a, head_b)]


def group_operands(values):
    low = lane_iota() < HEAD_DIM
    high, rest = halves(values)
    inner = jnp.concatenate([high, rest], axis=1).astype(BF16)
    return inner, jnp.where(low, high, rest).astype(BF16)


def picked_queries(pos_ref, q_ref, cos_ref, sin_ref, rows):
    count = rows.shape[1]
    for i in range(count):
        at = pl.ds(pos_ref[i], 1)
        for k, ref in enumerate((q_ref, cos_ref, sin_ref)):
            rows[k, i : i + 1, :] = ref[at, :]
    cosine, sine = rows[1], rows[2]
    turned = turn(rows[0], cosine, sine) * HEAD_DIM ** (-0.5)
    return jnp.concatenate(head_operands(turned), axis=0), cosine, sine


def picked_mask(pos_col_ref, seg_col_ref, segr_ref):
    positions = lax.broadcasted_iota(jnp.int32, (1, segr_ref.shape[1]), 1)
    allowed = (seg_col_ref[...] == segr_ref[...]) & (pos_col_ref[...] >= positions)
    return jnp.concatenate([allowed.astype(F32)] * 2, axis=0) > 0.5


def attn_fwd_kernel(
    pos_ref, q_ref, k_ref, v_ref, pos_col_ref, seg_col_ref, segr_ref, cos_ref, sin_ref, o_ref, rows
):
    group = pl.program_id(0) // 2
    low = lane_iota() < HEAD_DIM
    count = o_ref.shape[0]
    query, _, _ = picked_queries(pos_ref, q_ref, cos_ref, sin_ref, rows)
    key, _ = group_operands(doubled(turn(k_ref[...], cos_ref[...], sin_ref[...]), group))
    _, value = group_operands(doubled(v_ref[...], group))
    allowed = picked_mask(pos_col_ref, seg_col_ref, segr_ref)
    weights, total = attention_probs(query, key, allowed)
    high, rest = split(weights)
    out = fold(dot_nn(high, value) + dot_nn(rest, value)) / total
    o_ref[...] = jnp.where(low, out[:count], out[count:]).astype(BF16)


def attn_bwd_kernel(
    pos_ref, q_ref, k_ref, v_ref, pos_col_ref, seg_col_ref, segr_ref, cos_ref, sin_ref, g_ref,
    place_ref, into_ref, o_ref, rows, dk_s, dv_s,
):
    step = pl.program_id(0)
    pairs = HEADS // 2
    low = lane_iota() < HEAD_DIM

    @pl.when(step == 0)
    def _():
        dk_s[...] = jnp.zeros_like(dk_s)
        dv_s[...] = jnp.zeros_like(dv_s)

    @pl.when(step < pairs)
    def _():
        group = step // 2
        count = g_ref.shape[0]
        query, cosine, sine = picked_queries(pos_ref, q_ref, cos_ref, sin_ref, rows)
        grad = jnp.concatenate(head_operands(g_ref[...]), axis=0)
        key, key_out = group_operands(doubled(turn(k_ref[...], cos_ref[...], sin_ref[...]), group))
        value, _ = group_operands(doubled(v_ref[...], group))
        allowed = picked_mask(pos_col_ref, seg_col_ref, segr_ref)
        weights, total = attention_probs(query, key, allowed)
        probs = weights * (1.0 / total)
        dprobs = dot_nt(grad, value)
        delta = jnp.sum(probs * dprobs, axis=-1, keepdims=True)
        dscores = jnp.concatenate(split(probs * (dprobs - delta)), axis=0)
        dq = fold(dot_nn(dscores[: 2 * count], key_out) + dot_nn(dscores[2 * count :], key_out))
        dq = jnp.where(low, dq[:count], dq[count:]) * HEAD_DIM ** (-0.5)
        dq_low = turn_back(dq, cosine, sine).astype(BF16)
        o_ref[...] = dot_nn(place_ref[...], dq_low).astype(BF16)
        inner_q, inner_g = query[:, :LANES], grad[:, :LANES]
        dv_s[group] += dot_tn(
            jnp.concatenate(split(probs), axis=0), jnp.concatenate([inner_g, inner_g], axis=0)
        )
        dk_s[group] += dot_tn(dscores, jnp.concatenate([inner_q, inner_q], axis=0))

    @pl.when(step == pairs)
    def _():
        dk = jnp.where(low, fold(dk_s[0]), fold(dk_s[1]))
        o_ref[...] = turn_back(dk, cos_ref[...], sin_ref[...]).astype(BF16)

    @pl.when(step == pairs + 1)
    def _():
        o_ref[...] = jnp.where(low, fold(dv_s[0]), fold(dv_s[1])).astype(BF16)


def attention_specs(length, count, base):
    fixed = lambda *shape: pl.BlockSpec(shape, lambda p, pos: (0, 0))
    return [
        pl.BlockSpec((length, LANES), lambda p, pos: (0, base + jnp.minimum(p, 3))),
        pl.BlockSpec((length, LANES), lambda p, pos: (0, base + 4)),
        pl.BlockSpec((length, LANES), lambda p, pos: (0, base + 5)),
        fixed(count, 1),
        fixed(count, 1),
        fixed(1, length),
        fixed(length, LANES),
        fixed(length, LANES),
    ]


def attention_forward(both_proj, positions, pos_col, seg_col, segr, cosine, sine):
    length, count = both_proj.shape[0], positions.shape[0]
    base = (SSM_INNER + XBC_WIDTH) // LANES
    return pl.pallas_call(
        attn_fwd_kernel,
        grid_spec=pltpu.PrefetchScalarGridSpec(
            num_scalar_prefetch=1,
            grid=(HEADS // 2,),
            in_specs=attention_specs(length, count, base),
            out_specs=pl.BlockSpec((count, LANES), lambda p, pos: (0, p)),
            scratch_shapes=[pltpu.VMEM((3, count, LANES), F32)],
        ),
        out_shape=jax.ShapeDtypeStruct((count, HEADS * HEAD_DIM), BF16),
        compiler_params=params(),
        cost_estimate=cost(
            4 * HEADS * count * length * HEAD_DIM, 6 * length * D, HEADS * length * count
        ),
    )(positions, both_proj, both_proj, both_proj, pos_col, seg_col, segr, cosine, sine)


def attention_backward(
    both_proj, positions, pos_col, seg_col, segr, cosine, sine, grads, place, into
):
    length, count = both_proj.shape[0], positions.shape[0]
    base = (SSM_INNER + XBC_WIDTH) // LANES
    at = SSM_INNER // LANES
    pairs = HEADS // 2
    return pl.pallas_call(
        attn_bwd_kernel,
        grid_spec=pltpu.PrefetchScalarGridSpec(
            num_scalar_prefetch=1,
            grid=(pairs + 2,),
            in_specs=attention_specs(length, count, base)
            + [
                pl.BlockSpec((count, LANES), lambda p, pos: (0, at + jnp.minimum(p, 3))),
                pl.BlockSpec((length, count), lambda p, pos: (0, 0)),
                pl.BlockSpec(memory_space=pl.ANY),
            ],
            out_specs=pl.BlockSpec((length, LANES), lambda p, pos: (0, base + p)),
            scratch_shapes=[pltpu.VMEM((3, count, LANES), F32)]
            + [pltpu.VMEM((2, length, LANES), F32)] * 2,
        ),
        out_shape=jax.ShapeDtypeStruct(into.shape, BF16),
        input_output_aliases={11: 0},
        compiler_params=params(),
        cost_estimate=cost(
            10 * HEADS * count * length * HEAD_DIM, 10 * length * D, HEADS * length * count
        ),
    )(positions, both_proj, both_proj, both_proj, pos_col, seg_col, segr, cosine, sine, grads, place, into)


def chunk_masks(segc_ref, segr_ref, last_ref, chunk):
    doc_rows, doc_cols = segc_ref[...], segr_ref[...]
    row_pos = lax.broadcasted_iota(jnp.int32, (CHUNK, CHUNK), 0)
    col_pos = lax.broadcasted_iota(jnp.int32, (CHUNK, CHUNK), 1)
    same = (doc_rows == doc_cols) & (row_pos >= col_pos)
    madd = jnp.where(same, 0.0, -1e30)
    last = last_ref[chunk]
    previous = jnp.where(chunk > 0, last_ref[jnp.maximum(chunk - 1, 0)], -1)
    carried = jnp.where(doc_rows == previous, 1.0, 0.0)
    tail = jnp.where(doc_rows == last, 1.0, 0.0)
    keep = jnp.where(last == previous, 1.0, 0.0)
    return madd, carried, tail, keep


def spread(low, columns, a):
    return jnp.where(low, columns[:, a : a + 1], columns[:, a + 1 : a + 2])


def split(values):
    high = values.astype(BF16)
    return high, (values - high.astype(F32)).astype(BF16)


def wide_split(values):
    return jnp.concatenate(split(values), axis=1)


def both_sides(values):
    return values[:, :LANES] + values[:, LANES:]


def ssm_fwd_kernel(
    last_ref, proj_ref, near_ref, cw_ref, cb_ref, gain_ref, dt_ref, cum_ref, cumt_ref, skip_ref,
    segc_ref, segr_ref, y_ref, s_ref, xbc_ref, slope_ref, mix_ref, state, ext,
):
    chunk = pl.program_id(0)

    @pl.when(chunk == 0)
    def _():
        state[...] = jnp.zeros_like(state)
        ext[:8, :] = jnp.zeros((8, XBC_WIDTH), F32)

    ext[8:, :] = proj_ref[:, SSM_INNER : SSM_INNER + XBC_WIDTH]
    for k in range(XBC_WIDTH // BLOCK_COLS):
        cols = cols_of(k)
        total = ext[8:, cols] * cw_ref[CONV - 1 :, cols] + cb_ref[:, cols]
        for d in range(1, CONV):
            taken = ext[8 - d : 8 - d + CHUNK, cols] * near_ref[:, d : d + 1]
            total += taken * cw_ref[CONV - 1 - d : CONV - d, cols]
        sig = sigmoid(total)
        silu = total * sig
        xbc_ref[:, cols] = silu
        slope_ref[:, cols] = sig + silu * (1.0 - sig)
    ext[:8, :] = ext[CHUNK:, :]
    s_ref[...] = state[...].reshape(s_ref.shape)
    low = lane_iota() < SSM_HEAD_DIM
    madd, carried, tail, keep = chunk_masks(segc_ref, segr_ref, last_ref, chunk)
    dt, cum, cumt = dt_ref[...], cum_ref[...], cumt_ref[...]
    last_cum = cum[CHUNK - 1 : CHUNK, :]
    ecum = jnp.exp(cum) * carried
    tails = jnp.exp(last_cum - cum) * tail
    keeps = jnp.exp(last_cum) * keep
    into = xbc_ref[:, SSM_INNER : SSM_INNER + STATE]
    into_t = into.T
    into_high, into_rest = split(into_t)
    out_high, out_rest = split(xbc_ref[:, SSM_INNER + STATE :])
    out_both = jnp.concatenate([out_high, out_rest], axis=1)
    into_both = jnp.concatenate([into_high, into_rest], axis=1)
    gram = dot_nn(out_both, jnp.concatenate([into_high, into_high], axis=0)) + dot_nn(
        out_high, into_rest
    )
    for p in range(SSM_HEADS // 2):
        a, cols = 2 * p, slice(p * LANES, (p + 1) * LANES)
        heads = xbc_ref[:, cols]
        scaled = heads * spread(low, dt, a)
        decay_a = jnp.exp(cum[:, a : a + 1] - cumt[a : a + 1, :] + madd)
        decay_b = jnp.exp(cum[:, a + 1 : a + 2] - cumt[a + 1 : a + 2, :] + madd)
        mixing = wide_split(jnp.concatenate([decay_a * gram, decay_b * gram], axis=1))
        stacked_wide = wide_split(
            jnp.concatenate([jnp.where(low, scaled, 0.0), jnp.where(low, 0.0, scaled)], axis=0)
        )
        old = state[:, cols]
        old_wide = wide_split(old)
        carry_in = both_sides(dot_nn(out_both, jnp.concatenate([old_wide, old_wide], axis=0)))
        y_ref[:, cols] = (
            both_sides(dot_nn(mixing, jnp.concatenate([stacked_wide, stacked_wide], axis=0)))
            + spread(low, ecum, a) * carry_in
            + spread(low, skip_ref[...], a) * heads
        )
        tail_in = wide_split(scaled * spread(low, tails, a))
        fresh = both_sides(dot_nn(into_both, jnp.concatenate([tail_in, tail_in], axis=0)))
        state[:, cols] = spread(low, keeps, a) * old + fresh
    squares = jnp.zeros((CHUNK, 1), F32)
    for k in range(SSM_INNER // BLOCK_COLS):
        gate = proj_ref[:, cols_of(k)]
        gated = y_ref[:, cols_of(k)] * (gate * sigmoid(gate))
        squares += jnp.sum(gated * gated, axis=-1, keepdims=True)
    inv = lax.rsqrt(squares / SSM_INNER + 1e-05)
    for k in range(SSM_INNER // BLOCK_COLS):
        gate = proj_ref[:, cols_of(k)]
        gated = y_ref[:, cols_of(k)] * (gate * sigmoid(gate))
        mix_ref[:, cols_of(k)] = (gated * inv * gain_ref[:, cols_of(k)]).astype(BF16)


def ssm_bwd_kernel(
    last_ref, proj_ref, near_ref, cw_ref, gain_ref, xbc_ref, slope_ref, dt_ref, cum_ref, cumt_ref,
    skip_ref, segc_ref, segr_ref, s_ref, n_ref, y_ref, out_ref, grad_ref, sums_ref, ends_ref,
    vec_ref, dstate, g_ref, dext,
):
    chunk = pl.num_programs(0) - 1 - pl.program_id(0)

    @pl.when(pl.program_id(0) == 0)
    def _():
        dstate[...] = jnp.zeros_like(dstate)
        dext[CHUNK:, :] = jnp.zeros((8, XBC_WIDTH), F32)
        vec_ref[...] = jnp.zeros_like(vec_ref)

    squares = jnp.zeros((CHUNK, 1), F32)
    along = jnp.zeros((CHUNK, 1), F32)
    for k in range(SSM_INNER // BLOCK_COLS):
        cols = cols_of(k)
        gate = proj_ref[:, cols]
        gated = y_ref[:, cols] * (gate * sigmoid(gate))
        squares += jnp.sum(gated * gated, axis=-1, keepdims=True)
        along += jnp.sum(gated * out_ref[:, cols] * gain_ref[:, cols], axis=-1, keepdims=True)
    inv = lax.rsqrt(squares / SSM_INNER + 1e-05)
    along = along * inv / SSM_INNER
    for k in range(SSM_INNER // BLOCK_COLS):
        cols = cols_of(k)
        gate = proj_ref[:, cols]
        sig = sigmoid(gate)
        silu = gate * sig
        unit = y_ref[:, cols] * silu * inv
        vec_ref[5:6, cols] += jnp.sum(out_ref[:, cols] * unit, axis=0, keepdims=True)
        gated_grad = inv * (out_ref[:, cols] * gain_ref[:, cols] - unit * along)
        g_ref[:, cols] = gated_grad * silu
        gate_grad = gated_grad * y_ref[:, cols] * (sig + silu * (1.0 - sig))
        grad_ref[:, cols] = gate_grad.astype(BF16)
    low = lane_iota() < SSM_HEAD_DIM
    madd, carried, tail, keep = chunk_masks(segc_ref, segr_ref, last_ref, chunk)
    dt, cum, cumt = dt_ref[...], cum_ref[...], cumt_ref[...]
    last_cum = cum[CHUNK - 1 : CHUNK, :]
    ecum = jnp.exp(cum) * carried
    tails = jnp.exp(last_cum - cum) * tail
    keeps = jnp.exp(last_cum) * keep
    into, into_rest = split(xbc_ref[:, SSM_INNER : SSM_INNER + STATE])
    outof, outof_rest = split(xbc_ref[:, SSM_INNER + STATE :])
    outof_t = outof.T
    into_both = jnp.concatenate([into, into_rest], axis=1)
    gram = dot_nt(
        jnp.concatenate([outof, outof_rest], axis=1), jnp.concatenate([into, into], axis=1)
    ) + dot_nt(outof, into_rest)
    dgram = jnp.zeros((CHUNK, CHUNK), F32)
    d_into = jnp.zeros((CHUNK, STATE), F32)
    d_outof = jnp.zeros((CHUNK, STATE), F32)
    sum_y = jnp.zeros((CHUNK, LANES), F32)
    sum_xk = jnp.zeros((CHUNK, LANES), F32)
    ends = jnp.zeros((8, LANES), F32)
    lane_pos = lax.broadcasted_iota(jnp.int32, (LANES, LANES), 0) // SSM_HEAD_DIM
    head_pos = lax.broadcasted_iota(jnp.int32, (LANES, LANES), 1)

    def by_head(values, pick):
        high = values.astype(BF16)
        rest = (values - high.astype(F32)).astype(BF16)
        return dot_nn(jnp.concatenate([high, rest], axis=1), pick)

    for p in range(SSM_HEADS // 2):
        a, cols = 2 * p, slice(p * LANES, (p + 1) * LANES)
        pick = jnp.where(lane_pos + a == head_pos, 1.0, 0.0).astype(BF16)
        pick_next = jnp.where(lane_pos + a + SSM_HEADS == head_pos, 1.0, 0.0).astype(BF16)
        pick_two = jnp.concatenate([pick, pick_next], axis=0)
        pick = jnp.concatenate([pick, pick], axis=0)
        heads, grad = xbc_ref[:, cols], g_ref[:, cols]
        dt_wide = spread(low, dt, a)
        skip_wide = spread(low, skip_ref[...], a)
        tail_wide = spread(low, tails, a)
        keep_wide = spread(low, keeps, a)
        scaled = heads * dt_wide
        scaled_low = scaled.astype(BF16)
        decay_a = jnp.exp(cum[:, a : a + 1] - cumt[a : a + 1, :] + madd)
        decay_b = jnp.exp(cum[:, a + 1 : a + 2] - cumt[a + 1 : a + 2, :] + madd)
        grads = wide_split(
            jnp.concatenate([jnp.where(low, grad, 0.0), jnp.where(low, 0.0, grad)], axis=0)
        )
        dmix = dot_nt(grads, jnp.concatenate([scaled_low, scaled_low], axis=1))
        dgram += decay_a * dmix[:CHUNK] + decay_b * dmix[CHUNK:]
        mixing = split(jnp.concatenate([decay_a * gram, decay_b * gram], axis=0))
        d_new = dstate[:, cols]
        d_new_wide = wide_split(d_new)
        d_new_low = d_new_wide[:, :LANES]
        d_inner = dot_tn(jnp.concatenate(mixing, axis=0), jnp.concatenate([grads, grads], axis=0))
        d_scaled = both_sides(d_inner) + tail_wide * both_sides(
            dot_nn(into_both, jnp.concatenate([d_new_wide, d_new_wide], axis=0))
        )
        old = s_ref[0, :, cols]
        d_carry = (spread(low, ecum, a) * grad).astype(BF16)
        d_outof += dot_nt(d_carry, old.astype(BF16))
        d_into += dot_nt((scaled * tail_wide).astype(BF16), d_new_low)
        ends += jnp.sum((d_new * n_ref[0, :, cols]).reshape(STATE // 8, 8, LANES), axis=0) @ pick[
            :LANES
        ].astype(F32)
        dstate[:, cols] = keep_wide * d_new + dot_nn(outof_t, d_carry)
        dext[:CHUNK, cols] = (d_scaled * dt_wide + skip_wide * grad) * slope_ref[:, cols]
        both = grad * heads
        sum_y += by_head(grad * y_ref[:, cols] - skip_wide * both - scaled * d_scaled, pick)
        pair = jnp.concatenate([heads * d_scaled, both], axis=1).astype(BF16)
        sum_xk += dot_nn(pair, pick_two)
    dgram_low = dgram.astype(BF16)
    cols = slice(SSM_INNER, SSM_INNER + STATE)
    dext[:CHUNK, cols] = (d_into + dot_tn(dgram_low, outof)) * slope_ref[:, cols]
    cols = slice(SSM_INNER + STATE, XBC_WIDTH)
    dext[:CHUNK, cols] = (d_outof + dot_nn(dgram_low, into)) * slope_ref[:, cols]
    for k in range(XBC_WIDTH // BLOCK_COLS):
        cols = cols_of(k)
        at = slice(SSM_INNER + k * BLOCK_COLS, SSM_INNER + (k + 1) * BLOCK_COLS)
        before = proj_ref[:, at]
        here = dext[:CHUNK, cols]
        total = here * cw_ref[CONV - 1 :, cols]
        vec_ref[CONV - 1 : CONV, cols] += jnp.sum(here * before, axis=0, keepdims=True)
        vec_ref[CONV : CONV + 1, cols] += jnp.sum(here, axis=0, keepdims=True)
        for d in range(1, CONV):
            later = dext[d : d + CHUNK, cols] * near_ref[:, CONV + d : CONV + d + 1]
            total += later * cw_ref[CONV - 1 - d : CONV - d, cols]
            vec_ref[CONV - 1 - d : CONV - d, cols] += jnp.sum(later * before, axis=0, keepdims=True)
        grad_ref[:, at] = total.astype(BF16)
    dext[CHUNK:, :] = dext[:8, :]
    sums_ref[:, :LANES] = sum_y
    sums_ref[:, LANES:] = sum_xk
    ends_ref[...] = ends.reshape(ends_ref.shape)


def scan_specs(at):
    here = lambda i, last: (at(i), 0)
    across = lambda i, last: (0, at(i))
    return dict(
        rows=lambda width: pl.BlockSpec((CHUNK, width), here),
        cols=lambda height: pl.BlockSpec((height, CHUNK), across),
        fixed=lambda *shape: pl.BlockSpec(shape, lambda i, last: (0,) * len(shape)),
    )


def ssm_forward(last, both_proj, near, conv_w, conv_b, gain, dt, cum, cumt, skip, segc, segr):
    length, width = both_proj.shape
    chunks = length // CHUNK
    spec = scan_specs(lambda i: i)
    return pl.pallas_call(
        ssm_fwd_kernel,
        grid_spec=pltpu.PrefetchScalarGridSpec(
            num_scalar_prefetch=1,
            grid=(chunks,),
            in_specs=[
                spec["rows"](width),
                spec["rows"](2 * CONV),
                spec["fixed"](CONV, XBC_WIDTH),
                spec["fixed"](1, XBC_WIDTH),
                spec["fixed"](1, SSM_INNER),
                spec["rows"](SSM_HEADS),
                spec["rows"](SSM_HEADS),
                spec["cols"](SSM_HEADS),
                spec["fixed"](1, SSM_HEADS),
                spec["rows"](1),
                spec["cols"](1),
            ],
            out_specs=[
                spec["rows"](SSM_INNER),
                pl.BlockSpec((1, STATE, SSM_INNER), lambda c, last: (c, 0, 0)),
                spec["rows"](XBC_WIDTH),
                spec["rows"](XBC_WIDTH),
                spec["rows"](SSM_INNER),
            ],
            scratch_shapes=[
                pltpu.VMEM((STATE, SSM_INNER), F32),
                pltpu.VMEM((CHUNK + 8, XBC_WIDTH), F32),
            ],
        ),
        out_shape=[
            jax.ShapeDtypeStruct((length, SSM_INNER), F32),
            jax.ShapeDtypeStruct((chunks, STATE, SSM_INNER), F32),
            jax.ShapeDtypeStruct((length, XBC_WIDTH), F32),
            jax.ShapeDtypeStruct((length, XBC_WIDTH), F32),
            jax.ShapeDtypeStruct((length, SSM_INNER), BF16),
        ],
        compiler_params=params(),
        cost_estimate=cost(
            8 * length * SSM_INNER * STATE, 40 * length * SSM_INNER, length * CHUNK * SSM_HEADS
        ),
    )(last, both_proj, near, conv_w, conv_b, gain, dt, cum, cumt, skip, segc, segr)


def ssm_backward(
    last, both_proj, near, conv_w, gain, xbc, slope, dt, cum, cumt, skip, segc, segr, states, outputs,
    grads,
):
    length, width = both_proj.shape
    chunks = length // CHUNK
    end = chunks - 1
    spec = scan_specs(lambda i: end - i)
    return pl.pallas_call(
        ssm_bwd_kernel,
        grid_spec=pltpu.PrefetchScalarGridSpec(
            num_scalar_prefetch=1,
            grid=(chunks,),
            in_specs=[
                spec["rows"](width),
                spec["rows"](2 * CONV),
                spec["fixed"](CONV, XBC_WIDTH),
                spec["fixed"](1, SSM_INNER),
                spec["rows"](XBC_WIDTH),
                spec["rows"](XBC_WIDTH),
                spec["rows"](SSM_HEADS),
                spec["rows"](SSM_HEADS),
                spec["cols"](SSM_HEADS),
                spec["fixed"](1, SSM_HEADS),
                spec["rows"](1),
                spec["cols"](1),
                pl.BlockSpec((1, STATE, SSM_INNER), lambda i, last: (end - i, 0, 0)),
                pl.BlockSpec(
                    (1, STATE, SSM_INNER), lambda i, last: (jnp.minimum(end - i + 1, end), 0, 0)
                ),
                spec["rows"](SSM_INNER),
                spec["rows"](grads.shape[1]),
            ],
            out_specs=[
                spec["rows"](width),
                spec["rows"](2 * LANES),
                pl.BlockSpec((1, 8, LANES), lambda i, last: (end - i, 0, 0)),
                spec["fixed"](8, XBC_WIDTH),
            ],
            scratch_shapes=[
                pltpu.VMEM((STATE, SSM_INNER), F32),
                pltpu.VMEM((CHUNK, SSM_INNER), F32),
                pltpu.VMEM((CHUNK + 8, XBC_WIDTH), F32),
            ],
        ),
        out_shape=[
            jax.ShapeDtypeStruct((length, width), BF16),
            jax.ShapeDtypeStruct((length, 2 * LANES), F32),
            jax.ShapeDtypeStruct((chunks, 8, LANES), F32),
            jax.ShapeDtypeStruct((8, XBC_WIDTH), F32),
        ],
        compiler_params=params(),
        cost_estimate=cost(
            24 * length * SSM_INNER * STATE, 60 * length * SSM_INNER, length * CHUNK * SSM_HEADS
        ),
    )(
        last, both_proj, near, conv_w, gain, xbc, slope, dt, cum, cumt, skip, segc, segr, states, states,
        outputs, grads,
    )


def neighbours(segment):
    length = segment.shape[0]
    columns = []
    for d in range(CONV):
        earlier = jnp.pad(segment, (d, 0), constant_values=-1)[:length]
        columns.append(earlier == segment)
    for d in range(CONV):
        later = jnp.pad(segment, (0, d), constant_values=-1)[d:]
        columns.append(later == segment)
    return jnp.stack(columns, axis=1).astype(F32)


def rows_kernel(counts, lo_ref, hi_ref, ids_ref, *rest):
    step = pl.program_id(0)
    g_refs, (o_ref, wide) = rest[:-2], rest[-2:]
    group = wide.shape[0] // LISTS

    @pl.when(step == 0)
    def _():
        o_ref[...] = jnp.zeros_like(o_ref)

    before = 0
    for count, g_ref in zip(counts, g_refs):

        @pl.when((step >= before) & (step < before + count))
        def _(g_ref=g_ref):
            wide[...] = g_ref[...].astype(F32)

        before = before + count
    for q in range(LISTS):
        at = step * LISTS + q
        low, high = lo_ref[at], hi_ref[at]

        def one(j, at=at, q=q):
            o_ref[pl.ds(ids_ref[at * group + j], 1), :] += wide[pl.ds(q * group + j, 1), :]

        def eight(k, carry, one=one, low=low):
            for u in range(8):
                one(low + 8 * k + u)
            return carry

        def rest_of(j, carry, one=one):
            one(j)
            return carry

        eights = (high - low) // 8
        lax.fori_loop(0, eights, eight, 0)
        lax.fori_loop(low + 8 * eights, high, rest_of, 0)


def rows_by_token(local_ids, grads, shard_rows, group):
    width = grads[0].shape[1]
    counts = [g.shape[0] // (LISTS * group) for g in grads]
    lists = local_ids.reshape(-1, group)
    low = jnp.sum((lists < 0).astype(jnp.int32), axis=1)
    high = jnp.sum((lists < shard_rows).astype(jnp.int32), axis=1)
    specs, before = [], 0
    for count in counts:
        specs.append(
            pl.BlockSpec(
                (LISTS * group, width),
                lambda i, lo, hi, ids, before=before, count=count: (
                    jnp.clip(i - before, 0, count - 1),
                    0,
                ),
            )
        )
        before = before + count
    return pl.pallas_call(
        functools.partial(rows_kernel, counts),
        grid_spec=pltpu.PrefetchScalarGridSpec(
            num_scalar_prefetch=3,
            grid=(before,),
            in_specs=specs,
            out_specs=pl.BlockSpec((shard_rows, width), lambda i, lo, hi, ids: (0, 0)),
            scratch_shapes=[pltpu.VMEM((LISTS * group, width), F32)],
        ),
        out_shape=jax.ShapeDtypeStruct((shard_rows, width), F32),
        compiler_params=params(),
        cost_estimate=cost(before * group * width * LANES, before * group * width * 8),
    )(low, high, local_ids, *grads)


def split_nn(left, right):
    left_high, left_rest = split(left)
    right_high, right_rest = split(right)
    return dot_nn(left_high, right_high) + dot_nn(left_rest, right_high) + dot_nn(left_high, right_rest)


def rotate_kernel(l_ref, g_ref, r_ref, o_ref):
    grad = g_ref[...].reshape(D, BLOCK_COLS)
    left_high, left_rest = split(l_ref[0])
    part = dot_nn(left_high, grad) + dot_nn(left_rest, grad)
    o_ref[0] = split_nn(part, r_ref[0])


def rotate_blocks(left_basis, grad_whole, right_basis):
    slots, depth, _ = left_basis.shape
    rows = grad_whole.shape[0]
    return pl.pallas_call(
        rotate_kernel,
        grid=(slots,),
        in_specs=[
            pl.BlockSpec((1, depth, D), lambda k: (k, 0, 0)),
            pl.BlockSpec((rows, 1, depth, BLOCK_COLS), lambda k: (0, k, 0, 0)),
            pl.BlockSpec((1, BLOCK_COLS, BLOCK_COLS), lambda k: (k, 0, 0)),
        ],
        out_specs=pl.BlockSpec((1, depth, BLOCK_COLS), lambda k: (k, 0, 0)),
        out_shape=jax.ShapeDtypeStruct((slots, depth, BLOCK_COLS), F32),
        compiler_params=params(),
        cost_estimate=cost(6 * slots * depth * D * BLOCK_COLS, slots * depth * D * 5),
    )(left_basis, grad_whole, right_basis)


def step_kernel(scale_ref, rot_ref, m_ref, v_ref, l_ref, r_ref, mo_ref, vo_ref, u_ref):
    rotated = rot_ref[0] * scale_ref[0]
    first_new = soap_first * m_ref[0] + (1.0 - soap_first) * rotated
    second_new = soap_second * v_ref[0] + (1.0 - soap_second) * rotated * rotated
    mo_ref[0], vo_ref[0] = first_new, second_new
    direction = (first_new / scale_ref[1]) / (jnp.sqrt(second_new / scale_ref[2]) + adam_eps)
    turned = split_nn(direction, r_ref[0].T).astype(BF16)
    left_high, left_rest = split(l_ref[0])
    update = dot_nn(left_high.T, turned) + dot_nn(left_rest.T, turned)
    u_ref[0] = update.astype(BF16)


def step_blocks(scales, rotated, block_first, block_second, left_basis, right_basis):
    slots, depth, _ = left_basis.shape
    own = pl.BlockSpec((1, depth, BLOCK_COLS), lambda k: (k, 0, 0))
    small = jax.ShapeDtypeStruct((slots, depth, BLOCK_COLS), F32)
    return pl.pallas_call(
        step_kernel,
        grid=(slots,),
        in_specs=[
            pl.BlockSpec(memory_space=pltpu.SMEM),
            own,
            own,
            own,
            pl.BlockSpec((1, depth, D), lambda k: (k, 0, 0)),
            pl.BlockSpec((1, BLOCK_COLS, BLOCK_COLS), lambda k: (k, 0, 0)),
        ],
        out_specs=[own, own, pl.BlockSpec((1, D, BLOCK_COLS), lambda k: (k, 0, 0))],
        out_shape=[small, small, jax.ShapeDtypeStruct((slots, D, BLOCK_COLS), BF16)],
        compiler_params=params(),
        cost_estimate=cost(6 * slots * depth * D * BLOCK_COLS, slots * depth * D * 7),
    )(scales, rotated, block_first, block_second, left_basis, right_basis)


def to_peers(axis, extent, place, src, box, send_sem, recv_sem):
    copies = []
    for k in range(1, extent):
        peer = list(place)
        peer[axis] = lax.rem(place[axis] + k, extent)
        copies.append(
            pltpu.make_async_remote_copy(
                src_ref=src,
                dst_ref=box.at[place[axis]],
                send_sem=send_sem.at[k],
                recv_sem=recv_sem.at[k],
                device_id=tuple(peer),
                device_id_type=MESH,
            )
        )
    return copies


def greet_peers(axes, place):
    barrier = pltpu.get_barrier_semaphore()
    count = 0
    for axis, extent in axes:
        for k in range(1, extent):
            peer = list(place)
            peer[axis] = lax.rem(place[axis] + k, extent)
            pl.semaphore_signal(barrier, inc=1, device_id=tuple(peer), device_id_type=MESH)
            count += 1
    pl.semaphore_wait(barrier, count)


def total_kernel(rows, cols, x_ref, o_ref, col_box, row_box, col_send, col_recv, row_send, row_recv):
    place = (lax.axis_index("row"), lax.axis_index("col"))
    greet_peers(((0, rows), (1, cols)), place)
    total = x_ref[...]
    for axis, extent, box, send_sem, recv_sem in (
        (1, cols, col_box, col_send, col_recv),
        (0, rows, row_box, row_send, row_recv),
    ):
        o_ref[...] = total
        box[place[axis]] = total
        copies = to_peers(axis, extent, place, o_ref, box, send_sem, recv_sem)
        for copy in copies:
            copy.start()
        for copy in copies:
            copy.wait()
        total = jnp.sum(box[...], axis=0)
    o_ref[...] = total


def total_over_all(values, rows, cols, collective_id):
    dma = pltpu.SemaphoreType.DMA
    return pl.pallas_call(
        functools.partial(total_kernel, rows, cols),
        in_specs=[pl.BlockSpec(memory_space=pltpu.VMEM)],
        out_specs=pl.BlockSpec(memory_space=pltpu.VMEM),
        out_shape=jax.ShapeDtypeStruct(values.shape, F32),
        scratch_shapes=[
            pltpu.VMEM((cols,) + values.shape, F32),
            pltpu.VMEM((rows,) + values.shape, F32),
            dma((cols,)),
            dma((cols,)),
            dma((rows,)),
            dma((rows,)),
        ],
        compiler_params=params(collective_id=collective_id, has_side_effects=True),
        cost_estimate=cost(rows * cols * values.size, rows * cols * values.size * 4),
    )(values)


def ring_bits(rows, cols):
    bits = []
    for axis, extent in ((0, rows), (1, cols)):
        bit = extent // 2
        while bit >= 1:
            bits.append((axis, bit))
            bit = bit // 2
    return bits


def scatter_orders(rows, cols):
    bits = ring_bits(rows, cols)
    row_bits = [b for b in reversed(bits) if b[0] == 0]
    col_bits = [b for b in reversed(bits) if b[0] == 1]
    return col_bits + row_bits, col_bits[:1] + col_bits[1:][::-1] + row_bits


def tail_kernel(rows, cols, slots, g_ref, p_ref, v_ref, whole_ref, tok_ref, vec_ref, own, *rest):
    bits = ring_bits(rows, cols)
    stages = len(bits)
    row_bits = [b for b in bits if b[0] == 0]
    col_bits = [b for b in bits if b[0] == 1]
    boxes, rest = rest[:stages], rest[stages:]
    vec_box, vec_sum, send_sem, recv_sem, own_sem = rest[:5]
    join_send, join_recv, tok_send, tok_recv, tok_own, vec_send, vec_recv = rest[5:]
    place = (lax.axis_index("row"), lax.axis_index("col"))
    half = whole_ref.shape[-2] // 2
    orders = scatter_orders(rows, cols)

    def side(which):
        axis, bit = which
        return place[axis] // bit % 2

    def partner(which):
        axis, bit = which
        moved = place[axis] + bit - 2 * bit * side(which)
        return (moved, place[1]) if axis == 0 else (place[0], moved)

    def remote(src, dst, send, recv, which):
        return pltpu.make_async_remote_copy(
            src_ref=src,
            dst_ref=dst,
            send_sem=send,
            recv_sem=recv,
            device_id=partner(which),
            device_id_type=MESH,
        )

    barrier = pltpu.get_barrier_semaphore()
    for which in bits:
        pl.semaphore_signal(barrier, inc=1, device_id=partner(which), device_id_type=MESH)
    pl.semaphore_wait(barrier, stages)
    units = [(slot, h) for slot in range(slots) for h in range(2)]

    def pick(ref, before, which, side_of, after):
        at = before.index(which)
        return ref.at[(slice(None),) * at + (side_of,) + (slice(None),) * (len(before) - at - 1) + after]

    def part(slot, h, side_of):
        return pick(g_ref, bits, orders[h][0], side_of, (slot, slice(h * half, (h + 1) * half)))

    def cut(stage, u, side_of):
        order = orders[units[u][1]]
        left = [b for b in bits if b not in order[: stage + 1]]
        return pick(boxes[stage].at[u], left, order[stage + 1], side_of, ())

    def send(stage, u):
        slot, h = units[u]
        which = orders[h][stage]
        other = 1 - side(which)
        return remote(
            part(slot, h, other) if stage == 0 else cut(stage - 1, u, other),
            boxes[stage].at[u],
            send_sem.at[stage, u],
            recv_sem.at[stage, u],
            which,
        )

    def keep(u):
        slot, h = units[u]
        return pltpu.make_async_copy(part(slot, h, side(orders[h][0])), own.at[u], own_sem.at[u])

    def joined(ref, order, of_bits, stage, after):
        at = tuple(slice(None) if b in order[:stage] else side(b) for b in of_bits)
        return ref.at[at + after]

    def join(stage, u):
        slot, h = units[u]
        region = joined(whole_ref, row_bits, row_bits, stage, (slot, slice(h * half, (h + 1) * half)))
        return remote(region, region, join_send.at[stage, u], join_recv.at[stage, u], row_bits[stage])

    def tok(stage, h):
        order = (orders[h][1 : len(col_bits)] + orders[h][:1])
        region = joined(tok_ref, order, col_bits, stage, (h,))
        return remote(
            p_ref.at[h] if stage == 0 else region, region, tok_send.at[stage, h],
            tok_recv.at[stage, h], order[stage],
        )

    def tok_keep():
        region = joined(tok_ref, [], col_bits, 0, ())
        return pltpu.make_async_copy(p_ref, region, tok_own)

    def vec(stage):
        return remote(
            vec_sum.at[stage], vec_box.at[stage], vec_send.at[stage], vec_recv.at[stage], bits[stage]
        )

    sent = []

    def start(copy):
        copy.start()
        sent.append(copy)
        return copy

    flying = {}
    vec_sum[0] = v_ref[...]
    flying["vec", 0] = start(vec(0))
    for u in range(len(units)):
        flying[0, u] = start(send(0, u))
        keep(u).start()
        if u == 1:
            tok_keep().start()
            for h in range(2):
                flying["tok", 0, h] = start(tok(0, h))
    steps = slots + stages + len(row_bits) - 1
    tok_at = [steps - 1 - 2 * (len(col_bits) - 1 - k) for k in range(len(col_bits))]
    for t in range(steps):
        if t < stages:
            flying["vec", t].wait_recv()
            if t + 1 < stages:
                vec_sum[t + 1] = vec_sum[t] + vec_box[t]
                flying["vec", t + 1] = start(vec(t + 1))
            else:
                vec_ref[...] = vec_sum[t] + vec_box[t]
        for k, at in enumerate(tok_at):
            if at == t:
                if k == 0:
                    tok_keep().wait()
                for h in range(2):
                    flying["tok", k, h].wait_recv()
                    if k + 1 < len(col_bits):
                        flying["tok", k + 1, h] = start(tok(k + 1, h))
        for stage in reversed(range(stages + len(row_bits))):
            slot = t - stage
            if not 0 <= slot < slots:
                continue
            for h in range(2):
                u = 2 * slot + h
                if stage >= stages:
                    flying["join", stage - stages, u].wait_recv()
                    if stage - stages + 1 < len(row_bits):
                        flying["join", stage - stages + 1, u] = start(join(stage - stages + 1, u))
                    continue
                flying[stage, u].wait_recv()
                box = boxes[stage].at[u]
                if stage == 0:
                    keep(u).wait()
                    held = own.at[u]
                else:
                    held = cut(stage - 1, u, side(orders[h][stage]))
                if stage == stages - 1:
                    total = held[...].astype(F32) + box[...].astype(F32)
                    mine = joined(
                        whole_ref, [], row_bits, 0, (slot, slice(h * half, (h + 1) * half))
                    )
                    mine[...] = total.astype(BF16)
                    flying["join", 0, u] = start(join(0, u))
                    continue
                extents = box.shape[:-2]

                def add(k, carry, box=box, held=held, extents=extents):
                    at = []
                    for extent in reversed(extents):
                        at.append(k % extent)
                        k = k // extent
                    at = tuple(reversed(at))
                    box[at] = (held[at].astype(F32) + box[at].astype(F32)).astype(BF16)
                    return carry

                lax.fori_loop(0, 2 ** len(extents), add, 0)
                flying[stage + 1, u] = start(send(stage + 1, u))
    for copy in sent:
        copy.wait_send()


def tail_exchange(grads, pieces, vectors, rows, cols, collective_id):
    _, nslots, depth, _ = grads.shape
    slots = nslots // cols
    bits = ring_bits(rows, cols)
    stages = len(bits)
    row_stages, col_stages = (rows - 1).bit_length(), (cols - 1).bit_length()
    units, half = 2 * slots, depth // 2
    count, width = pieces.shape
    boxes = [
        pltpu.VMEM((units,) + (2,) * (stages - s - 1) + (half, BLOCK_COLS), BF16)
        for s in range(stages)
    ]
    vec_shape = (stages,) + vectors.shape
    whole, tokens, total = pl.pallas_call(
        functools.partial(tail_kernel, rows, cols, slots),
        in_specs=[
            pl.BlockSpec(memory_space=pl.ANY),
            pl.BlockSpec(memory_space=pl.ANY),
            pl.BlockSpec(memory_space=pltpu.VMEM),
        ],
        out_specs=[
            pl.BlockSpec(memory_space=pltpu.VMEM),
            pl.BlockSpec(memory_space=pl.ANY),
            pl.BlockSpec(memory_space=pltpu.VMEM),
        ],
        out_shape=[
            jax.ShapeDtypeStruct((2,) * row_stages + (slots, depth, BLOCK_COLS), BF16),
            jax.ShapeDtypeStruct((2,) * col_stages + (2, count // 2, width), BF16),
            jax.ShapeDtypeStruct(vectors.shape, F32),
        ],
        scratch_shapes=[pltpu.VMEM(boxes[0].shape, BF16)]
        + boxes
        + [
            pltpu.VMEM(vec_shape, F32),
            pltpu.VMEM(vec_shape, F32),
            pltpu.SemaphoreType.DMA((stages, units)),
            pltpu.SemaphoreType.DMA((stages, units)),
            pltpu.SemaphoreType.DMA((units,)),
            pltpu.SemaphoreType.DMA((row_stages, units)),
            pltpu.SemaphoreType.DMA((row_stages, units)),
            pltpu.SemaphoreType.DMA((col_stages, 2)),
            pltpu.SemaphoreType.DMA((col_stages, 2)),
            pltpu.SemaphoreType.DMA,
            pltpu.SemaphoreType.DMA((stages,)),
            pltpu.SemaphoreType.DMA((stages,)),
        ],
        compiler_params=params(collective_id=collective_id, has_side_effects=True),
        cost_estimate=cost(rows * nslots * depth * BLOCK_COLS, rows * nslots * depth * BLOCK_COLS * 6),
    )(
        grads.reshape((2,) * stages + (slots, depth, BLOCK_COLS)),
        pieces.reshape(2, count // 2, width),
        vectors,
    )
    return whole.reshape(rows, slots, depth, BLOCK_COLS), tokens.reshape(cols * count, width), total


def doubling(place, bits):
    def side(which):
        axis, bit = which
        return place[axis] // bit % 2

    def partner(which):
        axis, bit = which
        moved = place[axis] + bit - 2 * bit * side(which)
        return (moved, place[1]) if axis == 0 else (place[0], moved)

    return side, partner


def greet(bits, partner):
    barrier = pltpu.get_barrier_semaphore()
    for which in bits:
        pl.semaphore_signal(barrier, inc=1, device_id=partner(which), device_id_type=MESH)
    pl.semaphore_wait(barrier, len(bits))


def joiner(side, partner, src, out, of_bits, order, after, send_sem, recv_sem):
    def copy(k):
        at = tuple(slice(None) if b in order[:k] else side(b) for b in of_bits)
        region = out.at[at + after]
        return pltpu.make_async_remote_copy(
            src_ref=src if k == 0 else region,
            dst_ref=region,
            send_sem=send_sem.at[k],
            recv_sem=recv_sem.at[k],
            device_id=partner(order[k]),
            device_id_type=MESH,
        )

    return copy


def front_kernel(rows, cols, i_ref, t_ref, w_ref, io_ref, to_ref, wo_ref, *sems):
    bits = ring_bits(rows, cols)
    row_bits = [b for b in bits if b[0] == 0]
    col_bits = [b for b in bits if b[0] == 1]
    place = (lax.axis_index("row"), lax.axis_index("col"))
    side, partner = doubling(place, bits)
    i_send, i_recv, t_send, t_recv, w_send, w_recv, keep_sem = sems
    greet(bits, partner)
    own_row, own_col = tuple(side(b) for b in row_bits), tuple(side(b) for b in col_bits)
    keeps = [
        pltpu.make_async_copy(i_ref, io_ref.at[own_row + own_col], keep_sem.at[0]),
        pltpu.make_async_copy(t_ref, to_ref.at[own_col], keep_sem.at[1]),
        pltpu.make_async_copy(w_ref, wo_ref.at[own_row], keep_sem.at[2]),
    ]
    orders = [o[1 : len(col_bits)] + o[:1] for o in scatter_orders(rows, cols)]
    jobs = {}
    jobs["i", 0] = (joiner(side, partner, i_ref, io_ref, bits, bits[::-1], (), i_send, i_recv), 0, 1)
    for p in range(t_ref.shape[0]):
        copy = joiner(
            side, partner, t_ref.at[p], to_ref, col_bits, orders[p % 2], (p,), t_send.at[p], t_recv.at[p]
        )
        jobs["t", p] = (copy, 1 + p // 2, 3)
    for p in range(w_ref.shape[0]):
        copy = joiner(
            side, partner, w_ref.at[p], wo_ref, row_bits, row_bits, (p,), w_send.at[p], w_recv.at[p]
        )
        jobs["w", p] = (copy, p, 1)
    run_joins(jobs, {"i": len(bits), "t": len(col_bits), "w": len(row_bits)}, keeps)


def run_joins(jobs, stages, keeps, done=None):
    for copy in keeps:
        copy.start()
    sent = []
    for copy, _, _ in jobs.values():
        sent.append(copy(0))
        sent[-1].start()
    for copy in keeps:
        copy.wait()
    ends = [at + every * (stages[name[0]] - 1) for name, (_, at, every) in jobs.items()]
    for t in range(max(ends) + 1):
        for name, (copy, at, every) in jobs.items():
            k = (t - at) // every
            if t < at or (t - at) % every or k >= stages[name[0]]:
                continue
            copy(k).wait_recv()
            if k + 1 < stages[name[0]]:
                sent.append(copy(k + 1))
                sent[-1].start()
            elif done is not None:
                done(name[1])
    for copy in sent:
        copy.wait_send()


def front_exchange(ints, table_low, weights_low, rows, cols, collective_id):
    row_stages, col_stages = (rows - 1).bit_length(), (cols - 1).bit_length()
    parts = TABLE_PARTS
    shard, width = table_low.shape
    slots = weights_low.shape[0]
    dma = pltpu.SemaphoreType.DMA
    ints = ints.reshape(-1, LANES)
    outs = pl.pallas_call(
        functools.partial(front_kernel, rows, cols),
        in_specs=[pl.BlockSpec(memory_space=pl.ANY)] * 3,
        out_specs=[pl.BlockSpec(memory_space=pltpu.VMEM)] * 3,
        out_shape=[
            jax.ShapeDtypeStruct((2,) * (row_stages + col_stages) + ints.shape, jnp.int32),
            jax.ShapeDtypeStruct((2,) * col_stages + (parts, shard // parts, width), BF16),
            jax.ShapeDtypeStruct((2,) * row_stages + weights_low.shape, BF16),
        ],
        scratch_shapes=[
            dma((row_stages + col_stages,)),
            dma((row_stages + col_stages,)),
            dma((parts, col_stages)),
            dma((parts, col_stages)),
            dma((slots, row_stages)),
            dma((slots, row_stages)),
            dma((3,)),
        ],
        compiler_params=params(collective_id=collective_id, has_side_effects=True),
        cost_estimate=cost(1 << 20, cols * shard * width * 4),
    )(ints, table_low.reshape(parts, shard // parts, width), weights_low)
    return (
        outs[0].reshape(rows, cols, -1),
        outs[1].reshape(cols * shard, width),
        outs[2].reshape((rows,) + weights_low.shape),
    )


def weights_kernel(rows, cols, w_ref, o_ref, box, send_sem, recv_sem, keep_sem, out_sem):
    bits = ring_bits(rows, cols)
    col_bits = [b for b in bits if b[0] == 1]
    place = (lax.axis_index("row"), lax.axis_index("col"))
    side, partner = doubling(place, bits)
    greet(col_bits, partner)
    own = tuple(side(b) for b in col_bits)
    slots, half = w_ref.shape[1], w_ref.shape[2] // 2
    orders = [o[1 : len(col_bits)] + o[:1] for o in scatter_orders(rows, cols)]
    keeps = [
        pltpu.make_async_copy(w_ref, box.at[(slice(None),) + own], keep_sem),
    ]
    jobs = {}
    outs = []

    def done(u):
        part = (slice(None),) * (1 + len(col_bits)) + parts[u]
        outs.append(pltpu.make_async_copy(box.at[part], o_ref.at[part], out_sem.at[u]))
        outs[-1].start()

    parts = [(slot, slice(h * half, (h + 1) * half)) for slot in range(slots) for h in range(2)]
    for slot in range(slots):
        for h in range(2):
            part = (slot, slice(h * half, (h + 1) * half))
            u = 2 * slot + h

            def copy(k, part=part, order=orders[h], u=u):
                at = tuple(slice(None) if b in order[:k] else side(b) for b in col_bits)
                region = box.at[(slice(None),) + at + part]
                return pltpu.make_async_remote_copy(
                    src_ref=w_ref.at[(slice(None),) + part] if k == 0 else region,
                    dst_ref=region,
                    send_sem=send_sem.at[u, k],
                    recv_sem=recv_sem.at[u, k],
                    device_id=partner(order[k]),
                    device_id_type=MESH,
                )

            jobs["w", u] = (copy, slot, 1)
    run_joins(jobs, {"w": len(col_bits)}, keeps, done)
    for copy in outs:
        copy.wait()


def gather_weights(weights, rows, cols, collective_id):
    _, slots, depth, width = weights.shape
    col_stages = (cols - 1).bit_length()
    dma = pltpu.SemaphoreType.DMA
    shape = (rows,) + (2,) * col_stages + (slots, depth, width)
    out = pl.pallas_call(
        functools.partial(weights_kernel, rows, cols),
        in_specs=[pl.BlockSpec(memory_space=pl.ANY)],
        out_specs=pl.BlockSpec(memory_space=pl.ANY),
        out_shape=jax.ShapeDtypeStruct(shape, BF16),
        scratch_shapes=[
            pltpu.VMEM(shape, BF16),
            dma((2 * slots, col_stages)),
            dma((2 * slots, col_stages)),
            dma,
            dma((2 * slots,)),
        ],
        compiler_params=params(collective_id=collective_id, has_side_effects=True),
        cost_estimate=cost(1 << 20, 4 * cols * weights.size),
    )(weights)
    return out.reshape(rows, cols * slots, depth, width)


def columns_kernel(cols, x_ref, o_ref, send_sem, recv_sem):
    place = (lax.axis_index("row"), lax.axis_index("col"))
    greet_peers(((1, cols),), place)
    o_ref[place[1]] = x_ref[...]
    copies = to_peers(1, cols, place, x_ref, o_ref, send_sem, recv_sem)
    for copy in copies:
        copy.start()
    for copy in copies:
        copy.wait()


def gather_columns(values, cols, collective_id):
    dma = pltpu.SemaphoreType.DMA
    return pl.pallas_call(
        functools.partial(columns_kernel, cols),
        in_specs=[pl.BlockSpec(memory_space=pltpu.VMEM)],
        out_specs=pl.BlockSpec(memory_space=pltpu.VMEM),
        out_shape=jax.ShapeDtypeStruct((cols,) + values.shape, values.dtype),
        scratch_shapes=[dma((cols,)), dma((cols,))],
        compiler_params=params(collective_id=collective_id, has_side_effects=True),
        cost_estimate=cost(1024, cols * values.size * 4),
    )(values)


def rows_gather_kernel(rows, cols, x_ref, o_ref, send_sem, recv_sem):
    col_bits = [b for b in ring_bits(rows, cols) if b[0] == 1]
    place = (lax.axis_index("row"), lax.axis_index("col"))
    side, partner = doubling(place, col_bits)
    orders = [o[1 : len(col_bits)] + o[:1] for o in scatter_orders(rows, cols)]
    greet(col_bits, partner)
    own = tuple(side(b) for b in col_bits)
    jobs = {}
    for h in range(2):
        o_ref[own + (h,)] = x_ref[h]
        copy = joiner(
            side, partner, x_ref.at[h], o_ref, col_bits, orders[h], (h,), send_sem.at[h], recv_sem.at[h]
        )
        jobs["x", h] = (copy, 0, 1)
    run_joins(jobs, {"x": len(col_bits)}, [])


def gather_rows(values, rows, cols, collective_id):
    count, width = values.shape
    stages = (cols - 1).bit_length()
    dma = pltpu.SemaphoreType.DMA
    out = pl.pallas_call(
        functools.partial(rows_gather_kernel, rows, cols),
        in_specs=[pl.BlockSpec(memory_space=pltpu.VMEM)],
        out_specs=pl.BlockSpec(memory_space=pltpu.VMEM),
        out_shape=jax.ShapeDtypeStruct((2,) * stages + (2, count // 2, width), values.dtype),
        scratch_shapes=[dma((2, stages)), dma((2, stages))],
        compiler_params=params(collective_id=collective_id, has_side_effects=True),
        cost_estimate=cost(1024, cols * values.size * 4),
    )(values.reshape(2, count // 2, width))
    return out.reshape(cols * count, width)


def scatter_columns_kernel(rows, cols, x_ref, o_ref, *rest):
    bits = [b for b in ring_bits(rows, cols) if b[0] == 1]
    stages = len(bits)
    boxes, (send_sem, recv_sem) = rest[:stages], rest[stages:]
    place = (lax.axis_index("row"), lax.axis_index("col"))
    side, partner = doubling(place, bits)
    orders = [o[:stages] for o in scatter_orders(rows, cols)]
    greet(bits, partner)

    def held(stage, h, side_of):
        left = [b for b in bits if b not in orders[h][:stage]]
        at = tuple(side_of if b == orders[h][stage] else slice(None) for b in left)
        return x_ref.at[at + (h,)] if stage == 0 else boxes[stage - 1].at[(h,) + at]

    def send(stage, h):
        which = orders[h][stage]
        return pltpu.make_async_remote_copy(
            src_ref=held(stage, h, 1 - side(which)),
            dst_ref=boxes[stage].at[h],
            send_sem=send_sem.at[stage, h],
            recv_sem=recv_sem.at[stage, h],
            device_id=partner(which),
            device_id_type=MESH,
        )

    sent = []
    for stage in range(stages + 1):
        for h in range(2):
            if stage > 0:
                sent[2 * (stage - 1) + h].wait_recv()
                total = held(stage - 1, h, side(orders[h][stage - 1]))[...] + boxes[stage - 1][h]
                if stage == stages:
                    o_ref[h] = total
                else:
                    boxes[stage - 1][h] = total
            if stage < stages:
                sent.append(send(stage, h))
                sent[-1].start()
    for copy in sent:
        copy.wait_send()


def scatter_columns(values, rows, cols, collective_id):
    count, width = values.shape[0] // cols, values.shape[1]
    stages = (cols - 1).bit_length()
    dma = pltpu.SemaphoreType.DMA
    out = pl.pallas_call(
        functools.partial(scatter_columns_kernel, rows, cols),
        in_specs=[pl.BlockSpec(memory_space=pltpu.VMEM)],
        out_specs=pl.BlockSpec(memory_space=pltpu.VMEM),
        out_shape=jax.ShapeDtypeStruct((2, count // 2, width), F32),
        scratch_shapes=[
            pltpu.VMEM((2,) + (2,) * (stages - s - 1) + (count // 2, width), F32)
            for s in range(stages)
        ]
        + [dma((stages, 2)), dma((stages, 2))],
        compiler_params=params(collective_id=collective_id, has_side_effects=True),
        cost_estimate=cost(values.size, values.size * 8),
    )(values.reshape((2,) * stages + (2, count // 2, width)))
    return out.reshape(count, width)


def piece_order(rows):
    order = [0] + [k for pair in range(1, rows // 2 + 1) for k in (pair, rows - pair)][: rows - 1]
    return order[: rows // 4], order[rows // 4 :]


def exchange_rows(values, rows):
    row = lax.axis_index("row")
    width = values.shape[1] // rows
    arrived = []
    for group in piece_order(rows):
        parts = []
        for k in group:
            part = lax.dynamic_slice_in_dim(values, (row + k) % rows * width, width, 1)
            if k > 0:
                part = lax.ppermute(part, "row", [(r, (r + k) % rows) for r in range(rows)])
            parts.append(part)
        arrived.append(jnp.concatenate(parts, axis=0))
    return arrived


def adam_step(weights, grads, first, second, steps_done, decay, rate):
    first_new = adam_first * first + (1.0 - adam_first) * grads
    second_new = adam_second * second + (1.0 - adam_second) * grads * grads
    direction = (
        first_new
        / (1.0 - adam_first**steps_done)
        / (jnp.sqrt(second_new / (1.0 - adam_second**steps_done)) + adam_eps)
    )
    return (weights - rate * (direction + decay * weights), first_new, second_new)


def body(
    rows,
    cols,
    token_ids,
    segment_ids,
    loss_positions,
    loss_targets,
    loss_valid,
    block_owner,
    step_count,
    block_weights,
    block_first,
    block_second,
    left_basis,
    right_basis,
    table,
    table_first,
    table_second,
    vector_params,
    vector_first,
    vector_second,
):
    col_index = lax.axis_index("col")
    tokens = token_ids[0]
    segment = segment_ids[0]
    length = tokens.shape[0]
    in_cols = 2 * SSM_INNER + 2 * STATE
    in_blocks = (in_cols + (HEADS + 2 * KV_HEADS) * HEAD_DIM) // BLOCK_COLS
    branch_blocks = (SSM_INNER + HEADS * HEAD_DIM) // BLOCK_COLS
    gate_blocks = 2 * FF // BLOCK_COLS
    down_blocks = FF // BLOCK_COLS
    branch_at = in_blocks
    gate_at = branch_at + branch_blocks
    down_at = gate_at + gate_blocks
    nblocks = block_owner.shape[0]
    depth = block_weights.shape[1]
    shard_rows = table.shape[0]

    row_index = lax.axis_index("row")
    devices = rows * cols
    count_rows = loss_positions.shape[1]
    table_low = table.astype(BF16)
    shard_padded = -(-shard_rows // PAD_ROWS) * PAD_ROWS
    padded = jnp.pad(table_low, ((0, shard_padded - shard_rows), (0, 0)))
    in_order = jnp.sort(tokens)
    repeats = jnp.pad(in_order[1:] == in_order[:-1], (1, 0))
    different = jnp.sort(jnp.where(repeats, NO_TOKEN, in_order))
    token_place = jnp.sum((different[:, None] < tokens[None, :]).astype(jnp.int32), axis=0)
    sent = jnp.concatenate([tokens, different, loss_targets[0], loss_valid[0]])
    ints, table_cols, weight_rows = front_exchange(
        sent, padded, block_weights.astype(BF16), rows, cols, 2
    )
    padded, weight_rows, table_cols = lax.optimization_barrier((padded, weight_rows, table_cols))
    table_rows = lax.all_gather(padded, "row", axis=1, tiled=True)
    token_list = lax.dynamic_index_in_dim(ints, col_index, 1, False)[:, :length].reshape(-1)
    owners = token_list // shard_rows
    looked_up = jnp.take(
        table_cols, token_list + owners * (shard_padded - shard_rows), axis=0, mode="clip"
    )
    looked_up, weight_rows = lax.optimization_barrier((looked_up, weight_rows))
    arrived = lax.all_to_all(
        looked_up.reshape(rows, length, -1), "row", split_axis=0, concat_axis=0, tiled=True
    )
    gathered = gather_weights(weight_rows, rows, cols, 3)
    sorted_ints = ints[:, :, length : 2 * length]
    sorted_all = [
        jnp.stack(
            [
                lax.dynamic_index_in_dim(sorted_ints, (row_index - k) % rows, 0, False)
                for k in part
            ],
            axis=1,
        ).reshape(-1)
        for part in piece_order(rows)
    ]
    sorted_all = jnp.concatenate(sorted_all)
    labels_all = lax.dynamic_index_in_dim(ints, row_index, 0, False)[:, 2 * length :]
    targets_all = labels_all[:, :count_rows].reshape(-1)
    valid_all = labels_all[:, count_rows:].reshape(-1)
    valid_count = jnp.sum(ints[:, :, 2 * length + count_rows :]).astype(F32)

    conv_weight, conv_bias, time_bias, decay_log, skip_gain, mixer_gain, norm_gains, time_proj = (
        unpack(vector_params)
    )
    gain_rows = norm_gains.reshape(3, D)
    time_low = time_proj.reshape(D, SSM_HEADS).astype(BF16)
    segc, segr = segment[:, None], segment[None, :]
    chunks = length // CHUNK
    last_docs = segment.reshape(chunks, CHUNK)[:, CHUNK - 1]
    cosine, sine = rope_tables(length)

    embedded, normed = embed_and_norm(arrived, gain_rows[0])
    both_proj = project(normed, gathered, block_owner, 0, in_blocks)
    time_raw = jnp.dot(normed, time_low, preferred_element_type=F32)

    def steps_of(time_in, bias_in, decay_in):
        step_size = jax.nn.softplus(time_in + bias_in[None, :])
        return step_size, step_size * -jnp.exp(decay_in)[None, :]

    (step_size, decays), steps_back = jax.vjp(steps_of, time_raw, time_bias, decay_log)
    earlier = jnp.tril(jnp.ones((CHUNK, CHUNK), F32))
    decays_cut = decays.reshape(chunks, CHUNK, SSM_HEADS)
    cum = jnp.einsum("ts,csh->cth", earlier, decays_cut, precision=highest).reshape(
        length, SSM_HEADS
    )
    cumt = cum.T
    near = neighbours(segment)
    conv_rows = conv_weight.reshape(CONV, XBC_WIDTH)
    gain_row = mixer_gain.reshape(1, SSM_INNER)
    times = (step_size, cum, cumt, skip_gain[None, :], segc, segr)
    scan_out, states, act_xbc, slope, mixed = ssm_forward(
        last_docs, both_proj, near, conv_rows, conv_bias[None, :], gain_row, *times
    )
    positions = loss_positions[0]
    pos_col = positions[:, None]
    hits = pos_col == jnp.arange(length, dtype=jnp.int32)[None, :]
    chosen, place = hits.astype(BF16), hits.T.astype(BF16)
    seg_col = jnp.sum(jnp.where(hits, segr, 0), axis=1, keepdims=True)
    choose = lambda values: jnp.dot(chosen, values, preferred_element_type=F32).astype(BF16)
    spread_rows = lambda values: jnp.dot(hits.T.astype(F32), values, precision=highest)
    picked_in = (positions, pos_col, seg_col, segr, cosine, sine)
    context = attention_forward(both_proj, *picked_in)
    branch_in = jnp.concatenate([choose(mixed), context], axis=1)
    hidden_one, normed_two = back_then_norm(
        branch_in, gathered, block_owner, branch_at, branch_blocks, choose(embedded), gain_rows[1]
    )
    gate_val, up_val, act_low = project_gate_up(
        normed_two, gathered, block_owner, gate_at, down_blocks
    )
    hidden_two, picked_rows = back_then_norm(
        act_low, gathered, block_owner, down_at, down_blocks, hidden_one, gain_rows[2]
    )
    rows_all = gather_rows(picked_rows, rows, cols, 4)

    logits = jnp.einsum("rd,vd->rv", rows_all, table_rows, preferred_element_type=F32)
    local_target = targets_all - col_index * shard_rows
    places = jnp.arange(shard_padded, dtype=jnp.int32)[None, :]
    onehot = (places == local_target[:, None]) & (places < shard_rows)
    logits = jnp.where(places < shard_rows, logits, -1e30)
    row_top = jnp.max(logits, axis=1)
    row_total = jnp.sum(jnp.exp(logits - row_top[:, None]), axis=1)
    target_logit = jnp.sum(jnp.where(onehot, logits, 0.0), axis=1)
    no_part = jnp.zeros_like(row_top)
    parts = gather_columns(
        jnp.stack([row_top, row_total, target_logit] + [no_part] * 5), cols, 5
    )
    top_all = jnp.max(parts[:, 0], axis=0)
    total_all = jnp.sum(parts[:, 1] * jnp.exp(parts[:, 0] - top_all[None, :]), axis=0)
    target_all = jnp.sum(parts[:, 2], axis=0)
    log_total = top_all + jnp.log(total_all)
    valid_wide = valid_all.astype(F32)
    own_loss = lax.dynamic_slice_in_dim(
        (log_total - target_all) * valid_wide, col_index * count_rows, count_rows
    )
    logit_grad = (
        (jnp.exp(logits - log_total[:, None]) - onehot.astype(F32))
        * (valid_wide / valid_count)[:, None]
    ).astype(BF16)
    rows_part = jnp.einsum("rv,vd->rd", logit_grad, table_rows, preferred_element_type=F32)
    table_loss_grad = jnp.einsum("rv,rd->vd", logit_grad, rows_all, preferred_element_type=F32)
    table_loss_low, rows_part = lax.optimization_barrier((table_loss_grad.astype(BF16), rows_part))
    rows_grad = scatter_columns(rows_part, rows, cols, 6)
    table_loss_mine = lax.psum_scatter(table_loss_low, "row", scatter_dimension=1, tiled=True)
    equal = pos_col == positions[None, :]
    numbers = jnp.arange(count_rows, dtype=jnp.int32)
    again = jnp.any(equal & (numbers[None, :] < numbers[:, None]), axis=1)
    adds = jnp.where(again[:, None], 0.0, equal.astype(F32))
    final_grad = jnp.dot(adds, rows_grad, precision=highest)
    _, final_norm_back = jax.vjp(rms_gain, hidden_two, gain_rows[2])
    hidden_two_grad, gain_final_grad = final_norm_back(final_grad)
    down_in = hidden_two_grad.astype(BF16)
    like = (rows, nblocks, depth, BLOCK_COLS)
    gate_up_grad = project_act_back(
        down_in, gate_val, up_val, gathered, block_owner, down_at, down_blocks
    )
    hidden_one_grad, branch_grad_low, gain_ff_grad = back_through_norm(
        gate_up_grad,
        gathered,
        block_owner,
        gate_at,
        gate_blocks,
        jnp.zeros((count_rows, D), F32),
        hidden_one,
        gain_rows[1],
        hidden_two_grad,
    )
    branch_out_grad = project(branch_grad_low, gathered, block_owner, branch_at, branch_blocks)

    in_grad_low, sums, ends, mixer_vectors = ssm_backward(
        last_docs,
        both_proj,
        near,
        conv_rows,
        gain_row,
        act_xbc,
        slope,
        *times,
        states,
        scan_out,
        spread_rows(branch_out_grad[:, :SSM_INNER]),
    )
    in_grad_low = attention_backward(
        both_proj, *picked_in, branch_out_grad, place, in_grad_low
    )
    sum_y, sum_x, sum_k = (
        sums[:, at : at + SSM_HEADS] for at in (0, LANES, LANES + SSM_HEADS)
    )
    skip_grad = jnp.sum(sum_k, axis=0)
    cum_grad = sum_y.reshape(chunks, CHUNK, SSM_HEADS)
    decays_grad = jnp.einsum("ts,cth->csh", earlier, cum_grad, precision=highest)
    decays_grad = decays_grad + jnp.sum(ends, axis=1)[:, None, :SSM_HEADS]
    time_grad, time_bias_grad, decay_log_grad = steps_back(
        (sum_x, decays_grad.reshape(length, SSM_HEADS))
    )
    time_grad_low = time_grad.astype(BF16)
    grad_time = jnp.einsum("td,th->dh", normed, time_grad_low, preferred_element_type=F32)
    time_part = jnp.einsum("th,dh->td", time_grad_low, time_low, preferred_element_type=F32)
    _, embed_grad, gain_in_grad = back_through_norm(
        in_grad_low[None],
        gathered,
        block_owner,
        0,
        in_blocks,
        time_part,
        embedded,
        gain_rows[0],
        spread_rows(hidden_one_grad),
    )
    placed = (jnp.arange(length, dtype=jnp.int32)[:, None] == token_place[None, :]).astype(BF16)
    embed_sorted = jnp.dot(placed, embed_grad, preferred_element_type=F32).astype(BF16)
    embed_sorted, table_loss_mine, down_in, normed_two, branch_grad_low, normed = (
        lax.optimization_barrier(
            (embed_sorted, table_loss_mine, down_in, normed_two, branch_grad_low, normed)
        )
    )
    early, late = exchange_rows(embed_sorted, rows)
    grad_slots = weight_grad(down_in, act_low[None], block_owner, down_at, like, None)
    grad_slots = weight_grad(normed_two, gate_up_grad, block_owner, gate_at, like, grad_slots)
    early_tokens = lax.all_gather(early, "col", axis=0, tiled=True)
    grad_slots = weight_grad(
        branch_grad_low, branch_in[None], block_owner, branch_at, like, grad_slots
    )
    grad_slots = weight_grad(normed, in_grad_low[None], block_owner, 0, like, grad_slots)
    early_tokens, late, grad_slots = lax.optimization_barrier((early_tokens, late, grad_slots))
    vector_grad = jnp.concatenate(
        [
            mixer_vectors[:CONV].reshape(-1),
            mixer_vectors[CONV],
            time_bias_grad,
            decay_log_grad,
            skip_grad,
            mixer_vectors[CONV + 1, :SSM_INNER],
            gain_in_grad[0],
            gain_ff_grad[0],
            gain_final_grad,
            grad_time.reshape(-1),
            jnp.sum(own_loss)[None],
        ]
    )
    nvec = vector_params.shape[0]
    packed_len = -(-(nvec + 1) // (8 * LANES)) * 8 * LANES
    to_sum = jnp.pad(vector_grad, (0, packed_len - nvec - 1)).reshape(-1, LANES)
    grad_whole, late_tokens, summed = tail_exchange(grad_slots, late, to_sum, rows, cols, 1)
    summed = summed.reshape(-1)
    vector_total, loss_sum = summed[:nvec], summed[nvec]
    table_input_grad = rows_by_token(
        sorted_all - col_index * shard_rows, (early_tokens, late_tokens), shard_rows, length
    )
    table_grad = table_loss_mine[:shard_rows].astype(F32) + table_input_grad
    grad_mine_wide = lax.dynamic_index_in_dim(grad_whole, row_index, 0, False).astype(F32)
    square_part = jnp.sum(grad_mine_wide * grad_mine_wide) + jnp.sum(table_grad * table_grad)
    square_total = total_over_all(jnp.full((8, LANES), square_part), rows, cols, 0)[0, 0]
    rotated = rotate_blocks(left_basis, grad_whole, right_basis)
    mean_loss = loss_sum / valid_count
    grad_norm = jnp.sqrt(square_total + jnp.sum(vector_total * vector_total))
    clip_scale = jnp.minimum(1.0, clip_limit / (grad_norm + 1e-06))
    steps_done = step_count[0].astype(F32)
    scales = jnp.stack(
        [clip_scale, 1.0 - soap_first**steps_done, 1.0 - soap_second**steps_done]
    )
    first_new, second_new, partial_update = step_blocks(
        scales, rotated, block_first, block_second, left_basis, right_basis
    )
    update = lax.psum_scatter(
        partial_update, "row", scatter_dimension=1, tiled=True
    ).astype(F32)
    new_blocks = block_weights - learn_rate * (update + weight_decay * block_weights)
    new_table, table_first_new, table_second_new = adam_step(
        table,
        table_grad * clip_scale,
        table_first,
        table_second,
        steps_done,
        weight_decay,
        learn_rate,
    )
    new_vectors, vector_first_new, vector_second_new = adam_step(
        vector_params,
        vector_total * clip_scale,
        vector_first,
        vector_second,
        steps_done,
        0.0,
        vector_rate,
    )
    return (
        mean_loss,
        grad_norm,
        new_blocks,
        first_new,
        second_new,
        new_table,
        table_first_new,
        table_second_new,
        new_vectors,
        vector_first_new,
        vector_second_new,
    )


def solution(mesh):
    rows, cols = mesh.shape["row"], mesh.shape["col"]
    placed = (
        P(("row", "col"), None),
        P(("row", "col"), None),
        P(("row", "col"), None),
        P(("row", "col"), None),
        P(("row", "col"), None),
        P(),
        P(),
        P("col", "row", None),
        P("col", "row", None),
        P("col", "row", None),
        P("col", "row", None),
        P("col", None, None),
        P("col", "row"),
        P("col", "row"),
        P("col", "row"),
        P(),
        P(),
        P(),
    )
    return jax.shard_map(
        functools.partial(body, rows, cols),
        mesh=mesh,
        in_specs=placed,
        out_specs=(
            P(),
            P(),
            P("col", "row", None),
            P("col", "row", None),
            P("col", "row", None),
            P("col", "row"),
            P("col", "row"),
            P("col", "row"),
            P(),
            P(),
            P(),
        ),
        check_vma=False,
    )
```
